32 devices in a mesh: dp: 8 (over z, x), head: 4 (over y, core).
Axes of the slice: x: 2, y: 2, z: 4, core: 2. Of those that a mesh axis runs over, the one named last changes fastest.
Arguments:
- hidden: bfloat16 [16384, 768], P(('dp', 'head')), may hold values from -6 to 6
- lengths: int32 [8, 3], P('dp'), may hold values from 1 to 1536, as said below
- norm_gain: float32 [768], replicated, may hold values from 0.5 to 1.5
- gate_proj: bfloat16 [768, 1536], P(None, 'head'), may hold values from -0.21875 to 0.21875
- value_proj: bfloat16 [768, 1536], P(None, 'head'), may hold values from -0.21875 to 0.21875
- state_proj: bfloat16 [768, 256], replicated, may hold values from -0.21875 to 0.21875
- step_proj: bfloat16 [768, 24], P(None, 'head'), may hold values from -0.21875 to 0.21875
- value_taps: float32 [4, 1536], P(None, 'head'), may hold values from -3 to 3
- value_bias: float32 [1536], P('head'), may hold values from -3 to 3
- state_taps: float32 [4, 256], replicated, may hold values from -3 to 3
- state_bias: float32 [256], replicated, may hold values from -3 to 3
- step_bias: float32 [24], P('head'), may hold values from -5 to -1
- decay_log: float32 [24], P('head'), may hold values from 0 to 2.7
- skip_gain: float32 [24], P('head'), may hold values from 0.5 to 2
- out_gain: float32 [1536], P('head'), may hold values from 0.5 to 1.5
- out_proj: bfloat16 [1536, 768], P('head'), may hold values from -0.15625 to 0.15625
- cotangent: bfloat16 [16384, 768], P(('dp', 'head')), may hold values from -6 to 6
Outputs:
- mixed: bfloat16 [16384, 768], P(('dp', 'head'))
- grad_hidden: float32 [16384, 768], P(('dp', 'head'))
- grad_norm_gain: float32 [768], replicated
- grad_gate_proj: float32 [768, 1536], P(None, 'head')
- grad_value_proj: float32 [768, 1536], P(None, 'head')
- grad_state_proj: float32 [768, 256], replicated
- grad_step_proj: float32 [768, 24], P(None, 'head')
- grad_value_taps: float32 [4, 1536], P(None, 'head')
- grad_value_bias: float32 [1536], P('head')
- grad_state_taps: float32 [4, 256], replicated
- grad_state_bias: float32 [256], replicated
- grad_step_bias: float32 [24], P('head')
- grad_decay_log: float32 [24], P('head')
- grad_skip_gain: float32 [24], P('head')
- grad_out_gain: float32 [1536], P('head')
- grad_out_proj: float32 [1536, 768], P('head')
The draws below stay inside these ranges and needn't reach their ends.
Inputs may be any that keep to these rules, and one draw needn't show every extreme that they name: lengths[g] gives group g's three sequences in slot order: the first and the third have at most 256 tokens and fill blocks 0 and 7; the second has more than (6) * 256 - 256 // 2 tokens and fills the blocks between; slots past a sequence's length are padding.
All inputs are finite; a program needn't handle non-finite values.
Results may differ from the reference program's by a relative error of at most 0.019.
Values may be sent and summed in bfloat16 or wider, within the bound.
No kernel may reach another device: no remote copies, remote signals or barrier semaphores. Data moves between devices by JAX's collectives and lax.ppermute only.
A program may use at most 192 MiB of HBM per device.

```python
import jax
import jax.numpy as jnp
from jax import lax

D = 768
DI = 1536
HEADS = 24
STATE = 128
K = 4
Q = 256
NCH = 8
GROUPS = 8
TOKENS = 16384


def draw_lengths(key, part):
    key = jax.random.fold_in(key, 7)
    first_key, second_key, third_key = jax.random.split(key, 3)
    shorter = jax.random.randint(first_key, (GROUPS, 2), 1, Q + 1)
    trimmed = jax.random.randint(second_key, (GROUPS,), 0, Q // 2)
    chosen = jax.random.randint(third_key, (), 0, GROUPS)
    trimmed = jnp.where(jnp.arange(GROUPS) == chosen, 0, trimmed)
    middle = (NCH - 2) * Q - trimmed
    return jnp.stack([shorter[:, 0], middle, shorter[:, 1]], axis=1).astype(jnp.int32)


def steps_of(key, shape, shards, low, largest):
    factor_of, own = 1.0, jax.random.fold_in(key, 6)
    for axis_at, shards_of in shards:
        draws = jnp.exp(jax.random.uniform(jax.random.fold_in(own, axis_at), (shards_of,), jnp.float32, low / len(shards), largest / len(shards)))
        factor_of = factor_of * jnp.repeat(draws, shape[axis_at] // shards_of).reshape([-1 if axis == axis_at else 1 for axis in range(len(shape))])
    return factor_of


def gaussian(key, extent, deviation, limit, cuts=(), kind=jnp.bfloat16):
    array = deviation * jax.random.normal(key, extent, jnp.float32)
    if cuts:
        array = array * steps_of(key, extent, cuts, -0.22, 0.18)
    return jnp.clip(array, -limit, limit).astype(kind)


def setup_inputs(seed: int = 0) -> dict:
    splits = jax.random.split(jax.random.key(seed), 18)
    return {
        "hidden": gaussian(splits[0], (TOKENS, D), 1.0, 6.0, ((0, 32),)),
        "lengths": draw_lengths(jax.random.fold_in(splits[17], 71), 0),
        "norm_gain": jnp.clip(1.0 + 0.1 * jax.random.normal(splits[2], (D,), jnp.float32), 0.5, 1.5),
        "gate_proj": gaussian(splits[3], (D, DI), D ** -0.5, 0.21875, ((1, 4),)),
        "value_proj": gaussian(splits[4], (D, DI), D ** -0.5, 0.21875, ((1, 4),)),
        "state_proj": gaussian(splits[5], (D, 2 * STATE), D ** -0.5, 0.21875),
        "step_proj": gaussian(splits[6], (D, HEADS), D ** -0.5, 0.21875, ((1, 4),)),
        "value_taps": gaussian(splits[7], (K, DI), 0.5, 3.0, ((1, 4),), jnp.float32),
        "value_bias": gaussian(splits[8], (DI,), 0.3, 3.0, ((0, 4),), jnp.float32),
        "state_taps": gaussian(splits[9], (K, 2 * STATE), 0.5, 3.0, (), jnp.float32),
        "state_bias": gaussian(splits[10], (2 * STATE,), 0.3, 3.0, (), jnp.float32),
        "step_bias": jnp.clip(-5.0 + 4.0 * jax.random.uniform(splits[11], (HEADS,), jnp.float32) ** steps_of(splits[11], (HEADS,), ((0, 4),), -0.2, 0.2), -5.0, -1.0),
        "decay_log": jnp.clip(2.7 * jax.random.uniform(splits[12], (HEADS,), jnp.float32) ** steps_of(splits[12], (HEADS,), ((0, 4),), -0.2, 0.2), 0.0, 2.7),
        "skip_gain": jnp.clip(0.5 + 1.5 * jax.random.uniform(splits[13], (HEADS,), jnp.float32) ** steps_of(splits[13], (HEADS,), ((0, 4),), -0.2, 0.2), 0.5, 2.0),
        "out_gain": jnp.clip(1.0 + 0.1 * jax.random.normal(splits[14], (DI,), jnp.float32), 0.5, 1.5),
        "out_proj": gaussian(splits[15], (DI, D), DI ** -0.5, 0.15625, ((0, 4),)),
        "cotangent": gaussian(splits[16], (TOKENS, D), 1.0, 6.0, ((0, 32),)),
    }


EPSILON = 1e-05

@jax.custom_vjp
def low(v):
    return lax.optimization_barrier(v.astype(jnp.bfloat16)).astype(jnp.float32)

@jax.custom_vjp
def low_back(v):
    return v

def low_keep(v):
    return (low(v), None)

def low_pass(kept, grad):
    return (grad,)

def back_keep(v):
    return (v, None)

def back_low(kept, grad):
    return (low(grad),)
low.defvjp(low_keep, low_pass)
low_back.defvjp(back_keep, back_low)

def rounded(values):
    return low_back(low(values))

def matmul(left, right):
    return jnp.dot(left, right, precision=lax.Precision.HIGHEST, preferred_element_type=jnp.float32)

def contract(formula, left, right):
    return jnp.einsum(formula, left, right, precision=lax.Precision.HIGHEST, preferred_element_type=jnp.float32)

def layout(lengths_row, span_rows):
    slots = jnp.arange(span_rows, dtype=jnp.int32)
    starts = jnp.where(slots < Q, 0, jnp.where(slots < span_rows - Q, Q, span_rows - Q)).astype(jnp.int32)
    seq_length = jnp.where(slots < Q, lengths_row[0], jnp.where(slots < span_rows - Q, lengths_row[1], lengths_row[2]))
    places = slots - starts
    valid_rows = (places < seq_length).astype(jnp.float32)
    return (places, valid_rows)

def conv_pre(values, taps, offset, places):
    total_rows = values.shape[0]
    result = offset + taps[K - 1] * values
    for distance in range(1, K):
        earlier = jnp.pad(values, ((distance, 0), (0, 0)))[:total_rows]
        keeper = (places >= distance).astype(jnp.float32)[:, None]
        result = result + taps[K - 1 - distance] * earlier * keeper
    return result

def mixer(x_conv, b_matrix, c_matrix, step_sizes, decay_rate, skip_weight):
    total_rows, channel_count = x_conv.shape
    head_count = step_sizes.shape[1]
    head_size = channel_count // head_count
    block_count = total_rows // Q
    state_size = b_matrix.shape[1]
    x_blocks = x_conv.reshape(block_count, Q, head_count, head_size)
    x_low = rounded(x_conv).reshape(block_count, Q, head_count, head_size)
    b_low = rounded(b_matrix).reshape(block_count, Q, state_size)
    c_low = rounded(c_matrix).reshape(block_count, Q, state_size)
    step_blocks = step_sizes.reshape(block_count, Q, head_count)
    log_decay = jnp.cumsum(step_blocks * decay_rate, axis=1)
    intersections = contract('cqn,csn->cqs', c_low, b_low)
    causal = jnp.arange(Q)[:, None] >= jnp.arange(Q)[None, :]

    def one_head(inputs):
        head_logs, head_steps, head_values = inputs
        spread = jnp.where(causal, head_logs[:, :, None] - head_logs[:, None, :], -jnp.inf)
        scores = rounded(intersections * jnp.exp(spread) * head_steps[:, None, :])
        return contract('cqs,csp->cqp', scores, head_values)
    intra = lax.map(jax.checkpoint(one_head), (jnp.moveaxis(log_decay, 2, 0), jnp.moveaxis(step_blocks, 2, 0), jnp.moveaxis(x_low, 2, 0)))
    intra = jnp.moveaxis(intra, 0, 2)
    final_log = log_decay[:, -1:, :]
    carry_weight = jnp.exp(final_log - log_decay) * step_blocks
    weighted_x = rounded(carry_weight[..., None] * x_blocks)
    block_state = contract('csn,cshp->chnp', b_low, weighted_x)
    block_index = jnp.arange(block_count)
    fresh = ((block_index == 0) | (block_index == 1) | (block_index == block_count - 1)).astype(jnp.float32)

    def advance(state, item):
        local_state, fading, flag = item
        arriving = state * (1.0 - flag)
        return (fading[:, None, None] * arriving + local_state, arriving)
    start_state = jnp.zeros((head_count, state_size, head_size), jnp.float32)
    _, incoming = lax.scan(advance, start_state, (block_state, jnp.exp(final_log[:, 0, :]), fresh))
    inter = contract('cqn,chnp->cqhp', c_low, rounded(incoming)) * jnp.exp(log_decay)[..., None]
    result = intra + inter + skip_weight[:, None] * x_blocks
    return result.reshape(total_rows, channel_count)

def group_forward(params, hidden_rows, lengths_row):
    norm_gain, gate_proj, value_proj, state_proj, step_proj, value_taps, value_bias, state_taps, state_bias, step_bias, decay_log, skip_gain, out_gain, out_proj = params
    span_rows = hidden_rows.shape[0]
    places, valid_rows = layout(lengths_row, span_rows)
    scale_in = lax.rsqrt(lax.optimization_barrier(jnp.mean(hidden_rows * hidden_rows, axis=1, keepdims=True)) + EPSILON)
    normed = rounded(hidden_rows * scale_in * norm_gain)
    gate_in = low_back(matmul(normed, gate_proj))
    inner_x = low_back(matmul(normed, value_proj))
    state_raw = low_back(matmul(normed, state_proj))
    step_raw = low_back(matmul(normed, step_proj))
    x_conv = jax.nn.silu(conv_pre(inner_x, value_taps, value_bias, places))
    state_conv = jax.nn.silu(conv_pre(state_raw, state_taps, state_bias, places))
    state_size = state_proj.shape[1] // 2
    step_sizes = jax.nn.softplus(step_raw + step_bias)
    mix_y = mixer(x_conv, state_conv[:, :state_size], state_conv[:, state_size:], step_sizes, -jnp.exp(decay_log), skip_gain)
    gated_y = mix_y * jax.nn.silu(gate_in)
    scale_y = lax.rsqrt(lax.optimization_barrier(jnp.mean(gated_y * gated_y, axis=1, keepdims=True)) + EPSILON)
    normed_y = rounded(gated_y * scale_y * out_gain)
    branch = low_back(matmul(normed_y, out_proj))
    return hidden_rows + valid_rows[:, None] * branch

def reference(hidden, lengths, norm_gain, gate_proj, value_proj, state_proj, step_proj, value_taps, value_bias, state_taps, state_bias, step_bias, decay_log, skip_gain, out_gain, out_proj, cotangent):
    params = (norm_gain, gate_proj.astype(jnp.float32), value_proj.astype(jnp.float32), state_proj.astype(jnp.float32), step_proj.astype(jnp.float32), value_taps, value_bias, state_taps, state_bias, step_bias, decay_log, skip_gain, out_gain, out_proj.astype(jnp.float32))
    group_count = lengths.shape[0]
    span_rows = hidden.shape[0] // group_count
    features = hidden.shape[1]
    inputs = hidden.astype(jnp.float32).reshape(group_count, span_rows, features)
    cotan_rows = cotangent.astype(jnp.float32).reshape(group_count, span_rows, features)

    def whole(weights, rows_in):
        forward = jax.checkpoint(group_forward)

        def visit(carry, item):
            return (carry, forward(weights, item[0], item[1]))
        _, results = lax.scan(visit, jnp.zeros((), jnp.float32), (rows_in, lengths))
        return results
    results, pullback = jax.vjp(whole, params, inputs)
    grads, grad_inputs = pullback(cotan_rows)
    return (results.reshape(-1, features).astype(jnp.bfloat16), grad_inputs.reshape(-1, features), grads[0], grads[1], grads[2], grads[3], grads[4], grads[5], grads[6], grads[7], grads[8], grads[9], grads[10], grads[11], grads[12], grads[13])
```

```python
import functools

import jax
import jax.numpy as jnp
from jax import lax
from jax.experimental import pallas as pl
from jax.experimental.pallas import tpu as pltpu
from jax.sharding import PartitionSpec as P

K = 4
Q = 256
HALO = 16
LANES = 128
EPSILON = 1e-05
F32 = jnp.float32
BF16 = jnp.bfloat16
HIGHEST = lax.Precision.HIGHEST


def mm(left, right, lc=1, rc=0, precision=None):
    return lax.dot_general(
        left,
        right,
        (((lc,), (rc,)), ((), ())),
        preferred_element_type=F32,
        precision=precision,
    )


def call(kernel, outs, args, scratch=(), flops=0, moved=0):
    specs = [pl.BlockSpec(memory_space=pltpu.SMEM)] + [
        pl.BlockSpec(memory_space=pltpu.VMEM) for _ in args[1:]
    ]
    return pl.pallas_call(
        kernel,
        out_shape=[jax.ShapeDtypeStruct(s, d) for s, d in outs],
        in_specs=specs,
        out_specs=[pl.BlockSpec(memory_space=pltpu.VMEM) for _ in outs],
        scratch_shapes=list(scratch),
        compiler_params=pltpu.CompilerParams(vmem_limit_bytes=60 * 1024 * 1024),
        cost_estimate=pl.CostEstimate(flops=flops, bytes_accessed=moved, transcendentals=0),
    )(*args)


def keeps_of(s_ref, block, blocks):
    place = s_ref[0] * blocks + block
    fresh = (place == 0) | (place == 1) | (place == s_ref[1] - 1)
    return fresh, jnp.where(fresh, 0.0, 1.0).astype(F32)


def row_keep(fresh, distance):
    rows = lax.broadcasted_iota(jnp.int32, (Q, 1), 0)
    return (rows >= jnp.where(fresh, distance, 0)).astype(F32)


def conv_block(ref, base, cols, taps, fresh):
    total = taps[K : K + 1] + taps[K - 1 : K] * ref[pl.ds(base, Q), cols]
    for distance in range(1, K):
        earlier = ref[pl.ds(base - distance, Q), cols]
        total = total + taps[K - 1 - distance : K - distance] * (earlier * row_keep(fresh, distance))
    return total


def silu_slope(values, sig):
    return sig * (1.0 + values * (1.0 - sig))


def first_lanes():
    return lax.broadcasted_iota(jnp.int32, (1, LANES), 1) < LANES // 2


def spread(cols, quantity):
    return jnp.where(
        first_lanes(), cols[:, 2 * quantity : 2 * quantity + 1], cols[:, 2 * quantity + 1 : 2 * quantity + 2]
    )


def head_lanes(rows, heads_first, head_size):
    lane = lax.broadcasted_iota(jnp.int32, rows, 1 if heads_first else 0)
    head = lax.broadcasted_iota(jnp.int32, rows, 0 if heads_first else 1)
    return (lane >= head * head_size) & (lane < (head + 1) * head_size)


def pre_kernel(blocks, s_ref, hid_ref, halo_ref, gain_ref, proj_ref, taps_ref,
               nx_ref, nt_ref, raw_ref, pre_ref, b_ref, c_ref, bt_ref, ct_ref, cb_ref, cbt_ref):
    gain = gain_ref[...]
    rows = blocks * Q

    def norm(v):
        v = v.astype(F32)
        return v * lax.rsqrt(jnp.mean(v * v, axis=1, keepdims=True) + EPSILON) * gain

    halo = norm(halo_ref[...])
    own = norm(hid_ref[...])
    nx_ref[0:HALO] = halo.astype(BF16)
    nx_ref[HALO:] = own.astype(BF16)
    nt_ref[:, 0:rows] = own.T.astype(BF16)
    raw_ref[...] = mm(nx_ref[...], proj_ref[...])
    taps = taps_ref[...]
    state = b_ref.shape[1]
    for block in range(blocks):
        fresh, _ = keeps_of(s_ref, block, blocks)
        pre = conv_block(raw_ref, HALO + block * Q, slice(None), taps, fresh)
        at = pl.ds(block * Q, Q)
        pre_ref[at] = pre
        conv = pre * jax.nn.sigmoid(pre)
        b_mat = conv[:, :state]
        c_mat = conv[:, state:]
        b_low = b_mat.astype(BF16)
        c_low = c_mat.astype(BF16)
        b_ref[at] = b_low
        c_ref[at] = c_low
        bt_ref[:, at] = b_mat.T.astype(BF16)
        ct_ref[:, at] = c_mat.T.astype(BF16)
        cb_ref[block] = mm(c_low, b_low, 1, 1)
        cbt_ref[block] = mm(b_low, c_low, 1, 1)


def step_kernel(blocks, head_size, s_ref, nx_ref, hp_ref, rowp_ref, colp_ref, step_ref, ratio_ref, sig_ref, chan_ref):
    rows = blocks * Q
    depth = nx_ref.shape[1]
    hp = hp_ref[...]
    raw = mm(hp[:, :depth].astype(BF16), nx_ref[HALO:], 1, 1)
    u = raw + hp[:, depth : depth + 1]
    step = jnp.maximum(u, 0.0) + jnp.log1p(jnp.exp(-jnp.abs(u)))
    sig = jax.nn.sigmoid(u)
    step_ref[...] = step
    sig_ref[...] = sig
    ratio_ref[...] = jnp.where(step > 1e-30, sig / jnp.maximum(step, 1e-30), 1.0)
    rate = -jnp.exp(hp[:, depth + 1 : depth + 2])
    move = step * rate
    upto = (
        lax.broadcasted_iota(jnp.int32, (Q, Q), 0) <= lax.broadcasted_iota(jnp.int32, (Q, Q), 1)
    ).astype(F32)
    heads = hp.shape[0]
    lane = lax.broadcasted_iota(jnp.int32, (heads, LANES), 1)
    last_cols = jnp.zeros((heads, LANES), F32)
    lstep = jnp.log(step)
    product = jnp.ones((heads, 1), F32)
    pairs = rowp_ref.shape[0]
    for block in range(blocks):
        at = slice(block * Q, (block + 1) * Q)
        logd = mm(move[:, at], upto, precision=HIGHEST)
        less = logd - lstep[:, at]
        last = logd[:, Q - 1 : Q]
        grown = jnp.exp(logd)
        carry = jnp.exp(last - less)
        final = jnp.exp(last)
        _, kept = keeps_of(s_ref, block, blocks)
        product = product * final * kept
        last_cols = jnp.where(lane == block, final, last_cols)
        for pair in range(pairs):
            for index, values in enumerate((logd, less, grown, carry)):
                rowp_ref[pair, 2 * index : 2 * index + 2, at] = values[2 * pair : 2 * pair + 2]
    last_cols = jnp.where(lane == 6, product, last_cols)
    last_cols = jnp.where(lane == 7, hp[:, depth + 2 : depth + 3], last_cols)
    spots = head_lanes((heads, chan_ref.shape[1]), True, head_size).astype(F32)
    chan_ref[...] = mm(last_cols.T[0:8], spots, precision=HIGHEST)
    for pair in range(pairs):
        colp_ref[pair] = rowp_ref[pair].T


def front_kernel(blocks, group, pieces, s_ref, nx_ref, par_ref, bt_ref, colp_ref, chan_ref, *refs):
    gates, values = refs[:pieces], refs[pieces : 2 * pieces]
    gate_ref, inner_ref, pre_ref, x_ref, s_out, carry_ref = refs[2 * pieces :]
    wide = gates[0].shape[1]
    for p in range(pieces):
        inner_ref[:, p * wide : (p + 1) * wide] = mm(nx_ref[...], values[p][...])
        gate_ref[:, p * wide : (p + 1) * wide] = mm(nx_ref[HALO:], gates[p][...])
    tiles = gate_ref.shape[1] // LANES

    def tile(i, none):
        cols = pl.ds(pl.multiple_of(i * LANES, LANES), LANES)
        far = pl.ds(pl.multiple_of((i + group * tiles) * LANES, LANES), LANES)
        taps = par_ref[:, far]
        for block in range(blocks):
            at = pl.ds(block * Q, Q)
            fresh, kept = keeps_of(s_ref, block, blocks)
            pre = conv_block(inner_ref, HALO + block * Q, cols, taps, fresh)
            pre_ref[at, cols] = pre
            x = pre * jax.nn.sigmoid(pre)
            x_ref[at, cols] = x
            weighted = (spread(colp_ref[i + group * tiles, at, :], 3) * x).astype(BF16)
            state = mm(bt_ref[:, at], weighted)
            s_out[block, :, cols] = state
            if block == 0:
                carry = state
            else:
                carry = chan_ref[block : block + 1, far] * (kept * carry) + state
        carry_ref[:, cols] = carry.astype(BF16)
        return none

    lax.fori_loop(0, tiles, tile, 0)


def intra_kernel(blocks, s_ref, rowp_ref, colp_ref, cb_ref, x0_ref, x1_ref, y_ref):
    half = Q // 2
    first = first_lanes()
    tri = lax.broadcasted_iota(jnp.int32, (half, half), 0) >= lax.broadcasted_iota(
        jnp.int32, (half, half), 1
    )
    for group, x_ref in enumerate((x0_ref, x1_ref)):
        tiles = x_ref.shape[1] // LANES

        def tile(i, none, group=group, x_ref=x_ref, tiles=tiles):
            cols = pl.ds(pl.multiple_of(i * LANES, LANES), LANES)
            pair = i + group * tiles
            far = pl.ds(pl.multiple_of(pair * LANES, LANES), LANES)
            for block in range(blocks):
                at = pl.ds(block * Q, Q)
                x = x_ref[at, cols].astype(BF16)
                both = [jnp.where(first, x, 0), jnp.where(first, 0, x)]
                cp = colp_ref[pair, at, :]
                rp = rowp_ref[pair, :, at]
                tops, bots = [], []
                for k in range(2):
                    ld, ls = cp[:, k : k + 1], rp[2 + k : 3 + k, :]
                    arg = jnp.where(tri, ld[:half] - ls[:, :half], -1e30)
                    tops.append((cb_ref[block, 0:half, 0:half] * jnp.exp(arg)).astype(BF16))
                    arg = ld[half:] - ls[:, :half]
                    bots.append((cb_ref[block, half:, 0:half] * jnp.exp(arg)).astype(BF16))
                    arg = jnp.where(tri, ld[half:] - ls[:, half:], -1e30)
                    bots.append((cb_ref[block, half:, half:] * jnp.exp(arg)).astype(BF16))
                top = mm(jnp.concatenate(tops, 1), jnp.concatenate([b[:half] for b in both], 0))
                bot = mm(jnp.concatenate(bots, 1), jnp.concatenate(both, 0))
                y_ref[pl.ds(block * Q, half), far] = top
                y_ref[pl.ds(block * Q + half, half), far] = bot
            return none

        lax.fori_loop(0, tiles, tile, 0)


def arrive(chan_ref, s_tiles, incoming, kept, far):
    result = []
    for block, state in enumerate(s_tiles):
        incoming = kept[block] * incoming
        result.append(incoming)
        incoming = chan_ref[block : block + 1, far] * incoming + state
    return result


def valid_of(s_ref, blocks, block):
    place = s_ref[0] * blocks + block
    last = place == s_ref[1] - 1
    length = jnp.where(place == 0, s_ref[2], jnp.where(last, s_ref[4], s_ref[3]))
    start = jnp.where(place == 0, 0, jnp.where(last, s_ref[1] - 1, 1))
    rows = lax.broadcasted_iota(jnp.int32, (Q, 1), 0) + (place - start) * Q
    return (rows < length).astype(F32)


def middle_kernel(blocks, pieces, head_size, s_ref, cot_ref, inc_in, colp_ref, chan_ref, par_ref, c_ref, ct_ref,
                  y_ref, *refs):
    outs_w = refs[:pieces]
    g_refs = refs[pieces : pieces + 2]
    x_refs = refs[pieces + 2 : pieces + 4]
    st_refs = refs[pieces + 4 : pieces + 6]
    (ny_ref, dgate_ref, dy_ref, di_ref, carry_ref, dc_ref, rowpart_ref, rows_ref,
     db_ref, dny_ref, mix_ref, sq_ref, cr_ref, inc_ref, dye_ref, hi_ref, lo_ref) = refs[pieces + 6 :]
    for block in range(blocks):
        at = slice(block * Q, (block + 1) * Q)
        db_ref[at] = (cot_ref[at].astype(F32) * valid_of(s_ref, blocks, block)).astype(BF16)
    wide = outs_w[0].shape[0]
    for p in range(pieces):
        dny_ref[:, p * wide : (p + 1) * wide] = mm(db_ref[...], outs_w[p][...], 1, 1).astype(BF16)
    sq_ref[...] = jnp.zeros_like(sq_ref)
    cr_ref[...] = jnp.zeros_like(cr_ref)
    kept = [keeps_of(s_ref, block, blocks)[1] for block in range(blocks)]
    for group in range(2):
        gate_ref, x_ref, st_ref = g_refs[group], x_refs[group], st_refs[group]
        tiles = x_ref.shape[1] // LANES

        def tile(i, none, group=group, gate_ref=gate_ref, x_ref=x_ref, st_ref=st_ref, tiles=tiles):
            cols = pl.ds(pl.multiple_of(i * LANES, LANES), LANES)
            pair = i + group * tiles
            far = pl.ds(pl.multiple_of(pair * LANES, LANES), LANES)
            incs = arrive(chan_ref, [st_ref[b, :, cols] for b in range(blocks)], inc_in[:, far], kept, far)
            gain = par_ref[5:6, far]
            for block in range(blocks):
                at = pl.ds(block * Q, Q)
                inc_low = incs[block].astype(BF16)
                inc_ref[block, :, far] = inc_low
                inter = mm(c_ref[at], inc_low) * spread(colp_ref[pair, at, :], 2)
                mix = y_ref[at, far] + inter + chan_ref[7:8, far] * x_ref[at, cols]
                mix_ref[at, far] = mix
                gate = gate_ref[at, cols]
                gated = mix * (gate * jax.nn.sigmoid(gate))
                sq_ref[at] += gated * gated
                cr_ref[at] += dny_ref[at, far].astype(F32) * gain * gated
            return none

        lax.fori_loop(0, tiles, tile, 0)
    total = 2 * x_refs[0].shape[1]
    scale = lax.rsqrt(jnp.sum(sq_ref[...], axis=1, keepdims=True) / total + EPSILON)
    coef = scale * scale * scale * (jnp.sum(cr_ref[...], axis=1, keepdims=True) / total)
    sq_ref[...] = jnp.broadcast_to(scale, sq_ref.shape)
    cr_ref[...] = jnp.broadcast_to(coef, cr_ref.shape)
    rows_ref[...] = jnp.zeros_like(rows_ref)
    for group in range(2):
        gate_ref, x_ref = g_refs[group], x_refs[group]
        tiles = x_ref.shape[1] // LANES

        def tile(i, none, group=group, gate_ref=gate_ref, x_ref=x_ref, tiles=tiles):
            cols = pl.ds(pl.multiple_of(i * LANES, LANES), LANES)
            pair = i + group * tiles
            far = pl.ds(pl.multiple_of(pair * LANES, LANES), LANES)
            gain = par_ref[5:6, far]
            skip = chan_ref[7:8, far]
            gain_row = jnp.zeros((1, LANES), F32)
            skip_row = jnp.zeros((1, LANES), F32)
            dis = []
            for block in range(blocks):
                at = pl.ds(block * Q, Q)
                gate, mix, x = gate_ref[at, cols], mix_ref[at, far], x_ref[at, cols]
                sig = jax.nn.sigmoid(gate)
                act = gate * sig
                gated = mix * act
                normed = gated * sq_ref[at]
                dny = dny_ref[at, far].astype(F32)
                ny_ref[at, far] = (normed * gain).astype(BF16)
                gain_row += jnp.sum(dny * normed, axis=0, keepdims=True)
                d_gated = dny * gain * sq_ref[at] - gated * cr_ref[at]
                dgate_ref[at, far] = (d_gated * mix * silu_slope(gate, sig)).astype(BF16)
                dy = d_gated * act
                dy_ref[at, far] = dy
                skip_row += jnp.sum(dy * x, axis=0, keepdims=True)
                part = dy.astype(BF16).astype(F32) * (mix - skip * x)
                high = part.astype(BF16)
                hi_ref[at, far] = high
                lo_ref[at, far] = (part - high.astype(F32)).astype(BF16)
                dye = (dy * spread(colp_ref[pair, at, :], 2)).astype(BF16)
                dye_ref[at, far] = dye
                di = mm(ct_ref[:, at], dye)
                di_ref[block, :, far] = di
                dis.append(di)
            rows_ref[0:1, far] = gain_row
            rows_ref[1:2, far] = skip_row
            back = jnp.zeros_like(dis[0])
            for block in reversed(range(blocks)):
                back = kept[block] * (dis[block] + chan_ref[block : block + 1, far] * back)
            carry_ref[:, far] = back.astype(BF16)
            return none

        lax.fori_loop(0, tiles, tile, 0)
    spots = head_lanes((rowpart_ref.shape[0], total), True, head_size).astype(F32).astype(BF16)
    rowpart_ref[...] = mm(spots, hi_ref[...], 1, 1) + mm(spots, lo_ref[...], 1, 1)
    for block in range(blocks):
        at = slice(block * Q, (block + 1) * Q)
        dc_ref[at] = mm(dye_ref[at], inc_ref[block], 1, 1)


def out_kernel(blocks, pieces, s_ref, hid_ref, cot_ref, nt_ref, ny_ref, dgate_ref, *refs):
    outs_w = refs[:pieces]
    mixed_ref = refs[pieces]
    g_outs = refs[pieces + 1 : 2 * pieces + 1]
    g_gates = refs[2 * pieces + 1 : 3 * pieces + 1]
    db_ref = refs[3 * pieces + 1]
    wide = outs_w[0].shape[0]
    rows = blocks * Q
    for block in range(blocks):
        at = slice(block * Q, (block + 1) * Q)
        db_ref[at] = (cot_ref[at].astype(F32) * valid_of(s_ref, blocks, block)).astype(BF16)
    for p in range(pieces):
        span = slice(p * wide, (p + 1) * wide)
        g_outs[p][...] = mm(ny_ref[:, span], db_ref[...], 0, 0).astype(BF16)
        g_gates[p][...] = mm(nt_ref[:, 0:rows], dgate_ref[:, span]).astype(BF16)
    for block in range(blocks):
        at = slice(block * Q, (block + 1) * Q)
        branch = mm(ny_ref[at, 0:wide], outs_w[0][...])
        for p in range(1, pieces):
            branch += mm(ny_ref[at, p * wide : (p + 1) * wide], outs_w[p][...])
        mixed_ref[at] = (hid_ref[at].astype(F32) + valid_of(s_ref, blocks, block) * branch).astype(BF16)


def back_kernel(blocks, s_ref, rowp_ref, colp_ref, cbt_ref, b_ref, c_ref, dy_ref, x0_ref, x1_ref,
                dx_ref, db_ref, dc_ref, acc_ref):
    half = Q // 2
    first = first_lanes()
    tri = lax.broadcasted_iota(jnp.int32, (half, half), 0) <= lax.broadcasted_iota(
        jnp.int32, (half, half), 1
    )
    acc_ref[...] = jnp.zeros_like(acc_ref)
    for group, x_ref in enumerate((x0_ref, x1_ref)):
        tiles = x_ref.shape[1] // LANES

        def tile(i, none, group=group, x_ref=x_ref, tiles=tiles):
            cols = pl.ds(pl.multiple_of(i * LANES, LANES), LANES)
            pair = i + group * tiles
            far = pl.ds(pl.multiple_of(pair * LANES, LANES), LANES)
            for block in range(blocks):
                at = pl.ds(block * Q, Q)
                x = x_ref[at, cols].astype(BF16)
                dy = dy_ref[at, far].astype(BF16)
                dys = [jnp.where(first, dy, 0), jnp.where(first, 0, dy)]
                xs = [jnp.where(first, x, 0), jnp.where(first, 0, x)]
                cp = colp_ref[pair, at, :]
                rp = rowp_ref[pair, :, at]
                tops, bots = [], []
                w00 = w01 = w11 = 0.0
                for k in range(2):
                    ls, ld = cp[:, 2 + k : 3 + k], rp[k : k + 1, :]
                    ds_top = mm(xs[k][:half], dy, 1, 1)
                    ds_bot = mm(xs[k][half:], dy[half:], 1, 1)
                    e00 = jnp.exp(jnp.where(tri, ld[:, :half] - ls[:half], -1e30))
                    e01 = jnp.exp(ld[:, half:] - ls[:half])
                    e11 = jnp.exp(jnp.where(tri, ld[:, half:] - ls[half:], -1e30))
                    tops.append((cbt_ref[block, 0:half, 0:half] * e00).astype(BF16))
                    tops.append((cbt_ref[block, 0:half, half:] * e01).astype(BF16))
                    bots.append((cbt_ref[block, half:, half:] * e11).astype(BF16))
                    w00 += ds_top[:, :half] * e00
                    w01 += ds_top[:, half:] * e01
                    w11 += ds_bot * e11
                acc_ref[block, 0:half, 0:half] += w00
                acc_ref[block, 0:half, half:] += w01
                acc_ref[block, half:, half:] += w11
                dx_ref[pl.ds(block * Q, half), far] = mm(jnp.concatenate(tops, 1), jnp.concatenate(dys, 0))
                dx_ref[pl.ds(block * Q + half, half), far] = mm(
                    jnp.concatenate(bots, 1), jnp.concatenate([d[half:] for d in dys], 0)
                )
            return none

        lax.fori_loop(0, tiles, tile, 0)
    for block in range(blocks):
        at = slice(block * Q, (block + 1) * Q)
        acc = acc_ref[block].astype(BF16)
        db_ref[at] = mm(acc, c_ref[at])
        dc_ref[at] = mm(acc, b_ref[at], 0, 0)


def tail_kernel(blocks, head_size, s_ref, back_in, inc_in, colp_ref, chan_ref, par_ref, b_ref, dx_ref, dy_ref, di_ref,
                dbin_ref, dcin_ref, dcx_ref, rowpart_ref, step_ref, ratio_ref, sig_ref, hp_ref, rows_ref,
                raw_ref, spre_ref, staps_ref, x0_ref, x1_ref, p0_ref, p1_ref, n0_ref, n1_ref, st0_ref, st1_ref,
                dinner_ref, dstate_ref, dstep_ref, vgrad_ref, sgrad_ref, hgrad_ref,
                wx_ref, gs_ref, hi_ref, lo_ref, last_ref, d_ref, e_ref):
    rows = blocks * Q
    kept = [keeps_of(s_ref, block, blocks)[1] for block in range(blocks)]
    total = dx_ref.shape[1]
    last_ref[...] = jnp.zeros_like(last_ref)
    d_ref[...] = jnp.zeros_like(d_ref)
    e_ref[...] = jnp.zeros_like(e_ref)
    vgrad_ref[...] = jnp.zeros_like(vgrad_ref)
    sgrad_ref[...] = jnp.zeros_like(sgrad_ref)

    def conv_back(work, taps, values_of, slope_of, store, grads, cols, grad_cols):
        sums = [0.0] * (K + 1)
        for block in range(blocks):
            at = pl.ds(block * Q, Q)
            fresh, _ = keeps_of(s_ref, block, blocks)
            d_pre = slope_of(block)
            work[0, pl.ds(HALO + block * Q, Q)] = d_pre
            sums[K] += jnp.sum(d_pre, axis=0, keepdims=True)
            sums[K - 1] += jnp.sum(d_pre * values_of(HALO + block * Q), axis=0, keepdims=True)
            for distance in range(1, K):
                held = d_pre * row_keep(fresh, distance)
                work[distance, pl.ds(HALO + block * Q, Q)] = held
                sums[K - 1 - distance] += jnp.sum(
                    held * values_of(HALO + block * Q - distance), axis=0, keepdims=True
                )
        for index in range(K + 1):
            grads[index : index + 1, grad_cols] = sums[index]
        for begin, count in [(0, HALO)] + [(HALO + b * Q, Q) for b in range(blocks)]:
            out = taps[K - 1 : K] * work[0, pl.ds(begin, count)]
            for distance in range(1, K):
                out = out + taps[K - 1 - distance : K - distance] * work[distance, pl.ds(begin + distance, count)]
            store(begin, count, out.astype(BF16))

    for group in range(2):
        x_ref, p_ref, n_ref, st_ref = (
            (x0_ref, x1_ref)[group], (p0_ref, p1_ref)[group], (n0_ref, n1_ref)[group], (st0_ref, st1_ref)[group],
        )
        tiles = x_ref.shape[1] // LANES

        def tile(i, none, group=group, x_ref=x_ref, p_ref=p_ref, n_ref=n_ref, st_ref=st_ref, tiles=tiles):
            cols = pl.ds(pl.multiple_of(i * LANES, LANES), LANES)
            pair = i + group * tiles
            far = pl.ds(pl.multiple_of(pair * LANES, LANES), LANES)
            taps = par_ref[:, far]
            skip = chan_ref[7:8, far]
            incs = arrive(chan_ref, [st_ref[b, :, cols] for b in range(blocks)], inc_in[:, far], kept, far)
            back = back_in[:, far]
            for block in reversed(range(blocks)):
                fade = chan_ref[block : block + 1, far]
                gs_ref[block, :, far] = back.astype(BF16)
                last_ref[block : block + 1, far] = fade * jnp.sum(incs[block] * back, axis=0, keepdims=True)
                back = kept[block] * (di_ref[block, :, far] + fade * back)

            def slope_of(block):
                at = pl.ds(block * Q, Q)
                x = x_ref[at, cols]
                carry = spread(colp_ref[pair, at, :], 3)
                weighted = carry * x
                wx_ref[at, far] = weighted.astype(BF16)
                d_weighted = mm(b_ref[at], gs_ref[block, :, far])
                dx = dx_ref[at, far]
                moved = weighted * d_weighted
                last_ref[block : block + 1, far] += jnp.sum(moved, axis=0, keepdims=True)
                part = x.astype(BF16).astype(F32) * dx + moved
                high = part.astype(BF16)
                hi_ref[at, far] = high
                lo_ref[at, far] = (part - high.astype(F32)).astype(BF16)
                d_x = dx + carry * d_weighted + skip * dy_ref[at, far]
                pre = p_ref[at, cols]
                return d_x * silu_slope(pre, jax.nn.sigmoid(pre))

            def store(begin, count, value):
                dinner_ref[pl.ds(begin, count), far] = value

            conv_back(d_ref, taps, lambda at: n_ref[pl.ds(at, Q), cols], slope_of, store, vgrad_ref, None, far)
            return none

        lax.fori_loop(0, tiles, tile, 0)

    wide = raw_ref.shape[1]
    state = wide // 2
    d_states = []
    for block in range(blocks):
        at = slice(block * Q, (block + 1) * Q)
        d_b = dbin_ref[at] + mm(wx_ref[at], gs_ref[block], 1, 1)
        d_c = dcin_ref[at] + dcx_ref[at]
        d_states.append(jnp.concatenate([d_b, d_c], 1))

    def state_slope(block):
        pre = spre_ref[pl.ds(block * Q, Q), :]
        return d_states[block] * silu_slope(pre, jax.nn.sigmoid(pre))

    def state_store(begin, count, value):
        dstate_ref[pl.ds(begin, count), :] = value

    conv_back(e_ref, staps_ref[...], lambda at: raw_ref[pl.ds(at, Q), :], state_slope, state_store, sgrad_ref, None, slice(None))

    heads = hp_ref.shape[0]
    depth = hp_ref.shape[1] - LANES
    spots = head_lanes((heads, total), True, head_size).astype(F32)
    low_spots = spots.astype(BF16)
    cols = mm(low_spots, hi_ref[...], 1, 1) + mm(low_spots, lo_ref[...], 1, 1)
    lasts = mm(spots, last_ref[...], 1, 1, precision=HIGHEST)
    skips = mm(spots, rows_ref[...], 1, 1, precision=HIGHEST)[:, 1:2]
    rate = -jnp.exp(hp_ref[:, depth + 1 : depth + 2])
    lane = lax.broadcasted_iota(jnp.int32, (heads, Q), 1)
    upto = (
        lax.broadcasted_iota(jnp.int32, (Q, Q), 0) >= lax.broadcasted_iota(jnp.int32, (Q, Q), 1)
    ).astype(F32)
    grad_bias = jnp.zeros((heads, 1), F32)
    grad_decay = jnp.zeros((heads, 1), F32)
    for block in range(blocks):
        at = slice(block * Q, (block + 1) * Q)
        d_log = rowpart_ref[:, at] - cols[:, at]
        d_log = d_log + jnp.where(lane == Q - 1, lasts[:, block : block + 1], 0.0)
        d_move = mm(d_log, upto, precision=HIGHEST)
        d_raw = cols[:, at] * ratio_ref[:, at] + rate * d_move * sig_ref[:, at]
        grad_bias += jnp.sum(d_raw, axis=1, keepdims=True)
        grad_decay += rate * jnp.sum(step_ref[:, at] * d_move, axis=1, keepdims=True)
        dstep_ref[:, at] = d_raw.astype(BF16)
    wide_lane = lax.broadcasted_iota(jnp.int32, (heads, LANES), 1)
    hgrad_ref[...] = jnp.where(
        wide_lane == 0, grad_bias, jnp.where(wide_lane == 1, grad_decay, jnp.where(wide_lane == 2, skips, 0.0))
    )


def value_kernel(pieces, s_ref, nx_ref, nt_ref, dinner_ref, dstep_ref, *refs):
    wide = refs[0].shape[1]
    rows = dinner_ref.shape[0] - HALO
    for p in range(pieces):
        span = slice(p * wide, (p + 1) * wide)
        total = mm(nt_ref[:, 0:rows], dinner_ref[HALO:, span])
        refs[p][...] = (total + mm(nx_ref[0:HALO], dinner_ref[0:HALO, span], 0, 0)).astype(BF16)
    refs[pieces][...] = mm(dstep_ref[...], nx_ref[HALO:])


def norm_kernel(pieces, s_ref, hid_ref, halo_ref, cot_ref, gain_ref, nx_ref, nt_ref, dgate_ref, dinner_ref, dstate_ref,
                dstep_ref, hp_ref, sproj_ref, sgrad_ref, *refs):
    gates, values = refs[:pieces], refs[pieces : 2 * pieces]
    grad_ref, extra_ref, d_ref = refs[2 * pieces :]
    wide = gates[0].shape[1]
    rows = hid_ref.shape[0]
    depth = hid_ref.shape[1]
    gain = gain_ref[...]
    gain_sum = jnp.zeros((1, depth), F32)

    def finish(values_in, d_normed):
        h = values_in.astype(F32)
        scale = lax.rsqrt(jnp.mean(h * h, axis=1, keepdims=True) + EPSILON)
        weighted = gain * d_normed
        inner = jnp.mean(weighted * h, axis=1, keepdims=True)
        return scale * weighted - h * (scale * scale * scale * inner), jnp.sum(d_normed * h * scale, axis=0, keepdims=True)

    total = mm(dinner_ref[0:HALO, 0:wide], values[0][...], 1, 1)
    for p in range(1, pieces):
        total += mm(dinner_ref[0:HALO, p * wide : (p + 1) * wide], values[p][...], 1, 1)
    total += mm(dstate_ref[0:HALO], sproj_ref[...], 1, 1)
    extra_ref[...], part = finish(halo_ref[...], total)
    gain_sum += part
    for begin in range(0, rows, Q):
        at = slice(begin, begin + Q)
        ext = slice(begin + HALO, begin + HALO + Q)
        total = mm(dstate_ref[ext], sproj_ref[...], 1, 1)
        total += mm(dstep_ref[:, at], hp_ref[:, 0:depth].astype(BF16), 0, 0)
        for p in range(pieces):
            span = slice(p * wide, (p + 1) * wide)
            total += mm(dgate_ref[at, span], gates[p][...], 1, 1)
            total += mm(dinner_ref[ext, span], values[p][...], 1, 1)
        d_hidden, part = finish(hid_ref[at], total.astype(BF16).astype(F32))
        gain_sum += part
        grad_ref[at] = cot_ref[at].astype(F32) + d_hidden
    state = mm(nt_ref[:, 0:rows], dstate_ref[HALO:]) + mm(nx_ref[0:HALO], dstate_ref[0:HALO], 0, 0)
    side = sgrad_ref.shape[1]
    d_ref[...] = jnp.zeros_like(d_ref)
    d_ref[0:depth] = state
    d_ref[depth : depth + 5] = sgrad_ref[0:5]
    for part_at in range(depth // side):
        d_ref[depth + 8 + part_at : depth + 9 + part_at] = gain_sum[:, part_at * side : (part_at + 1) * side]


def swap(value, axis, mask):
    size = lax.axis_size(axis)
    return lax.ppermute(value, axis, [(i, i ^ mask) for i in range(size)])


def pick(value, index):
    return lax.dynamic_index_in_dim(value, index, 0, keepdims=False)


def reduce_dp(value):
    size = lax.axis_size("dp")
    index = lax.axis_index("dp")
    rows, columns = value.shape
    side, deep = index & 1, (index >> 1) & 3
    halves = value.reshape(2, rows // 2, columns)
    got = swap(pick(halves, 1 - side).astype(BF16), "dp", 1)
    half = pick(halves, side).astype(F32) + got.astype(F32)
    quarters = half.astype(BF16).reshape(4, rows // 8, columns)
    sent = [swap(pick(quarters, deep ^ m), "dp", 2 * m) for m in (1, 2, 3)]
    own = pick(half.reshape(4, rows // 8, columns), deep)
    for part in sent:
        own = own + part.astype(F32)
    own = own.astype(BF16)
    bit = 8
    while bit < size:
        own = (own.astype(F32) + swap(own, "dp", bit).astype(F32)).astype(BF16)
        bit *= 2
    parts = jnp.stack([own] + [swap(own, "dp", 2 * m) for m in (1, 2, 3)])
    half = jnp.concatenate([pick(parts, deep ^ a) for a in range(4)], axis=0)
    other = swap(half, "dp", 1)
    return jnp.concatenate([jnp.where(side == 0, half, other), jnp.where(side == 0, other, half)], axis=0)


def gather_pieces(value):
    ways = lax.axis_size("head")
    pieces = {0: value}
    order = [1 << b for b in range(ways.bit_length() - 1)]
    far = order[1:] + order[:1]
    for mask in far[:-1]:
        for p in list(pieces):
            pieces[p | mask] = swap(pieces[p], "head", mask)
    for p in list(pieces):
        pieces[p | 1] = swap(pieces[p], "head", 1)
    return [pieces[p] for p in range(ways)]


def reduce_pieces(pieces):
    ways = len(pieces)
    mask = 1
    live = {p: v for p, v in enumerate(pieces)}
    order = [1 << b for b in range(ways.bit_length() - 1)]
    for mask in order:
        got = {p ^ mask: swap(live[p].astype(BF16), "head", mask) for p in live if p & mask}
        live = {p: live[p].astype(F32) + got[p].astype(F32) for p in live if not p & mask}
    return live[0]


def body(hidden, lengths, norm_gain, gate_proj, value_proj, state_proj, step_proj, value_taps, value_bias,
         state_taps, state_bias, step_bias, decay_log, skip_gain, out_gain, out_proj, cotangent):
    rows, depth = hidden.shape
    ways = lax.axis_size("head")
    me = lax.axis_index("head")
    blocks = rows // Q
    wide = gate_proj.shape[1]
    share = step_proj.shape[1]
    total = wide * ways
    heads = share * ways
    head_size = wide // share
    pairs = heads // 2
    side = state_proj.shape[1]
    state = side // 2
    group = total // 2
    padded = -(-heads // 32) * 32
    scalars = jnp.concatenate(
        [jnp.stack([me, blocks * ways]).astype(jnp.int32), lengths[0], jnp.zeros((3,), jnp.int32)]
    )

    halo = lax.ppermute(hidden[rows - HALO :], "head", [(i, i + 1) for i in range(ways - 1)])
    top = jnp.concatenate(
        [step_proj.T.astype(F32), step_bias[:, None], decay_log[:, None], skip_gain[:, None], jnp.zeros((share, LANES - 3), F32)],
        axis=1,
    )
    low = jnp.concatenate([value_taps, value_bias[None], out_gain[None]], axis=0)
    pack = jnp.concatenate(
        [
            jnp.pad(top, ((0, 8 - share), (0, 0))),
            jnp.pad(low, ((0, 2), (0, depth + LANES - wide))),
        ],
        axis=0,
    )
    packs = gather_pieces(pack)
    gates = gather_pieces(gate_proj)
    values = gather_pieces(value_proj)
    outs = gather_pieces(out_proj)

    def merged(parts, axis):
        if wide % LANES == 0:
            return parts
        return [jnp.concatenate(parts[i : i + 2], axis=axis) for i in range(0, len(parts), 2)]

    gates_m, values_m, outs_m = merged(gates, 1), merged(values, 1), merged(outs, 0)
    pieces = len(gates_m)
    half = pieces // 2
    hp = jnp.pad(jnp.concatenate([p[:share] for p in packs], axis=0), ((0, padded - heads), (0, 0)))
    par = jnp.concatenate([p[8:, :wide] for p in packs], axis=1)
    gain_in = norm_gain[None]
    staps = jnp.pad(jnp.concatenate([state_taps, state_bias[None]], axis=0), ((0, 3), (0, 0)))

    ext = rows + HALO
    (nx, nt, state_raw, state_pre, b_low, c_low, b_t, c_t, cb, cbt) = call(
        functools.partial(pre_kernel, blocks),
        [((ext, depth), BF16), ((depth, rows), BF16), ((ext, side), F32), ((rows, side), F32),
         ((rows, state), BF16), ((rows, state), BF16), ((state, rows), BF16), ((state, rows), BF16),
         ((blocks, Q, Q), F32), ((blocks, Q, Q), F32)],
        [scalars, hidden, halo, gain_in, state_proj, staps],
        flops=2 * ext * depth * side,
        moved=8 << 20,
    )
    rowp, colp, step, ratio, sig, chan = call(
        functools.partial(step_kernel, blocks, head_size),
        [((pairs, 8, rows), F32), ((pairs, rows, 8), F32), ((padded, rows), F32), ((padded, rows), F32),
         ((padded, rows), F32), ((8, total), F32)],
        [scalars, nx, hp],
        flops=2 * rows * depth * padded,
        moved=4 << 20,
    )
    fronts = []
    for g in range(2):
        fronts.append(
            call(
                functools.partial(front_kernel, blocks, g, half),
                [((rows, group), F32), ((ext, group), F32), ((rows, group), F32), ((rows, group), F32),
                 ((blocks, state, group), F32), ((state, group), BF16)],
                [scalars, nx, par, b_t, colp, chan, *gates_m[g * half : (g + 1) * half], *values_m[g * half : (g + 1) * half]],
                flops=4 * rows * depth * group,
                moved=12 << 20,
            )
        )
    (gate0, inner0, pre0, x0, st0, car0), (gate1, inner1, pre1, x1, st1, car1) = fronts
    (y_intra,) = call(
        functools.partial(intra_kernel, blocks),
        [((rows, total), F32)],
        [scalars, rowp, colp, cb, x0, x1],
        flops=2 * heads * rows * Q * LANES,
        moved=10 << 20,
    )

    fades = {0: chan[6:7]}

    def turned(value, mask):
        parts = [value[..., (p ^ mask) * wide : ((p ^ mask) + 1) * wide] for p in range(ways)]
        return jnp.concatenate(parts, axis=-1)

    order = [1 << b for b in range(ways.bit_length() - 1)]
    for mask in order:
        for p in list(fades):
            fades[p | mask] = turned(swap(fades[p], "head", mask), mask)

    def scan(own, forward):
        run, run_fade = own, fades[0]
        before = jnp.zeros_like(own, dtype=F32)
        before_fade = jnp.ones_like(run_fade)
        for mask in order:
            got = turned(swap(run.astype(BF16), "head", mask), mask).astype(F32)
            got_fade = functools.reduce(jnp.multiply, [fades[mask ^ low] for low in range(mask)])
            later = ((me & mask) != 0) if forward else ((me & mask) == 0)
            before = jnp.where(later, before_fade * got + before, before)
            before_fade = jnp.where(later, before_fade * got_fade, before_fade)
            if mask != order[-1]:
                mine = run.astype(F32)
                run = jnp.where(later, run_fade * got + mine, got_fade * mine + got)
                run_fade = run_fade * got_fade
        return before

    inc_in = scan(jnp.concatenate([car0, car1], axis=1), True)
    big = pltpu.VMEM
    (ny, d_gate, d_y, d_inc, back_car, dc_inter, rowpart, rows_sum) = call(
        functools.partial(middle_kernel, blocks, pieces, head_size),
        [((rows, total), BF16), ((rows, total), BF16), ((rows, total), F32), ((blocks, state, total), F32),
         ((state, total), BF16), ((rows, state), F32), ((padded, rows), F32), ((8, total), F32)],
        [scalars, cotangent, inc_in, colp, chan, par, c_low, c_t, y_intra, *outs_m, gate0, gate1, x0, x1, st0, st1],
        scratch=[big((rows, depth), BF16), big((rows, total), BF16), big((rows, total), F32), big((rows, LANES), F32),
                 big((rows, LANES), F32), big((blocks, state, total), BF16), big((rows, total), BF16),
                 big((rows, total), BF16), big((rows, total), BF16)],
        flops=2 * rows * depth * total,
        moved=30 << 20,
    )
    back_in = scan(back_car, False)
    res = call(
        functools.partial(out_kernel, blocks, pieces),
        [((rows, depth), BF16)] + [((total // pieces, depth), BF16)] * pieces + [((depth, total // pieces), BF16)] * pieces,
        [scalars, hidden, cotangent, nt, ny, d_gate, *outs_m],
        scratch=[big((rows, depth), BF16)],
        flops=6 * rows * depth * total,
        moved=12 << 20,
    )
    mixed, g_out, g_gate = res[0], res[1 : pieces + 1], res[pieces + 1 :]

    def split(parts, axis):
        if wide % LANES == 0:
            return list(parts)
        return [h for p in parts for h in jnp.split(p, 2, axis=axis)]

    grad_out = reduce_dp(reduce_pieces(split(g_out, 0)))
    grad_gate = reduce_dp(reduce_pieces(split(g_gate, 1)))

    (dx, db_in, dc_in) = call(
        functools.partial(back_kernel, blocks),
        [((rows, total), F32), ((rows, state), F32), ((rows, state), F32)],
        [scalars, rowp, colp, cbt, b_low, c_low, d_y, x0, x1],
        scratch=[big((blocks, Q, Q), F32)],
        flops=6 * heads * rows * Q * LANES,
        moved=14 << 20,
    )
    (d_inner, d_state, d_step, vgrad, sgrad, hgrad) = call(
        functools.partial(tail_kernel, blocks, head_size),
        [((ext, total), BF16), ((ext, side), BF16), ((padded, rows), BF16), ((8, total), F32), ((8, side), F32),
         ((padded, LANES), F32)],
        [scalars, back_in, inc_in, colp, chan, par, b_low, dx, d_y, d_inc, db_in, dc_in, dc_inter, rowpart, step, ratio,
         sig, hp, rows_sum, state_raw, state_pre, staps, x0, x1, pre0, pre1, inner0, inner1, st0, st1],
        scratch=[big((rows, total), BF16), big((blocks, state, total), BF16), big((rows, total), BF16),
                 big((rows, total), BF16), big((8, total), F32), big((K, rows + 2 * HALO, LANES), F32),
                 big((K, rows + 2 * HALO, side), F32)],
        flops=6 * rows * state * total,
        moved=30 << 20,
    )
    res = call(
        functools.partial(value_kernel, pieces),
        [((depth, total // pieces), BF16)] * pieces + [((padded, depth), F32)],
        [scalars, nx, nt, d_inner, d_step],
        flops=2 * rows * depth * total,
        moved=6 << 20,
    )
    g_value, g_step = res[:pieces], res[pieces]
    grad_value = reduce_dp(reduce_pieces(split(g_value, 1)))
    extra_rows = 832
    (grad_hidden, extra, d_pack) = call(
        functools.partial(norm_kernel, pieces),
        [((rows, depth), F32), ((HALO, depth), F32), ((extra_rows, side), F32)],
        [scalars, hidden, halo, cotangent, gain_in, nx, nt, d_gate, d_inner, d_state, d_step, hp, state_proj, sgrad,
         *gates_m, *values_m],
        flops=4 * rows * depth * total,
        moved=12 << 20,
    )
    extra = lax.ppermute(extra, "head", [(i + 1, i) for i in range(ways - 1)])
    grad_hidden = grad_hidden.at[rows - HALO :].add(extra)

    smalls = []
    for p in range(ways):
        span = slice(p * wide, (p + 1) * wide)
        some = slice(p * share, (p + 1) * share)
        flat = jnp.concatenate(
            [vgrad[0:5, span].reshape(-1), rows_sum[0, span], g_step[some].reshape(-1), hgrad[some, 0:3].reshape(-1)]
        )
        smalls.append(jnp.pad(flat, (0, 32 * side - flat.shape[0])).reshape(32, side))
    core = me & 1
    low_half, high_half = d_pack[: extra_rows // 2], d_pack[extra_rows // 2 :]
    got = swap(jnp.where(core == 0, high_half, low_half).astype(BF16), "head", 1)
    common = jnp.where(core == 0, low_half, high_half) + got.astype(F32)
    for mask in order[1:]:
        low_common = common.astype(BF16)
        common = low_common.astype(F32) + swap(low_common, "head", mask).astype(F32)
    own_small = reduce_pieces(smalls)
    both = reduce_dp(jnp.concatenate([common, own_small], axis=0))
    own_half = both[: extra_rows // 2]
    other = swap(own_half, "head", 1)
    d_all = jnp.concatenate(
        [jnp.where(core == 0, own_half, other), jnp.where(core == 0, other, own_half)], axis=0
    ).astype(F32)
    flat = both[extra_rows // 2 :].astype(F32).reshape(-1)
    grad_vtaps = flat[: 4 * wide].reshape(4, wide)
    grad_vbias = flat[4 * wide : 5 * wide]
    grad_gain = flat[5 * wide : 6 * wide]
    grad_step = flat[6 * wide : 6 * wide + share * depth].reshape(share, depth).T
    rest = flat[6 * wide + share * depth : 6 * wide + share * depth + 3 * share].reshape(share, 3)
    return (
        mixed,
        grad_hidden,
        d_all[depth + 8 : depth + 8 + depth // side].reshape(-1),
        grad_gate.astype(F32),
        grad_value.astype(F32),
        d_all[:depth],
        grad_step,
        grad_vtaps,
        grad_vbias,
        d_all[depth : depth + 4],
        d_all[depth + 4],
        rest[:, 0],
        rest[:, 1],
        rest[:, 2],
        grad_gain,
        grad_out.astype(F32),
    )


def solution(mesh):
    rows = P(("dp", "head"), None)
    in_specs = (
        rows, P("dp", None), P(), P(None, "head"), P(None, "head"), P(), P(None, "head"), P(None, "head"),
        P("head"), P(), P(), P("head"), P("head"), P("head"), P("head"), P("head", None), rows,
    )
    out_specs = (
        rows, rows, P(), P(None, "head"), P(None, "head"), P(), P(None, "head"), P(None, "head"),
        P("head"), P(), P(), P("head"), P("head"), P("head"), P("head"), P("head", None),
    )
    return jax.shard_map(body, mesh=mesh, in_specs=in_specs, out_specs=out_specs, check_vma=False)
```

```python
import functools

import jax
import jax.numpy as jnp
from jax import lax
from jax.experimental import pallas as pl
from jax.experimental.pallas import tpu as pltpu
from jax.sharding import PartitionSpec as P

K = 4
Q = 256
HALO = 16
LANES = 128
EPSILON = 1e-05
F32 = jnp.float32
BF16 = jnp.bfloat16
HIGHEST = lax.Precision.HIGHEST


def mm(left, right, lc=1, rc=0, precision=None):
    return lax.dot_general(
        left,
        right,
        (((lc,), (rc,)), ((), ())),
        preferred_element_type=F32,
        precision=precision,
    )


MIB = 1024 * 1024
PRE, FRONT, INTRA, MIDDLE, BACK, TAIL, STATE, FINAL = 12, 14, 12, 21, 12, 16, 12, 24


def whole(shape):
    return pl.BlockSpec(shape, lambda *_: (0,) * len(shape))


def call(kernel, outs, args, scratch=(), grid=(), ins=None, out_specs=None, aliases=None, mib=48, cost=0, pin=pltpu.VMEM, kinds=None):
    ins, out_specs, kinds = ins or {}, out_specs or {}, kinds or {}
    specs = [pl.BlockSpec(memory_space=pltpu.SMEM)]
    for at, value in enumerate(args[1:], 1):
        specs.append(ins[at] if at in ins else whole(value.shape))
    outs_specs = [out_specs[at] if at in out_specs else whole(o[0]) for at, o in enumerate(outs)]
    return pl.pallas_call(
        kernel,
        grid=grid,
        out_shape=[kinds[at](s, d) if at in kinds else pin(s, d) for at, (s, d) in enumerate(outs)],
        in_specs=specs,
        out_specs=outs_specs,
        scratch_shapes=list(scratch),
        input_output_aliases=aliases or {},
        compiler_params=pltpu.CompilerParams(vmem_limit_bytes=mib * MIB),
        cost_estimate=pl.CostEstimate(flops=int(cost * 4e8), bytes_accessed=int(cost * 3e5), transcendentals=0),
    )(*args)


def keeps_of(s_ref, block, blocks):
    place = s_ref[0] * blocks + block
    fresh = (place == 0) | (place == 1) | (place == s_ref[1] - 1)
    return fresh, jnp.where(fresh, 0.0, 1.0).astype(F32)


def row_keep(fresh, distance):
    rows = lax.broadcasted_iota(jnp.int32, (Q, 1), 0)
    return (rows >= jnp.where(fresh, distance, 0)).astype(F32)


def conv_block(ref, base, cols, taps, fresh):
    total = taps[K : K + 1] + taps[K - 1 : K] * ref[pl.ds(base, Q), cols]
    for distance in range(1, K):
        earlier = ref[pl.ds(base - distance, Q), cols]
        total = total + taps[K - 1 - distance : K - distance] * (earlier * row_keep(fresh, distance))
    return total


def silu_slope(values, sig):
    return sig * (1.0 + values * (1.0 - sig))


def first_lanes():
    return lax.broadcasted_iota(jnp.int32, (1, LANES), 1) < LANES // 2


def spread(cols, quantity):
    return jnp.where(
        first_lanes(), cols[:, 2 * quantity : 2 * quantity + 1], cols[:, 2 * quantity + 1 : 2 * quantity + 2]
    )


def head_lanes(rows, heads_first, head_size):
    lane = lax.broadcasted_iota(jnp.int32, rows, 1 if heads_first else 0)
    head = lax.broadcasted_iota(jnp.int32, rows, 0 if heads_first else 1)
    return (lane >= head * head_size) & (lane < (head + 1) * head_size)


def pre_kernel(blocks, s_ref, hid_ref, halo_ref, gain_ref, proj_ref, taps_ref,
               nx_ref, nt_ref, raw_ref, pre_ref, b_ref, c_ref, bt_ref, ct_ref, cb_ref, cbt_ref):
    gain = gain_ref[...]
    rows = blocks * Q

    def norm(v):
        v = v.astype(F32)
        return v * lax.rsqrt(jnp.mean(v * v, axis=1, keepdims=True) + EPSILON) * gain

    halo = norm(halo_ref[...])
    own = norm(hid_ref[...])
    nx_ref[0:HALO] = halo.astype(BF16)
    nx_ref[HALO:] = own.astype(BF16)
    nt_ref[:, 0:rows] = own.T.astype(BF16)
    raw_ref[...] = mm(nx_ref[...], proj_ref[...])
    taps = taps_ref[...]
    state = b_ref.shape[1]
    for block in range(blocks):
        fresh, _ = keeps_of(s_ref, block, blocks)
        pre = conv_block(raw_ref, HALO + block * Q, slice(None), taps, fresh)
        at = pl.ds(block * Q, Q)
        pre_ref[at] = pre
        conv = pre * jax.nn.sigmoid(pre)
        b_mat = conv[:, :state]
        c_mat = conv[:, state:]
        b_low = b_mat.astype(BF16)
        c_low = c_mat.astype(BF16)
        b_ref[at] = b_low
        c_ref[at] = c_low
        bt_ref[:, at] = b_mat.T.astype(BF16)
        ct_ref[:, at] = c_mat.T.astype(BF16)
        cb_ref[block] = mm(c_low, b_low, 1, 1)
        cbt_ref[block] = mm(b_low, c_low, 1, 1)


def step_kernel(blocks, head_size, s_ref, nx_ref, hp_ref, rowp_ref, colp_ref, step_ref, ratio_ref, sig_ref, chan_ref):
    depth = nx_ref.shape[1]
    hp = hp_ref[...]
    u = mm(hp[:, :depth].astype(BF16), nx_ref[HALO:], 1, 1) + hp[:, depth : depth + 1]
    step = jnp.maximum(u, 0.0) + jnp.log1p(jnp.exp(-jnp.abs(u)))
    sig = jax.nn.sigmoid(u)
    step_ref[...] = step
    sig_ref[...] = sig
    ratio_ref[...] = jnp.where(step > 1e-30, sig / jnp.maximum(step, 1e-30), 1.0)
    rate = -jnp.exp(hp[:, depth + 1 : depth + 2])
    move = step * rate
    upto = (
        lax.broadcasted_iota(jnp.int32, (Q, Q), 0) <= lax.broadcasted_iota(jnp.int32, (Q, Q), 1)
    ).astype(F32)
    heads = hp.shape[0]
    lane = lax.broadcasted_iota(jnp.int32, (heads, LANES), 1)
    last_cols = jnp.zeros((heads, LANES), F32)
    lstep = jnp.log(step)
    product = jnp.ones((heads, 1), F32)
    pairs = rowp_ref.shape[0]
    for block in range(blocks):
        at = slice(block * Q, (block + 1) * Q)
        logd = mm(move[:, at], upto, precision=HIGHEST)
        less = logd - lstep[:, at]
        last = logd[:, Q - 1 : Q]
        grown = jnp.exp(logd)
        carry = jnp.exp(last - less)
        final = jnp.exp(last)
        _, kept = keeps_of(s_ref, block, blocks)
        product = product * final * kept
        last_cols = jnp.where(lane == block, final, last_cols)
        for pair in range(pairs):
            for index, values in enumerate((logd, less, grown, carry)):
                rowp_ref[pair, 2 * index : 2 * index + 2, at] = values[2 * pair : 2 * pair + 2]
    last_cols = jnp.where(lane == 6, product, last_cols)
    last_cols = jnp.where(lane == 7, hp[:, depth + 2 : depth + 3], last_cols)
    spots = head_lanes((heads, chan_ref.shape[1]), True, head_size).astype(F32)
    chan_ref[...] = mm(last_cols.T[0:8], spots, precision=HIGHEST)
    for pair in range(pairs):
        colp_ref[pair] = rowp_ref[pair].T


def carry_block(ref, cols, carry, fades):
    state = carry.shape[0]
    ref[0:state, cols] = carry.astype(BF16)
    high = fades.astype(BF16).astype(F32)
    row = lax.broadcasted_iota(jnp.int32, (HALO, LANES), 0)
    ref[state:, cols] = jnp.where(row == 0, high, jnp.where(row == 1, fades - high, 0.0)).astype(BF16)


def tile_at(index):
    return pl.ds(pl.multiple_of(index * LANES, LANES), LANES)


def front_kernel(blocks, first_piece, pieces, s_ref, nx_ref, par_ref, bt_ref, colp_ref, chan_ref, *refs):
    weights = refs[:pieces]
    (gate_out, inner_out, pre_out, s_out, x_ref, carry_ref, turned_ref,
     gate_ref, inner_ref, pre_ref, st_ref, work, sems) = refs[-13:]
    done = refs[pieces:-13]
    wide = weights[0].shape[1] // 2
    for old, new in zip(done[4:], (x_ref, carry_ref, turned_ref)):
        new[:, 0 : first_piece * wide] = old[:, 0 : first_piece * wide]
    own = slice(first_piece * wide, (first_piece + pieces) * wide)
    moves = [(gate_ref, gate_out), (inner_ref, inner_out), (pre_ref, pre_out), (st_ref, s_out)]
    for p in range(pieces):
        here = slice(p * wide, (p + 1) * wide)
        work[:, here] = mm(nx_ref[...], weights[p][:, wide:])
        gate_ref[:, here] = mm(nx_ref[HALO:], weights[p][:, :wide]).astype(BF16)
    tiles = wide // LANES

    def tile(i, none):
        here = tile_at(i)
        pair = i + first_piece * tiles
        far = tile_at(pair)
        turned = tile_at(jnp.bitwise_xor(pair // tiles, 1) * tiles + pair % tiles)
        taps = par_ref[:, far]
        inner_ref[:, here] = work[:, here].astype(BF16)
        for block in range(blocks):
            at = pl.ds(block * Q, Q)
            fresh, kept = keeps_of(s_ref, block, blocks)
            pre = conv_block(work, HALO + block * Q, here, taps, fresh)
            pre_ref[at, here] = pre.astype(BF16)
            x = pre * jax.nn.sigmoid(pre)
            x_ref[at, far] = x.astype(BF16)
            weighted = (spread(colp_ref[pair, at, :], 3) * x).astype(BF16)
            state = mm(bt_ref[:, at], weighted)
            st_ref[block, :, here] = state
            if block == 0:
                carry = state
            else:
                carry = chan_ref[block : block + 1, far] * (kept * carry) + state
        carry_block(carry_ref, far, carry, chan_ref[6:7, far])
        carry_block(turned_ref, turned, carry, chan_ref[6:7, far])
        for index, (held, out) in enumerate(moves):
            pltpu.make_async_copy(held.at[..., here], out.at[..., far], sems.at[index]).start()
        return none

    lax.fori_loop(0, pieces * tiles, tile, 0)
    for index, (held, out) in enumerate(moves):
        pltpu.make_async_copy(held, out.at[..., own], sems.at[index]).wait()


def unpack_carry(ref):
    state = ref.shape[0] - HALO
    return ref[0:state].astype(F32), ref[state : state + 1].astype(F32) + ref[state + 1 : state + 2].astype(F32)


def join_kernel(forward, s_ref, own_ref, got_ref, out_ref):
    mine, my_fade = unpack_carry(own_ref)
    his, his_fade = unpack_carry(got_ref)
    later = (jnp.bitwise_and(s_ref[0], 1) == 1) == forward
    state = mine.shape[0]
    total = jnp.where(later, my_fade * his + mine, his_fade * mine + his)
    fade = my_fade * his_fade
    high = fade.astype(BF16).astype(F32)
    row = lax.broadcasted_iota(jnp.int32, (HALO, total.shape[1]), 0)
    out_ref[0:state] = total.astype(BF16)
    out_ref[state:] = jnp.where(row == 0, high, jnp.where(row == 1, fade - high, 0.0)).astype(BF16)


def arrive_kernel(forward, s_ref, near_ref, far_ref, out_ref):
    near, near_fade = unpack_carry(near_ref)
    wide = near.shape[1] // 2
    later = (jnp.bitwise_and(s_ref[0], 1) == 1) == forward
    far_later = (jnp.bitwise_and(s_ref[0], 2) == 2) == forward
    near = jnp.where(later, near, 0.0)
    fade = jnp.where(far_later, jnp.where(later, near_fade, 1.0), 0.0)
    for half in range(2):
        here, there = slice(half * wide, (half + 1) * wide), slice((1 - half) * wide, (2 - half) * wide)
        out_ref[:, here] = near[:, here] + fade[:, here] * far_ref[0 : near.shape[0], there].astype(F32)


def masked_cotangent(s_ref, cot_ref, blocks, block):
    at = slice(block * Q, (block + 1) * Q)
    return cot_ref[at].astype(F32) * valid_of(s_ref, blocks, block)


def intra_kernel(blocks, pieces, s_ref, rowp_ref, colp_ref, cb_ref, x_ref, cot_ref, *refs):
    outs_w = refs[:pieces]
    y_ref, dny_ref, db_ref = refs[pieces:]
    for block in range(blocks):
        db_ref[block * Q : (block + 1) * Q] = masked_cotangent(s_ref, cot_ref, blocks, block).astype(BF16)
    wide = outs_w[0].shape[0]
    for p in range(pieces):
        dny_ref[:, p * wide : (p + 1) * wide] = mm(db_ref[...], outs_w[p][...], 1, 1).astype(BF16)
    half = Q // 2
    first = first_lanes()
    tri = lax.broadcasted_iota(jnp.int32, (half, half), 0) >= lax.broadcasted_iota(
        jnp.int32, (half, half), 1
    )

    def work(pair):
        far = tile_at(pair)
        for block in range(blocks):
            at = pl.ds(block * Q, Q)
            x = x_ref[at, far]
            both = [jnp.where(first, x, 0), jnp.where(first, 0, x)]
            rp = rowp_ref[pair, :, at]
            cp = colp_ref[pair, at, :]
            tops, bots = [], []
            for k in range(2):
                ld, ls = cp[:, k : k + 1], rp[2 + k : 3 + k, :]
                arg = jnp.where(tri, ld[:half] - ls[:, :half], -1e30)
                tops.append((cb_ref[block, 0:half, 0:half] * jnp.exp(arg)).astype(BF16))
                arg = ld[half:] - ls[:, :half]
                bots.append((cb_ref[block, half:, 0:half] * jnp.exp(arg)).astype(BF16))
                arg = jnp.where(tri, ld[half:] - ls[:, half:], -1e30)
                bots.append((cb_ref[block, half:, half:] * jnp.exp(arg)).astype(BF16))
            y_ref[pl.ds(block * Q, half), far] = mm(jnp.concatenate(tops, 1), jnp.concatenate([b[:half] for b in both], 0))
            y_ref[pl.ds(block * Q + half, half), far] = mm(jnp.concatenate(bots, 1), jnp.concatenate(both, 0))

    def two(i, none):
        work(2 * i)
        work(2 * i + 1)
        return none

    lax.fori_loop(0, x_ref.shape[1] // (2 * LANES), two, 0)


def split_store(hi_ref, lo_ref, at, cols, part):
    high = part.astype(BF16)
    hi_ref[at, cols] = high
    lo_ref[at, cols] = (part - high.astype(F32)).astype(BF16)


def head_sums(heads, head_size, hi_ref, lo_ref):
    spots = head_lanes((heads, hi_ref.shape[1]), True, head_size).astype(F32).astype(BF16)
    return mm(spots, hi_ref[...], 1, 1) + mm(spots, lo_ref[...], 1, 1)


def valid_of(s_ref, blocks, block):
    place = s_ref[0] * blocks + block
    last = place == s_ref[1] - 1
    length = jnp.where(place == 0, s_ref[2], jnp.where(last, s_ref[4], s_ref[3]))
    start = jnp.where(place == 0, 0, jnp.where(last, s_ref[1] - 1, 1))
    rows = lax.broadcasted_iota(jnp.int32, (Q, 1), 0) + (place - start) * Q
    return (rows < length).astype(F32)


def piece_loop(total_tiles, tiles, work, store, keep_ref, send_ref):
    half = total_tiles // 2

    for odd, ref in ((1, send_ref), (0, keep_ref)):
        def place(i, odd=odd):
            return (2 * (i // tiles) + odd) * tiles + i % tiles

        def turn(i, none, place=place, ref=ref):
            before = jnp.maximum(2 * i - 2, 0)
            store([before, before + 1], [place(before), place(before + 1)], ref)
            work(place(2 * i))
            work(place(2 * i + 1))
            return none

        lax.fori_loop(0, half // 2, turn, 0)
        store([half - 2, half - 1], [place(half - 2), place(half - 1)], ref)


def store_grad(ref, at, tiles, rows_at, value):
    for j in range(2):
        slot, lane = at[j] // tiles, at[j] % tiles
        cols = tile_at(lane) if not isinstance(lane, int) else slice(lane * LANES, (lane + 1) * LANES)
        ref[slot, rows_at, cols] = value[:, j * LANES : (j + 1) * LANES]


def middle_kernel(blocks, tiles, head_size, s_ref, cot_ref, inc_in, colp_ref, chan_ref, par_ref, c_ref, ct_ref, nt_ref,
                  y_ref, dny_ref, gate_ref, x_ref, st_ref,
                  ny_out, dgate_out, keep_out, send_out, inc_ref, di_ref, dy_ref, carry_ref, turned_ref, dc_ref, rowpart_ref,
                  rows_ref, ny_ref, dgate_ref, keep_ref, send_ref,
                  dbt_ref, mix_ref, sq_ref, cr_ref, dye_ref, hi_ref, lo_ref, sems):
    moves = [(ny_ref, ny_out), (dgate_ref, dgate_out), (keep_ref, keep_out), (send_ref, send_out)]

    def move(index, *where):
        held, out = moves[index]
        pltpu.make_async_copy(held.at[where], out.at[where], sems.at[index]).start()

    depth = cot_ref.shape[1]
    total = chan_ref.shape[1]
    kept = [keeps_of(s_ref, block, blocks)[1] for block in range(blocks)]
    for block in range(blocks):
        at = slice(block * Q, (block + 1) * Q)
        dbt_ref[:, at] = masked_cotangent(s_ref, cot_ref, blocks, block).T.astype(BF16)
    sq_ref[...] = jnp.zeros_like(sq_ref)
    cr_ref[...] = jnp.zeros_like(cr_ref)

    def forward(i, none):
        for pair in (2 * i, 2 * i + 1):
            far = tile_at(pair)
            incoming = inc_in[:, far]
            for block in range(blocks):
                at = pl.ds(block * Q, Q)
                incoming = kept[block] * incoming
                inc_low = incoming.astype(BF16)
                inc_ref[block, :, far] = inc_low
                incoming = chan_ref[block : block + 1, far] * incoming + st_ref[block, :, far]
                inter = mm(c_ref[at], inc_low) * spread(colp_ref[pair, at, :], 2)
                mix = y_ref[at, far] + inter + chan_ref[7:8, far] * x_ref[at, far].astype(F32)
                mix_ref[at, far] = mix
                gate = gate_ref[at, far].astype(F32)
                gated = mix * (gate * jax.nn.sigmoid(gate))
                sq_ref[at] += gated * gated
                cr_ref[at] += dny_ref[at, far].astype(F32) * par_ref[5:6, far] * gated
        return none

    lax.fori_loop(0, total // (2 * LANES), forward, 0)
    scale = lax.rsqrt(jnp.sum(sq_ref[...], axis=1, keepdims=True) / total + EPSILON)
    coef = scale * scale * scale * (jnp.sum(cr_ref[...], axis=1, keepdims=True) / total)
    sq_ref[...] = jnp.broadcast_to(scale, sq_ref.shape)
    cr_ref[...] = jnp.broadcast_to(coef, cr_ref.shape)
    rows_ref[...] = jnp.zeros_like(rows_ref)

    def backward(pair):
        far = tile_at(pair)
        gain = par_ref[5:6, far]
        skip = chan_ref[7:8, far]
        gain_row = jnp.zeros((1, LANES), F32)
        skip_row = jnp.zeros((1, LANES), F32)
        dis = []
        for block in range(blocks):
            at = pl.ds(block * Q, Q)
            gate, mix, x = gate_ref[at, far].astype(F32), mix_ref[at, far], x_ref[at, far].astype(F32)
            sig = jax.nn.sigmoid(gate)
            act = gate * sig
            gated = mix * act
            normed = gated * sq_ref[at]
            dny = dny_ref[at, far].astype(F32)
            ny_ref[at, far] = (normed * gain).astype(BF16)
            gain_row += jnp.sum(dny * normed, axis=0, keepdims=True)
            d_gated = dny * gain * sq_ref[at] - gated * cr_ref[at]
            dgate_ref[at, far] = (d_gated * mix * silu_slope(gate, sig)).astype(BF16)
            dy = d_gated * act
            dy_low = dy.astype(BF16)
            dy_ref[at, far] = dy_low
            skip_row += jnp.sum(dy * x, axis=0, keepdims=True)
            split_store(hi_ref, lo_ref, at, far, dy_low.astype(F32) * (mix - skip * x))
            dye = (dy * spread(colp_ref[pair, at, :], 2)).astype(BF16)
            dye_ref[at, far] = dye
            di = mm(ct_ref[:, at], dye).astype(BF16)
            di_ref[block, :, far] = di
            dis.append(di.astype(F32))
        rows_ref[0:1, far] = gain_row
        rows_ref[1:2, far] = skip_row
        back = jnp.zeros_like(dis[0])
        for block in reversed(range(blocks)):
            back = kept[block] * (dis[block] + chan_ref[block : block + 1, far] * back)
        carry_block(carry_ref, far, back, chan_ref[6:7, far])
        turned = tile_at(jnp.bitwise_xor(pair // tiles, 1) * tiles + pair % tiles)
        carry_block(turned_ref, turned, back, chan_ref[6:7, far])
        move(0, slice(None), far)
        move(1, slice(None), far)

    def store(at, places, ref):
        cols = [tile_at(place) for place in places]
        normed = jnp.concatenate([ny_ref[:, c] for c in cols], 1)
        store_grad(ref, at, tiles, slice(0, depth), mm(dbt_ref[...], normed).astype(BF16))
        gates = jnp.concatenate([dgate_ref[:, c] for c in cols], 1)
        store_grad(ref, at, tiles, slice(depth, 2 * depth), mm(nt_ref[...], gates).astype(BF16))

    piece_loop(total // LANES, tiles, backward, store, keep_ref, send_ref)
    move(2)
    move(3)
    rowpart_ref[...] = head_sums(rowpart_ref.shape[0], head_size, hi_ref, lo_ref)
    for block in range(blocks):
        at = slice(block * Q, (block + 1) * Q)
        dc_ref[at] = mm(dye_ref[at], inc_ref[block], 1, 1)
    for index, (held, out) in enumerate(moves):
        pltpu.make_async_copy(held, out, sems.at[index]).wait()


def back_kernel(blocks, head_size, s_ref, rowp_ref, colp_ref, cbt_ref, b_ref, c_ref, dy_ref, x_ref,
                dx_ref, part_ref, db_ref, dc_ref, acc_ref, hi_ref, lo_ref):
    half = Q // 2
    first = first_lanes()
    tri = lax.broadcasted_iota(jnp.int32, (half, half), 0) <= lax.broadcasted_iota(
        jnp.int32, (half, half), 1
    )
    acc_ref[...] = jnp.zeros_like(acc_ref)

    def two(i, none):
        for block in range(blocks):
            at = pl.ds(block * Q, Q)
            w00 = w01 = w11 = 0.0
            for pair in (2 * i, 2 * i + 1):
                far = tile_at(pair)
                x, dy = x_ref[at, far], dy_ref[at, far]
                dys = [jnp.where(first, dy, 0), jnp.where(first, 0, dy)]
                xs = [jnp.where(first, x, 0), jnp.where(first, 0, x)]
                rp = rowp_ref[pair, :, at]
                cp = colp_ref[pair, at, :]
                tops, bots = [], []
                for k in range(2):
                    ls, ld = cp[:, 2 + k : 3 + k], rp[k : k + 1, :]
                    ds_top = mm(xs[k][:half], dy, 1, 1)
                    ds_bot = mm(xs[k][half:], dy[half:], 1, 1)
                    e00 = jnp.exp(jnp.where(tri, ld[:, :half] - ls[:half], -1e30))
                    e01 = jnp.exp(ld[:, half:] - ls[:half])
                    e11 = jnp.exp(jnp.where(tri, ld[:, half:] - ls[half:], -1e30))
                    tops.append((cbt_ref[block, 0:half, 0:half] * e00).astype(BF16))
                    tops.append((cbt_ref[block, 0:half, half:] * e01).astype(BF16))
                    bots.append((cbt_ref[block, half:, half:] * e11).astype(BF16))
                    w00 += ds_top[:, :half] * e00
                    w01 += ds_top[:, half:] * e01
                    w11 += ds_bot * e11
                dx_top = mm(jnp.concatenate(tops, 1), jnp.concatenate(dys, 0))
                dx_bot = mm(jnp.concatenate(bots, 1), jnp.concatenate([d[half:] for d in dys], 0))
                dx = jnp.concatenate([dx_top, dx_bot], 0)
                dx_ref[at, far] = dx.astype(BF16)
                split_store(hi_ref, lo_ref, at, far, x.astype(F32) * dx)
            acc_ref[block, 0:half, 0:half] += w00
            acc_ref[block, 0:half, half:] += w01
            acc_ref[block, half:, half:] += w11
        return none

    lax.fori_loop(0, x_ref.shape[1] // (2 * LANES), two, 0)
    part_ref[...] = head_sums(part_ref.shape[0], head_size, hi_ref, lo_ref)
    for block in range(blocks):
        at = slice(block * Q, (block + 1) * Q)
        acc = acc_ref[block].astype(BF16)
        db_ref[at] = mm(acc, c_ref[at])
        dc_ref[at] = mm(acc, b_ref[at], 0, 0)


def conv_back(s_ref, blocks, work, taps, values_of, slope_of, store):
    sums = [0.0] * (K + 1)
    for block in range(blocks):
        fresh, _ = keeps_of(s_ref, block, blocks)
        d_pre = slope_of(block)
        work[0, pl.ds(HALO + block * Q, Q)] = d_pre
        sums[K] += jnp.sum(d_pre, axis=0, keepdims=True)
        sums[K - 1] += jnp.sum(d_pre * values_of(HALO + block * Q), axis=0, keepdims=True)
        for distance in range(1, K):
            held = d_pre * row_keep(fresh, distance)
            work[distance, pl.ds(HALO + block * Q, Q)] = held
            sums[K - 1 - distance] += jnp.sum(
                held * values_of(HALO + block * Q - distance), axis=0, keepdims=True
            )
    for begin, count in [(0, HALO)] + [(HALO + b * Q, Q) for b in range(blocks)]:
        out = taps[K - 1 : K] * work[0, pl.ds(begin, count)]
        for distance in range(1, K):
            out = out + taps[K - 1 - distance : K - distance] * work[distance, pl.ds(begin + distance, count)]
        store(begin, count, out.astype(BF16))
    return sums


def tail_kernel(blocks, tiles, head_size, s_ref, back_in, colp_ref, chan_ref, par_ref, b_ref, nt_ref, nx_ref,
                inc_ref, dx_ref, dy_ref, di_ref, x_ref, pre_ref, inner_ref,
                dinner_ref, vgrad_ref, part_ref, lasts_ref, db_ref, keep_ref, send_ref,
                d_ref, in_ref, wx_ref, gs_ref, hi_ref, lo_ref):
    total = chan_ref.shape[1]
    kept = [keeps_of(s_ref, block, blocks)[1] for block in range(blocks)]
    d_ref[...] = jnp.zeros_like(d_ref)
    vgrad_ref[...] = jnp.zeros_like(vgrad_ref)
    lasts_ref[...] = jnp.zeros_like(lasts_ref)

    def work(pair):
        far = tile_at(pair)
        in_ref[...] = inner_ref[:, far].astype(F32)
        skip = chan_ref[7:8, far]
        back = back_in[:, far]
        lasts = [None] * blocks
        for block in reversed(range(blocks)):
            fade = chan_ref[block : block + 1, far]
            gs_ref[block, :, far] = back.astype(BF16)
            lasts[block] = fade * jnp.sum(inc_ref[block, :, far].astype(F32) * back, axis=0, keepdims=True)
            back = kept[block] * (di_ref[block, :, far].astype(F32) + fade * back)

        def slope_of(block):
            at = pl.ds(block * Q, Q)
            carry = spread(colp_ref[pair, at, :], 3)
            weighted = carry * x_ref[at, far].astype(F32)
            wx_ref[at, far] = weighted.astype(BF16)
            d_weighted = mm(b_ref[at], gs_ref[block, :, far])
            moved = weighted * d_weighted
            lasts_ref[block : block + 1, far] = lasts[block] + jnp.sum(moved, axis=0, keepdims=True)
            split_store(hi_ref, lo_ref, at, far, moved)
            d_x = dx_ref[at, far].astype(F32) + carry * d_weighted + skip * dy_ref[at, far].astype(F32)
            pre = pre_ref[at, far].astype(F32)
            return d_x * silu_slope(pre, jax.nn.sigmoid(pre))

        def store(begin, count, value):
            dinner_ref[pl.ds(begin, count), far] = value

        sums = conv_back(s_ref, blocks, d_ref, par_ref[:, far], lambda at: in_ref[pl.ds(at, Q)], slope_of, store)
        for index in range(K + 1):
            vgrad_ref[index : index + 1, far] = sums[index]

    def store_two(at, places, ref):
        cols = [tile_at(place) for place in places]
        own = jnp.concatenate([dinner_ref[HALO:, c] for c in cols], 1)
        halo = jnp.concatenate([dinner_ref[0:HALO, c] for c in cols], 1)
        grad = mm(nt_ref[...], own) + mm(nx_ref[0:HALO], halo, 0, 0)
        store_grad(ref, at, tiles, slice(None), grad.astype(BF16))

    piece_loop(total // LANES, tiles, work, store_two, keep_ref, send_ref)
    part_ref[...] = head_sums(part_ref.shape[0], head_size, hi_ref, lo_ref)
    for block in range(blocks):
        at = slice(block * Q, (block + 1) * Q)
        db_ref[at] = mm(wx_ref[at], gs_ref[block], 1, 1)


def state_kernel(blocks, head_size, shares, s_ref, dbx_ref, dbin_ref, dcin_ref, dcx_ref, raw_ref, spre_ref, staps_ref,
                 rowpart_ref, part_a, part_b, step_ref, ratio_ref, sig_ref, hp_ref, rows_ref, lasts_ref, vgrad_ref,
                 nt_ref, nx_ref, dstate_ref, dstep_ref, *refs):
    e_ref, all_ref, step_grad_ref = refs[-3:]
    outs = refs[:-3]
    e_ref[...] = jnp.zeros_like(e_ref)
    d_states = []
    for block in range(blocks):
        at = slice(block * Q, (block + 1) * Q)
        d_states.append(jnp.concatenate([dbin_ref[at] + dbx_ref[at], dcin_ref[at] + dcx_ref[at]], 1))

    def slope_of(block):
        pre = spre_ref[pl.ds(block * Q, Q), :]
        return d_states[block] * silu_slope(pre, jax.nn.sigmoid(pre))

    def store(begin, count, value):
        dstate_ref[pl.ds(begin, count), :] = value

    sgrad = conv_back(s_ref, blocks, e_ref, staps_ref[...], lambda at: raw_ref[pl.ds(at, Q), :], slope_of, store)
    heads = hp_ref.shape[0]
    total = lasts_ref.shape[1]
    depth = hp_ref.shape[1] - LANES
    spots = head_lanes((heads, total), True, head_size).astype(F32)
    lasts = mm(spots, lasts_ref[...], 1, 1, precision=HIGHEST)
    skips = mm(spots, rows_ref[...], 1, 1, precision=HIGHEST)[:, 1:2]
    rate = -jnp.exp(hp_ref[:, depth + 1 : depth + 2])
    lane = lax.broadcasted_iota(jnp.int32, (heads, Q), 1)
    upto = (
        lax.broadcasted_iota(jnp.int32, (Q, Q), 0) >= lax.broadcasted_iota(jnp.int32, (Q, Q), 1)
    ).astype(F32)
    grad_bias = jnp.zeros((heads, 1), F32)
    grad_decay = jnp.zeros((heads, 1), F32)
    for block in range(blocks):
        at = slice(block * Q, (block + 1) * Q)
        cols = part_a[:, at] + part_b[:, at]
        d_log = rowpart_ref[:, at] - cols + jnp.where(lane == Q - 1, lasts[:, block : block + 1], 0.0)
        d_move = mm(d_log, upto, precision=HIGHEST)
        d_raw = cols * ratio_ref[:, at] + rate * d_move * sig_ref[:, at]
        grad_bias += jnp.sum(d_raw, axis=1, keepdims=True)
        grad_decay += rate * jnp.sum(step_ref[:, at] * d_move, axis=1, keepdims=True)
        dstep_ref[:, at] = d_raw.astype(BF16)
    wide_lane = lax.broadcasted_iota(jnp.int32, (heads, LANES), 1)
    per_head = jnp.where(
        wide_lane == 0, grad_bias, jnp.where(wide_lane == 1, grad_decay, jnp.where(wide_lane == 2, skips, 0.0))
    )
    step_grad_ref[...] = mm(dstep_ref[...], nx_ref[HALO:])
    all_ref[...] = jnp.zeros_like(all_ref)
    all_ref[0:depth] = mm(nt_ref[...], dstate_ref[HALO:]) + mm(nx_ref[0:HALO], dstate_ref[0:HALO], 0, 0)
    for index in range(K + 1):
        all_ref[depth + index : depth + index + 1] = sgrad[index]
    if not shares:
        outs[0][...] = all_ref[...]
        outs[1][...] = step_grad_ref[...]
        outs[2][...] = per_head
        return
    ways, share, wide = shares
    quarter = all_ref.shape[0] // ways
    work = outs[-1]
    for p in range(ways):
        span = slice(p * wide, (p + 1) * wide)
        some = slice(p * share, (p + 1) * share)
        work[...] = jnp.zeros_like(work)
        work[0 : K + 1] = vgrad_ref[0 : K + 1, span]
        work[K + 1 : K + 2] = rows_ref[0:1, span]
        for part in range(depth // wide):
            begin = 8 + part * share
            work[begin : begin + share] = step_grad_ref[some, part * wide : (part + 1) * wide]
        work[24 : 24 + share, 0:LANES] = per_head[some]
        owner = jnp.bitwise_xor(s_ref[0], p)
        work[32 : 32 + quarter, 0 : all_ref.shape[1]] = all_ref[pl.ds(pl.multiple_of(owner * quarter, 8), quarter)]
        outs[p % 2][p // 2] = work[...].astype(BF16)


def final_kernel(pieces, blocks, s_ref, hid_ref, halo_ref, cot_ref, gain_ref, ny_ref, dgate_ref, dinner_ref, dstate_ref,
                 dstep_ref, hp_ref, sproj_ref, *refs):
    both, outs_w = refs[:pieces], refs[pieces : 2 * pieces]
    mixed_ref, grad_ref, extra_ref, gain_out = refs[2 * pieces :]
    wide = outs_w[0].shape[0]
    depth = hid_ref.shape[1]
    gain = gain_ref[...]
    gain_sum = jnp.zeros((1, depth), F32)

    def finish(values_in, d_normed):
        h = values_in.astype(F32)
        scale = lax.rsqrt(jnp.mean(h * h, axis=1, keepdims=True) + EPSILON)
        weighted = gain * d_normed
        inner = jnp.mean(weighted * h, axis=1, keepdims=True)
        return scale * weighted - h * (scale * scale * scale * inner), jnp.sum(d_normed * h * scale, axis=0, keepdims=True)

    total = mm(dstate_ref[0:HALO], sproj_ref[...], 1, 1)
    for p in range(pieces):
        total += mm(dinner_ref[0:HALO, p * wide : (p + 1) * wide], both[p][:, wide:], 1, 1)
    extra_ref[...], part = finish(halo_ref[...], total)
    gain_sum += part
    for block in range(blocks):
        at = slice(block * Q, (block + 1) * Q)
        ext = slice(HALO + block * Q, HALO + (block + 1) * Q)
        total = mm(dstate_ref[ext], sproj_ref[...], 1, 1)
        total += mm(dstep_ref[:, at], hp_ref[:, 0:depth].astype(BF16), 0, 0)
        branch = mm(ny_ref[at, 0:wide], outs_w[0][...])
        for p in range(pieces):
            span = slice(p * wide, (p + 1) * wide)
            total += mm(dgate_ref[at, span], both[p][:, :wide], 1, 1)
            total += mm(dinner_ref[ext, span], both[p][:, wide:], 1, 1)
            if p:
                branch += mm(ny_ref[at, span], outs_w[p][...])
        mixed_ref[at] = (hid_ref[at].astype(F32) + valid_of(s_ref, blocks, block) * branch).astype(BF16)
        d_hidden, part = finish(hid_ref[at], total.astype(BF16).astype(F32))
        gain_sum += part
        grad_ref[at] = cot_ref[at].astype(F32) + d_hidden
    gain_out[...] = jnp.zeros_like(gain_out)
    side = gain_out.shape[1]
    for index in range(depth // side):
        gain_out[index : index + 1] = gain_sum[:, index * side : (index + 1) * side]


def gather_far(value, ahead):
    ways = lax.axis_size("head")
    pieces = {0: value}
    far = {0: after(value, ahead)}
    mask = 2
    while mask < ways:
        for p in list(far):
            far[p | mask] = swap(far[p], "head", mask)
        mask *= 2
    return [value] + [far[p] for p in range(2, ways, 2)]


def near_pair(value, ahead):
    return value, swap(after(value, ahead) if len(ahead) else value, "head", 1)


def swap(value, axis, mask):
    size = lax.axis_size(axis)
    return lax.ppermute(value, axis, [(i, i ^ mask) for i in range(size)])


def pick(value, index):
    return lax.dynamic_index_in_dim(value, index, 0, keepdims=False)


def reduce_dp(own):
    size = lax.axis_size("dp")
    index = lax.axis_index("dp")
    masks = [1 << b for b in range(size.bit_length() - 1)]
    for mask in masks[1:3]:
        side = jnp.where((index & mask) != 0, 1, 0)
        parts = own.reshape(2, own.shape[0] // 2, own.shape[1])
        got = swap(pick(parts, 1 - side).astype(BF16), "dp", mask)
        own = pick(parts, side).astype(F32) + got.astype(F32)
    low = own.astype(BF16)
    for mask in masks[3:]:
        low = (low.astype(F32) + swap(low, "dp", mask).astype(F32)).astype(BF16)
    for mask in reversed(masks[1:3]):
        upper = (index & mask) != 0
        other = swap(low, "dp", mask)
        low = jnp.concatenate([jnp.where(upper, other, low), jnp.where(upper, low, other)], axis=0)
    return low


def after(value, *others):
    return lax.optimization_barrier((value, others))[0]


def gather_pieces(value, ahead=()):
    ways = lax.axis_size("head")
    pieces = {0: value, 1: swap(value, "head", 1)}
    far = {0: after(value, ahead) if ahead else value}
    mask = 2
    while mask < ways:
        for p in list(far):
            far[p | mask] = swap(far[p], "head", mask)
        mask *= 2
    for p in far:
        if p:
            pieces[p] = far[p]
            pieces[p | 1] = swap(far[p], "head", 1)
    return [pieces[p] for p in range(ways)]


def reduce_pieces(pieces):
    ways = len(pieces)
    mask = 1
    live = {p: v for p, v in enumerate(pieces)}
    order = [1 << b for b in range(ways.bit_length() - 1)]
    for mask in order:
        got = {p ^ mask: swap(live[p].astype(BF16), "head", mask) for p in live if p & mask}
        live = {p: live[p].astype(F32) + got[p].astype(F32) for p in live if not p & mask}
    return live[0]


def body(hidden, lengths, norm_gain, gate_proj, value_proj, state_proj, step_proj, value_taps, value_bias,
         state_taps, state_bias, step_bias, decay_log, skip_gain, out_gain, out_proj, cotangent):
    rows, depth = hidden.shape
    ways = lax.axis_size("head")
    me = lax.axis_index("head")
    blocks = rows // Q
    wide = gate_proj.shape[1]
    share = step_proj.shape[1]
    total = wide * ways
    heads = share * ways
    head_size = wide // share
    pairs = heads // 2
    side = state_proj.shape[1]
    state = side // 2
    padded = -(-heads // 32) * 32
    plain = wide % LANES == 0
    order = [1 << b for b in range(ways.bit_length() - 1)]
    scalars = jnp.concatenate(
        [jnp.stack([me, blocks * ways]).astype(jnp.int32), lengths[0], jnp.zeros((3,), jnp.int32)]
    )

    top = jnp.concatenate(
        [step_proj.T.astype(F32), step_bias[:, None], decay_log[:, None], skip_gain[:, None], jnp.zeros((share, LANES - 3), F32)],
        axis=1,
    )
    low = jnp.concatenate([value_taps, value_bias[None], out_gain[None]], axis=0)
    pack = jnp.concatenate(
        [
            jnp.pad(top, ((0, 8 - share), (0, 0))),
            jnp.pad(low, ((0, 2), (0, depth + LANES - wide))),
            jnp.pad(hidden[rows - HALO :].astype(F32), ((0, 0), (0, LANES))),
        ],
        axis=0,
    )
    packs = gather_pieces(pack)
    halo = jnp.zeros((HALO, depth), F32)
    for p in range(1, ways):
        halo = jnp.where((me ^ p) == me - 1, packs[p][16:, :depth], halo)
    halo = halo.astype(BF16)
    both = gather_far(jnp.concatenate([gate_proj, value_proj], axis=1), (packs[1],))
    outs = gather_far(out_proj, (packs, both[0]))

    def both_merged(pair):
        if plain:
            return list(pair)
        a, b = pair
        return [jnp.concatenate([a[:, :wide], b[:, :wide], a[:, wide:], b[:, wide:]], axis=1)]

    def outs_merged(pair):
        return list(pair) if plain else [jnp.concatenate(pair, axis=0)]

    pieces = ways if plain else ways // 2
    span = total // pieces
    tiles = span // LANES
    hp = jnp.pad(jnp.concatenate([p[:share] for p in packs], axis=0), ((0, padded - heads), (0, 0)))
    par = jnp.concatenate([p[8:16, :wide] for p in packs], axis=1)
    gain_in = norm_gain[None]
    staps = jnp.pad(jnp.concatenate([state_taps, state_bias[None]], axis=0), ((0, 3), (0, 0)))

    ext = rows + HALO
    (nx, nt, state_raw, state_pre, b_low, c_low, b_t, c_t, cb, cbt) = call(
        functools.partial(pre_kernel, blocks),
        [((ext, depth), BF16), ((depth, rows), BF16), ((ext, side), F32), ((rows, side), F32),
         ((rows, state), BF16), ((rows, state), BF16), ((state, rows), BF16), ((state, rows), BF16),
         ((blocks, Q, Q), F32), ((blocks, Q, Q), F32)],
        [scalars, hidden, halo, gain_in, state_proj, staps],
        cost=2, mib=PRE,
    )
    rowp, colp, step, ratio, sig, chan = call(
        functools.partial(step_kernel, blocks, head_size),
        [((pairs, 8, rows), F32), ((pairs, rows, 8), F32), ((padded, rows), F32), ((padded, rows), F32),
         ((padded, rows), F32), ((8, total), F32)],
        [scalars, nx, hp],
        cost=2,
        mib=PRE,
    )
    vmem = pltpu.VMEM
    hbm = pl.BlockSpec(memory_space=pltpu.HBM)
    front_outs = [((rows, total), BF16), ((ext, total), BF16), ((rows, total), BF16), ((blocks, state, total), F32),
                  ((rows, total), BF16), ((state + HALO, total), BF16), ((state + HALO, total), BF16)]
    fronts, all_both = [], []
    half = pieces // 2
    for begin in (0, half):
        pairs_of = range(begin // 2, begin // 2 + ways // 4) if plain else range(begin, begin + half)
        weights = [w for at in pairs_of for w in both_merged(near_pair(both[at], fronts))]
        all_both += weights
        args = [scalars, nx, par, b_t, colp, chan, *weights]
        aliases = {len(args) + at: at for at in range(len(fronts))}
        fronts = call(
            functools.partial(front_kernel, blocks, begin, half), front_outs, [*args, *fronts], aliases=aliases,
            ins={len(args) + at: hbm for at in range(min(4, len(fronts)))}, out_specs={at: hbm for at in range(4)},
            kinds={at: pltpu.HBM for at in range(4)},
            scratch=[vmem((rows, half * span), BF16), vmem((ext, half * span), BF16), vmem((rows, half * span), BF16),
                     vmem((blocks, state, half * span), F32), vmem((ext, half * span), F32), pltpu.SemaphoreType.DMA((4,))],
            cost=6, mib=FRONT,
        )
    gate, inner, pre, st, x, carry, carry_turned = fronts

    def turned(value, mask):
        parts = [value[..., (p ^ mask) * wide : ((p ^ mask) + 1) * wide] for p in range(ways)]
        return jnp.concatenate(parts, axis=-1)

    def scan(own, own_turned, forward):
        def fade_of(value):
            return value[state : state + 1].astype(F32) + value[state + 1 : state + 2].astype(F32)

        if plain and ways == 4:
            near = swap(own_turned, "head", 1)
            (run,) = call(functools.partial(join_kernel, forward), [(own.shape, BF16)], [scalars, own, near], mib=8)
            far = swap(run, "head", 2)
            return call(functools.partial(arrive_kernel, forward), [((state, total), F32)], [scalars, near, far], mib=8)[0]
        before = before_fade = None
        run = own
        for mask in order:
            if mask == 1 and plain:
                got = swap(own_turned, "head", 1)
            else:
                got = turned(swap(run, "head", mask), mask)
            got_fade, run_fade = fade_of(got), fade_of(run)
            got, mine = got[:state].astype(F32), run[:state].astype(F32)
            later = ((me & mask) != 0) if forward else ((me & mask) == 0)
            if before is None:
                before = jnp.where(later, got, 0.0)
                before_fade = jnp.where(later, got_fade, 1.0)
            else:
                before = jnp.where(later, before_fade * got + before, before)
                before_fade = jnp.where(later, before_fade * got_fade, before_fade)
            if mask != order[-1]:
                both_maps = jnp.where(later, run_fade * got + mine, got_fade * mine + got)
                fades = run_fade * got_fade
                high = fades.astype(BF16)
                low_part = (fades - high.astype(F32)).astype(BF16)
                run = jnp.concatenate(
                    [both_maps.astype(BF16), high, low_part, jnp.zeros((HALO - 2, total), BF16)], axis=0
                )
        return before

    inc_in = scan(carry, carry_turned, True)
    all_outs = [w for value in outs for w in outs_merged(near_pair(value, x))]
    y_intra, dny = call(
        functools.partial(intra_kernel, blocks, pieces),
        [((rows, total), F32), ((rows, total), BF16)],
        [scalars, rowp, colp, cb, x, cotangent, *all_outs],
        scratch=[vmem((rows, depth), BF16)],
        cost=7,
        mib=INTRA,
    )
    wide_bf = vmem((rows, total), BF16)
    held_outs = [((rows, total), BF16), ((rows, total), BF16),
                 ((pieces // 2, 2 * depth, span), BF16), ((pieces // 2, 2 * depth, span), BF16)]
    (ny, d_gate, a_keep, a_send, inc, d_inc, d_y, back_carry, back_turned, dc_inter, rowpart, rows_sum) = call(
        functools.partial(middle_kernel, blocks, tiles, head_size),
        [*held_outs, ((blocks, state, total), BF16), ((blocks, state, total), BF16),
         ((rows, total), BF16), ((state + HALO, total), BF16), ((state + HALO, total), BF16), ((rows, state), F32),
         ((padded, rows), F32), ((8, total), F32)],
        [scalars, cotangent, inc_in, colp, chan, par, c_low, c_t, nt, y_intra, dny, gate, x, st],
        out_specs={at: hbm for at in range(len(held_outs))}, kinds={at: pltpu.HBM for at in range(len(held_outs))},
        scratch=[*[vmem(*o) for o in held_outs], vmem((depth, rows), BF16), vmem((rows, total), F32), vmem((rows, LANES), F32),
                 vmem((rows, LANES), F32), wide_bf, wide_bf, wide_bf, pltpu.SemaphoreType.DMA((len(held_outs),))],
        cost=14, mib=MIDDLE,
    )
    back_in = scan(back_carry, back_turned, False)

    def over_head(keep, send):
        if not plain:
            parts = [None] * ways
            for m in range(pieces):
                merged = (keep, send)[m % 2][m // 2]
                parts[2 * m], parts[2 * m + 1] = merged[:, :wide], merged[:, wide:]
            return reduce_pieces(parts)
        got = swap(send, "head", 1)
        live = [keep[i].astype(F32) + got[i].astype(F32) for i in range(pieces // 2)]
        return live

    def finish_head(live):
        if not plain:
            return live
        return live[0] + swap(live[1].astype(BF16), "head", 2).astype(F32)

    def halve(value, axis_at=0):
        side = lax.axis_index("dp") & 1
        cut = value.shape[:axis_at] + (2, value.shape[axis_at] // 2) + value.shape[axis_at + 1 :]
        parts = jnp.moveaxis(value.reshape(cut), axis_at, 0)
        got = swap(pick(parts, 1 - side).astype(BF16), "dp", 1)
        return pick(parts, side).astype(F32) + got.astype(F32)

    a_live = over_head(a_keep, a_send)
    if plain:
        a_out = finish_head([v[:depth] for v in a_live])
        a_gate = halve(jnp.stack([v[depth:] for v in a_live]), 1)
        gates = (a_out, a_gate)
    else:
        gates = a_live
    dx, part_a, db_in, dc_in = call(
        functools.partial(back_kernel, blocks, head_size),
        [((rows, total), BF16), ((padded, rows), F32), ((rows, state), F32), ((rows, state), F32)],
        [scalars, rowp, colp, cbt, b_low, c_low, d_y, x],
        scratch=[vmem((blocks, Q, Q), F32), wide_bf, wide_bf],
        cost=8,
        mib=BACK,
    )
    (d_inner, vgrad, part_b, lasts, db_x, b_keep, b_send) = call(
        functools.partial(tail_kernel, blocks, tiles, head_size),
        [((ext, total), BF16), ((8, total), F32), ((padded, rows), F32), ((8, total), F32), ((rows, state), F32),
         ((pieces // 2, depth, span), BF16), ((pieces // 2, depth, span), BF16)],
        [scalars, after(back_in, a_live), colp, chan, par, b_low, nt, nx, inc, dx, d_y, d_inc, x, pre, inner],
        scratch=[vmem((K, rows + 2 * HALO, LANES), F32), vmem((ext, LANES), F32), wide_bf, vmem((blocks, state, total), BF16),
                 wide_bf, wide_bf],
        cost=10, mib=TAIL,
    )
    small_rows, all_rows = 256, 832
    if plain:
        small_outs = [((pieces // 2, small_rows, span), BF16)] * 2
        shares = (ways, share, wide)
        work = [vmem((small_rows, span), F32)]
    else:
        small_outs = [((all_rows, side), F32), ((padded, depth), F32), ((padded, LANES), F32)]
        shares = None
        work = []
    d_state, d_step, *smalls = call(
        functools.partial(state_kernel, blocks, head_size, shares),
        [((ext, side), BF16), ((padded, rows), BF16)] + small_outs,
        [scalars, after(db_x, gates), db_in, dc_in, dc_inter, state_raw, state_pre, staps, rowpart, part_a, part_b, step, ratio, sig, hp,
         rows_sum, lasts, vgrad, nt, nx],
        scratch=work + [vmem((K, rows + 2 * HALO, side), F32), vmem((all_rows, side), F32), vmem((padded, depth), F32)],
        cost=4, mib=STATE,
    )
    share_rows = all_rows // ways
    if not plain:
        all_grad, step_grad, per_head = smalls
        parts = []
        for p in range(ways):
            cols, some = slice(p * wide, (p + 1) * wide), slice(p * share, (p + 1) * share)
            flat = step_grad[some].reshape(share, depth // wide, wide).swapaxes(0, 1).reshape(-1, wide)
            own = lax.dynamic_slice_in_dim(all_grad, (me ^ p) * share_rows, share_rows, 0).reshape(-1)
            count = -(-own.shape[0] // wide)
            own = jnp.pad(own, (0, count * wide - own.shape[0])).reshape(count, wide)
            part = jnp.concatenate(
                [vgrad[0:5, cols], rows_sum[0:1, cols], jnp.zeros((2, wide), F32), flat, jnp.zeros((16 - flat.shape[0], wide), F32),
                 jnp.pad(per_head[some], ((0, 8 - share), (0, wide - LANES))), own], axis=0)
            parts.append(jnp.pad(part, ((0, small_rows - part.shape[0]), (0, 0))))
        c_live = reduce_pieces(parts)
    else:
        c_live = over_head(smalls[0], smalls[1])
    b_live = over_head(b_keep, after(b_send, gates))
    if plain:
        a_part = jnp.concatenate([halve(a_out), finish_head([a_gate[0], a_gate[1]])], axis=0)
    else:
        a_part = halve(a_live)
    mixed, grad_hidden, extra, gain_part = call(
        functools.partial(final_kernel, pieces, blocks),
        [((rows, depth), BF16), ((rows, depth), F32), ((HALO, depth), F32), ((8, span), F32)],
        [scalars, hidden, halo, cotangent, gain_in, after(ny, a_part), d_gate, d_inner, d_state, d_step, hp, state_proj, *all_both, *all_outs],
        cost=9,
        mib=FINAL,
        pin=jax.ShapeDtypeStruct,
    )
    extra = lax.ppermute(extra, "head", [(i + 1, i) for i in range(ways - 1)])
    grad_hidden = grad_hidden.at[rows - HALO :].add(extra)
    a_all = reduce_dp(a_part)
    if plain:
        b_whole = [jnp.concatenate([b, c], axis=0) for b, c in zip(b_live, c_live)]
        cut = b_whole[0].shape[0] // 2
        one = finish_head([v[:cut] for v in b_whole])
        two = halve(jnp.stack([v[cut:] for v in b_whole]), 1)
        b_part = jnp.concatenate([halve(one), finish_head([two[0], two[1]])], axis=0)
    else:
        b_part = halve(jnp.concatenate([b_live, c_live], axis=0))
    gain_rows = gain_part[: depth // span].reshape(depth // wide, wide)
    b_part = jnp.concatenate([b_part, gain_rows, jnp.zeros((32 - gain_rows.shape[0], wide), F32)], axis=0)
    b_all = reduce_dp(b_part)

    def unhalve(value, cuts):
        upper = (lax.axis_index("dp") & 1) != 0
        other = swap(value, "dp", 1)
        rows_out, begin = [], 0
        for count in cuts:
            mine, his = value[begin : begin + count], other[begin : begin + count]
            rows_out.append(jnp.concatenate([jnp.where(upper, his, mine), jnp.where(upper, mine, his)], axis=0))
            begin += count
        return rows_out

    a_out, a_gate = unhalve(a_all, [depth // 2, depth // 2]) if plain else jnp.split(unhalve(a_all, [depth])[0], 2)
    grad_out = a_out.T.astype(F32)
    grad_gate = a_gate.astype(F32)
    *b_rows, gain_all = unhalve(b_all, ([256, 256] if plain else [512]) + [32])
    b_all = jnp.concatenate(b_rows, axis=0)
    gain_all = (gain_all[:32].astype(F32) + gain_all[32:].astype(F32))[: depth // wide].reshape(1, depth)
    gain_all = jnp.pad(gain_all.reshape(-1, side), ((0, 16 - depth // side), (0, 0)))
    grad_value = b_all[:depth].astype(F32)
    small = b_all[depth:].astype(F32)
    grad_step = jnp.concatenate([small[8 + j * share : 8 + (j + 1) * share].T for j in range(depth // wide)], axis=0)
    if plain:
        own = b_all[depth + 32 : depth + 32 + share_rows, :side]
    else:
        own = b_all[depth + 32 : depth + 240].reshape(-1)[: share_rows * side].reshape(share_rows, side)
    stacked = own
    for mask in order:
        gain_low = gain_all.astype(BF16)
        got = swap(jnp.concatenate([stacked, gain_low], axis=0), "head", mask)
        stacked = jnp.concatenate([stacked, got[: stacked.shape[0]]], axis=0)
        gain_all = gain_low.astype(F32) + got[-16:].astype(F32)
    stacked = stacked.reshape(ways, share_rows, side)
    full = jnp.concatenate([pick(stacked, me ^ q) for q in range(ways)], axis=0).astype(F32)
    return (
        mixed,
        grad_hidden,
        gain_all[: depth // side].reshape(-1),
        grad_gate,
        grad_value,
        full[:depth],
        grad_step,
        small[0:4],
        small[4],
        full[depth : depth + 4],
        full[depth + 4],
        small[24 : 24 + share, 0],
        small[24 : 24 + share, 1],
        small[24 : 24 + share, 2],
        small[5],
        grad_out,
    )


def solution(mesh):
    rows = P(("dp", "head"), None)
    in_specs = (
        rows, P("dp", None), P(), P(None, "head"), P(None, "head"), P(), P(None, "head"), P(None, "head"),
        P("head"), P(), P(), P("head"), P("head"), P("head"), P("head"), P("head", None), rows,
    )
    out_specs = (
        rows, rows, P(), P(None, "head"), P(None, "head"), P(), P(None, "head"), P(None, "head"),
        P("head"), P(), P(), P("head"), P("head"), P("head"), P("head"), P("head", None),
    )
    return jax.shard_map(body, mesh=mesh, in_specs=in_specs, out_specs=out_specs, check_vma=False)
```

```python
import functools

import jax
import jax.numpy as jnp
from jax import lax
from jax.experimental import pallas as pl
from jax.experimental.pallas import tpu as pltpu
from jax.sharding import PartitionSpec as P

K = 4
Q = 256
HALO = 16
LANES = 128
EPSILON = 1e-05
F32 = jnp.float32
BF16 = jnp.bfloat16
HIGHEST = lax.Precision.HIGHEST


def mm(left, right, lc=1, rc=0, precision=None):
    return lax.dot_general(
        left,
        right,
        (((lc,), (rc,)), ((), ())),
        preferred_element_type=F32,
        precision=precision,
    )


MIB = 1024 * 1024
PRE, FRONT, INTRA, MIDDLE, BACK, TAIL, STATE, FINAL = 12, 14, 12, 18, 12, 14, 12, 56


def whole(shape):
    return pl.BlockSpec(shape, lambda *_: (0,) * len(shape))


def call(kernel, outs, args, scratch=(), grid=(), ins=None, out_specs=None, aliases=None, mib=48, cost=0, pin=pltpu.VMEM, kinds=None):
    ins, out_specs, kinds = ins or {}, out_specs or {}, kinds or {}
    specs = [pl.BlockSpec(memory_space=pltpu.SMEM)]
    for at, value in enumerate(args[1:], 1):
        specs.append(ins[at] if at in ins else whole(value.shape))
    outs_specs = [out_specs[at] if at in out_specs else whole(o[0]) for at, o in enumerate(outs)]
    return pl.pallas_call(
        kernel,
        grid=grid,
        out_shape=[kinds[at](s, d) if at in kinds else pin(s, d) for at, (s, d) in enumerate(outs)],
        in_specs=specs,
        out_specs=outs_specs,
        scratch_shapes=list(scratch),
        input_output_aliases=aliases or {},
        compiler_params=pltpu.CompilerParams(vmem_limit_bytes=mib * MIB),
        cost_estimate=pl.CostEstimate(flops=int(cost * 4e8), bytes_accessed=int(cost * 3e5), transcendentals=0),
    )(*args)


def keeps_of(s_ref, block, blocks):
    place = s_ref[0] * blocks + block
    fresh = (place == 0) | (place == 1) | (place == s_ref[1] - 1)
    return fresh, jnp.where(fresh, 0.0, 1.0).astype(F32)


def row_keep(fresh, distance):
    rows = lax.broadcasted_iota(jnp.int32, (Q, 1), 0)
    return (rows >= jnp.where(fresh, distance, 0)).astype(F32)


def conv_block(ref, base, cols, taps, fresh):
    total = taps[K : K + 1] + taps[K - 1 : K] * ref[pl.ds(base, Q), cols]
    for distance in range(1, K):
        earlier = ref[pl.ds(base - distance, Q), cols]
        total = total + taps[K - 1 - distance : K - distance] * (earlier * row_keep(fresh, distance))
    return total


def silu_slope(values, sig):
    return sig * (1.0 + values * (1.0 - sig))


def first_lanes():
    return lax.broadcasted_iota(jnp.int32, (1, LANES), 1) < LANES // 2


def spread(cols, quantity):
    return jnp.where(
        first_lanes(), cols[:, 2 * quantity : 2 * quantity + 1], cols[:, 2 * quantity + 1 : 2 * quantity + 2]
    )


def head_lanes(rows, heads_first, head_size):
    lane = lax.broadcasted_iota(jnp.int32, rows, 1 if heads_first else 0)
    head = lax.broadcasted_iota(jnp.int32, rows, 0 if heads_first else 1)
    return (lane >= head * head_size) & (lane < (head + 1) * head_size)


def pre_kernel(blocks, s_ref, hid_ref, halo_ref, gain_ref, proj_ref, taps_ref,
               nx_ref, nt_ref, raw_ref, pre_ref, b_ref, c_ref, bt_ref, ct_ref, cb_ref, cbt_ref):
    gain = gain_ref[...]
    rows = blocks * Q

    def norm(v):
        v = v.astype(F32)
        return v * lax.rsqrt(jnp.mean(v * v, axis=1, keepdims=True) + EPSILON) * gain

    halo = norm(halo_ref[...])
    own = norm(hid_ref[...])
    nx_ref[0:HALO] = halo.astype(BF16)
    nx_ref[HALO:] = own.astype(BF16)
    nt_ref[:, 0:rows] = own.T.astype(BF16)
    raw_ref[...] = mm(nx_ref[...], proj_ref[...])
    taps = taps_ref[...]
    state = b_ref.shape[1]
    for block in range(blocks):
        fresh, _ = keeps_of(s_ref, block, blocks)
        pre = conv_block(raw_ref, HALO + block * Q, slice(None), taps, fresh)
        at = pl.ds(block * Q, Q)
        pre_ref[at] = pre
        conv = pre * jax.nn.sigmoid(pre)
        b_mat = conv[:, :state]
        c_mat = conv[:, state:]
        b_low = b_mat.astype(BF16)
        c_low = c_mat.astype(BF16)
        b_ref[at] = b_low
        c_ref[at] = c_low
        bt_ref[:, at] = b_mat.T.astype(BF16)
        ct_ref[:, at] = c_mat.T.astype(BF16)
        cb_ref[block] = mm(c_low, b_low, 1, 1)
        cbt_ref[block] = mm(b_low, c_low, 1, 1)


def step_kernel(blocks, head_size, s_ref, nx_ref, hp_ref, rowp_ref, colp_ref, step_ref, ratio_ref, sig_ref, chan_ref):
    depth = nx_ref.shape[1]
    hp = hp_ref[...]
    u = mm(hp[:, :depth].astype(BF16), nx_ref[HALO:], 1, 1) + hp[:, depth : depth + 1]
    step = jnp.maximum(u, 0.0) + jnp.log1p(jnp.exp(-jnp.abs(u)))
    sig = jax.nn.sigmoid(u)
    step_ref[...] = step
    sig_ref[...] = sig
    ratio_ref[...] = jnp.where(step > 1e-30, sig / jnp.maximum(step, 1e-30), 1.0)
    rate = -jnp.exp(hp[:, depth + 1 : depth + 2])
    move = step * rate
    upto = (
        lax.broadcasted_iota(jnp.int32, (Q, Q), 0) <= lax.broadcasted_iota(jnp.int32, (Q, Q), 1)
    ).astype(F32)
    heads = hp.shape[0]
    lane = lax.broadcasted_iota(jnp.int32, (heads, LANES), 1)
    last_cols = jnp.zeros((heads, LANES), F32)
    lstep = jnp.log(step)
    product = jnp.ones((heads, 1), F32)
    pairs = rowp_ref.shape[0]
    for block in range(blocks):
        at = slice(block * Q, (block + 1) * Q)
        logd = mm(move[:, at], upto, precision=HIGHEST)
        less = logd - lstep[:, at]
        last = logd[:, Q - 1 : Q]
        grown = jnp.exp(logd)
        carry = jnp.exp(last - less)
        final = jnp.exp(last)
        _, kept = keeps_of(s_ref, block, blocks)
        product = product * final * kept
        last_cols = jnp.where(lane == block, final, last_cols)
        for pair in range(pairs):
            for index, values in enumerate((logd, less, grown, carry)):
                rowp_ref[pair, 2 * index : 2 * index + 2, at] = values[2 * pair : 2 * pair + 2]
    last_cols = jnp.where(lane == 6, product, last_cols)
    last_cols = jnp.where(lane == 7, hp[:, depth + 2 : depth + 3], last_cols)
    spots = head_lanes((heads, chan_ref.shape[1]), True, head_size).astype(F32)
    chan_ref[...] = mm(last_cols.T[0:8], spots, precision=HIGHEST)
    for pair in range(0, pairs, 2):
        colp_ref[pair // 2] = jnp.concatenate([rowp_ref[pair], rowp_ref[pair + 1]], 0).T


def carry_block(ref, cols, carry, fades):
    state = carry.shape[0]
    ref[0:state, cols] = carry.astype(BF16)
    high = fades.astype(BF16).astype(F32)
    row = lax.broadcasted_iota(jnp.int32, (HALO, LANES), 0)
    ref[state:, cols] = jnp.where(row == 0, high, jnp.where(row == 1, fades - high, 0.0)).astype(BF16)


def tile_at(index):
    return pl.ds(pl.multiple_of(index * LANES, LANES), LANES)


def front_kernel(blocks, first_piece, pieces, s_ref, nx_ref, par_ref, bt_ref, colp_ref, chan_ref, *refs):
    weights = refs[:pieces]
    (gate_out, inner_out, pre_out, s_out, x_ref, carry_ref, turned_ref,
     gate_ref, inner_ref, pre_ref, st_ref, work, sems) = refs[-13:]
    done = refs[pieces:-13]
    wide = weights[0].shape[1] // 2
    for old, new in zip(done[4:], (x_ref, carry_ref, turned_ref)):
        new[:, 0 : first_piece * wide] = old[:, 0 : first_piece * wide]
    own = slice(first_piece * wide, (first_piece + pieces) * wide)
    moves = [(gate_ref, gate_out), (inner_ref, inner_out), (pre_ref, pre_out), (st_ref, s_out)]
    for p in range(pieces):
        here = slice(p * wide, (p + 1) * wide)
        work[:, here] = mm(nx_ref[...], weights[p][:, wide:])
        gate_ref[:, here] = mm(nx_ref[HALO:], weights[p][:, :wide]).astype(BF16)
    tiles = wide // LANES

    def tile(i, cols_of):
        here = tile_at(i)
        pair = i + first_piece * tiles
        far = tile_at(pair)
        turned = tile_at(jnp.bitwise_xor(pair // tiles, 1) * tiles + pair % tiles)
        taps = par_ref[:, far]
        inner_ref[:, here] = work[:, here].astype(BF16)
        for block in range(blocks):
            at = pl.ds(block * Q, Q)
            fresh, kept = keeps_of(s_ref, block, blocks)
            pre = conv_block(work, HALO + block * Q, here, taps, fresh)
            pre_ref[at, here] = pre.astype(BF16)
            x = pre * jax.nn.sigmoid(pre)
            x_ref[at, far] = x.astype(BF16)
            weighted = (spread(cols_of(at), 3) * x).astype(BF16)
            state = mm(bt_ref[:, at], weighted)
            st_ref[block, :, here] = state
            if block == 0:
                carry = state
            else:
                carry = chan_ref[block : block + 1, far] * (kept * carry) + state
        carry_block(carry_ref, far, carry, chan_ref[6:7, far])
        carry_block(turned_ref, turned, carry, chan_ref[6:7, far])
        for index, (held, out) in enumerate(moves):
            pltpu.make_async_copy(held.at[..., here], out.at[..., far], sems.at[index]).start()

    def turn(i, none):
        for k in range(2):
            tile(2 * i + k, lambda at, k=k: colp_ref[i + first_piece * tiles // 2, at, 8 * k : 8 * k + 8])
        return none

    lax.fori_loop(0, pieces * tiles // 2, turn, 0)
    for index, (held, out) in enumerate(moves):
        pltpu.make_async_copy(held, out.at[..., own], sems.at[index]).wait()


def unpack_carry(ref):
    state = ref.shape[0] - HALO
    return ref[0:state].astype(F32), ref[state : state + 1].astype(F32) + ref[state + 1 : state + 2].astype(F32)


def join_kernel(forward, s_ref, own_ref, got_ref, out_ref):
    mine, my_fade = unpack_carry(own_ref)
    his, his_fade = unpack_carry(got_ref)
    later = (jnp.bitwise_and(s_ref[0], 1) == 1) == forward
    state = mine.shape[0]
    total = jnp.where(later, my_fade * his + mine, his_fade * mine + his)
    fade = my_fade * his_fade
    high = fade.astype(BF16).astype(F32)
    row = lax.broadcasted_iota(jnp.int32, (HALO, total.shape[1]), 0)
    out_ref[0:state] = total.astype(BF16)
    out_ref[state:] = jnp.where(row == 0, high, jnp.where(row == 1, fade - high, 0.0)).astype(BF16)


def arrive_kernel(forward, s_ref, near_ref, far_ref, out_ref):
    near, near_fade = unpack_carry(near_ref)
    wide = near.shape[1] // 2
    later = (jnp.bitwise_and(s_ref[0], 1) == 1) == forward
    far_later = (jnp.bitwise_and(s_ref[0], 2) == 2) == forward
    near = jnp.where(later, near, 0.0)
    fade = jnp.where(far_later, jnp.where(later, near_fade, 1.0), 0.0)
    for half in range(2):
        here, there = slice(half * wide, (half + 1) * wide), slice((1 - half) * wide, (2 - half) * wide)
        out_ref[:, here] = near[:, here] + fade[:, here] * far_ref[0 : near.shape[0], there].astype(F32)


def masked_cotangent(s_ref, cot_ref, blocks, block):
    at = slice(block * Q, (block + 1) * Q)
    return cot_ref[at].astype(F32) * valid_of(s_ref, blocks, block)


def masked_kernel(blocks, pieces, s_ref, cot_ref, *refs):
    outs_w = refs[:pieces]
    dny_ref, dbt_ref, db_ref = refs[pieces:]
    for block in range(blocks):
        at = slice(block * Q, (block + 1) * Q)
        masked = masked_cotangent(s_ref, cot_ref, blocks, block)
        db_ref[at] = masked.astype(BF16)
        dbt_ref[:, at] = masked.T.astype(BF16)
    wide = outs_w[0].shape[0]
    for p in range(pieces):
        dny_ref[:, p * wide : (p + 1) * wide] = mm(db_ref[...], outs_w[p][...], 1, 1).astype(BF16)


def intra_kernel(blocks, s_ref, rowp_ref, colp_ref, cb_ref, x_ref, y_ref):
    half = Q // 2
    first = first_lanes()
    tri = lax.broadcasted_iota(jnp.int32, (half, half), 0) >= lax.broadcasted_iota(
        jnp.int32, (half, half), 1
    )

    def work(i, k):
        pair = 2 * i + k
        far = tile_at(pair)
        for block in range(blocks):
            at = pl.ds(block * Q, Q)
            x = x_ref[at, far]
            both = [jnp.where(first, x, 0), jnp.where(first, 0, x)]
            rp = rowp_ref[pair, :, at]
            cp = colp_ref[i, at, 8 * k : 8 * k + 8]
            tops, bots = [], []
            for h in range(2):
                ld, ls = cp[:, h : h + 1], rp[2 + h : 3 + h, :]
                arg = jnp.where(tri, ld[:half] - ls[:, :half], -1e30)
                tops.append((cb_ref[block, 0:half, 0:half] * jnp.exp(arg)).astype(BF16))
                arg = ld[half:] - ls[:, :half]
                bots.append((cb_ref[block, half:, 0:half] * jnp.exp(arg)).astype(BF16))
                arg = jnp.where(tri, ld[half:] - ls[:, half:], -1e30)
                bots.append((cb_ref[block, half:, half:] * jnp.exp(arg)).astype(BF16))
            y_ref[pl.ds(block * Q, half), far] = mm(jnp.concatenate(tops, 1), jnp.concatenate([b[:half] for b in both], 0))
            y_ref[pl.ds(block * Q + half, half), far] = mm(jnp.concatenate(bots, 1), jnp.concatenate(both, 0))

    def two(i, none):
        work(i, 0)
        work(i, 1)
        return none

    lax.fori_loop(0, x_ref.shape[1] // (2 * LANES), two, 0)


def split_store(hi_ref, lo_ref, at, cols, part):
    high = part.astype(BF16)
    hi_ref[at, cols] = high
    lo_ref[at, cols] = (part - high.astype(F32)).astype(BF16)


def head_sums(heads, head_size, hi_ref, lo_ref):
    spots = head_lanes((heads, hi_ref.shape[1]), True, head_size).astype(F32).astype(BF16)
    return mm(spots, hi_ref[...], 1, 1) + mm(spots, lo_ref[...], 1, 1)


def valid_of(s_ref, blocks, block):
    place = s_ref[0] * blocks + block
    last = place == s_ref[1] - 1
    length = jnp.where(place == 0, s_ref[2], jnp.where(last, s_ref[4], s_ref[3]))
    start = jnp.where(place == 0, 0, jnp.where(last, s_ref[1] - 1, 1))
    rows = lax.broadcasted_iota(jnp.int32, (Q, 1), 0) + (place - start) * Q
    return (rows < length).astype(F32)


class Outbound:
    def __init__(self, held, sems, keep, send, tiles):
        self.held, self.sems, self.keep, self.send, self.tiles = held, sems, keep, send, tiles

    def wait(self, slot):
        for k in range(2):
            held = self.held.at[slot, :, k * LANES : (k + 1) * LANES]
            pltpu.make_async_copy(held, self.keep.at[0, :, 0:LANES], self.sems.at[slot, k]).wait()

    def start(self, turn, slot):
        for k in range(2):
            at = 2 * turn + k
            piece, lane = at // self.tiles, at % self.tiles
            held = self.held.at[slot, :, k * LANES : (k + 1) * LANES]
            cols = slice(lane * LANES, (lane + 1) * LANES) if isinstance(lane, int) else tile_at(lane)
            for odd, ref in enumerate((self.keep, self.send)):

                @pl.when(piece % 2 == odd)
                def _(ref=ref, held=held, piece=piece, cols=cols, k=k):
                    pltpu.make_async_copy(held, ref.at[piece // 2, :, cols], self.sems.at[slot, k]).start()


def turns_with_grads(turns, work, grads, out):
    def turn(i, none):
        before = jnp.maximum(i - 1, 0)
        slot = before % 2

        @pl.when(i >= 3)
        def _():
            out.wait(slot)

        grads(before, slot)
        work(i, 0)
        work(i, 1)

        @pl.when(i >= 1)
        def _():
            out.start(before, slot)

        return none

    lax.fori_loop(0, turns, turn, 0)
    last = turns - 1
    if last >= 2:
        out.wait(last % 2)
    grads(last, last % 2)
    out.start(jnp.int32(last), last % 2)
    for slot in range(min(2, turns)):
        out.wait(slot)


def middle_kernel(blocks, tiles, head_size, s_ref, dbt_ref, inc_in, colp_ref, chan_ref, par_ref, c_ref, ct_ref, nt_ref,
                  y_ref, dny_ref, gate_ref, x_ref, st_ref,
                  ny_out, dgate_out, keep_out, send_out, inc_out, di_out, dc_out, rowpart_out, rows_out,
                  dy_ref, carry_ref, turned_ref,
                  ny_ref, dgate_ref, inc_ref, di_ref, dc_ref, rowpart_ref, rows_ref, grad_ref,
                  mix_ref, sq_ref, cr_ref, hi_ref, lo_ref, sems, grad_sems):
    moves = [(ny_ref, ny_out), (dgate_ref, dgate_out), (inc_ref, inc_out), (di_ref, di_out), (dc_ref, dc_out), (rowpart_ref, rowpart_out), (rows_ref, rows_out)]

    def move(index, *where):
        held, out = moves[index]
        pltpu.make_async_copy(held.at[where], out.at[where], sems.at[index]).start()

    depth = dbt_ref.shape[0]
    total = chan_ref.shape[1]
    kept = [keeps_of(s_ref, block, blocks)[1] for block in range(blocks)]
    sq_ref[...] = jnp.zeros_like(sq_ref)
    cr_ref[...] = jnp.zeros_like(cr_ref)

    def forward(i, none):
        for k in range(2):
            far = tile_at(2 * i + k)
            incoming = inc_in[:, far]
            for block in range(blocks):
                at = pl.ds(block * Q, Q)
                incoming = kept[block] * incoming
                inc_low = incoming.astype(BF16)
                inc_ref[block, :, far] = inc_low
                incoming = chan_ref[block : block + 1, far] * incoming + st_ref[block, :, far]
                inter = mm(c_ref[at], inc_low) * spread(colp_ref[i, at, 8 * k : 8 * k + 8], 2)
                mix = y_ref[at, far] + inter + chan_ref[7:8, far] * x_ref[at, far].astype(F32)
                mix_ref[at, far] = mix
                gate = gate_ref[at, far].astype(F32)
                gated = mix * (gate * jax.nn.sigmoid(gate))
                sq_ref[at] += gated * gated
                cr_ref[at] += dny_ref[at, far].astype(F32) * par_ref[5:6, far] * gated
        return none

    lax.fori_loop(0, total // (2 * LANES), forward, 0)
    scale = lax.rsqrt(jnp.sum(sq_ref[...], axis=1, keepdims=True) / total + EPSILON)
    coef = scale * scale * scale * (jnp.sum(cr_ref[...], axis=1, keepdims=True) / total)
    sq_ref[...] = jnp.broadcast_to(scale, sq_ref.shape)
    cr_ref[...] = jnp.broadcast_to(coef, cr_ref.shape)
    rows_ref[...] = jnp.zeros_like(rows_ref)

    def backward(i, k):
        pair = 2 * i + k
        far = tile_at(pair)
        gain = par_ref[5:6, far]
        skip = chan_ref[7:8, far]
        gain_row = jnp.zeros((1, LANES), F32)
        skip_row = jnp.zeros((1, LANES), F32)
        dis = []
        for block in range(blocks):
            at = pl.ds(block * Q, Q)
            gate, mix, x = gate_ref[at, far].astype(F32), mix_ref[at, far], x_ref[at, far].astype(F32)
            sig = jax.nn.sigmoid(gate)
            act = gate * sig
            gated = mix * act
            normed = gated * sq_ref[at]
            dny = dny_ref[at, far].astype(F32)
            ny_ref[at, far] = (normed * gain).astype(BF16)
            gain_row += jnp.sum(dny * normed, axis=0, keepdims=True)
            d_gated = dny * gain * sq_ref[at] - gated * cr_ref[at]
            dgate_ref[at, far] = (d_gated * mix * silu_slope(gate, sig)).astype(BF16)
            dy = d_gated * act
            dy_low = dy.astype(BF16)
            dy_ref[at, far] = dy_low
            skip_row += jnp.sum(dy * x, axis=0, keepdims=True)
            split_store(hi_ref, lo_ref, at, far, dy_low.astype(F32) * (mix - skip * x))
            dye = (dy * spread(colp_ref[i, at, 8 * k : 8 * k + 8], 2)).astype(BF16)
            dc_ref[at] += mm(dye, inc_ref[block, :, far], 1, 1)
            di = mm(ct_ref[:, at], dye).astype(BF16)
            di_ref[block, :, far] = di
            dis.append(di.astype(F32))
        rows_ref[0:1, far] = gain_row
        rows_ref[1:2, far] = skip_row
        back = jnp.zeros_like(dis[0])
        for block in reversed(range(blocks)):
            back = kept[block] * (dis[block] + chan_ref[block : block + 1, far] * back)
        carry_block(carry_ref, far, back, chan_ref[6:7, far])
        turned = tile_at(jnp.bitwise_xor(pair // tiles, 1) * tiles + pair % tiles)
        carry_block(turned_ref, turned, back, chan_ref[6:7, far])
        move(0, slice(None), far)
        move(1, slice(None), far)

    def grads(turn, slot):
        cols = pl.ds(pl.multiple_of(turn * 2 * LANES, 2 * LANES), 2 * LANES)
        grad_ref[slot, 0:depth] = mm(dbt_ref[...], ny_ref[:, cols]).astype(BF16)
        grad_ref[slot, depth:] = mm(nt_ref[...], dgate_ref[:, cols]).astype(BF16)

    dc_ref[...] = jnp.zeros_like(dc_ref)
    turns_with_grads(total // (2 * LANES), backward, grads, Outbound(grad_ref, grad_sems, keep_out, send_out, tiles))
    for index in (2, 3, 4, 6):
        move(index)
    rowpart_ref[...] = head_sums(rowpart_ref.shape[0], head_size, hi_ref, lo_ref)
    move(5)
    for index, (held, out) in enumerate(moves):
        pltpu.make_async_copy(held, out, sems.at[index]).wait()


def back_kernel(blocks, head_size, s_ref, rowp_ref, colp_ref, cbt_ref, b_ref, c_ref, dy_ref, x_ref,
                dx_ref, part_ref, db_ref, dc_ref, acc_ref, hi_ref, lo_ref):
    half = Q // 2
    first = first_lanes()
    tri = lax.broadcasted_iota(jnp.int32, (half, half), 0) <= lax.broadcasted_iota(
        jnp.int32, (half, half), 1
    )
    acc_ref[...] = jnp.zeros_like(acc_ref)

    def two(i, none):
        for block in range(blocks):
            at = pl.ds(block * Q, Q)
            w00 = w01 = w11 = 0.0
            for k in range(2):
                pair = 2 * i + k
                far = tile_at(pair)
                x, dy = x_ref[at, far], dy_ref[at, far]
                dys = [jnp.where(first, dy, 0), jnp.where(first, 0, dy)]
                xs = [jnp.where(first, x, 0), jnp.where(first, 0, x)]
                rp = rowp_ref[pair, :, at]
                cp = colp_ref[i, at, 8 * k : 8 * k + 8]
                tops, bots = [], []
                for h in range(2):
                    ls, ld = cp[:, 2 + h : 3 + h], rp[h : h + 1, :]
                    ds_top = mm(xs[h][:half], dy, 1, 1)
                    ds_bot = mm(xs[h][half:], dy[half:], 1, 1)
                    e00 = jnp.exp(jnp.where(tri, ld[:, :half] - ls[:half], -1e30))
                    e01 = jnp.exp(ld[:, half:] - ls[:half])
                    e11 = jnp.exp(jnp.where(tri, ld[:, half:] - ls[half:], -1e30))
                    tops.append((cbt_ref[block, 0:half, 0:half] * e00).astype(BF16))
                    tops.append((cbt_ref[block, 0:half, half:] * e01).astype(BF16))
                    bots.append((cbt_ref[block, half:, half:] * e11).astype(BF16))
                    w00 += ds_top[:, :half] * e00
                    w01 += ds_top[:, half:] * e01
                    w11 += ds_bot * e11
                dx_top = mm(jnp.concatenate(tops, 1), jnp.concatenate(dys, 0))
                dx_bot = mm(jnp.concatenate(bots, 1), jnp.concatenate([d[half:] for d in dys], 0))
                dx = jnp.concatenate([dx_top, dx_bot], 0)
                dx_ref[at, far] = dx.astype(BF16)
                split_store(hi_ref, lo_ref, at, far, x.astype(F32) * dx)
            acc_ref[block, 0:half, 0:half] += w00
            acc_ref[block, 0:half, half:] += w01
            acc_ref[block, half:, half:] += w11
        return none

    lax.fori_loop(0, x_ref.shape[1] // (2 * LANES), two, 0)
    part_ref[...] = head_sums(part_ref.shape[0], head_size, hi_ref, lo_ref)
    for block in range(blocks):
        at = slice(block * Q, (block + 1) * Q)
        acc = acc_ref[block].astype(BF16)
        db_ref[at] = mm(acc, c_ref[at])
        dc_ref[at] = mm(acc, b_ref[at], 0, 0)


def conv_back(s_ref, blocks, work, taps, values_of, slope_of, store):
    sums = [0.0] * (K + 1)
    for block in range(blocks):
        fresh, _ = keeps_of(s_ref, block, blocks)
        d_pre = slope_of(block)
        work[0, pl.ds(HALO + block * Q, Q)] = d_pre
        sums[K] += jnp.sum(d_pre, axis=0, keepdims=True)
        sums[K - 1] += jnp.sum(d_pre * values_of(HALO + block * Q), axis=0, keepdims=True)
        for distance in range(1, K):
            held = d_pre * row_keep(fresh, distance)
            work[distance, pl.ds(HALO + block * Q, Q)] = held
            sums[K - 1 - distance] += jnp.sum(
                held * values_of(HALO + block * Q - distance), axis=0, keepdims=True
            )
    for begin, count in [(0, HALO)] + [(HALO + b * Q, Q) for b in range(blocks)]:
        out = taps[K - 1 : K] * work[0, pl.ds(begin, count)]
        for distance in range(1, K):
            out = out + taps[K - 1 - distance : K - distance] * work[distance, pl.ds(begin + distance, count)]
        store(begin, count, out.astype(BF16))
    return sums


def tail_kernel(blocks, tiles, head_size, s_ref, back_in, colp_ref, chan_ref, par_ref, b_ref, nt_ref, nx_ref,
                inc_ref, dx_ref, dy_ref, di_ref, x_ref, pre_ref, inner_ref,
                dinner_ref, vgrad_ref, part_ref, lasts_ref, db_ref, keep_out, send_out,
                d_ref, in_ref, hi_ref, lo_ref, grad_ref, grad_sems):
    total = chan_ref.shape[1]
    kept = [keeps_of(s_ref, block, blocks)[1] for block in range(blocks)]
    d_ref[...] = jnp.zeros_like(d_ref)
    vgrad_ref[...] = jnp.zeros_like(vgrad_ref)
    lasts_ref[...] = jnp.zeros_like(lasts_ref)
    db_ref[...] = jnp.zeros_like(db_ref)

    def work(i, k):
        far = tile_at(2 * i + k)
        in_ref[k] = inner_ref[:, far].astype(F32)
        skip = chan_ref[7:8, far]
        back = back_in[:, far]
        lasts, lows = [None] * blocks, [None] * blocks
        for block in reversed(range(blocks)):
            fade = chan_ref[block : block + 1, far]
            lows[block] = back.astype(BF16)
            lasts[block] = fade * jnp.sum(inc_ref[block, :, far].astype(F32) * back, axis=0, keepdims=True)
            back = kept[block] * (di_ref[block, :, far].astype(F32) + fade * back)

        def slope_of(block):
            at = pl.ds(block * Q, Q)
            carry = spread(colp_ref[i, at, 8 * k : 8 * k + 8], 3)
            weighted = carry * x_ref[at, far].astype(F32)
            db_ref[at] += mm(weighted.astype(BF16), lows[block], 1, 1)
            d_weighted = mm(b_ref[at], lows[block])
            moved = weighted * d_weighted
            lasts_ref[block : block + 1, far] = lasts[block] + jnp.sum(moved, axis=0, keepdims=True)
            split_store(hi_ref, lo_ref, at, far, moved)
            d_x = dx_ref[at, far].astype(F32) + carry * d_weighted + skip * dy_ref[at, far].astype(F32)
            pre = pre_ref[at, far].astype(F32)
            return d_x * silu_slope(pre, jax.nn.sigmoid(pre))

        def store(begin, count, value):
            dinner_ref[pl.ds(begin, count), far] = value

        sums = conv_back(
            s_ref, blocks, d_ref.at[k], par_ref[:, far], lambda at: in_ref[k, pl.ds(at, Q)], slope_of, store
        )
        for index in range(K + 1):
            vgrad_ref[index : index + 1, far] = sums[index]

    def grads(turn, slot):
        cols = pl.ds(pl.multiple_of(turn * 2 * LANES, 2 * LANES), 2 * LANES)
        grad = mm(nt_ref[...], dinner_ref[HALO:, cols]) + mm(nx_ref[0:HALO], dinner_ref[0:HALO, cols], 0, 0)
        grad_ref[slot] = grad.astype(BF16)

    turns_with_grads(total // (2 * LANES), work, grads, Outbound(grad_ref, grad_sems, keep_out, send_out, tiles))
    part_ref[...] = head_sums(part_ref.shape[0], head_size, hi_ref, lo_ref)


def state_kernel(blocks, head_size, shares, s_ref, dbx_ref, dbin_ref, dcin_ref, dcx_ref, raw_ref, spre_ref, staps_ref,
                 rowpart_ref, part_a, part_b, step_ref, ratio_ref, sig_ref, hp_ref, rows_ref, lasts_ref, vgrad_ref,
                 nt_ref, nx_ref, dstate_ref, dstep_ref, *refs):
    e_ref, all_ref, step_grad_ref = refs[-3:]
    outs = refs[:-3]
    e_ref[...] = jnp.zeros_like(e_ref)
    d_states = []
    for block in range(blocks):
        at = slice(block * Q, (block + 1) * Q)
        d_states.append(jnp.concatenate([dbin_ref[at] + dbx_ref[at], dcin_ref[at] + dcx_ref[at]], 1))

    def slope_of(block):
        pre = spre_ref[pl.ds(block * Q, Q), :]
        return d_states[block] * silu_slope(pre, jax.nn.sigmoid(pre))

    def store(begin, count, value):
        dstate_ref[pl.ds(begin, count), :] = value

    sgrad = conv_back(s_ref, blocks, e_ref, staps_ref[...], lambda at: raw_ref[pl.ds(at, Q), :], slope_of, store)
    heads = hp_ref.shape[0]
    total = lasts_ref.shape[1]
    depth = hp_ref.shape[1] - LANES
    spots = head_lanes((heads, total), True, head_size).astype(F32)
    lasts = mm(spots, lasts_ref[...], 1, 1, precision=HIGHEST)
    skips = mm(spots, rows_ref[...], 1, 1, precision=HIGHEST)[:, 1:2]
    rate = -jnp.exp(hp_ref[:, depth + 1 : depth + 2])
    lane = lax.broadcasted_iota(jnp.int32, (heads, Q), 1)
    upto = (
        lax.broadcasted_iota(jnp.int32, (Q, Q), 0) >= lax.broadcasted_iota(jnp.int32, (Q, Q), 1)
    ).astype(F32)
    grad_bias = jnp.zeros((heads, 1), F32)
    grad_decay = jnp.zeros((heads, 1), F32)
    for block in range(blocks):
        at = slice(block * Q, (block + 1) * Q)
        cols = part_a[:, at] + part_b[:, at]
        d_log = rowpart_ref[:, at] - cols + jnp.where(lane == Q - 1, lasts[:, block : block + 1], 0.0)
        d_move = mm(d_log, upto, precision=HIGHEST)
        d_raw = cols * ratio_ref[:, at] + rate * d_move * sig_ref[:, at]
        grad_bias += jnp.sum(d_raw, axis=1, keepdims=True)
        grad_decay += rate * jnp.sum(step_ref[:, at] * d_move, axis=1, keepdims=True)
        dstep_ref[:, at] = d_raw.astype(BF16)
    wide_lane = lax.broadcasted_iota(jnp.int32, (heads, LANES), 1)
    per_head = jnp.where(
        wide_lane == 0, grad_bias, jnp.where(wide_lane == 1, grad_decay, jnp.where(wide_lane == 2, skips, 0.0))
    )
    step_grad_ref[...] = mm(dstep_ref[...], nx_ref[HALO:])
    all_ref[...] = jnp.zeros_like(all_ref)
    all_ref[0:depth] = mm(nt_ref[...], dstate_ref[HALO:]) + mm(nx_ref[0:HALO], dstate_ref[0:HALO], 0, 0)
    for index in range(K + 1):
        all_ref[depth + index : depth + index + 1] = sgrad[index]
    if not shares:
        outs[0][...] = all_ref[...]
        outs[1][...] = step_grad_ref[...]
        outs[2][...] = per_head
        return
    ways, share, wide = shares
    quarter = all_ref.shape[0] // ways
    work = outs[-1]
    for p in range(ways):
        span = slice(p * wide, (p + 1) * wide)
        some = slice(p * share, (p + 1) * share)
        work[...] = jnp.zeros_like(work)
        work[0 : K + 1] = vgrad_ref[0 : K + 1, span]
        work[K + 1 : K + 2] = rows_ref[0:1, span]
        for part in range(depth // wide):
            begin = 8 + part * share
            work[begin : begin + share] = step_grad_ref[some, part * wide : (part + 1) * wide]
        work[24 : 24 + share, 0:LANES] = per_head[some]
        owner = jnp.bitwise_xor(s_ref[0], p)
        work[32 : 32 + quarter, 0 : all_ref.shape[1]] = all_ref[pl.ds(pl.multiple_of(owner * quarter, 8), quarter)]
        outs[p % 2][p // 2] = work[...].astype(BF16)


def mixed_kernel(pieces, blocks, s_ref, hid_ref, ny_ref, *refs):
    outs_w, mixed_ref = refs[:pieces], refs[pieces]
    wide = outs_w[0].shape[0]
    for block in range(blocks):
        at = slice(block * Q, (block + 1) * Q)
        branch = mm(ny_ref[at, 0:wide], outs_w[0][...])
        for p in range(1, pieces):
            branch += mm(ny_ref[at, p * wide : (p + 1) * wide], outs_w[p][...])
        mixed_ref[at] = (hid_ref[at].astype(F32) + valid_of(s_ref, blocks, block) * branch).astype(BF16)


def final_kernel(pieces, blocks, mine, s_ref, hid_ref, halo_ref, cot_ref, gain_ref, dgate_ref, dinner_ref,
                 dstate_ref, dstep_ref, hp_ref, sproj_ref, *refs):
    both_in = refs[:pieces]
    grad_out, extra_ref, gain_out, grad_ref, sems, both, dgate_here, dinner_here, in_sems = refs[-9:]
    wide = both.shape[2] // 2
    depth = hid_ref.shape[1]
    own = pl.ds(mine[0] * Q, len(mine) * Q)
    waits = [
        pltpu.make_async_copy(dinner_ref.at[pl.ds(mine[0] * Q, len(mine) * Q + HALO)], dinner_here, in_sems.at[0]),
        pltpu.make_async_copy(dgate_ref.at[own], dgate_here, in_sems.at[1]),
    ]
    for copy in waits:
        copy.start()
    loads = [pltpu.make_async_copy(both_in[p], both.at[p], in_sems.at[2 + p]) for p in range(pieces)]
    for copy in loads:
        copy.start()
    gain = gain_ref[...]
    gain_sum = jnp.zeros((1, depth), F32)

    def finish(values_in, d_normed):
        h = values_in.astype(F32)
        scale = lax.rsqrt(jnp.mean(h * h, axis=1, keepdims=True) + EPSILON)
        weighted = gain * d_normed
        inner = jnp.mean(weighted * h, axis=1, keepdims=True)
        return scale * weighted - h * (scale * scale * scale * inner), jnp.sum(d_normed * h * scale, axis=0, keepdims=True)

    moves = []
    totals = [mm(dstate_ref[0:HALO], sproj_ref[...], 1, 1)]
    for block in mine:
        ext = slice(HALO + block * Q, HALO + (block + 1) * Q)
        part = mm(dstate_ref[ext], sproj_ref[...], 1, 1)
        totals.append(part + mm(dstep_ref[:, block * Q : (block + 1) * Q], hp_ref[:, 0:depth].astype(BF16), 0, 0))
    for copy in waits:
        copy.wait()
    for p in range(pieces):
        loads[p].wait()
        span = slice(p * wide, (p + 1) * wide)
        if mine[0] == 0:
            totals[0] += mm(dinner_here[0:HALO, span], both[p, :, wide:], 1, 1)
        for index in range(len(mine)):
            here = slice(index * Q, (index + 1) * Q)
            ext = slice(HALO + index * Q, HALO + (index + 1) * Q)
            totals[index + 1] += mm(dgate_here[here, span], both[p, :, :wide], 1, 1)
            totals[index + 1] += mm(dinner_here[ext, span], both[p, :, wide:], 1, 1)
    if mine[0] == 0:
        extra_ref[...], part = finish(halo_ref[...], totals[0])
        gain_sum += part
    else:
        extra_ref[...] = jnp.zeros_like(extra_ref)
    for index, block in enumerate(mine):
        at = slice(block * Q, (block + 1) * Q)
        here = slice(index * Q, (index + 1) * Q)
        d_hidden, part = finish(hid_ref[at], totals[index + 1].astype(BF16).astype(F32))
        gain_sum += part
        grad_ref[here] = cot_ref[at].astype(F32) + d_hidden
        moves.append(pltpu.make_async_copy(grad_ref.at[here], grad_out.at[at], sems.at[index]))
        moves[-1].start()
    gain_out[...] = jnp.zeros_like(gain_out)
    side = gain_out.shape[1]
    for index in range(depth // side):
        gain_out[index : index + 1] = gain_sum[:, index * side : (index + 1) * side]
    for copy in moves:
        copy.wait()


def gather_far(value, ahead):
    ways = lax.axis_size("head")
    pieces = {0: value}
    far = {0: after(value, ahead)}
    mask = 2
    while mask < ways:
        for p in list(far):
            far[p | mask] = swap(far[p], "head", mask)
        mask *= 2
    return [value] + [far[p] for p in range(2, ways, 2)]


def near_pair(value, ahead):
    return value, swap(after(value, ahead) if len(ahead) else value, "head", 1)


def swap(value, axis, mask):
    size = lax.axis_size(axis)
    return lax.ppermute(value, axis, [(i, i ^ mask) for i in range(size)])


def pick(value, index):
    return lax.dynamic_index_in_dim(value, index, 0, keepdims=False)


def half_of(value, mask):
    side = jnp.where((lax.axis_index("dp") & mask) != 0, 1, 0)
    parts = value.reshape(2, value.shape[0] // 2, value.shape[1])
    return pick(parts, side).astype(F32), pick(parts, 1 - side).astype(BF16)


def whole_dp(low):
    for bit in range(3, lax.axis_size("dp").bit_length() - 1):
        low = (low.astype(F32) + swap(low, "dp", 1 << bit).astype(F32)).astype(BF16)
    return low


def both_of(low, mask, other):
    upper = (lax.axis_index("dp") & mask) != 0
    return jnp.concatenate([jnp.where(upper, other, low), jnp.where(upper, low, other)], axis=0)


def after(value, *others):
    return lax.optimization_barrier((value, others))[0]


def gather_pieces(value, ahead=()):
    ways = lax.axis_size("head")
    pieces = {0: value, 1: swap(value, "head", 1)}
    far = {0: after(value, ahead) if ahead else value}
    mask = 2
    while mask < ways:
        for p in list(far):
            far[p | mask] = swap(far[p], "head", mask)
        mask *= 2
    for p in far:
        if p:
            pieces[p] = far[p]
            pieces[p | 1] = swap(far[p], "head", 1)
    return [pieces[p] for p in range(ways)]


def reduce_pieces(pieces):
    ways = len(pieces)
    mask = 1
    live = {p: v for p, v in enumerate(pieces)}
    order = [1 << b for b in range(ways.bit_length() - 1)]
    for mask in order:
        got = {p ^ mask: swap(live[p].astype(BF16), "head", mask) for p in live if p & mask}
        live = {p: live[p].astype(F32) + got[p].astype(F32) for p in live if not p & mask}
    return live[0]


def body(hidden, lengths, norm_gain, gate_proj, value_proj, state_proj, step_proj, value_taps, value_bias,
         state_taps, state_bias, step_bias, decay_log, skip_gain, out_gain, out_proj, cotangent):
    rows, depth = hidden.shape
    ways = lax.axis_size("head")
    me = lax.axis_index("head")
    blocks = rows // Q
    wide = gate_proj.shape[1]
    share = step_proj.shape[1]
    total = wide * ways
    heads = share * ways
    head_size = wide // share
    pairs = heads // 2
    side = state_proj.shape[1]
    state = side // 2
    padded = -(-heads // 32) * 32
    plain = wide % LANES == 0
    order = [1 << b for b in range(ways.bit_length() - 1)]
    scalars = jnp.concatenate(
        [jnp.stack([me, blocks * ways]).astype(jnp.int32), lengths[0], jnp.zeros((3,), jnp.int32)]
    )

    top = jnp.concatenate(
        [step_proj.T.astype(F32), step_bias[:, None], decay_log[:, None], skip_gain[:, None], jnp.zeros((share, LANES - 3), F32)],
        axis=1,
    )
    low = jnp.concatenate([value_taps, value_bias[None], out_gain[None]], axis=0)
    pack = jnp.concatenate(
        [
            jnp.pad(top, ((0, 8 - share), (0, 0))),
            jnp.pad(low, ((0, 2), (0, depth + LANES - wide))),
            jnp.pad(hidden[rows - HALO :].astype(F32), ((0, 0), (0, LANES))),
        ],
        axis=0,
    )
    packs = gather_pieces(pack)
    halo = jnp.zeros((HALO, depth), F32)
    for p in range(1, ways):
        halo = jnp.where((me ^ p) == me - 1, packs[p][16:, :depth], halo)
    halo = halo.astype(BF16)
    both = gather_far(jnp.concatenate([gate_proj, value_proj], axis=1), (packs[1],))
    outs = gather_far(out_proj, (packs, both[0]))

    def both_merged(pair):
        if plain:
            return list(pair)
        a, b = pair
        return [jnp.concatenate([a[:, :wide], b[:, :wide], a[:, wide:], b[:, wide:]], axis=1)]

    def outs_merged(pair):
        return list(pair) if plain else [jnp.concatenate(pair, axis=0)]

    pieces = ways if plain else ways // 2
    span = total // pieces
    tiles = span // LANES
    hp = jnp.pad(jnp.concatenate([p[:share] for p in packs], axis=0), ((0, padded - heads), (0, 0)))
    par = jnp.concatenate([p[8:16, :wide] for p in packs], axis=1)
    gain_in = norm_gain[None]
    staps = jnp.pad(jnp.concatenate([state_taps, state_bias[None]], axis=0), ((0, 3), (0, 0)))

    ext = rows + HALO
    (nx, nt, state_raw, state_pre, b_low, c_low, b_t, c_t, cb, cbt) = call(
        functools.partial(pre_kernel, blocks),
        [((ext, depth), BF16), ((depth, rows), BF16), ((ext, side), F32), ((rows, side), F32),
         ((rows, state), BF16), ((rows, state), BF16), ((state, rows), BF16), ((state, rows), BF16),
         ((blocks, Q, Q), F32), ((blocks, Q, Q), F32)],
        [scalars, hidden, halo, gain_in, state_proj, staps],
        cost=2, mib=PRE,
    )
    rowp, colp, step, ratio, sig, chan = call(
        functools.partial(step_kernel, blocks, head_size),
        [((pairs, 8, rows), F32), ((pairs // 2, rows, 16), F32), ((padded, rows), F32), ((padded, rows), F32),
         ((padded, rows), F32), ((8, total), F32)],
        [scalars, nx, hp],
        cost=2,
        mib=PRE,
    )
    vmem = pltpu.VMEM
    hbm = pl.BlockSpec(memory_space=pltpu.HBM)
    front_outs = [((rows, total), BF16), ((ext, total), BF16), ((rows, total), BF16), ((blocks, state, total), F32),
                  ((rows, total), BF16), ((state + HALO, total), BF16), ((state + HALO, total), BF16)]
    fronts, all_both = [], []
    half = pieces // 2
    for begin in (0, half):
        pairs_of = range(begin // 2, begin // 2 + ways // 4) if plain else range(begin, begin + half)
        weights = [w for at in pairs_of for w in both_merged(near_pair(both[at], fronts))]
        all_both += weights
        args = [scalars, nx, par, b_t, colp, chan, *weights]
        aliases = {len(args) + at: at for at in range(len(fronts))}
        fronts = call(
            functools.partial(front_kernel, blocks, begin, half), front_outs, [*args, *fronts], aliases=aliases,
            ins={len(args) + at: hbm for at in range(min(4, len(fronts)))}, out_specs={at: hbm for at in range(4)},
            kinds={at: pltpu.HBM for at in range(4)},
            scratch=[vmem((rows, half * span), BF16), vmem((ext, half * span), BF16), vmem((rows, half * span), BF16),
                     vmem((blocks, state, half * span), F32), vmem((ext, half * span), F32), pltpu.SemaphoreType.DMA((4,))],
            cost=6, mib=FRONT,
        )
    gate, inner, pre, st, x, carry, carry_turned = fronts

    def turned(value, mask):
        parts = [value[..., (p ^ mask) * wide : ((p ^ mask) + 1) * wide] for p in range(ways)]
        return jnp.concatenate(parts, axis=-1)

    def scan(own, own_turned, forward):
        def fade_of(value):
            return value[state : state + 1].astype(F32) + value[state + 1 : state + 2].astype(F32)

        if plain and ways == 4:
            near = swap(own_turned, "head", 1)
            (run,) = call(functools.partial(join_kernel, forward), [(own.shape, BF16)], [scalars, own, near], mib=8)
            far = swap(run, "head", 2)
            (result,) = call(functools.partial(arrive_kernel, forward), [((state, total), F32)], [scalars, near, far], mib=8)
            return result, run
        before = before_fade = None
        run = own
        for mask in order:
            if mask == 1 and plain:
                got = swap(own_turned, "head", 1)
            else:
                got = turned(swap(run, "head", mask), mask)
            got_fade, run_fade = fade_of(got), fade_of(run)
            got, mine = got[:state].astype(F32), run[:state].astype(F32)
            later = ((me & mask) != 0) if forward else ((me & mask) == 0)
            if before is None:
                before = jnp.where(later, got, 0.0)
                before_fade = jnp.where(later, got_fade, 1.0)
            else:
                before = jnp.where(later, before_fade * got + before, before)
                before_fade = jnp.where(later, before_fade * got_fade, before_fade)
            if mask != order[-1]:
                both_maps = jnp.where(later, run_fade * got + mine, got_fade * mine + got)
                fades = run_fade * got_fade
                high = fades.astype(BF16)
                low_part = (fades - high.astype(F32)).astype(BF16)
                run = jnp.concatenate(
                    [both_maps.astype(BF16), high, low_part, jnp.zeros((HALO - 2, total), BF16)], axis=0
                )
        return before, run

    inc_in, run = scan(carry, carry_turned, True)
    (y_intra,) = call(
        functools.partial(intra_kernel, blocks),
        [((rows, total), F32)],
        [scalars, rowp, colp, cb, after(x, run)],
        cost=5,
        mib=INTRA,
    )
    all_outs = [w for value in outs for w in outs_merged(near_pair(value, run))]
    dny, dbt = call(
        functools.partial(masked_kernel, blocks, pieces),
        [((rows, total), BF16), ((depth, rows), BF16)],
        [scalars, cotangent, *all_outs],
        scratch=[vmem((rows, depth), BF16)],
        cost=3,
        mib=INTRA,
    )
    wide_bf = vmem((rows, total), BF16)
    held_outs = [((rows, total), BF16), ((rows, total), BF16),
                 ((pieces // 2, 2 * depth, span), BF16), ((pieces // 2, 2 * depth, span), BF16),
                 ((blocks, state, total), BF16), ((blocks, state, total), BF16), ((rows, state), F32),
                 ((padded, rows), F32), ((8, total), F32)]
    (ny, d_gate, a_keep, a_send, inc, d_inc, dc_inter, rowpart, rows_sum, d_y, back_carry, back_turned) = call(
        functools.partial(middle_kernel, blocks, tiles, head_size),
        [*held_outs, ((rows, total), BF16), ((state + HALO, total), BF16), ((state + HALO, total), BF16)],
        [scalars, dbt, inc_in, colp, chan, par, c_low, c_t, nt, y_intra, dny, gate, x, st],
        out_specs={at: hbm for at in range(len(held_outs))}, kinds={at: pltpu.HBM for at in range(len(held_outs))},
        scratch=[*[vmem(*o) for at, o in enumerate(held_outs) if at not in (2, 3)], vmem((2, 2 * depth, 2 * LANES), BF16), vmem((rows, total), F32), vmem((rows, LANES), F32),
                 vmem((rows, LANES), F32), wide_bf, wide_bf, pltpu.SemaphoreType.DMA((len(held_outs) - 2,)),
                 pltpu.SemaphoreType.DMA((2, 2))],
        cost=14, mib=MIDDLE,
    )
    back_in, back_run = scan(back_carry, back_turned, False)

    def over_head(keep, send):
        if not plain:
            parts = [None] * ways
            for m in range(pieces):
                merged = (keep, send)[m % 2][m // 2]
                parts[2 * m], parts[2 * m + 1] = merged[:, :wide], merged[:, wide:]
            return reduce_pieces(parts)
        got = swap(send, "head", 1)
        live = [keep[i].astype(F32) + got[i].astype(F32) for i in range(pieces // 2)]
        return live

    def finish_head(live):
        if not plain:
            return live
        return live[0] + swap(live[1].astype(BF16), "head", 2).astype(F32)

    def halve(value, axis_at=0):
        side = lax.axis_index("dp") & 1
        cut = value.shape[:axis_at] + (2, value.shape[axis_at] // 2) + value.shape[axis_at + 1 :]
        parts = jnp.moveaxis(value.reshape(cut), axis_at, 0)
        got = swap(pick(parts, 1 - side).astype(BF16), "dp", 1)
        return pick(parts, side).astype(F32) + got.astype(F32)

    a_live = over_head(a_keep, after(a_send, back_run))
    if plain:
        a_out = finish_head([v[:depth] for v in a_live])
        a_gate = halve(jnp.stack([v[depth:] for v in a_live]), 1)
        gates = (a_out, a_gate)
    else:
        gates = a_live
    dx, part_a, db_in, dc_in = call(
        functools.partial(back_kernel, blocks, head_size),
        [((rows, total), BF16), ((padded, rows), F32), ((rows, state), F32), ((rows, state), F32)],
        [scalars, rowp, colp, cbt, b_low, c_low, d_y, x],
        scratch=[vmem((blocks, Q, Q), F32), wide_bf, wide_bf],
        cost=8,
        mib=BACK,
    )
    (d_inner, vgrad, part_b, lasts, db_x, b_keep, b_send) = call(
        functools.partial(tail_kernel, blocks, tiles, head_size),
        [((ext, total), BF16), ((8, total), F32), ((padded, rows), F32), ((8, total), F32), ((rows, state), F32),
         ((pieces // 2, depth, span), BF16), ((pieces // 2, depth, span), BF16)],
        [scalars, after(back_in, a_live), colp, chan, par, b_low, nt, nx, inc, dx, d_y, d_inc, x, pre, inner],
        out_specs={5: hbm, 6: hbm}, kinds={5: pltpu.HBM, 6: pltpu.HBM},
        scratch=[vmem((2, K, rows + 2 * HALO, LANES), F32), vmem((2, ext, LANES), F32), wide_bf, wide_bf,
                 vmem((2, depth, 2 * LANES), BF16), pltpu.SemaphoreType.DMA((2, 2))],
        cost=10, mib=TAIL,
    )
    small_rows, all_rows = 256, 832
    if plain:
        small_outs = [((pieces // 2, small_rows, span), BF16)] * 2
        shares = (ways, share, wide)
        work = [vmem((small_rows, span), F32)]
    else:
        small_outs = [((all_rows, side), F32), ((padded, depth), F32), ((padded, LANES), F32)]
        shares = None
        work = []
    d_state, d_step, *smalls = call(
        functools.partial(state_kernel, blocks, head_size, shares),
        [((ext, side), BF16), ((padded, rows), BF16)] + small_outs,
        [scalars, after(db_x, gates), db_in, dc_in, dc_inter, state_raw, state_pre, staps, rowpart, part_a, part_b, step, ratio, sig, hp,
         rows_sum, lasts, vgrad, nt, nx],
        scratch=work + [vmem((K, rows + 2 * HALO, side), F32), vmem((all_rows, side), F32), vmem((padded, depth), F32)],
        cost=4, mib=STATE,
    )
    share_rows = all_rows // ways
    if not plain:
        all_grad, step_grad, per_head = smalls
        parts = []
        for p in range(ways):
            cols, some = slice(p * wide, (p + 1) * wide), slice(p * share, (p + 1) * share)
            flat = step_grad[some].reshape(share, depth // wide, wide).swapaxes(0, 1).reshape(-1, wide)
            own = lax.dynamic_slice_in_dim(all_grad, (me ^ p) * share_rows, share_rows, 0).reshape(-1)
            count = -(-own.shape[0] // wide)
            own = jnp.pad(own, (0, count * wide - own.shape[0])).reshape(count, wide)
            part = jnp.concatenate(
                [vgrad[0:5, cols], rows_sum[0:1, cols], jnp.zeros((2, wide), F32), flat, jnp.zeros((16 - flat.shape[0], wide), F32),
                 jnp.pad(per_head[some], ((0, 8 - share), (0, wide - LANES))), own], axis=0)
            parts.append(jnp.pad(part, ((0, small_rows - part.shape[0]), (0, 0))))
        c_live = reduce_pieces(parts)
    else:
        c_live = over_head(smalls[0], smalls[1])
    b_live = over_head(b_keep, after(b_send, gates))
    if plain:
        a_part = jnp.concatenate([halve(a_out), finish_head([a_gate[0], a_gate[1]])], axis=0)
    else:
        a_part = halve(a_live)
    a_keep_z, a_send_z = half_of(a_part, 2)
    if plain:
        b_whole = [jnp.concatenate([b, c], axis=0) for b, c in zip(b_live, c_live)]
        cut = b_whole[0].shape[0] // 2
        side_x = lax.axis_index("dp") & 1
        low, high = [v[:cut] for v in b_whole], jnp.stack([v[cut:] for v in b_whole])
        high = jnp.moveaxis(high.reshape(2, 2, cut // 2, wide), 1, 0)
        b_sends = low[1].astype(BF16), pick(high, 1 - side_x).astype(BF16)
    else:
        b_sends = ()
    a_got_z = swap(after(a_send_z, b_sends), "dp", 2)
    if plain:
        b_got = swap(b_sends[0], "head", 2), swap(b_sends[1], "dp", 1)
    mine = list(range(blocks))
    args = [scalars, hidden, halo, cotangent, gain_in, after(d_gate, b_sends, a_send_z), d_inner, d_state, d_step, hp, state_proj,
            *all_both]
    results = call(
        functools.partial(final_kernel, pieces, blocks, mine),
        [((rows, depth), F32), ((HALO, depth), F32), ((8, span), F32)],
        args,
        ins={at: hbm for at in (5, 6, *range(len(args) - pieces, len(args)))},
        out_specs={0: hbm},
        kinds={0: pltpu.HBM},
        scratch=[vmem((rows, depth), F32), pltpu.SemaphoreType.DMA((blocks,)), vmem((pieces, depth, 2 * span), BF16),
                 vmem((rows, total), BF16), vmem((ext, total), BF16), pltpu.SemaphoreType.DMA((2 + pieces,))],
        cost=9,
        mib=FINAL,
    )
    grad_hidden, extra, gain_part = results
    extra = lax.ppermute(extra, "head", [(i + 1, i) for i in range(ways - 1)])
    grad_hidden = grad_hidden.at[rows - HALO :].add(extra)
    if plain:
        one = low[0] + after(b_got[0], results).astype(F32)
        two = pick(high, side_x) + after(b_got[1], results).astype(F32)
        one_keep, one_send = half_of(one, 1)
        b_sends = one_send, two[1].astype(BF16)
        b_part = [one_keep + swap(one_send, "dp", 1).astype(F32), two[0] + swap(b_sends[1], "head", 2).astype(F32)]
        b_part = jnp.concatenate(b_part, axis=0)
    else:
        b_part = halve(jnp.concatenate([b_live, c_live], axis=0))
    gain_rows = gain_part[: depth // span].reshape(depth // wide, wide)
    b_part = jnp.concatenate([b_part, gain_rows, jnp.zeros((32 - gain_rows.shape[0], wide), F32)], axis=0)
    a_low = (a_keep_z + after(a_got_z, results).astype(F32)).astype(BF16)
    a_got_y = swap(a_low, "dp", 4)
    a_low = whole_dp((a_low.astype(F32) + after(a_got_y, b_sends).astype(F32)).astype(BF16))
    b_keep_z, b_send_z = half_of(b_part, 2)
    b_got_z = swap(after(b_send_z, a_low), "dp", 2)
    a_got_z = swap(a_low, "dp", 2)
    (mixed,) = call(
        functools.partial(mixed_kernel, pieces, blocks),
        [((rows, depth), BF16)],
        [scalars, hidden, after(ny, a_low, b_send_z), *all_outs],
        pin=jax.ShapeDtypeStruct,
        cost=4,
        mib=FINAL,
    )
    b_low = (b_keep_z + after(b_got_z, a_low, mixed).astype(F32)).astype(BF16)
    b_got_y = swap(b_low, "dp", 4)
    a_all = both_of(a_low, 2, a_got_z)
    a_other = swap(a_all, "dp", 1)
    b_low = whole_dp((b_low.astype(F32) + after(b_got_y, a_all).astype(F32)).astype(BF16))
    b_all = both_of(b_low, 2, swap(b_low, "dp", 2))

    def unhalve(value, cuts, other=None):
        upper = (lax.axis_index("dp") & 1) != 0
        other = swap(value, "dp", 1) if other is None else other
        rows_out, begin = [], 0
        for count in cuts:
            mine, his = value[begin : begin + count], other[begin : begin + count]
            rows_out.append(jnp.concatenate([jnp.where(upper, his, mine), jnp.where(upper, mine, his)], axis=0))
            begin += count
        return rows_out

    b_all = after(b_all, a_other)
    a_cuts = [depth // 2, depth // 2] if plain else [depth]
    a_out, a_gate = unhalve(a_all, a_cuts, a_other) if plain else jnp.split(unhalve(a_all, a_cuts, a_other)[0], 2)
    grad_out = a_out.T.astype(F32)
    grad_gate = a_gate.astype(F32)
    cut = b_all.shape[0] - 32 - 256
    *b_rows, gain_all = unhalve(b_all[cut:], [256, 32])
    b_rows = unhalve(b_all[:cut], [cut]) + b_rows
    if not plain:
        *b_rows, gain_all = unhalve(b_all, [cut + 256, 32])
    b_all = jnp.concatenate(b_rows, axis=0)
    gain_all = (gain_all[:32].astype(F32) + gain_all[32:].astype(F32))[: depth // wide].reshape(1, depth)
    gain_all = jnp.pad(gain_all.reshape(-1, side), ((0, 16 - depth // side), (0, 0)))
    grad_value = b_all[:depth].astype(F32)
    small = b_all[depth:].astype(F32)
    grad_step = jnp.concatenate([small[8 + j * share : 8 + (j + 1) * share].T for j in range(depth // wide)], axis=0)
    if plain:
        own = b_all[depth + 32 : depth + 32 + share_rows, :side]
    else:
        own = b_all[depth + 32 : depth + 240].reshape(-1)[: share_rows * side].reshape(share_rows, side)
    stacked, members = own, [0]
    for mask in reversed(order):
        members += [p | mask for p in members]
        gain_low = gain_all.astype(BF16)
        sent = jnp.concatenate([stacked, gain_low], axis=0)
        got = swap(after(sent, grad_value) if mask == 1 else sent, "head", mask)
        stacked = jnp.concatenate([stacked, got[: stacked.shape[0]]], axis=0)
        gain_all = gain_low.astype(F32) + got[-16:].astype(F32)
    stacked = stacked.reshape(ways, share_rows, side)
    stacked = jnp.stack([stacked[members.index(p)] for p in range(ways)])
    full = jnp.concatenate([pick(stacked, me ^ q) for q in range(ways)], axis=0).astype(F32)
    return (
        mixed,
        grad_hidden,
        gain_all[: depth // side].reshape(-1),
        grad_gate,
        grad_value,
        full[:depth],
        grad_step,
        small[0:4],
        small[4],
        full[depth : depth + 4],
        full[depth + 4],
        small[24 : 24 + share, 0],
        small[24 : 24 + share, 1],
        small[24 : 24 + share, 2],
        small[5],
        grad_out,
    )


def solution(mesh):
    rows = P(("dp", "head"), None)
    in_specs = (
        rows, P("dp", None), P(), P(None, "head"), P(None, "head"), P(), P(None, "head"), P(None, "head"),
        P("head"), P(), P(), P("head"), P("head"), P("head"), P("head"), P("head", None), rows,
    )
    out_specs = (
        rows, rows, P(), P(None, "head"), P(None, "head"), P(), P(None, "head"), P(None, "head"),
        P("head"), P(), P(), P("head"), P("head"), P("head"), P("head"), P("head", None),
    )
    return jax.shard_map(body, mesh=mesh, in_specs=in_specs, out_specs=out_specs, check_vma=False)
```

```python
import functools

import jax
import jax.numpy as jnp
from jax import lax
from jax.experimental import pallas as pl
from jax.experimental.pallas import tpu as pltpu
from jax.sharding import PartitionSpec as P

K = 4
Q = 256
HALO = 16
LANES = 128
EPSILON = 1e-05
F32 = jnp.float32
BF16 = jnp.bfloat16
HIGHEST = lax.Precision.HIGHEST


def mm(left, right, lc=1, rc=0, precision=None):
    return lax.dot_general(
        left,
        right,
        (((lc,), (rc,)), ((), ())),
        preferred_element_type=F32,
        precision=precision,
    )


MIB = 1024 * 1024
PRE, FRONT, INTRA, MIDDLE, BACK, TAIL, STATE, FINAL = 12, 14, 12, 18, 56, 14, 12, 56


def whole(shape):
    return pl.BlockSpec(shape, lambda *_: (0,) * len(shape))


def call(kernel, outs, args, scratch=(), grid=(), ins=None, out_specs=None, aliases=None, mib=48, cost=0, pin=pltpu.VMEM, kinds=None):
    ins, out_specs, kinds = ins or {}, out_specs or {}, kinds or {}
    specs = [pl.BlockSpec(memory_space=pltpu.SMEM)]
    for at, value in enumerate(args[1:], 1):
        specs.append(ins[at] if at in ins else whole(value.shape))
    outs_specs = [out_specs[at] if at in out_specs else whole(o[0]) for at, o in enumerate(outs)]
    return pl.pallas_call(
        kernel,
        grid=grid,
        out_shape=[kinds[at](s, d) if at in kinds else pin(s, d) for at, (s, d) in enumerate(outs)],
        in_specs=specs,
        out_specs=outs_specs,
        scratch_shapes=list(scratch),
        input_output_aliases=aliases or {},
        compiler_params=pltpu.CompilerParams(vmem_limit_bytes=mib * MIB),
        cost_estimate=pl.CostEstimate(flops=int(cost * 4e8), bytes_accessed=int(cost * 3e5), transcendentals=0),
    )(*args)


def keeps_of(s_ref, block, blocks):
    place = s_ref[0] * blocks + block
    fresh = (place == 0) | (place == 1) | (place == s_ref[1] - 1)
    return fresh, jnp.where(fresh, 0.0, 1.0).astype(F32)


def row_keep(fresh, distance):
    rows = lax.broadcasted_iota(jnp.int32, (Q, 1), 0)
    return (rows >= jnp.where(fresh, distance, 0)).astype(F32)


def conv_block(ref, base, cols, taps, fresh):
    total = taps[K : K + 1] + taps[K - 1 : K] * ref[pl.ds(base, Q), cols]
    for distance in range(1, K):
        earlier = ref[pl.ds(base - distance, Q), cols]
        total = total + taps[K - 1 - distance : K - distance] * (earlier * row_keep(fresh, distance))
    return total


def silu_slope(values, sig):
    return sig * (1.0 + values * (1.0 - sig))


def first_lanes():
    return lax.broadcasted_iota(jnp.int32, (1, LANES), 1) < LANES // 2


def spread(cols, quantity):
    return jnp.where(
        first_lanes(), cols[:, 2 * quantity : 2 * quantity + 1], cols[:, 2 * quantity + 1 : 2 * quantity + 2]
    )


def head_lanes(rows, heads_first, head_size):
    lane = lax.broadcasted_iota(jnp.int32, rows, 1 if heads_first else 0)
    head = lax.broadcasted_iota(jnp.int32, rows, 0 if heads_first else 1)
    return (lane >= head * head_size) & (lane < (head + 1) * head_size)


def pre_kernel(blocks, s_ref, hid_ref, halo_ref, gain_ref, proj_ref, taps_ref,
               nx_ref, nt_ref, raw_ref, pre_ref, b_ref, c_ref, bt_ref, ct_ref, cb_ref, cbt_ref):
    gain = gain_ref[...]
    rows = blocks * Q

    def norm(v):
        v = v.astype(F32)
        return v * lax.rsqrt(jnp.mean(v * v, axis=1, keepdims=True) + EPSILON) * gain

    halo = norm(halo_ref[...])
    own = norm(hid_ref[...])
    nx_ref[0:HALO] = halo.astype(BF16)
    nx_ref[HALO:] = own.astype(BF16)
    nt_ref[:, 0:rows] = own.T.astype(BF16)
    raw_ref[...] = mm(nx_ref[...], proj_ref[...])
    taps = taps_ref[...]
    state = b_ref.shape[1]
    for block in range(blocks):
        fresh, _ = keeps_of(s_ref, block, blocks)
        pre = conv_block(raw_ref, HALO + block * Q, slice(None), taps, fresh)
        at = pl.ds(block * Q, Q)
        pre_ref[at] = pre
        conv = pre * jax.nn.sigmoid(pre)
        b_mat = conv[:, :state]
        c_mat = conv[:, state:]
        b_low = b_mat.astype(BF16)
        c_low = c_mat.astype(BF16)
        b_ref[at] = b_low
        c_ref[at] = c_low
        bt_ref[:, at] = b_mat.T.astype(BF16)
        ct_ref[:, at] = c_mat.T.astype(BF16)
        cb_ref[block] = mm(c_low, b_low, 1, 1)
        cbt_ref[block] = mm(b_low, c_low, 1, 1)


def step_kernel(blocks, head_size, s_ref, nx_ref, hp_ref, rowp_ref, colp_ref, step_ref, ratio_ref, sig_ref, chan_ref):
    depth = nx_ref.shape[1]
    hp = hp_ref[...]
    u = mm(hp[:, :depth].astype(BF16), nx_ref[HALO:], 1, 1) + hp[:, depth : depth + 1]
    step = jnp.maximum(u, 0.0) + jnp.log1p(jnp.exp(-jnp.abs(u)))
    sig = jax.nn.sigmoid(u)
    step_ref[...] = step
    sig_ref[...] = sig
    ratio_ref[...] = jnp.where(step > 1e-30, sig / jnp.maximum(step, 1e-30), 1.0)
    rate = -jnp.exp(hp[:, depth + 1 : depth + 2])
    move = step * rate
    upto = (
        lax.broadcasted_iota(jnp.int32, (Q, Q), 0) <= lax.broadcasted_iota(jnp.int32, (Q, Q), 1)
    ).astype(F32)
    heads = hp.shape[0]
    lane = lax.broadcasted_iota(jnp.int32, (heads, LANES), 1)
    last_cols = jnp.zeros((heads, LANES), F32)
    lstep = jnp.log(step)
    product = jnp.ones((heads, 1), F32)
    pairs = rowp_ref.shape[0]
    for block in range(blocks):
        at = slice(block * Q, (block + 1) * Q)
        logd = mm(move[:, at], upto, precision=HIGHEST)
        less = logd - lstep[:, at]
        last = logd[:, Q - 1 : Q]
        grown = jnp.exp(logd)
        carry = jnp.exp(last - less)
        final = jnp.exp(last)
        _, kept = keeps_of(s_ref, block, blocks)
        product = product * final * kept
        last_cols = jnp.where(lane == block, final, last_cols)
        for pair in range(pairs):
            for index, values in enumerate((logd, less, grown, carry)):
                rowp_ref[pair, 2 * index : 2 * index + 2, at] = values[2 * pair : 2 * pair + 2]
    last_cols = jnp.where(lane == 6, product, last_cols)
    last_cols = jnp.where(lane == 7, hp[:, depth + 2 : depth + 3], last_cols)
    spots = head_lanes((heads, chan_ref.shape[1]), True, head_size).astype(F32)
    chan_ref[...] = mm(last_cols.T[0:8], spots, precision=HIGHEST)
    for pair in range(0, pairs, 2):
        colp_ref[pair // 2] = jnp.concatenate([rowp_ref[pair], rowp_ref[pair + 1]], 0).T


def carry_block(ref, cols, carry, fades):
    state = carry.shape[0]
    ref[0:state, cols] = carry.astype(BF16)
    high = fades.astype(BF16).astype(F32)
    row = lax.broadcasted_iota(jnp.int32, (HALO, LANES), 0)
    ref[state:, cols] = jnp.where(row == 0, high, jnp.where(row == 1, fades - high, 0.0)).astype(BF16)


def tile_at(index):
    return pl.ds(pl.multiple_of(index * LANES, LANES), LANES)


def front_kernel(blocks, first_piece, pieces, s_ref, nx_ref, par_ref, bt_ref, colp_ref, chan_ref, *refs):
    weights = refs[:pieces]
    (gate_out, inner_out, pre_out, s_out, x_ref, carry_ref, turned_ref,
     gate_ref, inner_ref, pre_ref, st_ref, work, sems) = refs[-13:]
    done = refs[pieces:-13]
    wide = weights[0].shape[1] // 2
    for old, new in zip(done[4:], (x_ref, carry_ref, turned_ref)):
        new[:, 0 : first_piece * wide] = old[:, 0 : first_piece * wide]
    own = slice(first_piece * wide, (first_piece + pieces) * wide)
    moves = [(gate_ref, gate_out), (inner_ref, inner_out), (pre_ref, pre_out), (st_ref, s_out)]
    for p in range(pieces):
        here = slice(p * wide, (p + 1) * wide)
        work[:, here] = mm(nx_ref[...], weights[p][:, wide:])
        gate_ref[:, here] = mm(nx_ref[HALO:], weights[p][:, :wide]).astype(BF16)
    tiles = wide // LANES

    def tile(i, cols_of):
        here = tile_at(i)
        pair = i + first_piece * tiles
        far = tile_at(pair)
        turned = tile_at(jnp.bitwise_xor(pair // tiles, 1) * tiles + pair % tiles)
        taps = par_ref[:, far]
        inner_ref[:, here] = work[:, here].astype(BF16)
        for block in range(blocks):
            at = pl.ds(block * Q, Q)
            fresh, kept = keeps_of(s_ref, block, blocks)
            pre = conv_block(work, HALO + block * Q, here, taps, fresh)
            pre_ref[at, here] = pre.astype(BF16)
            x = pre * jax.nn.sigmoid(pre)
            x_ref[at, far] = x.astype(BF16)
            weighted = (spread(cols_of(at), 3) * x).astype(BF16)
            state = mm(bt_ref[:, at], weighted)
            st_ref[block, :, here] = state
            if block == 0:
                carry = state
            else:
                carry = chan_ref[block : block + 1, far] * (kept * carry) + state
        carry_block(carry_ref, far, carry, chan_ref[6:7, far])
        carry_block(turned_ref, turned, carry, chan_ref[6:7, far])
        for index, (held, out) in enumerate(moves):
            pltpu.make_async_copy(held.at[..., here], out.at[..., far], sems.at[index]).start()

    def turn(i, none):
        for k in range(2):
            tile(2 * i + k, lambda at, k=k: colp_ref[i + first_piece * tiles // 2, at, 8 * k : 8 * k + 8])
        return none

    lax.fori_loop(0, pieces * tiles // 2, turn, 0)
    for index, (held, out) in enumerate(moves):
        pltpu.make_async_copy(held, out.at[..., own], sems.at[index]).wait()


def unpack_carry(ref):
    state = ref.shape[0] - HALO
    return ref[0:state].astype(F32), ref[state : state + 1].astype(F32) + ref[state + 1 : state + 2].astype(F32)


def join_kernel(forward, s_ref, own_ref, got_ref, out_ref):
    mine, my_fade = unpack_carry(own_ref)
    his, his_fade = unpack_carry(got_ref)
    later = (jnp.bitwise_and(s_ref[0], 1) == 1) == forward
    state = mine.shape[0]
    total = jnp.where(later, my_fade * his + mine, his_fade * mine + his)
    fade = my_fade * his_fade
    high = fade.astype(BF16).astype(F32)
    row = lax.broadcasted_iota(jnp.int32, (HALO, total.shape[1]), 0)
    out_ref[0:state] = total.astype(BF16)
    out_ref[state:] = jnp.where(row == 0, high, jnp.where(row == 1, fade - high, 0.0)).astype(BF16)


def arrive_kernel(forward, s_ref, near_ref, far_ref, out_ref):
    near, near_fade = unpack_carry(near_ref)
    wide = near.shape[1] // 2
    later = (jnp.bitwise_and(s_ref[0], 1) == 1) == forward
    far_later = (jnp.bitwise_and(s_ref[0], 2) == 2) == forward
    near = jnp.where(later, near, 0.0)
    fade = jnp.where(far_later, jnp.where(later, near_fade, 1.0), 0.0)
    for half in range(2):
        here, there = slice(half * wide, (half + 1) * wide), slice((1 - half) * wide, (2 - half) * wide)
        out_ref[:, here] = near[:, here] + fade[:, here] * far_ref[0 : near.shape[0], there].astype(F32)


def masked_cotangent(s_ref, cot_ref, blocks, block):
    at = slice(block * Q, (block + 1) * Q)
    return cot_ref[at].astype(F32) * valid_of(s_ref, blocks, block)


def masked_kernel(blocks, pieces, s_ref, cot_ref, *refs):
    outs_w = refs[:pieces]
    dny_ref, dbt_ref, db_ref = refs[pieces:]
    for block in range(blocks):
        at = slice(block * Q, (block + 1) * Q)
        masked = masked_cotangent(s_ref, cot_ref, blocks, block)
        db_ref[at] = masked.astype(BF16)
        dbt_ref[:, at] = masked.T.astype(BF16)
    wide = outs_w[0].shape[0]
    for p in range(pieces):
        dny_ref[:, p * wide : (p + 1) * wide] = mm(db_ref[...], outs_w[p][...], 1, 1).astype(BF16)


def intra_kernel(blocks, s_ref, rowp_ref, colp_ref, cb_ref, x_ref, y_ref):
    half = Q // 2
    first = first_lanes()
    tri = lax.broadcasted_iota(jnp.int32, (half, half), 0) >= lax.broadcasted_iota(
        jnp.int32, (half, half), 1
    )

    def work(i, k):
        pair = 2 * i + k
        far = tile_at(pair)
        for block in range(blocks):
            at = pl.ds(block * Q, Q)
            x = x_ref[at, far]
            both = [jnp.where(first, x, 0), jnp.where(first, 0, x)]
            rp = rowp_ref[pair, :, at]
            cp = colp_ref[i, at, 8 * k : 8 * k + 8]
            tops, bots = [], []
            for h in range(2):
                ld, ls = cp[:, h : h + 1], rp[2 + h : 3 + h, :]
                arg = jnp.where(tri, ld[:half] - ls[:, :half], -1e30)
                tops.append((cb_ref[block, 0:half, 0:half] * jnp.exp(arg)).astype(BF16))
                arg = ld[half:] - ls[:, :half]
                bots.append((cb_ref[block, half:, 0:half] * jnp.exp(arg)).astype(BF16))
                arg = jnp.where(tri, ld[half:] - ls[:, half:], -1e30)
                bots.append((cb_ref[block, half:, half:] * jnp.exp(arg)).astype(BF16))
            y_ref[pl.ds(block * Q, half), far] = mm(jnp.concatenate(tops, 1), jnp.concatenate([b[:half] for b in both], 0))
            y_ref[pl.ds(block * Q + half, half), far] = mm(jnp.concatenate(bots, 1), jnp.concatenate(both, 0))

    def two(i, none):
        work(i, 0)
        work(i, 1)
        return none

    lax.fori_loop(0, x_ref.shape[1] // (2 * LANES), two, 0)


def split_store(hi_ref, lo_ref, at, cols, part):
    high = part.astype(BF16)
    hi_ref[at, cols] = high
    lo_ref[at, cols] = (part - high.astype(F32)).astype(BF16)


def head_sums(heads, head_size, hi_ref, lo_ref):
    spots = head_lanes((heads, hi_ref.shape[1]), True, head_size).astype(F32).astype(BF16)
    return mm(spots, hi_ref[...], 1, 1) + mm(spots, lo_ref[...], 1, 1)


def valid_of(s_ref, blocks, block):
    place = s_ref[0] * blocks + block
    last = place == s_ref[1] - 1
    length = jnp.where(place == 0, s_ref[2], jnp.where(last, s_ref[4], s_ref[3]))
    start = jnp.where(place == 0, 0, jnp.where(last, s_ref[1] - 1, 1))
    rows = lax.broadcasted_iota(jnp.int32, (Q, 1), 0) + (place - start) * Q
    return (rows < length).astype(F32)


class Outbound:
    def __init__(self, held, sems, keep, send, tiles):
        self.held, self.sems, self.keep, self.send, self.tiles = held, sems, keep, send, tiles

    def wait(self, slot):
        for k in range(2):
            held = self.held.at[slot, :, k * LANES : (k + 1) * LANES]
            pltpu.make_async_copy(held, self.keep.at[0, :, 0:LANES], self.sems.at[slot, k]).wait()

    def start(self, turn, slot):
        for k in range(2):
            at = 2 * turn + k
            piece, lane = at // self.tiles, at % self.tiles
            held = self.held.at[slot, :, k * LANES : (k + 1) * LANES]
            cols = slice(lane * LANES, (lane + 1) * LANES) if isinstance(lane, int) else tile_at(lane)
            for odd, ref in enumerate((self.keep, self.send)):

                @pl.when(piece % 2 == odd)
                def _(ref=ref, held=held, piece=piece, cols=cols, k=k):
                    pltpu.make_async_copy(held, ref.at[piece // 2, :, cols], self.sems.at[slot, k]).start()


def turns_with_grads(turns, work, grads, out):
    def turn(i, none):
        before = jnp.maximum(i - 1, 0)
        slot = before % 2

        @pl.when(i >= 3)
        def _():
            out.wait(slot)

        grads(before, slot)
        work(i, 0)
        work(i, 1)

        @pl.when(i >= 1)
        def _():
            out.start(before, slot)

        return none

    lax.fori_loop(0, turns, turn, 0)
    last = turns - 1
    if last >= 2:
        out.wait(last % 2)
    grads(last, last % 2)
    out.start(jnp.int32(last), last % 2)
    for slot in range(min(2, turns)):
        out.wait(slot)


def middle_kernel(blocks, tiles, head_size, s_ref, dbt_ref, inc_in, colp_ref, chan_ref, par_ref, c_ref, ct_ref, nt_ref,
                  y_ref, dny_ref, gate_ref, x_ref, st_ref,
                  ny_out, dgate_out, keep_out, send_out, inc_out, di_out, dc_out, rowpart_out, rows_out,
                  dy_ref, carry_ref, turned_ref,
                  ny_ref, dgate_ref, inc_ref, di_ref, dc_ref, rowpart_ref, rows_ref, grad_ref,
                  mix_ref, sq_ref, cr_ref, hi_ref, lo_ref, sems, grad_sems):
    moves = [(ny_ref, ny_out), (dgate_ref, dgate_out), (inc_ref, inc_out), (di_ref, di_out), (dc_ref, dc_out), (rowpart_ref, rowpart_out), (rows_ref, rows_out)]

    def move(index, *where):
        held, out = moves[index]
        pltpu.make_async_copy(held.at[where], out.at[where], sems.at[index]).start()

    depth = dbt_ref.shape[0]
    total = chan_ref.shape[1]
    kept = [keeps_of(s_ref, block, blocks)[1] for block in range(blocks)]
    sq_ref[...] = jnp.zeros_like(sq_ref)
    cr_ref[...] = jnp.zeros_like(cr_ref)

    def forward(i, none):
        for k in range(2):
            far = tile_at(2 * i + k)
            incoming = inc_in[:, far]
            for block in range(blocks):
                at = pl.ds(block * Q, Q)
                incoming = kept[block] * incoming
                inc_low = incoming.astype(BF16)
                inc_ref[block, :, far] = inc_low
                incoming = chan_ref[block : block + 1, far] * incoming + st_ref[block, :, far]
                inter = mm(c_ref[at], inc_low) * spread(colp_ref[i, at, 8 * k : 8 * k + 8], 2)
                mix = y_ref[at, far] + inter + chan_ref[7:8, far] * x_ref[at, far].astype(F32)
                mix_ref[at, far] = mix
                gate = gate_ref[at, far].astype(F32)
                gated = mix * (gate * jax.nn.sigmoid(gate))
                sq_ref[at] += gated * gated
                cr_ref[at] += dny_ref[at, far].astype(F32) * par_ref[5:6, far] * gated
        return none

    lax.fori_loop(0, total // (2 * LANES), forward, 0)
    scale = lax.rsqrt(jnp.sum(sq_ref[...], axis=1, keepdims=True) / total + EPSILON)
    coef = scale * scale * scale * (jnp.sum(cr_ref[...], axis=1, keepdims=True) / total)
    sq_ref[...] = jnp.broadcast_to(scale, sq_ref.shape)
    cr_ref[...] = jnp.broadcast_to(coef, cr_ref.shape)
    rows_ref[...] = jnp.zeros_like(rows_ref)

    def backward(i, k):
        pair = 2 * i + k
        far = tile_at(pair)
        gain = par_ref[5:6, far]
        skip = chan_ref[7:8, far]
        gain_row = jnp.zeros((1, LANES), F32)
        skip_row = jnp.zeros((1, LANES), F32)
        dis = []
        for block in range(blocks):
            at = pl.ds(block * Q, Q)
            gate, mix, x = gate_ref[at, far].astype(F32), mix_ref[at, far], x_ref[at, far].astype(F32)
            sig = jax.nn.sigmoid(gate)
            act = gate * sig
            gated = mix * act
            normed = gated * sq_ref[at]
            dny = dny_ref[at, far].astype(F32)
            ny_ref[at, far] = (normed * gain).astype(BF16)
            gain_row += jnp.sum(dny * normed, axis=0, keepdims=True)
            d_gated = dny * gain * sq_ref[at] - gated * cr_ref[at]
            dgate_ref[at, far] = (d_gated * mix * silu_slope(gate, sig)).astype(BF16)
            dy = d_gated * act
            dy_low = dy.astype(BF16)
            dy_ref[at, far] = dy_low
            skip_row += jnp.sum(dy * x, axis=0, keepdims=True)
            split_store(hi_ref, lo_ref, at, far, dy_low.astype(F32) * (mix - skip * x))
            dye = (dy * spread(colp_ref[i, at, 8 * k : 8 * k + 8], 2)).astype(BF16)
            dc_ref[at] += mm(dye, inc_ref[block, :, far], 1, 1)
            di = mm(ct_ref[:, at], dye).astype(BF16)
            di_ref[block, :, far] = di
            dis.append(di.astype(F32))
        rows_ref[0:1, far] = gain_row
        rows_ref[1:2, far] = skip_row
        back = jnp.zeros_like(dis[0])
        for block in reversed(range(blocks)):
            back = kept[block] * (dis[block] + chan_ref[block : block + 1, far] * back)
        carry_block(carry_ref, far, back, chan_ref[6:7, far])
        turned = tile_at(jnp.bitwise_xor(pair // tiles, 1) * tiles + pair % tiles)
        carry_block(turned_ref, turned, back, chan_ref[6:7, far])
        move(0, slice(None), far)
        move(1, slice(None), far)

    def grads(turn, slot):
        cols = pl.ds(pl.multiple_of(turn * 2 * LANES, 2 * LANES), 2 * LANES)
        grad_ref[slot, 0:depth] = mm(dbt_ref[...], ny_ref[:, cols]).astype(BF16)
        grad_ref[slot, depth:] = mm(nt_ref[...], dgate_ref[:, cols]).astype(BF16)

    dc_ref[...] = jnp.zeros_like(dc_ref)
    turns_with_grads(total // (2 * LANES), backward, grads, Outbound(grad_ref, grad_sems, keep_out, send_out, tiles))
    for index in (2, 3, 4, 6):
        move(index)
    rowpart_ref[...] = head_sums(rowpart_ref.shape[0], head_size, hi_ref, lo_ref)
    move(5)
    for index, (held, out) in enumerate(moves):
        pltpu.make_async_copy(held, out, sems.at[index]).wait()


def back_kernel(blocks, head_size, s_ref, rowp_ref, colp_ref, cbt_ref, b_ref, c_ref, dy_ref, x_ref,
                dx_ref, part_ref, db_ref, dc_ref, acc_ref, hi_ref, lo_ref):
    half = Q // 2
    first = first_lanes()
    tri = lax.broadcasted_iota(jnp.int32, (half, half), 0) <= lax.broadcasted_iota(
        jnp.int32, (half, half), 1
    )
    acc_ref[...] = jnp.zeros_like(acc_ref)

    def two(i, none):
        for block in range(blocks):
            at = pl.ds(block * Q, Q)
            w00 = w01 = w11 = 0.0
            for k in range(2):
                pair = 2 * i + k
                far = tile_at(pair)
                x, dy = x_ref[at, far], dy_ref[at, far]
                dys = [jnp.where(first, dy, 0), jnp.where(first, 0, dy)]
                xs = [jnp.where(first, x, 0), jnp.where(first, 0, x)]
                rp = rowp_ref[pair, :, at]
                cp = colp_ref[i, at, 8 * k : 8 * k + 8]
                tops, bots = [], []
                for h in range(2):
                    ls, ld = cp[:, 2 + h : 3 + h], rp[h : h + 1, :]
                    ds_top = mm(xs[h][:half], dy, 1, 1)
                    ds_bot = mm(xs[h][half:], dy[half:], 1, 1)
                    e00 = jnp.exp(jnp.where(tri, ld[:, :half] - ls[:half], -1e30))
                    e01 = jnp.exp(ld[:, half:] - ls[:half])
                    e11 = jnp.exp(jnp.where(tri, ld[:, half:] - ls[half:], -1e30))
                    tops.append((cbt_ref[block, 0:half, 0:half] * e00).astype(BF16))
                    tops.append((cbt_ref[block, 0:half, half:] * e01).astype(BF16))
                    bots.append((cbt_ref[block, half:, half:] * e11).astype(BF16))
                    w00 += ds_top[:, :half] * e00
                    w01 += ds_top[:, half:] * e01
                    w11 += ds_bot * e11
                dx_top = mm(jnp.concatenate(tops, 1), jnp.concatenate(dys, 0))
                dx_bot = mm(jnp.concatenate(bots, 1), jnp.concatenate([d[half:] for d in dys], 0))
                dx = jnp.concatenate([dx_top, dx_bot], 0)
                dx_ref[at, far] = dx.astype(BF16)
                split_store(hi_ref, lo_ref, at, far, x.astype(F32) * dx)
            acc_ref[block, 0:half, 0:half] += w00
            acc_ref[block, 0:half, half:] += w01
            acc_ref[block, half:, half:] += w11
        return none

    lax.fori_loop(0, x_ref.shape[1] // (2 * LANES), two, 0)
    part_ref[...] = head_sums(part_ref.shape[0], head_size, hi_ref, lo_ref)
    for block in range(blocks):
        at = slice(block * Q, (block + 1) * Q)
        acc = acc_ref[block].astype(BF16)
        db_ref[at] = mm(acc, c_ref[at])
        dc_ref[at] = mm(acc, b_ref[at], 0, 0)


def conv_back(s_ref, blocks, work, taps, values_of, slope_of, store):
    sums = [0.0] * (K + 1)
    for block in range(blocks):
        fresh, _ = keeps_of(s_ref, block, blocks)
        d_pre = slope_of(block)
        work[0, pl.ds(HALO + block * Q, Q)] = d_pre
        sums[K] += jnp.sum(d_pre, axis=0, keepdims=True)
        sums[K - 1] += jnp.sum(d_pre * values_of(HALO + block * Q), axis=0, keepdims=True)
        for distance in range(1, K):
            held = d_pre * row_keep(fresh, distance)
            work[distance, pl.ds(HALO + block * Q, Q)] = held
            sums[K - 1 - distance] += jnp.sum(
                held * values_of(HALO + block * Q - distance), axis=0, keepdims=True
            )
    for begin, count in [(0, HALO)] + [(HALO + b * Q, Q) for b in range(blocks)]:
        out = taps[K - 1 : K] * work[0, pl.ds(begin, count)]
        for distance in range(1, K):
            out = out + taps[K - 1 - distance : K - distance] * work[distance, pl.ds(begin + distance, count)]
        store(begin, count, out.astype(BF16))
    return sums


def tail_kernel(blocks, tiles, head_size, s_ref, back_in, colp_ref, chan_ref, par_ref, b_ref, nt_ref, nx_ref,
                inc_ref, dx_ref, dy_ref, di_ref, x_ref, pre_ref, inner_ref,
                dinner_ref, vgrad_ref, part_ref, lasts_ref, db_ref, keep_out, send_out,
                d_ref, in_ref, hi_ref, lo_ref, grad_ref, grad_sems):
    total = chan_ref.shape[1]
    kept = [keeps_of(s_ref, block, blocks)[1] for block in range(blocks)]
    d_ref[...] = jnp.zeros_like(d_ref)
    vgrad_ref[...] = jnp.zeros_like(vgrad_ref)
    lasts_ref[...] = jnp.zeros_like(lasts_ref)
    db_ref[...] = jnp.zeros_like(db_ref)

    def work(i, k):
        far = tile_at(2 * i + k)
        in_ref[k] = inner_ref[:, far].astype(F32)
        skip = chan_ref[7:8, far]
        back = back_in[:, far]
        lasts, lows = [None] * blocks, [None] * blocks
        for block in reversed(range(blocks)):
            fade = chan_ref[block : block + 1, far]
            lows[block] = back.astype(BF16)
            lasts[block] = fade * jnp.sum(inc_ref[block, :, far].astype(F32) * back, axis=0, keepdims=True)
            back = kept[block] * (di_ref[block, :, far].astype(F32) + fade * back)

        def slope_of(block):
            at = pl.ds(block * Q, Q)
            carry = spread(colp_ref[i, at, 8 * k : 8 * k + 8], 3)
            weighted = carry * x_ref[at, far].astype(F32)
            db_ref[at] += mm(weighted.astype(BF16), lows[block], 1, 1)
            d_weighted = mm(b_ref[at], lows[block])
            moved = weighted * d_weighted
            lasts_ref[block : block + 1, far] = lasts[block] + jnp.sum(moved, axis=0, keepdims=True)
            split_store(hi_ref, lo_ref, at, far, moved)
            d_x = dx_ref[at, far].astype(F32) + carry * d_weighted + skip * dy_ref[at, far].astype(F32)
            pre = pre_ref[at, far].astype(F32)
            return d_x * silu_slope(pre, jax.nn.sigmoid(pre))

        def store(begin, count, value):
            dinner_ref[pl.ds(begin, count), far] = value

        sums = conv_back(
            s_ref, blocks, d_ref.at[k], par_ref[:, far], lambda at: in_ref[k, pl.ds(at, Q)], slope_of, store
        )
        for index in range(K + 1):
            vgrad_ref[index : index + 1, far] = sums[index]

    def grads(turn, slot):
        cols = pl.ds(pl.multiple_of(turn * 2 * LANES, 2 * LANES), 2 * LANES)
        grad = mm(nt_ref[...], dinner_ref[HALO:, cols]) + mm(nx_ref[0:HALO], dinner_ref[0:HALO, cols], 0, 0)
        grad_ref[slot] = grad.astype(BF16)

    turns_with_grads(total // (2 * LANES), work, grads, Outbound(grad_ref, grad_sems, keep_out, send_out, tiles))
    part_ref[...] = head_sums(part_ref.shape[0], head_size, hi_ref, lo_ref)


def state_kernel(blocks, head_size, shares, s_ref, dbx_ref, dbin_ref, dcin_ref, dcx_ref, raw_ref, spre_ref, staps_ref,
                 rowpart_ref, part_a, part_b, step_ref, ratio_ref, sig_ref, hp_ref, rows_ref, lasts_ref, vgrad_ref,
                 nt_ref, nx_ref, dstate_ref, dstep_ref, *refs):
    e_ref, all_ref, step_grad_ref = refs[-3:]
    outs = refs[:-3]
    e_ref[...] = jnp.zeros_like(e_ref)
    d_states = []
    for block in range(blocks):
        at = slice(block * Q, (block + 1) * Q)
        d_states.append(jnp.concatenate([dbin_ref[at] + dbx_ref[at], dcin_ref[at] + dcx_ref[at]], 1))

    def slope_of(block):
        pre = spre_ref[pl.ds(block * Q, Q), :]
        return d_states[block] * silu_slope(pre, jax.nn.sigmoid(pre))

    def store(begin, count, value):
        dstate_ref[pl.ds(begin, count), :] = value

    sgrad = conv_back(s_ref, blocks, e_ref, staps_ref[...], lambda at: raw_ref[pl.ds(at, Q), :], slope_of, store)
    heads = hp_ref.shape[0]
    total = lasts_ref.shape[1]
    depth = hp_ref.shape[1] - LANES
    spots = head_lanes((heads, total), True, head_size).astype(F32)
    lasts = mm(spots, lasts_ref[...], 1, 1, precision=HIGHEST)
    skips = mm(spots, rows_ref[...], 1, 1, precision=HIGHEST)[:, 1:2]
    rate = -jnp.exp(hp_ref[:, depth + 1 : depth + 2])
    lane = lax.broadcasted_iota(jnp.int32, (heads, Q), 1)
    upto = (
        lax.broadcasted_iota(jnp.int32, (Q, Q), 0) >= lax.broadcasted_iota(jnp.int32, (Q, Q), 1)
    ).astype(F32)
    grad_bias = jnp.zeros((heads, 1), F32)
    grad_decay = jnp.zeros((heads, 1), F32)
    for block in range(blocks):
        at = slice(block * Q, (block + 1) * Q)
        cols = part_a[:, at] + part_b[:, at]
        d_log = rowpart_ref[:, at] - cols + jnp.where(lane == Q - 1, lasts[:, block : block + 1], 0.0)
        d_move = mm(d_log, upto, precision=HIGHEST)
        d_raw = cols * ratio_ref[:, at] + rate * d_move * sig_ref[:, at]
        grad_bias += jnp.sum(d_raw, axis=1, keepdims=True)
        grad_decay += rate * jnp.sum(step_ref[:, at] * d_move, axis=1, keepdims=True)
        dstep_ref[:, at] = d_raw.astype(BF16)
    wide_lane = lax.broadcasted_iota(jnp.int32, (heads, LANES), 1)
    per_head = jnp.where(
        wide_lane == 0, grad_bias, jnp.where(wide_lane == 1, grad_decay, jnp.where(wide_lane == 2, skips, 0.0))
    )
    step_grad_ref[...] = mm(dstep_ref[...], nx_ref[HALO:])
    all_ref[...] = jnp.zeros_like(all_ref)
    all_ref[0:depth] = mm(nt_ref[...], dstate_ref[HALO:]) + mm(nx_ref[0:HALO], dstate_ref[0:HALO], 0, 0)
    for index in range(K + 1):
        all_ref[depth + index : depth + index + 1] = sgrad[index]
    if not shares:
        outs[0][...] = all_ref[...]
        outs[1][...] = step_grad_ref[...]
        outs[2][...] = per_head
        return
    ways, share, wide = shares
    quarter = all_ref.shape[0] // ways
    work = outs[-1]
    for p in range(ways):
        span = slice(p * wide, (p + 1) * wide)
        some = slice(p * share, (p + 1) * share)
        work[...] = jnp.zeros_like(work)
        work[0 : K + 1] = vgrad_ref[0 : K + 1, span]
        work[K + 1 : K + 2] = rows_ref[0:1, span]
        for part in range(depth // wide):
            begin = 8 + part * share
            work[begin : begin + share] = step_grad_ref[some, part * wide : (part + 1) * wide]
        work[24 : 24 + share, 0:LANES] = per_head[some]
        owner = jnp.bitwise_xor(s_ref[0], p)
        work[32 : 32 + quarter, 0 : all_ref.shape[1]] = all_ref[pl.ds(pl.multiple_of(owner * quarter, 8), quarter)]
        outs[p % 2][p // 2] = work[...].astype(BF16)


def mixed_kernel(pieces, blocks, s_ref, hid_ref, ny_ref, *refs):
    outs_w, mixed_ref = refs[:pieces], refs[pieces]
    wide = outs_w[0].shape[0]
    for block in range(blocks):
        at = slice(block * Q, (block + 1) * Q)
        branch = mm(ny_ref[at, 0:wide], outs_w[0][...])
        for p in range(1, pieces):
            branch += mm(ny_ref[at, p * wide : (p + 1) * wide], outs_w[p][...])
        mixed_ref[at] = (hid_ref[at].astype(F32) + valid_of(s_ref, blocks, block) * branch).astype(BF16)


def final_kernel(pieces, blocks, mine, s_ref, hid_ref, halo_ref, cot_ref, gain_ref, dgate_ref, dinner_ref,
                 dstate_ref, dstep_ref, hp_ref, sproj_ref, *refs):
    both_in = refs[:pieces]
    grad_out, extra_ref, gain_out, grad_ref, sems, both, dgate_here, dinner_here, in_sems = refs[-9:]
    wide = both.shape[2] // 2
    depth = hid_ref.shape[1]
    own = pl.ds(mine[0] * Q, len(mine) * Q)
    waits = [
        pltpu.make_async_copy(dinner_ref.at[pl.ds(mine[0] * Q, len(mine) * Q + HALO)], dinner_here, in_sems.at[0]),
        pltpu.make_async_copy(dgate_ref.at[own], dgate_here, in_sems.at[1]),
    ]
    for copy in waits:
        copy.start()
    loads = [pltpu.make_async_copy(both_in[p], both.at[p], in_sems.at[2 + p]) for p in range(pieces)]
    for copy in loads:
        copy.start()
    gain = gain_ref[...]
    gain_sum = jnp.zeros((1, depth), F32)

    def finish(values_in, d_normed):
        h = values_in.astype(F32)
        scale = lax.rsqrt(jnp.mean(h * h, axis=1, keepdims=True) + EPSILON)
        weighted = gain * d_normed
        inner = jnp.mean(weighted * h, axis=1, keepdims=True)
        return scale * weighted - h * (scale * scale * scale * inner), jnp.sum(d_normed * h * scale, axis=0, keepdims=True)

    moves = []
    totals = [mm(dstate_ref[0:HALO], sproj_ref[...], 1, 1)]
    for block in mine:
        ext = slice(HALO + block * Q, HALO + (block + 1) * Q)
        part = mm(dstate_ref[ext], sproj_ref[...], 1, 1)
        totals.append(part + mm(dstep_ref[:, block * Q : (block + 1) * Q], hp_ref[:, 0:depth].astype(BF16), 0, 0))
    for copy in waits:
        copy.wait()
    for p in range(pieces):
        loads[p].wait()
        span = slice(p * wide, (p + 1) * wide)
        if mine[0] == 0:
            totals[0] += mm(dinner_here[0:HALO, span], both[p, :, wide:], 1, 1)
        for index in range(len(mine)):
            here = slice(index * Q, (index + 1) * Q)
            ext = slice(HALO + index * Q, HALO + (index + 1) * Q)
            totals[index + 1] += mm(dgate_here[here, span], both[p, :, :wide], 1, 1)
            totals[index + 1] += mm(dinner_here[ext, span], both[p, :, wide:], 1, 1)
    if mine[0] == 0:
        extra_ref[...], part = finish(halo_ref[...], totals[0])
        gain_sum += part
    else:
        extra_ref[...] = jnp.zeros_like(extra_ref)
    for index, block in enumerate(mine):
        at = slice(block * Q, (block + 1) * Q)
        here = slice(index * Q, (index + 1) * Q)
        d_hidden, part = finish(hid_ref[at], totals[index + 1].astype(BF16).astype(F32))
        gain_sum += part
        grad_ref[here] = cot_ref[at].astype(F32) + d_hidden
        moves.append(pltpu.make_async_copy(grad_ref.at[here], grad_out.at[at], sems.at[index]))
        moves[-1].start()
    gain_out[...] = jnp.zeros_like(gain_out)
    side = gain_out.shape[1]
    for index in range(depth // side):
        gain_out[index : index + 1] = gain_sum[:, index * side : (index + 1) * side]
    for copy in moves:
        copy.wait()


def gather_far(value, ahead):
    ways = lax.axis_size("head")
    pieces = {0: value}
    far = {0: after(value, ahead)}
    mask = 2
    while mask < ways:
        for p in list(far):
            far[p | mask] = swap(far[p], "head", mask)
        mask *= 2
    return [value] + [far[p] for p in range(2, ways, 2)]


def near_pair(value, ahead):
    return value, swap(after(value, ahead) if len(ahead) else value, "head", 1)


def swap(value, axis, mask):
    size = lax.axis_size(axis)
    return lax.ppermute(value, axis, [(i, i ^ mask) for i in range(size)])


def pick(value, index):
    return lax.dynamic_index_in_dim(value, index, 0, keepdims=False)


def half_of(value, mask):
    side = jnp.where((lax.axis_index("dp") & mask) != 0, 1, 0)
    parts = value.reshape(2, value.shape[0] // 2, value.shape[1])
    return pick(parts, side).astype(F32), pick(parts, 1 - side).astype(BF16)


def whole_dp(low):
    for bit in range(3, lax.axis_size("dp").bit_length() - 1):
        low = (low.astype(F32) + swap(low, "dp", 1 << bit).astype(F32)).astype(BF16)
    return low


def both_of(low, mask, other):
    upper = (lax.axis_index("dp") & mask) != 0
    return jnp.concatenate([jnp.where(upper, other, low), jnp.where(upper, low, other)], axis=0)


def after(value, *others):
    return lax.optimization_barrier((value, others))[0]


def gather_pieces(value, ahead=()):
    ways = lax.axis_size("head")
    pieces = {0: value, 1: swap(value, "head", 1)}
    far = {0: after(value, ahead) if ahead else value}
    mask = 2
    while mask < ways:
        for p in list(far):
            far[p | mask] = swap(far[p], "head", mask)
        mask *= 2
    for p in far:
        if p:
            pieces[p] = far[p]
            pieces[p | 1] = swap(far[p], "head", 1)
    return [pieces[p] for p in range(ways)]


def reduce_pieces(pieces):
    ways = len(pieces)
    mask = 1
    live = {p: v for p, v in enumerate(pieces)}
    order = [1 << b for b in range(ways.bit_length() - 1)]
    for mask in order:
        got = {p ^ mask: swap(live[p].astype(BF16), "head", mask) for p in live if p & mask}
        live = {p: live[p].astype(F32) + got[p].astype(F32) for p in live if not p & mask}
    return live[0]


def body(hidden, lengths, norm_gain, gate_proj, value_proj, state_proj, step_proj, value_taps, value_bias,
         state_taps, state_bias, step_bias, decay_log, skip_gain, out_gain, out_proj, cotangent):
    rows, depth = hidden.shape
    ways = lax.axis_size("head")
    me = lax.axis_index("head")
    blocks = rows // Q
    wide = gate_proj.shape[1]
    share = step_proj.shape[1]
    total = wide * ways
    heads = share * ways
    head_size = wide // share
    pairs = heads // 2
    side = state_proj.shape[1]
    state = side // 2
    padded = -(-heads // 32) * 32
    plain = wide % LANES == 0
    order = [1 << b for b in range(ways.bit_length() - 1)]
    scalars = jnp.concatenate(
        [jnp.stack([me, blocks * ways]).astype(jnp.int32), lengths[0], jnp.zeros((3,), jnp.int32)]
    )

    top = jnp.concatenate(
        [step_proj.T.astype(F32), step_bias[:, None], decay_log[:, None], skip_gain[:, None], jnp.zeros((share, LANES - 3), F32)],
        axis=1,
    )
    low = jnp.concatenate([value_taps, value_bias[None], out_gain[None]], axis=0)
    pack = jnp.concatenate(
        [
            jnp.pad(top, ((0, 8 - share), (0, 0))),
            jnp.pad(low, ((0, 2), (0, depth + LANES - wide))),
            jnp.pad(hidden[rows - HALO :].astype(F32), ((0, 0), (0, LANES))),
        ],
        axis=0,
    )
    packs = gather_pieces(pack)
    halo = jnp.zeros((HALO, depth), F32)
    for p in range(1, ways):
        halo = jnp.where((me ^ p) == me - 1, packs[p][16:, :depth], halo)
    halo = halo.astype(BF16)
    both = gather_far(jnp.concatenate([gate_proj, value_proj], axis=1), (packs[1],))
    outs = gather_far(out_proj, (packs, both[0]))

    def both_merged(pair):
        if plain:
            return list(pair)
        a, b = pair
        return [jnp.concatenate([a[:, :wide], b[:, :wide], a[:, wide:], b[:, wide:]], axis=1)]

    def outs_merged(pair):
        return list(pair) if plain else [jnp.concatenate(pair, axis=0)]

    pieces = ways if plain else ways // 2
    span = total // pieces
    tiles = span // LANES
    hp = jnp.pad(jnp.concatenate([p[:share] for p in packs], axis=0), ((0, padded - heads), (0, 0)))
    par = jnp.concatenate([p[8:16, :wide] for p in packs], axis=1)
    gain_in = norm_gain[None]
    staps = jnp.pad(jnp.concatenate([state_taps, state_bias[None]], axis=0), ((0, 3), (0, 0)))

    ext = rows + HALO
    (nx, nt, state_raw, state_pre, b_low, c_low, b_t, c_t, cb, cbt) = call(
        functools.partial(pre_kernel, blocks),
        [((ext, depth), BF16), ((depth, rows), BF16), ((ext, side), F32), ((rows, side), F32),
         ((rows, state), BF16), ((rows, state), BF16), ((state, rows), BF16), ((state, rows), BF16),
         ((blocks, Q, Q), F32), ((blocks, Q, Q), F32)],
        [scalars, hidden, halo, gain_in, state_proj, staps],
        cost=2, mib=PRE,
    )
    rowp, colp, step, ratio, sig, chan = call(
        functools.partial(step_kernel, blocks, head_size),
        [((pairs, 8, rows), F32), ((pairs // 2, rows, 16), F32), ((padded, rows), F32), ((padded, rows), F32),
         ((padded, rows), F32), ((8, total), F32)],
        [scalars, nx, hp],
        cost=2,
        mib=PRE,
    )
    vmem = pltpu.VMEM
    hbm = pl.BlockSpec(memory_space=pltpu.HBM)
    front_outs = [((rows, total), BF16), ((ext, total), BF16), ((rows, total), BF16), ((blocks, state, total), F32),
                  ((rows, total), BF16), ((state + HALO, total), BF16), ((state + HALO, total), BF16)]
    fronts, all_both = [], []
    half = pieces // 2
    for begin in (0, half):
        pairs_of = range(begin // 2, begin // 2 + ways // 4) if plain else range(begin, begin + half)
        weights = [w for at in pairs_of for w in both_merged(near_pair(both[at], fronts))]
        all_both += weights
        args = [scalars, nx, par, b_t, colp, chan, *weights]
        aliases = {len(args) + at: at for at in range(len(fronts))}
        fronts = call(
            functools.partial(front_kernel, blocks, begin, half), front_outs, [*args, *fronts], aliases=aliases,
            ins={len(args) + at: hbm for at in range(min(4, len(fronts)))}, out_specs={at: hbm for at in range(4)},
            kinds={at: pltpu.HBM for at in range(4)},
            scratch=[vmem((rows, half * span), BF16), vmem((ext, half * span), BF16), vmem((rows, half * span), BF16),
                     vmem((blocks, state, half * span), F32), vmem((ext, half * span), F32), pltpu.SemaphoreType.DMA((4,))],
            cost=6, mib=FRONT,
        )
    gate, inner, pre, st, x, carry, carry_turned = fronts

    def turned(value, mask):
        parts = [value[..., (p ^ mask) * wide : ((p ^ mask) + 1) * wide] for p in range(ways)]
        return jnp.concatenate(parts, axis=-1)

    def scan(own, own_turned, forward, beside=lambda run: ()):
        def fade_of(value):
            return value[state : state + 1].astype(F32) + value[state + 1 : state + 2].astype(F32)

        if plain and ways == 4:
            near = swap(own_turned, "head", 1)
            (run,) = call(functools.partial(join_kernel, forward), [(own.shape, BF16)], [scalars, own, near], mib=8)
            far = swap(run, "head", 2)
            between = beside(run)
            far = after(far, between[1]) if between else far
            (result,) = call(functools.partial(arrive_kernel, forward), [((state, total), F32)], [scalars, near, far], mib=8)
            return result, between
        before = before_fade = None
        run = own
        for mask in order:
            if mask == 1 and plain:
                got = swap(own_turned, "head", 1)
            else:
                got = turned(swap(run, "head", mask), mask)
            got_fade, run_fade = fade_of(got), fade_of(run)
            got, mine = got[:state].astype(F32), run[:state].astype(F32)
            later = ((me & mask) != 0) if forward else ((me & mask) == 0)
            if before is None:
                before = jnp.where(later, got, 0.0)
                before_fade = jnp.where(later, got_fade, 1.0)
            else:
                before = jnp.where(later, before_fade * got + before, before)
                before_fade = jnp.where(later, before_fade * got_fade, before_fade)
            if mask != order[-1]:
                both_maps = jnp.where(later, run_fade * got + mine, got_fade * mine + got)
                fades = run_fade * got_fade
                high = fades.astype(BF16)
                low_part = (fades - high.astype(F32)).astype(BF16)
                run = jnp.concatenate(
                    [both_maps.astype(BF16), high, low_part, jnp.zeros((HALO - 2, total), BF16)], axis=0
                )
        return before, beside(run)

    def within(run):
        (y_intra,) = call(
            functools.partial(intra_kernel, blocks),
            [((rows, total), F32)],
            [scalars, rowp, colp, cb, after(x, run)],
            cost=5,
            mib=INTRA,
        )
        all_outs = [w for value in outs for w in outs_merged(near_pair(value, run))]
        dny, dbt = call(
            functools.partial(masked_kernel, blocks, pieces),
            [((rows, total), BF16), ((depth, rows), BF16)],
            [scalars, cotangent, *all_outs],
            scratch=[vmem((rows, depth), BF16)],
            cost=3,
            mib=INTRA,
        )
        return y_intra, dny, dbt, all_outs

    inc_in, (y_intra, dny, dbt, all_outs) = scan(carry, carry_turned, True, within)
    wide_bf = vmem((rows, total), BF16)
    held_outs = [((rows, total), BF16), ((rows, total), BF16),
                 ((pieces // 2, 2 * depth, span), BF16), ((pieces // 2, 2 * depth, span), BF16),
                 ((blocks, state, total), BF16), ((blocks, state, total), BF16), ((rows, state), F32),
                 ((padded, rows), F32), ((8, total), F32)]
    (ny, d_gate, a_keep, a_send, inc, d_inc, dc_inter, rowpart, rows_sum, d_y, back_carry, back_turned) = call(
        functools.partial(middle_kernel, blocks, tiles, head_size),
        [*held_outs, ((rows, total), BF16), ((state + HALO, total), BF16), ((state + HALO, total), BF16)],
        [scalars, dbt, inc_in, colp, chan, par, c_low, c_t, nt, y_intra, dny, gate, x, st],
        out_specs={at: hbm for at in range(len(held_outs))}, kinds={at: pltpu.HBM for at in range(len(held_outs))},
        scratch=[*[vmem(*o) for at, o in enumerate(held_outs) if at not in (2, 3)], vmem((2, 2 * depth, 2 * LANES), BF16), vmem((rows, total), F32), vmem((rows, LANES), F32),
                 vmem((rows, LANES), F32), wide_bf, wide_bf, pltpu.SemaphoreType.DMA((len(held_outs) - 2,)),
                 pltpu.SemaphoreType.DMA((2, 2))],
        cost=14, mib=MIDDLE,
    )
    back_runs = []
    back_in, _ = scan(back_carry, back_turned, False, lambda run: back_runs.append(run))

    def over_head(keep, send):
        if not plain:
            parts = [None] * ways
            for m in range(pieces):
                merged = (keep, send)[m % 2][m // 2]
                parts[2 * m], parts[2 * m + 1] = merged[:, :wide], merged[:, wide:]
            return reduce_pieces(parts)
        got = swap(send, "head", 1)
        live = [keep[i].astype(F32) + got[i].astype(F32) for i in range(pieces // 2)]
        return live

    def finish_head(live):
        if not plain:
            return live
        return live[0] + swap(live[1].astype(BF16), "head", 2).astype(F32)

    def halve(value, axis_at=0):
        side = lax.axis_index("dp") & 1
        cut = value.shape[:axis_at] + (2, value.shape[axis_at] // 2) + value.shape[axis_at + 1 :]
        parts = jnp.moveaxis(value.reshape(cut), axis_at, 0)
        got = swap(pick(parts, 1 - side).astype(BF16), "dp", 1)
        return pick(parts, side).astype(F32) + got.astype(F32)

    a_live = over_head(a_keep, after(a_send, *back_runs))
    if plain:
        a_out = finish_head([v[:depth] for v in a_live])
        a_gate = halve(jnp.stack([v[depth:] for v in a_live]), 1)
        gates = (a_out, a_gate)
    else:
        gates = a_live
    dx, part_a, db_in, dc_in = call(
        functools.partial(back_kernel, blocks, head_size),
        [((rows, total), BF16), ((padded, rows), F32), ((rows, state), F32), ((rows, state), F32)],
        [scalars, rowp, colp, cbt, b_low, c_low, d_y, x],
        scratch=[vmem((blocks, Q, Q), F32), wide_bf, wide_bf],
        cost=8,
        mib=BACK,
    )
    (d_inner, vgrad, part_b, lasts, db_x, b_keep, b_send) = call(
        functools.partial(tail_kernel, blocks, tiles, head_size),
        [((ext, total), BF16), ((8, total), F32), ((padded, rows), F32), ((8, total), F32), ((rows, state), F32),
         ((pieces // 2, depth, span), BF16), ((pieces // 2, depth, span), BF16)],
        [scalars, after(back_in, a_live), colp, chan, par, b_low, nt, nx, inc, dx, d_y, d_inc, x, pre, inner],
        out_specs={5: hbm, 6: hbm}, kinds={5: pltpu.HBM, 6: pltpu.HBM},
        scratch=[vmem((2, K, rows + 2 * HALO, LANES), F32), vmem((2, ext, LANES), F32), wide_bf, wide_bf,
                 vmem((2, depth, 2 * LANES), BF16), pltpu.SemaphoreType.DMA((2, 2))],
        cost=10, mib=TAIL,
    )
    small_rows, all_rows = 256, 832
    if plain:
        small_outs = [((pieces // 2, small_rows, span), BF16)] * 2
        shares = (ways, share, wide)
        work = [vmem((small_rows, span), F32)]
    else:
        small_outs = [((all_rows, side), F32), ((padded, depth), F32), ((padded, LANES), F32)]
        shares = None
        work = []
    d_state, d_step, *smalls = call(
        functools.partial(state_kernel, blocks, head_size, shares),
        [((ext, side), BF16), ((padded, rows), BF16)] + small_outs,
        [scalars, after(db_x, gates), db_in, dc_in, dc_inter, state_raw, state_pre, staps, rowpart, part_a, part_b, step, ratio, sig, hp,
         rows_sum, lasts, vgrad, nt, nx],
        scratch=work + [vmem((K, rows + 2 * HALO, side), F32), vmem((all_rows, side), F32), vmem((padded, depth), F32)],
        cost=4, mib=STATE,
    )
    share_rows = all_rows // ways
    if not plain:
        all_grad, step_grad, per_head = smalls
        parts = []
        for p in range(ways):
            cols, some = slice(p * wide, (p + 1) * wide), slice(p * share, (p + 1) * share)
            flat = step_grad[some].reshape(share, depth // wide, wide).swapaxes(0, 1).reshape(-1, wide)
            own = lax.dynamic_slice_in_dim(all_grad, (me ^ p) * share_rows, share_rows, 0).reshape(-1)
            count = -(-own.shape[0] // wide)
            own = jnp.pad(own, (0, count * wide - own.shape[0])).reshape(count, wide)
            part = jnp.concatenate(
                [vgrad[0:5, cols], rows_sum[0:1, cols], jnp.zeros((2, wide), F32), flat, jnp.zeros((16 - flat.shape[0], wide), F32),
                 jnp.pad(per_head[some], ((0, 8 - share), (0, wide - LANES))), own], axis=0)
            parts.append(jnp.pad(part, ((0, small_rows - part.shape[0]), (0, 0))))
        c_live = reduce_pieces(parts)
    else:
        c_live = over_head(smalls[0], smalls[1])
    b_live = over_head(b_keep, after(b_send, gates))
    if plain:
        a_part = jnp.concatenate([halve(a_out), finish_head([a_gate[0], a_gate[1]])], axis=0)
    else:
        a_part = halve(a_live)
    a_keep_z, a_send_z = half_of(a_part, 2)
    if plain:
        b_whole = [jnp.concatenate([b, c], axis=0) for b, c in zip(b_live, c_live)]
        cut = b_whole[0].shape[0] // 2
        side_x = lax.axis_index("dp") & 1
        low, high = [v[:cut] for v in b_whole], jnp.stack([v[cut:] for v in b_whole])
        high = jnp.moveaxis(high.reshape(2, 2, cut // 2, wide), 1, 0)
        b_sends = low[1].astype(BF16), pick(high, 1 - side_x).astype(BF16)
    else:
        b_sends = ()
    a_got_z = swap(after(a_send_z, b_sends), "dp", 2)
    if plain:
        b_got = swap(b_sends[0], "head", 2), swap(b_sends[1], "dp", 1)
    mine = list(range(blocks))
    args = [scalars, hidden, halo, cotangent, gain_in, after(d_gate, b_sends, a_send_z), d_inner, d_state, d_step, hp, state_proj,
            *all_both]
    results = call(
        functools.partial(final_kernel, pieces, blocks, mine),
        [((rows, depth), F32), ((HALO, depth), F32), ((8, span), F32)],
        args,
        ins={at: hbm for at in (5, 6, *range(len(args) - pieces, len(args)))},
        out_specs={0: hbm},
        kinds={0: pltpu.HBM},
        scratch=[vmem((rows, depth), F32), pltpu.SemaphoreType.DMA((blocks,)), vmem((pieces, depth, 2 * span), BF16),
                 vmem((rows, total), BF16), vmem((ext, total), BF16), pltpu.SemaphoreType.DMA((2 + pieces,))],
        cost=9,
        mib=FINAL,
    )
    grad_hidden, extra, gain_part = results
    extra = lax.ppermute(extra, "head", [(i + 1, i) for i in range(ways - 1)])
    grad_hidden = grad_hidden.at[rows - HALO :].add(extra)
    if plain:
        one = low[0] + after(b_got[0], results).astype(F32)
        two = pick(high, side_x) + after(b_got[1], results).astype(F32)
        one_keep, one_send = half_of(one, 1)
        b_sends = one_send, two[1].astype(BF16)
        b_part = [one_keep + swap(one_send, "dp", 1).astype(F32), two[0] + swap(b_sends[1], "head", 2).astype(F32)]
        b_part = jnp.concatenate(b_part, axis=0)
    else:
        b_part = halve(jnp.concatenate([b_live, c_live], axis=0))
    gain_rows = gain_part[: depth // span].reshape(depth // wide, wide)
    b_part = jnp.concatenate([b_part, gain_rows, jnp.zeros((32 - gain_rows.shape[0], wide), F32)], axis=0)
    a_low = (a_keep_z + after(a_got_z, results).astype(F32)).astype(BF16)
    a_got_y = swap(a_low, "dp", 4)
    a_low = whole_dp((a_low.astype(F32) + after(a_got_y, b_sends).astype(F32)).astype(BF16))
    b_keep_z, b_send_z = half_of(b_part, 2)
    b_got_z = swap(after(b_send_z, a_low), "dp", 2)
    a_got_z = swap(a_low, "dp", 2)
    (mixed,) = call(
        functools.partial(mixed_kernel, pieces, blocks),
        [((rows, depth), BF16)],
        [scalars, hidden, after(ny, a_low, b_send_z), *all_outs],
        pin=jax.ShapeDtypeStruct,
        cost=4,
        mib=FINAL,
    )
    b_low = (b_keep_z + after(b_got_z, a_low, mixed).astype(F32)).astype(BF16)
    b_got_y = swap(b_low, "dp", 4)
    a_all = both_of(a_low, 2, a_got_z)
    a_other = swap(a_all, "dp", 1)
    b_low = whole_dp((b_low.astype(F32) + after(b_got_y, a_all).astype(F32)).astype(BF16))
    b_all = both_of(b_low, 2, swap(b_low, "dp", 2))

    def unhalve(value, cuts, other=None):
        upper = (lax.axis_index("dp") & 1) != 0
        other = swap(value, "dp", 1) if other is None else other
        rows_out, begin = [], 0
        for count in cuts:
            mine, his = value[begin : begin + count], other[begin : begin + count]
            rows_out.append(jnp.concatenate([jnp.where(upper, his, mine), jnp.where(upper, mine, his)], axis=0))
            begin += count
        return rows_out

    b_all = after(b_all, a_other)
    a_cuts = [depth // 2, depth // 2] if plain else [depth]
    a_out, a_gate = unhalve(a_all, a_cuts, a_other) if plain else jnp.split(unhalve(a_all, a_cuts, a_other)[0], 2)
    grad_out = a_out.T.astype(F32)
    grad_gate = a_gate.astype(F32)
    cut = b_all.shape[0] - 32 - 256
    *b_rows, gain_all = unhalve(b_all[cut:], [256, 32])
    b_rows = unhalve(b_all[:cut], [cut]) + b_rows
    if not plain:
        *b_rows, gain_all = unhalve(b_all, [cut + 256, 32])
    b_all = jnp.concatenate(b_rows, axis=0)
    gain_all = (gain_all[:32].astype(F32) + gain_all[32:].astype(F32))[: depth // wide].reshape(1, depth)
    gain_all = jnp.pad(gain_all.reshape(-1, side), ((0, 16 - depth // side), (0, 0)))
    grad_value = b_all[:depth].astype(F32)
    small = b_all[depth:].astype(F32)
    grad_step = jnp.concatenate([small[8 + j * share : 8 + (j + 1) * share].T for j in range(depth // wide)], axis=0)
    if plain:
        own = b_all[depth + 32 : depth + 32 + share_rows, :side]
    else:
        own = b_all[depth + 32 : depth + 240].reshape(-1)[: share_rows * side].reshape(share_rows, side)
    smaller = (grad_value, grad_step, small[0:4], small[4], small[5], *[small[24 : 24 + share, at] for at in range(3)])
    stacked, members = own, [0]
    for mask in reversed(order):
        members += [p | mask for p in members]
        gain_low = gain_all.astype(BF16)
        sent = jnp.concatenate([stacked, gain_low], axis=0)
        got = swap(after(sent, smaller if mask == 1 else (grad_out, grad_gate, grad_hidden)), "head", mask)
        stacked = jnp.concatenate([stacked, got[: stacked.shape[0]]], axis=0)
        gain_all = gain_low.astype(F32) + got[-16:].astype(F32)
    stacked = stacked.reshape(ways, share_rows, side)
    stacked = jnp.stack([stacked[members.index(p)] for p in range(ways)])
    full = jnp.concatenate([pick(stacked, me ^ q) for q in range(ways)], axis=0).astype(F32)
    return (
        mixed,
        grad_hidden,
        gain_all[: depth // side].reshape(-1),
        grad_gate,
        smaller[0],
        full[:depth],
        smaller[1],
        smaller[2],
        smaller[3],
        full[depth : depth + 4],
        full[depth + 4],
        smaller[5],
        smaller[6],
        smaller[7],
        smaller[4],
        grad_out,
    )


def solution(mesh):
    rows = P(("dp", "head"), None)
    in_specs = (
        rows, P("dp", None), P(), P(None, "head"), P(None, "head"), P(), P(None, "head"), P(None, "head"),
        P("head"), P(), P(), P("head"), P("head"), P("head"), P("head"), P("head", None), rows,
    )
    out_specs = (
        rows, rows, P(), P(None, "head"), P(None, "head"), P(), P(None, "head"), P(None, "head"),
        P("head"), P(), P(), P("head"), P("head"), P("head"), P("head"), P("head", None),
    )
    return jax.shard_map(body, mesh=mesh, in_specs=in_specs, out_specs=out_specs, check_vma=False)
```

```python
import functools

import jax
import jax.numpy as jnp
from jax import lax
from jax.experimental import pallas as pl
from jax.experimental.pallas import tpu as pltpu
from jax.sharding import PartitionSpec as P

K = 4
Q = 256
HALO = 16
LANES = 128
EPSILON = 1e-05
F32 = jnp.float32
BF16 = jnp.bfloat16
HIGHEST = lax.Precision.HIGHEST


def mm(left, right, lc=1, rc=0, precision=None):
    return lax.dot_general(
        left,
        right,
        (((lc,), (rc,)), ((), ())),
        preferred_element_type=F32,
        precision=precision,
    )


MIB = 1024 * 1024
PRE, FRONT, INTRA, MIDDLE, BACK, TAIL, STATE, FINAL = 12, 14, 12, 18, 56, 14, 12, 56


def whole(shape):
    return pl.BlockSpec(shape, lambda *_: (0,) * len(shape))


def call(kernel, outs, args, scratch=(), grid=(), ins=None, out_specs=None, aliases=None, mib=48, cost=0, pin=pltpu.VMEM, kinds=None):
    ins, out_specs, kinds = ins or {}, out_specs or {}, kinds or {}
    specs = [pl.BlockSpec(memory_space=pltpu.SMEM)]
    for at, value in enumerate(args[1:], 1):
        specs.append(ins[at] if at in ins else whole(value.shape))
    outs_specs = [out_specs[at] if at in out_specs else whole(o[0]) for at, o in enumerate(outs)]
    return pl.pallas_call(
        kernel,
        grid=grid,
        out_shape=[kinds[at](s, d) if at in kinds else pin(s, d) for at, (s, d) in enumerate(outs)],
        in_specs=specs,
        out_specs=outs_specs,
        scratch_shapes=list(scratch),
        input_output_aliases=aliases or {},
        compiler_params=pltpu.CompilerParams(vmem_limit_bytes=mib * MIB),
        cost_estimate=pl.CostEstimate(flops=int(cost * 4e8), bytes_accessed=int(cost * 3e5), transcendentals=0),
    )(*args)


def keeps_of(s_ref, block, blocks):
    place = s_ref[0] * blocks + block
    fresh = (place == 0) | (place == 1) | (place == s_ref[1] - 1)
    return fresh, jnp.where(fresh, 0.0, 1.0).astype(F32)


def row_keep(fresh, distance):
    rows = lax.broadcasted_iota(jnp.int32, (Q, 1), 0)
    return (rows >= jnp.where(fresh, distance, 0)).astype(F32)


def conv_block(ref, base, cols, taps, fresh):
    total = taps[K : K + 1] + taps[K - 1 : K] * ref[pl.ds(base, Q), cols]
    for distance in range(1, K):
        earlier = ref[pl.ds(base - distance, Q), cols]
        total = total + taps[K - 1 - distance : K - distance] * (earlier * row_keep(fresh, distance))
    return total


def silu_slope(values, sig):
    return sig * (1.0 + values * (1.0 - sig))


def first_lanes():
    return lax.broadcasted_iota(jnp.int32, (1, LANES), 1) < LANES // 2


def spread(cols, quantity):
    return jnp.where(
        first_lanes(), cols[:, 2 * quantity : 2 * quantity + 1], cols[:, 2 * quantity + 1 : 2 * quantity + 2]
    )


def head_lanes(rows, heads_first, head_size):
    lane = lax.broadcasted_iota(jnp.int32, rows, 1 if heads_first else 0)
    head = lax.broadcasted_iota(jnp.int32, rows, 0 if heads_first else 1)
    return (lane >= head * head_size) & (lane < (head + 1) * head_size)


def pre_kernel(blocks, s_ref, hid_ref, halo_ref, gain_ref, proj_ref, taps_ref,
               nx_ref, nt_ref, raw_ref, pre_ref, b_ref, c_ref, bt_ref, ct_ref, cb_ref, cbt_ref):
    gain = gain_ref[...]
    rows = blocks * Q

    def norm(v):
        v = v.astype(F32)
        return v * lax.rsqrt(jnp.mean(v * v, axis=1, keepdims=True) + EPSILON) * gain

    halo = norm(halo_ref[...])
    own = norm(hid_ref[...])
    nx_ref[0:HALO] = halo.astype(BF16)
    nx_ref[HALO:] = own.astype(BF16)
    nt_ref[:, 0:rows] = own.T.astype(BF16)
    raw_ref[...] = mm(nx_ref[...], proj_ref[...])
    taps = taps_ref[...]
    state = b_ref.shape[1]
    for block in range(blocks):
        fresh, _ = keeps_of(s_ref, block, blocks)
        pre = conv_block(raw_ref, HALO + block * Q, slice(None), taps, fresh)
        at = pl.ds(block * Q, Q)
        pre_ref[at] = pre
        conv = pre * jax.nn.sigmoid(pre)
        b_mat = conv[:, :state]
        c_mat = conv[:, state:]
        b_low = b_mat.astype(BF16)
        c_low = c_mat.astype(BF16)
        b_ref[at] = b_low
        c_ref[at] = c_low
        bt_ref[:, at] = b_mat.T.astype(BF16)
        ct_ref[:, at] = c_mat.T.astype(BF16)
        cb_ref[block] = mm(c_low, b_low, 1, 1)
        cbt_ref[block] = mm(b_low, c_low, 1, 1)


def step_kernel(blocks, head_size, s_ref, nx_ref, hp_ref, rowp_ref, colp_ref, step_ref, ratio_ref, sig_ref, chan_ref):
    depth = nx_ref.shape[1]
    hp = hp_ref[...]
    u = mm(hp[:, :depth].astype(BF16), nx_ref[HALO:], 1, 1) + hp[:, depth : depth + 1]
    step = jnp.maximum(u, 0.0) + jnp.log1p(jnp.exp(-jnp.abs(u)))
    sig = jax.nn.sigmoid(u)
    step_ref[...] = step
    sig_ref[...] = sig
    ratio_ref[...] = jnp.where(step > 1e-30, sig / jnp.maximum(step, 1e-30), 1.0)
    rate = -jnp.exp(hp[:, depth + 1 : depth + 2])
    move = step * rate
    upto = (
        lax.broadcasted_iota(jnp.int32, (Q, Q), 0) <= lax.broadcasted_iota(jnp.int32, (Q, Q), 1)
    ).astype(F32)
    heads = hp.shape[0]
    lane = lax.broadcasted_iota(jnp.int32, (heads, LANES), 1)
    last_cols = jnp.zeros((heads, LANES), F32)
    lstep = jnp.log(step)
    product = jnp.ones((heads, 1), F32)
    pairs = rowp_ref.shape[0]
    for block in range(blocks):
        at = slice(block * Q, (block + 1) * Q)
        logd = mm(move[:, at], upto, precision=HIGHEST)
        less = logd - lstep[:, at]
        last = logd[:, Q - 1 : Q]
        grown = jnp.exp(logd)
        carry = jnp.exp(last - less)
        final = jnp.exp(last)
        _, kept = keeps_of(s_ref, block, blocks)
        product = product * final * kept
        last_cols = jnp.where(lane == block, final, last_cols)
        for pair in range(pairs):
            for index, values in enumerate((logd, less, grown, carry)):
                rowp_ref[pair, 2 * index : 2 * index + 2, at] = values[2 * pair : 2 * pair + 2]
    last_cols = jnp.where(lane == 6, product, last_cols)
    last_cols = jnp.where(lane == 7, hp[:, depth + 2 : depth + 3], last_cols)
    spots = head_lanes((heads, chan_ref.shape[1]), True, head_size).astype(F32)
    chan_ref[...] = mm(last_cols.T[0:8], spots, precision=HIGHEST)
    for pair in range(0, pairs, 2):
        colp_ref[pair // 2] = jnp.concatenate([rowp_ref[pair], rowp_ref[pair + 1]], 0).T


def carry_block(ref, cols, carry, fades):
    state = carry.shape[0]
    ref[0:state, cols] = carry.astype(BF16)
    high = fades.astype(BF16).astype(F32)
    row = lax.broadcasted_iota(jnp.int32, (HALO, LANES), 0)
    ref[state:, cols] = jnp.where(row == 0, high, jnp.where(row == 1, fades - high, 0.0)).astype(BF16)


def tile_at(index):
    return pl.ds(pl.multiple_of(index * LANES, LANES), LANES)


def front_kernel(blocks, first_piece, pieces, s_ref, nx_ref, par_ref, bt_ref, colp_ref, chan_ref, *refs):
    weights = refs[:pieces]
    (gate_out, inner_out, pre_out, s_out, x_ref, carry_ref, turned_ref,
     gate_ref, inner_ref, pre_ref, st_ref, work, sems) = refs[-13:]
    done = refs[pieces:-13]
    wide = weights[0].shape[1] // 2
    for old, new in zip(done[4:], (x_ref, carry_ref, turned_ref)):
        new[:, 0 : first_piece * wide] = old[:, 0 : first_piece * wide]
    own = slice(first_piece * wide, (first_piece + pieces) * wide)
    moves = [(gate_ref, gate_out), (inner_ref, inner_out), (pre_ref, pre_out), (st_ref, s_out)]
    for p in range(pieces):
        here = slice(p * wide, (p + 1) * wide)
        work[:, here] = mm(nx_ref[...], weights[p][:, wide:])
        gate_ref[:, here] = mm(nx_ref[HALO:], weights[p][:, :wide]).astype(BF16)
    tiles = wide // LANES

    def tile(i, cols_of):
        here = tile_at(i)
        pair = i + first_piece * tiles
        far = tile_at(pair)
        turned = tile_at(jnp.bitwise_xor(pair // tiles, 1) * tiles + pair % tiles)
        taps = par_ref[:, far]
        inner_ref[:, here] = work[:, here].astype(BF16)
        for block in range(blocks):
            at = pl.ds(block * Q, Q)
            fresh, kept = keeps_of(s_ref, block, blocks)
            pre = conv_block(work, HALO + block * Q, here, taps, fresh)
            pre_ref[at, here] = pre.astype(BF16)
            x = pre * jax.nn.sigmoid(pre)
            x_ref[at, far] = x.astype(BF16)
            weighted = (spread(cols_of(at), 3) * x).astype(BF16)
            state = mm(bt_ref[:, at], weighted)
            st_ref[block, :, here] = state
            if block == 0:
                carry = state
            else:
                carry = chan_ref[block : block + 1, far] * (kept * carry) + state
        carry_block(carry_ref, far, carry, chan_ref[6:7, far])
        carry_block(turned_ref, turned, carry, chan_ref[6:7, far])
        for index, (held, out) in enumerate(moves):
            pltpu.make_async_copy(held.at[..., here], out.at[..., far], sems.at[index]).start()

    def turn(i, none):
        for k in range(2):
            tile(2 * i + k, lambda at, k=k: colp_ref[i + first_piece * tiles // 2, at, 8 * k : 8 * k + 8])
        return none

    lax.fori_loop(0, pieces * tiles // 2, turn, 0)
    for index, (held, out) in enumerate(moves):
        pltpu.make_async_copy(held, out.at[..., own], sems.at[index]).wait()


def unpack_carry(ref):
    state = ref.shape[0] - HALO
    fades = ref[state:].astype(F32)
    return ref[0:state].astype(F32), fades[0:1] + fades[1:2]


def join_kernel(forward, s_ref, own_ref, got_ref, out_ref):
    mine, my_fade = unpack_carry(own_ref)
    his, his_fade = unpack_carry(got_ref)
    later = (jnp.bitwise_and(s_ref[0], 1) == 1) == forward
    state = mine.shape[0]
    total = jnp.where(later, my_fade * his + mine, his_fade * mine + his)
    fade = my_fade * his_fade
    high = fade.astype(BF16).astype(F32)
    row = lax.broadcasted_iota(jnp.int32, (HALO, total.shape[1]), 0)
    out_ref[0:state] = total.astype(BF16)
    out_ref[state:] = jnp.where(row == 0, high, jnp.where(row == 1, fade - high, 0.0)).astype(BF16)


def arrive_kernel(forward, s_ref, near_ref, far_ref, out_ref):
    near, near_fade = unpack_carry(near_ref)
    wide = near.shape[1] // 2
    later = (jnp.bitwise_and(s_ref[0], 1) == 1) == forward
    far_later = (jnp.bitwise_and(s_ref[0], 2) == 2) == forward
    near = jnp.where(later, near, 0.0)
    fade = jnp.where(far_later, jnp.where(later, near_fade, 1.0), 0.0)
    for half in range(2):
        here, there = slice(half * wide, (half + 1) * wide), slice((1 - half) * wide, (2 - half) * wide)
        out_ref[:, here] = near[:, here] + fade[:, here] * far_ref[0 : near.shape[0], there].astype(F32)


def masked_cotangent(s_ref, cot_ref, blocks, block):
    at = slice(block * Q, (block + 1) * Q)
    return cot_ref[at].astype(F32) * valid_of(s_ref, blocks, block)


def masked_kernel(blocks, pieces, s_ref, cot_ref, *refs):
    outs_w = refs[:pieces]
    dny_ref, dbt_ref, db_ref = refs[pieces:]
    for block in range(blocks):
        at = slice(block * Q, (block + 1) * Q)
        masked = masked_cotangent(s_ref, cot_ref, blocks, block)
        db_ref[at] = masked.astype(BF16)
        dbt_ref[:, at] = masked.T.astype(BF16)
    wide = outs_w[0].shape[0]
    for p in range(pieces):
        dny_ref[:, p * wide : (p + 1) * wide] = mm(db_ref[...], outs_w[p][...], 1, 1).astype(BF16)


def intra_kernel(blocks, s_ref, rowp_ref, colp_ref, cb_ref, x_ref, y_ref):
    half = Q // 2
    first = first_lanes()
    tri = lax.broadcasted_iota(jnp.int32, (half, half), 0) >= lax.broadcasted_iota(
        jnp.int32, (half, half), 1
    )

    def work(i, k):
        pair = 2 * i + k
        far = tile_at(pair)
        for block in range(blocks):
            at = pl.ds(block * Q, Q)
            x = x_ref[at, far]
            both = [jnp.where(first, x, 0), jnp.where(first, 0, x)]
            rp = rowp_ref[pair, :, at]
            cp = colp_ref[i, at, 8 * k : 8 * k + 8]
            tops, bots = [], []
            for h in range(2):
                ld, ls = cp[:, h : h + 1], rp[2 + h : 3 + h, :]
                arg = jnp.where(tri, ld[:half] - ls[:, :half], -1e30)
                tops.append((cb_ref[block, 0:half, 0:half] * jnp.exp(arg)).astype(BF16))
                arg = ld[half:] - ls[:, :half]
                bots.append((cb_ref[block, half:, 0:half] * jnp.exp(arg)).astype(BF16))
                arg = jnp.where(tri, ld[half:] - ls[:, half:], -1e30)
                bots.append((cb_ref[block, half:, half:] * jnp.exp(arg)).astype(BF16))
            y_ref[pl.ds(block * Q, half), far] = mm(jnp.concatenate(tops, 1), jnp.concatenate([b[:half] for b in both], 0))
            y_ref[pl.ds(block * Q + half, half), far] = mm(jnp.concatenate(bots, 1), jnp.concatenate(both, 0))

    def two(i, none):
        work(i, 0)
        work(i, 1)
        return none

    lax.fori_loop(0, x_ref.shape[1] // (2 * LANES), two, 0)


def split_store(hi_ref, lo_ref, at, cols, part):
    high = part.astype(BF16)
    hi_ref[at, cols] = high
    lo_ref[at, cols] = (part - high.astype(F32)).astype(BF16)


def head_sums(heads, head_size, hi_ref, lo_ref):
    spots = head_lanes((heads, hi_ref.shape[1]), True, head_size).astype(F32).astype(BF16)
    return mm(spots, hi_ref[...], 1, 1) + mm(spots, lo_ref[...], 1, 1)


def valid_of(s_ref, blocks, block):
    place = s_ref[0] * blocks + block
    last = place == s_ref[1] - 1
    length = jnp.where(place == 0, s_ref[2], jnp.where(last, s_ref[4], s_ref[3]))
    start = jnp.where(place == 0, 0, jnp.where(last, s_ref[1] - 1, 1))
    rows = lax.broadcasted_iota(jnp.int32, (Q, 1), 0) + (place - start) * Q
    return (rows < length).astype(F32)


class Outbound:
    def __init__(self, held, sems, keep, send, tiles):
        self.held, self.sems, self.keep, self.send, self.tiles = held, sems, keep, send, tiles

    def wait(self, slot):
        for k in range(2):
            held = self.held.at[slot, :, k * LANES : (k + 1) * LANES]
            pltpu.make_async_copy(held, self.keep.at[0, :, 0:LANES], self.sems.at[slot, k]).wait()

    def start(self, turn, slot):
        for k in range(2):
            at = 2 * turn + k
            piece, lane = at // self.tiles, at % self.tiles
            held = self.held.at[slot, :, k * LANES : (k + 1) * LANES]
            cols = slice(lane * LANES, (lane + 1) * LANES) if isinstance(lane, int) else tile_at(lane)
            for odd, ref in enumerate((self.keep, self.send)):

                @pl.when(piece % 2 == odd)
                def _(ref=ref, held=held, piece=piece, cols=cols, k=k):
                    pltpu.make_async_copy(held, ref.at[piece // 2, :, cols], self.sems.at[slot, k]).start()


def turns_with_grads(turns, work, grads, out):
    def turn(i, none):
        before = jnp.maximum(i - 1, 0)
        slot = before % 2

        @pl.when(i >= 3)
        def _():
            out.wait(slot)

        grads(before, slot)
        work(i, 0)
        work(i, 1)

        @pl.when(i >= 1)
        def _():
            out.start(before, slot)

        return none

    lax.fori_loop(0, turns, turn, 0)
    last = turns - 1
    if last >= 2:
        out.wait(last % 2)
    grads(last, last % 2)
    out.start(jnp.int32(last), last % 2)
    for slot in range(min(2, turns)):
        out.wait(slot)


def middle_kernel(blocks, tiles, head_size, s_ref, dbt_ref, inc_in, colp_ref, chan_ref, par_ref, c_ref, ct_ref, nt_ref,
                  y_ref, dny_ref, gate_ref, x_ref, st_ref,
                  ny_out, dgate_out, keep_out, send_out, inc_out, di_out, dc_out, rowpart_out, rows_out,
                  dy_ref, carry_ref, turned_ref,
                  ny_ref, dgate_ref, inc_ref, di_ref, dc_ref, rowpart_ref, rows_ref, grad_ref,
                  mix_ref, sq_ref, cr_ref, hi_ref, lo_ref, sems, grad_sems):
    moves = [(ny_ref, ny_out), (dgate_ref, dgate_out), (inc_ref, inc_out), (di_ref, di_out), (dc_ref, dc_out), (rowpart_ref, rowpart_out), (rows_ref, rows_out)]

    def move(index, *where):
        held, out = moves[index]
        pltpu.make_async_copy(held.at[where], out.at[where], sems.at[index]).start()

    depth = dbt_ref.shape[0]
    total = chan_ref.shape[1]
    kept = [keeps_of(s_ref, block, blocks)[1] for block in range(blocks)]
    sq_ref[...] = jnp.zeros_like(sq_ref)
    cr_ref[...] = jnp.zeros_like(cr_ref)

    def forward(i, none):
        for k in range(2):
            far = tile_at(2 * i + k)
            incoming = inc_in[:, far]
            for block in range(blocks):
                at = pl.ds(block * Q, Q)
                incoming = kept[block] * incoming
                inc_low = incoming.astype(BF16)
                inc_ref[block, :, far] = inc_low
                incoming = chan_ref[block : block + 1, far] * incoming + st_ref[block, :, far]
                inter = mm(c_ref[at], inc_low) * spread(colp_ref[i, at, 8 * k : 8 * k + 8], 2)
                mix = y_ref[at, far] + inter + chan_ref[7:8, far] * x_ref[at, far].astype(F32)
                mix_ref[at, far] = mix
                gate = gate_ref[at, far].astype(F32)
                gated = mix * (gate * jax.nn.sigmoid(gate))
                sq_ref[at] += gated * gated
                cr_ref[at] += dny_ref[at, far].astype(F32) * par_ref[5:6, far] * gated
        return none

    lax.fori_loop(0, total // (2 * LANES), forward, 0)
    scale = lax.rsqrt(jnp.sum(sq_ref[...], axis=1, keepdims=True) / total + EPSILON)
    coef = scale * scale * scale * (jnp.sum(cr_ref[...], axis=1, keepdims=True) / total)
    sq_ref[...] = jnp.broadcast_to(scale, sq_ref.shape)
    cr_ref[...] = jnp.broadcast_to(coef, cr_ref.shape)
    rows_ref[...] = jnp.zeros_like(rows_ref)

    def backward(i, k):
        pair = 2 * i + k
        far = tile_at(pair)
        gain = par_ref[5:6, far]
        skip = chan_ref[7:8, far]
        gain_row = jnp.zeros((1, LANES), F32)
        skip_row = jnp.zeros((1, LANES), F32)
        dis = []
        for block in range(blocks):
            at = pl.ds(block * Q, Q)
            gate, mix, x = gate_ref[at, far].astype(F32), mix_ref[at, far], x_ref[at, far].astype(F32)
            sig = jax.nn.sigmoid(gate)
            act = gate * sig
            gated = mix * act
            normed = gated * sq_ref[at]
            dny = dny_ref[at, far].astype(F32)
            ny_ref[at, far] = (normed * gain).astype(BF16)
            gain_row += jnp.sum(dny * normed, axis=0, keepdims=True)
            d_gated = dny * gain * sq_ref[at] - gated * cr_ref[at]
            dgate_ref[at, far] = (d_gated * mix * silu_slope(gate, sig)).astype(BF16)
            dy = d_gated * act
            dy_low = dy.astype(BF16)
            dy_ref[at, far] = dy_low
            skip_row += jnp.sum(dy * x, axis=0, keepdims=True)
            split_store(hi_ref, lo_ref, at, far, dy_low.astype(F32) * (mix - skip * x))
            dye = (dy * spread(colp_ref[i, at, 8 * k : 8 * k + 8], 2)).astype(BF16)
            dc_ref[at] += mm(dye, inc_ref[block, :, far], 1, 1)
            di = mm(ct_ref[:, at], dye).astype(BF16)
            di_ref[block, :, far] = di
            dis.append(di.astype(F32))
        rows_ref[0:1, far] = gain_row
        rows_ref[1:2, far] = skip_row
        back = jnp.zeros_like(dis[0])
        for block in reversed(range(blocks)):
            back = kept[block] * (dis[block] + chan_ref[block : block + 1, far] * back)
        carry_block(carry_ref, far, back, chan_ref[6:7, far])
        turned = tile_at(jnp.bitwise_xor(pair // tiles, 1) * tiles + pair % tiles)
        carry_block(turned_ref, turned, back, chan_ref[6:7, far])
        move(0, slice(None), far)
        move(1, slice(None), far)

    def grads(turn, slot):
        cols = pl.ds(pl.multiple_of(turn * 2 * LANES, 2 * LANES), 2 * LANES)
        grad_ref[slot, 0:depth] = mm(dbt_ref[...], ny_ref[:, cols]).astype(BF16)
        grad_ref[slot, depth:] = mm(nt_ref[...], dgate_ref[:, cols]).astype(BF16)

    dc_ref[...] = jnp.zeros_like(dc_ref)
    turns_with_grads(total // (2 * LANES), backward, grads, Outbound(grad_ref, grad_sems, keep_out, send_out, tiles))
    for index in (2, 3, 4, 6):
        move(index)
    rowpart_ref[...] = head_sums(rowpart_ref.shape[0], head_size, hi_ref, lo_ref)
    move(5)
    for index, (held, out) in enumerate(moves):
        pltpu.make_async_copy(held, out, sems.at[index]).wait()


def back_kernel(blocks, head_size, s_ref, rowp_ref, colp_ref, cbt_ref, b_ref, c_ref, dy_ref, x_ref,
                dx_ref, part_ref, db_ref, dc_ref, acc_ref, hi_ref, lo_ref):
    half = Q // 2
    first = first_lanes()
    tri = lax.broadcasted_iota(jnp.int32, (half, half), 0) <= lax.broadcasted_iota(
        jnp.int32, (half, half), 1
    )
    acc_ref[...] = jnp.zeros_like(acc_ref)

    def two(i, none):
        for block in range(blocks):
            at = pl.ds(block * Q, Q)
            w00 = w01 = w11 = 0.0
            for k in range(2):
                pair = 2 * i + k
                far = tile_at(pair)
                x, dy = x_ref[at, far], dy_ref[at, far]
                dys = [jnp.where(first, dy, 0), jnp.where(first, 0, dy)]
                xs = [jnp.where(first, x, 0), jnp.where(first, 0, x)]
                rp = rowp_ref[pair, :, at]
                cp = colp_ref[i, at, 8 * k : 8 * k + 8]
                tops, bots = [], []
                for h in range(2):
                    ls, ld = cp[:, 2 + h : 3 + h], rp[h : h + 1, :]
                    ds_top = mm(xs[h][:half], dy, 1, 1)
                    ds_bot = mm(xs[h][half:], dy[half:], 1, 1)
                    e00 = jnp.exp(jnp.where(tri, ld[:, :half] - ls[:half], -1e30))
                    e01 = jnp.exp(ld[:, half:] - ls[:half])
                    e11 = jnp.exp(jnp.where(tri, ld[:, half:] - ls[half:], -1e30))
                    tops.append((cbt_ref[block, 0:half, 0:half] * e00).astype(BF16))
                    tops.append((cbt_ref[block, 0:half, half:] * e01).astype(BF16))
                    bots.append((cbt_ref[block, half:, half:] * e11).astype(BF16))
                    w00 += ds_top[:, :half] * e00
                    w01 += ds_top[:, half:] * e01
                    w11 += ds_bot * e11
                dx_top = mm(jnp.concatenate(tops, 1), jnp.concatenate(dys, 0))
                dx_bot = mm(jnp.concatenate(bots, 1), jnp.concatenate([d[half:] for d in dys], 0))
                dx = jnp.concatenate([dx_top, dx_bot], 0)
                dx_ref[at, far] = dx.astype(BF16)
                split_store(hi_ref, lo_ref, at, far, x.astype(F32) * dx)
            acc_ref[block, 0:half, 0:half] += w00
            acc_ref[block, 0:half, half:] += w01
            acc_ref[block, half:, half:] += w11
        return none

    lax.fori_loop(0, x_ref.shape[1] // (2 * LANES), two, 0)
    part_ref[...] = head_sums(part_ref.shape[0], head_size, hi_ref, lo_ref)
    for block in range(blocks):
        at = slice(block * Q, (block + 1) * Q)
        acc = acc_ref[block].astype(BF16)
        db_ref[at] = mm(acc, c_ref[at])
        dc_ref[at] = mm(acc, b_ref[at], 0, 0)


def conv_back(s_ref, blocks, work, taps, values_of, slope_of, store):
    sums = [0.0] * (K + 1)
    for block in range(blocks):
        fresh, _ = keeps_of(s_ref, block, blocks)
        d_pre = slope_of(block)
        work[0, pl.ds(HALO + block * Q, Q)] = d_pre
        sums[K] += jnp.sum(d_pre, axis=0, keepdims=True)
        sums[K - 1] += jnp.sum(d_pre * values_of(HALO + block * Q), axis=0, keepdims=True)
        for distance in range(1, K):
            held = d_pre * row_keep(fresh, distance)
            work[distance, pl.ds(HALO + block * Q, Q)] = held
            sums[K - 1 - distance] += jnp.sum(
                held * values_of(HALO + block * Q - distance), axis=0, keepdims=True
            )
    for begin, count in [(0, HALO)] + [(HALO + b * Q, Q) for b in range(blocks)]:
        out = taps[K - 1 : K] * work[0, pl.ds(begin, count)]
        for distance in range(1, K):
            out = out + taps[K - 1 - distance : K - distance] * work[distance, pl.ds(begin + distance, count)]
        store(begin, count, out.astype(BF16))
    return sums


def tail_kernel(blocks, tiles, head_size, s_ref, back_in, colp_ref, chan_ref, par_ref, b_ref, nt_ref, nx_ref,
                inc_ref, dx_ref, dy_ref, di_ref, x_ref, pre_ref, inner_ref,
                dinner_ref, vgrad_ref, part_ref, lasts_ref, db_ref, keep_out, send_out,
                d_ref, in_ref, hi_ref, lo_ref, grad_ref, grad_sems):
    total = chan_ref.shape[1]
    kept = [keeps_of(s_ref, block, blocks)[1] for block in range(blocks)]
    d_ref[...] = jnp.zeros_like(d_ref)
    vgrad_ref[...] = jnp.zeros_like(vgrad_ref)
    lasts_ref[...] = jnp.zeros_like(lasts_ref)
    db_ref[...] = jnp.zeros_like(db_ref)

    def work(i, k):
        far = tile_at(2 * i + k)
        in_ref[k] = inner_ref[:, far].astype(F32)
        skip = chan_ref[7:8, far]
        back = back_in[:, far]
        lasts, lows = [None] * blocks, [None] * blocks
        for block in reversed(range(blocks)):
            fade = chan_ref[block : block + 1, far]
            lows[block] = back.astype(BF16)
            lasts[block] = fade * jnp.sum(inc_ref[block, :, far].astype(F32) * back, axis=0, keepdims=True)
            back = kept[block] * (di_ref[block, :, far].astype(F32) + fade * back)

        def slope_of(block):
            at = pl.ds(block * Q, Q)
            carry = spread(colp_ref[i, at, 8 * k : 8 * k + 8], 3)
            weighted = carry * x_ref[at, far].astype(F32)
            db_ref[at] += mm(weighted.astype(BF16), lows[block], 1, 1)
            d_weighted = mm(b_ref[at], lows[block])
            moved = weighted * d_weighted
            lasts_ref[block : block + 1, far] = lasts[block] + jnp.sum(moved, axis=0, keepdims=True)
            split_store(hi_ref, lo_ref, at, far, moved)
            d_x = dx_ref[at, far].astype(F32) + carry * d_weighted + skip * dy_ref[at, far].astype(F32)
            pre = pre_ref[at, far].astype(F32)
            return d_x * silu_slope(pre, jax.nn.sigmoid(pre))

        def store(begin, count, value):
            dinner_ref[pl.ds(begin, count), far] = value

        sums = conv_back(
            s_ref, blocks, d_ref.at[k], par_ref[:, far], lambda at: in_ref[k, pl.ds(at, Q)], slope_of, store
        )
        for index in range(K + 1):
            vgrad_ref[index : index + 1, far] = sums[index]

    def grads(turn, slot):
        cols = pl.ds(pl.multiple_of(turn * 2 * LANES, 2 * LANES), 2 * LANES)
        grad = mm(nt_ref[...], dinner_ref[HALO:, cols]) + mm(nx_ref[0:HALO], dinner_ref[0:HALO, cols], 0, 0)
        grad_ref[slot] = grad.astype(BF16)

    turns_with_grads(total // (2 * LANES), work, grads, Outbound(grad_ref, grad_sems, keep_out, send_out, tiles))
    part_ref[...] = head_sums(part_ref.shape[0], head_size, hi_ref, lo_ref)


def state_kernel(blocks, head_size, shares, s_ref, dbx_ref, dbin_ref, dcin_ref, dcx_ref, raw_ref, spre_ref, staps_ref,
                 rowpart_ref, part_a, part_b, step_ref, ratio_ref, sig_ref, hp_ref, rows_ref, lasts_ref, vgrad_ref,
                 nt_ref, nx_ref, dstate_ref, dstep_ref, *refs):
    e_ref, all_ref, step_grad_ref = refs[-3:]
    outs = refs[:-3]
    e_ref[...] = jnp.zeros_like(e_ref)
    d_states = []
    for block in range(blocks):
        at = slice(block * Q, (block + 1) * Q)
        d_states.append(jnp.concatenate([dbin_ref[at] + dbx_ref[at], dcin_ref[at] + dcx_ref[at]], 1))

    def slope_of(block):
        pre = spre_ref[pl.ds(block * Q, Q), :]
        return d_states[block] * silu_slope(pre, jax.nn.sigmoid(pre))

    def store(begin, count, value):
        dstate_ref[pl.ds(begin, count), :] = value

    sgrad = conv_back(s_ref, blocks, e_ref, staps_ref[...], lambda at: raw_ref[pl.ds(at, Q), :], slope_of, store)
    heads = hp_ref.shape[0]
    total = lasts_ref.shape[1]
    depth = hp_ref.shape[1] - LANES
    spots = head_lanes((heads, total), True, head_size).astype(F32)
    lasts = mm(spots, lasts_ref[...], 1, 1, precision=HIGHEST)
    skips = mm(spots, rows_ref[...], 1, 1, precision=HIGHEST)[:, 1:2]
    rate = -jnp.exp(hp_ref[:, depth + 1 : depth + 2])
    lane = lax.broadcasted_iota(jnp.int32, (heads, Q), 1)
    upto = (
        lax.broadcasted_iota(jnp.int32, (Q, Q), 0) >= lax.broadcasted_iota(jnp.int32, (Q, Q), 1)
    ).astype(F32)
    grad_bias = jnp.zeros((heads, 1), F32)
    grad_decay = jnp.zeros((heads, 1), F32)
    for block in range(blocks):
        at = slice(block * Q, (block + 1) * Q)
        cols = part_a[:, at] + part_b[:, at]
        d_log = rowpart_ref[:, at] - cols + jnp.where(lane == Q - 1, lasts[:, block : block + 1], 0.0)
        d_move = mm(d_log, upto, precision=HIGHEST)
        d_raw = cols * ratio_ref[:, at] + rate * d_move * sig_ref[:, at]
        grad_bias += jnp.sum(d_raw, axis=1, keepdims=True)
        grad_decay += rate * jnp.sum(step_ref[:, at] * d_move, axis=1, keepdims=True)
        dstep_ref[:, at] = d_raw.astype(BF16)
    wide_lane = lax.broadcasted_iota(jnp.int32, (heads, LANES), 1)
    per_head = jnp.where(
        wide_lane == 0, grad_bias, jnp.where(wide_lane == 1, grad_decay, jnp.where(wide_lane == 2, skips, 0.0))
    )
    step_grad_ref[...] = mm(dstep_ref[...], nx_ref[HALO:])
    all_ref[...] = jnp.zeros_like(all_ref)
    all_ref[0:depth] = mm(nt_ref[...], dstate_ref[HALO:]) + mm(nx_ref[0:HALO], dstate_ref[0:HALO], 0, 0)
    for index in range(K + 1):
        all_ref[depth + index : depth + index + 1] = sgrad[index]
    if not shares:
        outs[0][...] = all_ref[...]
        outs[1][...] = step_grad_ref[...]
        outs[2][...] = per_head
        return
    ways, share, wide = shares
    quarter = all_ref.shape[0] // ways
    work = outs[-1]
    for p in range(ways):
        span = slice(p * wide, (p + 1) * wide)
        some = slice(p * share, (p + 1) * share)
        work[...] = jnp.zeros_like(work)
        work[0 : K + 1] = vgrad_ref[0 : K + 1, span]
        work[K + 1 : K + 2] = rows_ref[0:1, span]
        for part in range(depth // wide):
            begin = 8 + part * share
            work[begin : begin + share] = step_grad_ref[some, part * wide : (part + 1) * wide]
        work[24 : 24 + share, 0:LANES] = per_head[some]
        owner = jnp.bitwise_xor(s_ref[0], p)
        work[32 : 32 + quarter, 0 : all_ref.shape[1]] = all_ref[pl.ds(pl.multiple_of(owner * quarter, 8), quarter)]
        outs[p % 2][p // 2] = work[...].astype(BF16)


def mixed_kernel(pieces, blocks, s_ref, hid_ref, ny_ref, *refs):
    outs_w, mixed_ref = refs[:pieces], refs[pieces]
    wide = outs_w[0].shape[0]
    for block in range(blocks):
        at = slice(block * Q, (block + 1) * Q)
        branch = mm(ny_ref[at, 0:wide], outs_w[0][...])
        for p in range(1, pieces):
            branch += mm(ny_ref[at, p * wide : (p + 1) * wide], outs_w[p][...])
        mixed_ref[at] = (hid_ref[at].astype(F32) + valid_of(s_ref, blocks, block) * branch).astype(BF16)


def final_kernel(pieces, blocks, mine, s_ref, hid_ref, halo_ref, cot_ref, gain_ref, dgate_ref, dinner_ref,
                 dstate_ref, dstep_ref, hp_ref, sproj_ref, *refs):
    both_in = refs[:pieces]
    grad_out, extra_ref, gain_out, grad_ref, sems, both, dgate_here, dinner_here, in_sems = refs[-9:]
    wide = both.shape[2] // 2
    depth = hid_ref.shape[1]
    own = pl.ds(mine[0] * Q, len(mine) * Q)
    waits = [
        pltpu.make_async_copy(dinner_ref.at[pl.ds(mine[0] * Q, len(mine) * Q + HALO)], dinner_here, in_sems.at[0]),
        pltpu.make_async_copy(dgate_ref.at[own], dgate_here, in_sems.at[1]),
    ]
    for copy in waits:
        copy.start()
    loads = [pltpu.make_async_copy(both_in[p], both.at[p], in_sems.at[2 + p]) for p in range(pieces)]
    for copy in loads:
        copy.start()
    gain = gain_ref[...]
    gain_sum = jnp.zeros((1, depth), F32)

    def finish(values_in, d_normed):
        h = values_in.astype(F32)
        scale = lax.rsqrt(jnp.mean(h * h, axis=1, keepdims=True) + EPSILON)
        weighted = gain * d_normed
        inner = jnp.mean(weighted * h, axis=1, keepdims=True)
        return scale * weighted - h * (scale * scale * scale * inner), jnp.sum(d_normed * h * scale, axis=0, keepdims=True)

    moves = []
    totals = [mm(dstate_ref[0:HALO], sproj_ref[...], 1, 1)]
    for block in mine:
        ext = slice(HALO + block * Q, HALO + (block + 1) * Q)
        part = mm(dstate_ref[ext], sproj_ref[...], 1, 1)
        totals.append(part + mm(dstep_ref[:, block * Q : (block + 1) * Q], hp_ref[:, 0:depth].astype(BF16), 0, 0))
    for copy in waits:
        copy.wait()
    for p in range(pieces):
        loads[p].wait()
        span = slice(p * wide, (p + 1) * wide)
        if mine[0] == 0:
            totals[0] += mm(dinner_here[0:HALO, span], both[p, :, wide:], 1, 1)
        for index in range(len(mine)):
            here = slice(index * Q, (index + 1) * Q)
            ext = slice(HALO + index * Q, HALO + (index + 1) * Q)
            totals[index + 1] += mm(dgate_here[here, span], both[p, :, :wide], 1, 1)
            totals[index + 1] += mm(dinner_here[ext, span], both[p, :, wide:], 1, 1)
    if mine[0] == 0:
        extra_ref[...], part = finish(halo_ref[...], totals[0])
        gain_sum += part
    else:
        extra_ref[...] = jnp.zeros_like(extra_ref)
    for index, block in enumerate(mine):
        at = slice(block * Q, (block + 1) * Q)
        here = slice(index * Q, (index + 1) * Q)
        d_hidden, part = finish(hid_ref[at], totals[index + 1].astype(BF16).astype(F32))
        gain_sum += part
        grad_ref[here] = cot_ref[at].astype(F32) + d_hidden
        moves.append(pltpu.make_async_copy(grad_ref.at[here], grad_out.at[at], sems.at[index]))
        moves[-1].start()
    gain_out[...] = jnp.zeros_like(gain_out)
    side = gain_out.shape[1]
    for index in range(depth // side):
        gain_out[index : index + 1] = gain_sum[:, index * side : (index + 1) * side]
    for copy in moves:
        copy.wait()


def gather_far(value, ahead):
    ways = lax.axis_size("head")
    pieces = {0: value}
    far = {0: after(value, ahead)}
    mask = 2
    while mask < ways:
        for p in list(far):
            far[p | mask] = swap(far[p], "head", mask)
        mask *= 2
    return [value] + [far[p] for p in range(2, ways, 2)]


def near_pair(value, ahead):
    return value, swap(after(value, ahead) if len(ahead) else value, "head", 1)


def swap(value, axis, mask):
    size = lax.axis_size(axis)
    return lax.ppermute(value, axis, [(i, i ^ mask) for i in range(size)])


def pick(value, index):
    return lax.dynamic_index_in_dim(value, index, 0, keepdims=False)


def half_of(value, mask):
    side = jnp.where((lax.axis_index("dp") & mask) != 0, 1, 0)
    parts = value.reshape(2, value.shape[0] // 2, value.shape[1])
    return pick(parts, side).astype(F32), pick(parts, 1 - side).astype(BF16)


def whole_dp(low):
    for bit in range(3, lax.axis_size("dp").bit_length() - 1):
        low = (low.astype(F32) + swap(low, "dp", 1 << bit).astype(F32)).astype(BF16)
    return low


def both_of(low, mask, other):
    upper = (lax.axis_index("dp") & mask) != 0
    return jnp.concatenate([jnp.where(upper, other, low), jnp.where(upper, low, other)], axis=0)


def after(value, *others):
    return lax.optimization_barrier((value, others))[0]


def gather_pieces(value, ahead=()):
    ways = lax.axis_size("head")
    pieces = {0: value, 1: swap(value, "head", 1)}
    far = {0: after(value, ahead) if ahead else value}
    mask = 2
    while mask < ways:
        for p in list(far):
            far[p | mask] = swap(far[p], "head", mask)
        mask *= 2
    for p in far:
        if p:
            pieces[p] = far[p]
            pieces[p | 1] = swap(far[p], "head", 1)
    return [pieces[p] for p in range(ways)]


def reduce_pieces(pieces):
    ways = len(pieces)
    mask = 1
    live = {p: v for p, v in enumerate(pieces)}
    order = [1 << b for b in range(ways.bit_length() - 1)]
    for mask in order:
        got = {p ^ mask: swap(live[p].astype(BF16), "head", mask) for p in live if p & mask}
        live = {p: live[p].astype(F32) + got[p].astype(F32) for p in live if not p & mask}
    return live[0]


def body(hidden, lengths, norm_gain, gate_proj, value_proj, state_proj, step_proj, value_taps, value_bias,
         state_taps, state_bias, step_bias, decay_log, skip_gain, out_gain, out_proj, cotangent):
    rows, depth = hidden.shape
    ways = lax.axis_size("head")
    me = lax.axis_index("head")
    blocks = rows // Q
    wide = gate_proj.shape[1]
    share = step_proj.shape[1]
    total = wide * ways
    heads = share * ways
    head_size = wide // share
    pairs = heads // 2
    side = state_proj.shape[1]
    state = side // 2
    padded = -(-heads // 32) * 32
    plain = wide % LANES == 0
    order = [1 << b for b in range(ways.bit_length() - 1)]
    scalars = jnp.concatenate(
        [jnp.stack([me, blocks * ways]).astype(jnp.int32), lengths[0], jnp.zeros((3,), jnp.int32)]
    )

    top = jnp.concatenate(
        [step_proj.T.astype(F32), step_bias[:, None], decay_log[:, None], skip_gain[:, None], jnp.zeros((share, LANES - 3), F32)],
        axis=1,
    )
    low = jnp.concatenate([value_taps, value_bias[None], out_gain[None]], axis=0)
    pack = jnp.concatenate(
        [
            jnp.pad(top, ((0, 8 - share), (0, 0))),
            jnp.pad(low, ((0, 2), (0, depth + LANES - wide))),
            jnp.pad(hidden[rows - HALO :].astype(F32), ((0, 0), (0, LANES))),
        ],
        axis=0,
    )
    packs = gather_pieces(pack)
    halo = jnp.zeros((HALO, depth), F32)
    for p in range(1, ways):
        halo = jnp.where((me ^ p) == me - 1, packs[p][16:, :depth], halo)
    halo = halo.astype(BF16)
    both = gather_far(jnp.concatenate([gate_proj, value_proj], axis=1), (packs[1],))
    outs = gather_far(out_proj, (packs, both[0]))

    def both_merged(pair):
        if plain:
            return list(pair)
        a, b = pair
        return [jnp.concatenate([a[:, :wide], b[:, :wide], a[:, wide:], b[:, wide:]], axis=1)]

    def outs_merged(pair):
        return list(pair) if plain else [jnp.concatenate(pair, axis=0)]

    pieces = ways if plain else ways // 2
    span = total // pieces
    tiles = span // LANES
    hp = jnp.pad(jnp.concatenate([p[:share] for p in packs], axis=0), ((0, padded - heads), (0, 0)))
    par = jnp.concatenate([p[8:16, :wide] for p in packs], axis=1)
    gain_in = norm_gain[None]
    staps = jnp.pad(jnp.concatenate([state_taps, state_bias[None]], axis=0), ((0, 3), (0, 0)))

    ext = rows + HALO
    (nx, nt, state_raw, state_pre, b_low, c_low, b_t, c_t, cb, cbt) = call(
        functools.partial(pre_kernel, blocks),
        [((ext, depth), BF16), ((depth, rows), BF16), ((ext, side), F32), ((rows, side), F32),
         ((rows, state), BF16), ((rows, state), BF16), ((state, rows), BF16), ((state, rows), BF16),
         ((blocks, Q, Q), F32), ((blocks, Q, Q), F32)],
        [scalars, hidden, halo, gain_in, state_proj, staps],
        cost=2, mib=PRE,
    )
    rowp, colp, step, ratio, sig, chan = call(
        functools.partial(step_kernel, blocks, head_size),
        [((pairs, 8, rows), F32), ((pairs // 2, rows, 16), F32), ((padded, rows), F32), ((padded, rows), F32),
         ((padded, rows), F32), ((8, total), F32)],
        [scalars, nx, hp],
        cost=2,
        mib=PRE,
    )
    vmem = pltpu.VMEM
    hbm = pl.BlockSpec(memory_space=pltpu.HBM)
    front_outs = [((rows, total), BF16), ((ext, total), BF16), ((rows, total), BF16), ((blocks, state, total), F32),
                  ((rows, total), BF16), ((state + HALO, total), BF16), ((state + HALO, total), BF16)]
    fronts, all_both = [], []
    half = pieces // 2
    for begin in (0, half):
        pairs_of = range(begin // 2, begin // 2 + ways // 4) if plain else range(begin, begin + half)
        weights = [w for at in pairs_of for w in both_merged(near_pair(both[at], fronts))]
        all_both += weights
        args = [scalars, nx, par, b_t, colp, chan, *weights]
        aliases = {len(args) + at: at for at in range(len(fronts))}
        fronts = call(
            functools.partial(front_kernel, blocks, begin, half), front_outs, [*args, *fronts], aliases=aliases,
            ins={len(args) + at: hbm for at in range(min(4, len(fronts)))}, out_specs={at: hbm for at in range(4)},
            kinds={at: pltpu.HBM for at in range(4)},
            scratch=[vmem((rows, half * span), BF16), vmem((ext, half * span), BF16), vmem((rows, half * span), BF16),
                     vmem((blocks, state, half * span), F32), vmem((ext, half * span), F32), pltpu.SemaphoreType.DMA((4,))],
            cost=6, mib=FRONT,
        )
    gate, inner, pre, st, x, carry, carry_turned = fronts

    def turned(value, mask):
        parts = [value[..., (p ^ mask) * wide : ((p ^ mask) + 1) * wide] for p in range(ways)]
        return jnp.concatenate(parts, axis=-1)

    def scan(own, own_turned, forward, beside=lambda run: ()):
        def fade_of(value):
            return value[state : state + 1].astype(F32) + value[state + 1 : state + 2].astype(F32)

        if plain and ways == 4:
            near = swap(own_turned, "head", 1)
            (run,) = call(functools.partial(join_kernel, forward), [(own.shape, BF16)], [scalars, own, near], mib=8)
            far = swap(run, "head", 2)
            between = beside(run)
            far = after(far, between[1]) if between else far
            (result,) = call(functools.partial(arrive_kernel, forward), [((state, total), F32)], [scalars, near, far], mib=8)
            return result, between
        before = before_fade = None
        run = own
        for mask in order:
            if mask == 1 and plain:
                got = swap(own_turned, "head", 1)
            else:
                got = turned(swap(run, "head", mask), mask)
            got_fade, run_fade = fade_of(got), fade_of(run)
            got, mine = got[:state].astype(F32), run[:state].astype(F32)
            later = ((me & mask) != 0) if forward else ((me & mask) == 0)
            if before is None:
                before = jnp.where(later, got, 0.0)
                before_fade = jnp.where(later, got_fade, 1.0)
            else:
                before = jnp.where(later, before_fade * got + before, before)
                before_fade = jnp.where(later, before_fade * got_fade, before_fade)
            if mask != order[-1]:
                both_maps = jnp.where(later, run_fade * got + mine, got_fade * mine + got)
                fades = run_fade * got_fade
                high = fades.astype(BF16)
                low_part = (fades - high.astype(F32)).astype(BF16)
                run = jnp.concatenate(
                    [both_maps.astype(BF16), high, low_part, jnp.zeros((HALO - 2, total), BF16)], axis=0
                )
        return before, beside(run)

    def within(run):
        (y_intra,) = call(
            functools.partial(intra_kernel, blocks),
            [((rows, total), F32)],
            [scalars, rowp, colp, cb, after(x, run)],
            cost=5,
            mib=INTRA,
        )
        all_outs = [w for value in outs for w in outs_merged(near_pair(value, run))]
        dny, dbt = call(
            functools.partial(masked_kernel, blocks, pieces),
            [((rows, total), BF16), ((depth, rows), BF16)],
            [scalars, cotangent, *all_outs],
            scratch=[vmem((rows, depth), BF16)],
            cost=3,
            mib=INTRA,
        )
        return y_intra, dny, dbt, all_outs

    inc_in, (y_intra, dny, dbt, all_outs) = scan(carry, carry_turned, True, within)
    wide_bf = vmem((rows, total), BF16)
    held_outs = [((rows, total), BF16), ((rows, total), BF16),
                 ((pieces // 2, 2 * depth, span), BF16), ((pieces // 2, 2 * depth, span), BF16),
                 ((blocks, state, total), BF16), ((blocks, state, total), BF16), ((rows, state), F32),
                 ((padded, rows), F32), ((8, total), F32)]
    (ny, d_gate, a_keep, a_send, inc, d_inc, dc_inter, rowpart, rows_sum, d_y, back_carry, back_turned) = call(
        functools.partial(middle_kernel, blocks, tiles, head_size),
        [*held_outs, ((rows, total), BF16), ((state + HALO, total), BF16), ((state + HALO, total), BF16)],
        [scalars, dbt, inc_in, colp, chan, par, c_low, c_t, nt, y_intra, dny, gate, x, st],
        out_specs={at: hbm for at in range(len(held_outs))}, kinds={at: pltpu.HBM for at in range(len(held_outs))},
        scratch=[*[vmem(*o) for at, o in enumerate(held_outs) if at not in (2, 3)], vmem((2, 2 * depth, 2 * LANES), BF16), vmem((rows, total), F32), vmem((rows, LANES), F32),
                 vmem((rows, LANES), F32), wide_bf, wide_bf, pltpu.SemaphoreType.DMA((len(held_outs) - 2,)),
                 pltpu.SemaphoreType.DMA((2, 2))],
        cost=14, mib=MIDDLE,
    )
    back_runs = []
    back_in, _ = scan(back_carry, back_turned, False, lambda run: back_runs.append(run))

    def over_head(keep, send):
        if not plain:
            parts = [None] * ways
            for m in range(pieces):
                merged = (keep, send)[m % 2][m // 2]
                parts[2 * m], parts[2 * m + 1] = merged[:, :wide], merged[:, wide:]
            return reduce_pieces(parts)
        got = swap(send, "head", 1)
        live = [keep[i].astype(F32) + got[i].astype(F32) for i in range(pieces // 2)]
        return live

    def finish_head(live):
        if not plain:
            return live
        return live[0] + swap(live[1].astype(BF16), "head", 2).astype(F32)

    def halve(value, axis_at=0):
        side = lax.axis_index("dp") & 1
        cut = value.shape[:axis_at] + (2, value.shape[axis_at] // 2) + value.shape[axis_at + 1 :]
        parts = jnp.moveaxis(value.reshape(cut), axis_at, 0)
        got = swap(pick(parts, 1 - side).astype(BF16), "dp", 1)
        return pick(parts, side).astype(F32) + got.astype(F32)

    a_live = over_head(a_keep, after(a_send, *back_runs))
    if plain:
        a_out = finish_head([v[:depth] for v in a_live])
        a_gate = halve(jnp.stack([v[depth:] for v in a_live]), 1)
        gates = (a_out, a_gate)
    else:
        gates = a_live
    dx, part_a, db_in, dc_in = call(
        functools.partial(back_kernel, blocks, head_size),
        [((rows, total), BF16), ((padded, rows), F32), ((rows, state), F32), ((rows, state), F32)],
        [scalars, rowp, colp, cbt, b_low, c_low, d_y, x],
        scratch=[vmem((blocks, Q, Q), F32), wide_bf, wide_bf],
        cost=8,
        mib=BACK,
    )
    (d_inner, vgrad, part_b, lasts, db_x, b_keep, b_send) = call(
        functools.partial(tail_kernel, blocks, tiles, head_size),
        [((ext, total), BF16), ((8, total), F32), ((padded, rows), F32), ((8, total), F32), ((rows, state), F32),
         ((pieces // 2, depth, span), BF16), ((pieces // 2, depth, span), BF16)],
        [scalars, after(back_in, a_live), colp, chan, par, b_low, nt, nx, inc, dx, d_y, d_inc, x, pre, inner],
        out_specs={5: hbm, 6: hbm}, kinds={5: pltpu.HBM, 6: pltpu.HBM},
        scratch=[vmem((2, K, rows + 2 * HALO, LANES), F32), vmem((2, ext, LANES), F32), wide_bf, wide_bf,
                 vmem((2, depth, 2 * LANES), BF16), pltpu.SemaphoreType.DMA((2, 2))],
        cost=10, mib=TAIL,
    )
    small_rows, all_rows = 256, 832
    if plain:
        small_outs = [((pieces // 2, small_rows, span), BF16)] * 2
        shares = (ways, share, wide)
        work = [vmem((small_rows, span), F32)]
    else:
        small_outs = [((all_rows, side), F32), ((padded, depth), F32), ((padded, LANES), F32)]
        shares = None
        work = []
    d_state, d_step, *smalls = call(
        functools.partial(state_kernel, blocks, head_size, shares),
        [((ext, side), BF16), ((padded, rows), BF16)] + small_outs,
        [scalars, after(db_x, gates), db_in, dc_in, dc_inter, state_raw, state_pre, staps, rowpart, part_a, part_b, step, ratio, sig, hp,
         rows_sum, lasts, vgrad, nt, nx],
        scratch=work + [vmem((K, rows + 2 * HALO, side), F32), vmem((all_rows, side), F32), vmem((padded, depth), F32)],
        cost=4, mib=STATE,
    )
    share_rows = all_rows // ways
    if not plain:
        all_grad, step_grad, per_head = smalls
        parts = []
        for p in range(ways):
            cols, some = slice(p * wide, (p + 1) * wide), slice(p * share, (p + 1) * share)
            flat = step_grad[some].reshape(share, depth // wide, wide).swapaxes(0, 1).reshape(-1, wide)
            own = lax.dynamic_slice_in_dim(all_grad, (me ^ p) * share_rows, share_rows, 0).reshape(-1)
            count = -(-own.shape[0] // wide)
            own = jnp.pad(own, (0, count * wide - own.shape[0])).reshape(count, wide)
            part = jnp.concatenate(
                [vgrad[0:5, cols], rows_sum[0:1, cols], jnp.zeros((2, wide), F32), flat, jnp.zeros((16 - flat.shape[0], wide), F32),
                 jnp.pad(per_head[some], ((0, 8 - share), (0, wide - LANES))), own], axis=0)
            parts.append(jnp.pad(part, ((0, small_rows - part.shape[0]), (0, 0))))
        c_live = reduce_pieces(parts)
    else:
        c_live = over_head(smalls[0], smalls[1])
    b_live = over_head(b_keep, after(b_send, gates))
    if plain:
        a_part = jnp.concatenate([halve(a_out), finish_head([a_gate[0], a_gate[1]])], axis=0)
    else:
        a_part = halve(a_live)
    a_keep_z, a_send_z = half_of(a_part, 2)
    if plain:
        b_whole = [jnp.concatenate([b, c], axis=0) for b, c in zip(b_live, c_live)]
        cut = b_whole[0].shape[0] // 2
        side_x = lax.axis_index("dp") & 1
        low, high = [v[:cut] for v in b_whole], jnp.stack([v[cut:] for v in b_whole])
        high = jnp.moveaxis(high.reshape(2, 2, cut // 2, wide), 1, 0)
        b_sends = low[1].astype(BF16), pick(high, 1 - side_x).astype(BF16)
    else:
        b_sends = ()
    a_got_z = swap(after(a_send_z, b_sends), "dp", 2)
    if plain:
        b_got = swap(b_sends[0], "head", 2), swap(b_sends[1], "dp", 1)
    mine = list(range(blocks))
    args = [scalars, hidden, halo, cotangent, gain_in, after(d_gate, b_sends, a_send_z), d_inner, d_state, d_step, hp, state_proj,
            *all_both]
    results = call(
        functools.partial(final_kernel, pieces, blocks, mine),
        [((rows, depth), F32), ((HALO, depth), F32), ((8, span), F32)],
        args,
        ins={at: hbm for at in (5, 6, *range(len(args) - pieces, len(args)))},
        out_specs={0: hbm},
        kinds={0: pltpu.HBM},
        scratch=[vmem((rows, depth), F32), pltpu.SemaphoreType.DMA((blocks,)), vmem((pieces, depth, 2 * span), BF16),
                 vmem((rows, total), BF16), vmem((ext, total), BF16), pltpu.SemaphoreType.DMA((2 + pieces,))],
        cost=9,
        mib=FINAL,
    )
    grad_hidden, extra, gain_part = results
    extra = lax.ppermute(extra, "head", [(i + 1, i) for i in range(ways - 1)])
    grad_hidden = grad_hidden.at[rows - HALO :].add(extra)
    if plain:
        one = low[0] + after(b_got[0], results).astype(F32)
        two = pick(high, side_x) + after(b_got[1], results).astype(F32)
        one_keep, one_send = half_of(one, 1)
        b_sends = one_send, two[1].astype(BF16)
        b_part = [one_keep + swap(one_send, "dp", 1).astype(F32), two[0] + swap(b_sends[1], "head", 2).astype(F32)]
        b_part = jnp.concatenate(b_part, axis=0)
    else:
        b_part = halve(jnp.concatenate([b_live, c_live], axis=0))
    gain_rows = gain_part[: depth // span].reshape(depth // wide, wide)
    b_part = jnp.concatenate([b_part, gain_rows, jnp.zeros((32 - gain_rows.shape[0], wide), F32)], axis=0)
    a_low = (a_keep_z + after(a_got_z, results).astype(F32)).astype(BF16)
    a_got_y = swap(a_low, "dp", 4)
    a_low = whole_dp((a_low.astype(F32) + after(a_got_y, b_sends).astype(F32)).astype(BF16))
    b_keep_z, b_send_z = half_of(b_part, 2)
    b_got_z = swap(after(b_send_z, a_low), "dp", 2)
    a_got_z = swap(a_low, "dp", 2)
    (mixed,) = call(
        functools.partial(mixed_kernel, pieces, blocks),
        [((rows, depth), BF16)],
        [scalars, hidden, after(ny, a_low, b_send_z), *all_outs],
        pin=jax.ShapeDtypeStruct,
        cost=4,
        mib=FINAL,
    )
    b_low = (b_keep_z + after(b_got_z, a_low, mixed).astype(F32)).astype(BF16)
    b_got_y = swap(b_low, "dp", 4)
    a_all = both_of(a_low, 2, a_got_z)
    a_other = swap(a_all, "dp", 1)
    b_low = whole_dp((b_low.astype(F32) + after(b_got_y, a_all).astype(F32)).astype(BF16))
    b_all = both_of(b_low, 2, swap(b_low, "dp", 2))

    def unhalve(value, cuts, other=None):
        upper = (lax.axis_index("dp") & 1) != 0
        other = swap(value, "dp", 1) if other is None else other
        rows_out, begin = [], 0
        for count in cuts:
            mine, his = value[begin : begin + count], other[begin : begin + count]
            rows_out.append(jnp.concatenate([jnp.where(upper, his, mine), jnp.where(upper, mine, his)], axis=0))
            begin += count
        return rows_out

    b_all = after(b_all, a_other)
    a_cuts = [depth // 2, depth // 2] if plain else [depth]
    a_out, a_gate = unhalve(a_all, a_cuts, a_other) if plain else jnp.split(unhalve(a_all, a_cuts, a_other)[0], 2)
    grad_out = a_out.T.astype(F32)
    grad_gate = a_gate.astype(F32)
    cut = b_all.shape[0] - 32 - 256
    *b_rows, gain_all = unhalve(b_all[cut:], [256, 32])
    b_rows = unhalve(b_all[:cut], [cut]) + b_rows
    if not plain:
        *b_rows, gain_all = unhalve(b_all, [cut + 256, 32])
    b_all = jnp.concatenate(b_rows, axis=0)
    gain_all = (gain_all[:32].astype(F32) + gain_all[32:].astype(F32))[: depth // wide].reshape(1, depth)
    gain_all = jnp.pad(gain_all.reshape(-1, side), ((0, 16 - depth // side), (0, 0)))
    grad_value = b_all[:depth].astype(F32)
    small = b_all[depth:].astype(F32)
    grad_step = jnp.concatenate([small[8 + j * share : 8 + (j + 1) * share].T for j in range(depth // wide)], axis=0)
    if plain:
        own = b_all[depth + 32 : depth + 32 + share_rows, :side]
    else:
        own = b_all[depth + 32 : depth + 240].reshape(-1)[: share_rows * side].reshape(share_rows, side)
    smaller = (grad_value, grad_step, small[0:4], small[4], small[5], *[small[24 : 24 + share, at] for at in range(3)])
    stacked, members = own, [0]
    for mask in reversed(order):
        members += [p | mask for p in members]
        gain_low = gain_all.astype(BF16)
        sent = jnp.concatenate([stacked, gain_low], axis=0)
        got = swap(after(sent, smaller if mask == 1 else (grad_out, grad_gate, grad_hidden)), "head", mask)
        stacked = jnp.concatenate([stacked, got[: stacked.shape[0]]], axis=0)
        gain_all = gain_low.astype(F32) + got[-16:].astype(F32)
    stacked = stacked.reshape(ways, share_rows, side)
    stacked = jnp.stack([stacked[members.index(p)] for p in range(ways)])
    full = jnp.concatenate([pick(stacked, me ^ q) for q in range(ways)], axis=0).astype(F32)
    return (
        mixed,
        grad_hidden,
        gain_all[: depth // side].reshape(-1),
        grad_gate,
        smaller[0],
        full[:depth],
        smaller[1],
        smaller[2],
        smaller[3],
        full[depth : depth + 4],
        full[depth + 4],
        smaller[5],
        smaller[6],
        smaller[7],
        smaller[4],
        grad_out,
    )


def solution(mesh):
    rows = P(("dp", "head"), None)
    in_specs = (
        rows, P("dp", None), P(), P(None, "head"), P(None, "head"), P(), P(None, "head"), P(None, "head"),
        P("head"), P(), P(), P("head"), P("head"), P("head"), P("head"), P("head", None), rows,
    )
    out_specs = (
        rows, rows, P(), P(None, "head"), P(None, "head"), P(), P(None, "head"), P(None, "head"),
        P("head"), P(), P(), P("head"), P("head"), P("head"), P("head"), P("head", None),
    )
    return jax.shard_map(body, mesh=mesh, in_specs=in_specs, out_specs=out_specs, check_vma=False)
```

```python
import functools

import jax
import jax.numpy as jnp
from jax import lax
from jax.experimental import pallas as pl
from jax.experimental.pallas import tpu as pltpu
from jax.sharding import PartitionSpec as P

K = 4
Q = 256
HALO = 16
LANES = 128
EPSILON = 1e-05
F32 = jnp.float32
BF16 = jnp.bfloat16
HIGHEST = lax.Precision.HIGHEST


def mm(left, right, lc=1, rc=0, precision=None):
    return lax.dot_general(
        left,
        right,
        (((lc,), (rc,)), ((), ())),
        preferred_element_type=F32,
        precision=precision,
    )


MIB = 1024 * 1024
PRE, FRONT, INTRA, MIDDLE, BACK, TAIL, STATE, FINAL = 12, 14, 12, 18, 56, 14, 12, 56


def whole(shape):
    return pl.BlockSpec(shape, lambda *_: (0,) * len(shape))


def call(kernel, outs, args, scratch=(), grid=(), ins=None, out_specs=None, aliases=None, mib=48, cost=0, pin=pltpu.VMEM, kinds=None):
    ins, out_specs, kinds = ins or {}, out_specs or {}, kinds or {}
    specs = [pl.BlockSpec(memory_space=pltpu.SMEM)]
    for at, value in enumerate(args[1:], 1):
        specs.append(ins[at] if at in ins else whole(value.shape))
    outs_specs = [out_specs[at] if at in out_specs else whole(o[0]) for at, o in enumerate(outs)]
    return pl.pallas_call(
        kernel,
        grid=grid,
        out_shape=[kinds[at](s, d) if at in kinds else pin(s, d) for at, (s, d) in enumerate(outs)],
        in_specs=specs,
        out_specs=outs_specs,
        scratch_shapes=list(scratch),
        input_output_aliases=aliases or {},
        compiler_params=pltpu.CompilerParams(vmem_limit_bytes=mib * MIB),
        cost_estimate=pl.CostEstimate(flops=int(cost * 4e8), bytes_accessed=int(cost * 3e5), transcendentals=0),
    )(*args)


def keeps_of(s_ref, block, blocks):
    place = s_ref[0] * blocks + block
    fresh = (place == 0) | (place == 1) | (place == s_ref[1] - 1)
    return fresh, jnp.where(fresh, 0.0, 1.0).astype(F32)


def row_keep(fresh, distance):
    rows = lax.broadcasted_iota(jnp.int32, (Q, 1), 0)
    return (rows >= jnp.where(fresh, distance, 0)).astype(F32)


def conv_block(ref, base, cols, taps, fresh):
    total = taps[K : K + 1] + taps[K - 1 : K] * ref[pl.ds(base, Q), cols]
    for distance in range(1, K):
        earlier = ref[pl.ds(base - distance, Q), cols]
        total = total + taps[K - 1 - distance : K - distance] * (earlier * row_keep(fresh, distance))
    return total


def silu_slope(values, sig):
    return sig * (1.0 + values * (1.0 - sig))


def first_lanes():
    return lax.broadcasted_iota(jnp.int32, (1, LANES), 1) < LANES // 2


def spread(cols, quantity):
    return jnp.where(
        first_lanes(), cols[:, 2 * quantity : 2 * quantity + 1], cols[:, 2 * quantity + 1 : 2 * quantity + 2]
    )


def head_lanes(rows, heads_first, head_size):
    lane = lax.broadcasted_iota(jnp.int32, rows, 1 if heads_first else 0)
    head = lax.broadcasted_iota(jnp.int32, rows, 0 if heads_first else 1)
    return (lane >= head * head_size) & (lane < (head + 1) * head_size)


def pre_kernel(blocks, s_ref, hid_ref, halo_ref, gain_ref, proj_ref, taps_ref,
               nx_ref, nt_ref, raw_ref, pre_ref, b_ref, c_ref, bt_ref, ct_ref, cb_ref, cbt_ref):
    gain = gain_ref[...]
    rows = blocks * Q

    def norm(v):
        v = v.astype(F32)
        return v * lax.rsqrt(jnp.mean(v * v, axis=1, keepdims=True) + EPSILON) * gain

    halo = norm(halo_ref[...])
    own = norm(hid_ref[...])
    nx_ref[0:HALO] = halo.astype(BF16)
    nx_ref[HALO:] = own.astype(BF16)
    nt_ref[:, 0:rows] = own.T.astype(BF16)
    raw_ref[...] = mm(nx_ref[...], proj_ref[...])
    taps = taps_ref[...]
    state = b_ref.shape[1]
    for block in range(blocks):
        fresh, _ = keeps_of(s_ref, block, blocks)
        pre = conv_block(raw_ref, HALO + block * Q, slice(None), taps, fresh)
        at = pl.ds(block * Q, Q)
        pre_ref[at] = pre
        conv = pre * jax.nn.sigmoid(pre)
        b_mat = conv[:, :state]
        c_mat = conv[:, state:]
        b_low = b_mat.astype(BF16)
        c_low = c_mat.astype(BF16)
        b_ref[at] = b_low
        c_ref[at] = c_low
        bt_ref[:, at] = b_mat.T.astype(BF16)
        ct_ref[:, at] = c_mat.T.astype(BF16)
        cb_ref[block] = mm(c_low, b_low, 1, 1)
        cbt_ref[block] = mm(b_low, c_low, 1, 1)


def step_kernel(blocks, head_size, s_ref, nx_ref, hp_ref, rowp_ref, colp_ref, step_ref, ratio_ref, sig_ref, chan_ref):
    depth = nx_ref.shape[1]
    hp = hp_ref[...]
    u = mm(hp[:, :depth].astype(BF16), nx_ref[HALO:], 1, 1) + hp[:, depth : depth + 1]
    step = jnp.maximum(u, 0.0) + jnp.log1p(jnp.exp(-jnp.abs(u)))
    sig = jax.nn.sigmoid(u)
    step_ref[...] = step
    sig_ref[...] = sig
    ratio_ref[...] = jnp.where(step > 1e-30, sig / jnp.maximum(step, 1e-30), 1.0)
    rate = -jnp.exp(hp[:, depth + 1 : depth + 2])
    move = step * rate
    upto = (
        lax.broadcasted_iota(jnp.int32, (Q, Q), 0) <= lax.broadcasted_iota(jnp.int32, (Q, Q), 1)
    ).astype(F32)
    heads = hp.shape[0]
    lane = lax.broadcasted_iota(jnp.int32, (heads, LANES), 1)
    last_cols = jnp.zeros((heads, LANES), F32)
    lstep = jnp.log(step)
    product = jnp.ones((heads, 1), F32)
    pairs = rowp_ref.shape[0]
    for block in range(blocks):
        at = slice(block * Q, (block + 1) * Q)
        logd = mm(move[:, at], upto, precision=HIGHEST)
        less = logd - lstep[:, at]
        last = logd[:, Q - 1 : Q]
        grown = jnp.exp(logd)
        carry = jnp.exp(last - less)
        final = jnp.exp(last)
        _, kept = keeps_of(s_ref, block, blocks)
        product = product * final * kept
        last_cols = jnp.where(lane == block, final, last_cols)
        for pair in range(pairs):
            for index, values in enumerate((logd, less, grown, carry)):
                rowp_ref[pair, 2 * index : 2 * index + 2, at] = values[2 * pair : 2 * pair + 2]
    last_cols = jnp.where(lane == 6, product, last_cols)
    last_cols = jnp.where(lane == 7, hp[:, depth + 2 : depth + 3], last_cols)
    spots = head_lanes((heads, chan_ref.shape[1]), True, head_size).astype(F32)
    chan_ref[...] = mm(last_cols.T[0:8], spots, precision=HIGHEST)
    for pair in range(0, pairs, 2):
        colp_ref[pair // 2] = jnp.concatenate([rowp_ref[pair], rowp_ref[pair + 1]], 0).T


def carry_block(ref, cols, carry, fades):
    state = carry.shape[0]
    ref[0:state, cols] = carry.astype(BF16)
    high = fades.astype(BF16).astype(F32)
    row = lax.broadcasted_iota(jnp.int32, (HALO, LANES), 0)
    ref[state:, cols] = jnp.where(row == 0, high, jnp.where(row == 1, fades - high, 0.0)).astype(BF16)


def tile_at(index):
    return pl.ds(pl.multiple_of(index * LANES, LANES), LANES)


def front_kernel(blocks, first_piece, pieces, s_ref, nx_ref, par_ref, bt_ref, colp_ref, chan_ref, *refs):
    weights = refs[:pieces]
    (gate_out, inner_out, pre_out, s_out, x_ref, carry_ref, turned_ref,
     gate_ref, inner_ref, pre_ref, st_ref, work, sems) = refs[-13:]
    done = refs[pieces:-13]
    wide = weights[0].shape[1] // 2
    for old, new in zip(done[4:], (x_ref, carry_ref, turned_ref)):
        new[:, 0 : first_piece * wide] = old[:, 0 : first_piece * wide]
    own = slice(first_piece * wide, (first_piece + pieces) * wide)
    moves = [(gate_ref, gate_out), (inner_ref, inner_out), (pre_ref, pre_out), (st_ref, s_out)]
    for p in range(pieces):
        here = slice(p * wide, (p + 1) * wide)
        work[:, here] = mm(nx_ref[...], weights[p][:, wide:])
        gate_ref[:, here] = mm(nx_ref[HALO:], weights[p][:, :wide]).astype(BF16)
    tiles = wide // LANES

    def tile(i, cols_of):
        here = tile_at(i)
        pair = i + first_piece * tiles
        far = tile_at(pair)
        turned = tile_at(jnp.bitwise_xor(pair // tiles, 1) * tiles + pair % tiles)
        taps = par_ref[:, far]
        inner_ref[:, here] = work[:, here].astype(BF16)
        for block in range(blocks):
            at = pl.ds(block * Q, Q)
            fresh, kept = keeps_of(s_ref, block, blocks)
            pre = conv_block(work, HALO + block * Q, here, taps, fresh)
            pre_ref[at, here] = pre.astype(BF16)
            x = pre * jax.nn.sigmoid(pre)
            x_ref[at, far] = x.astype(BF16)
            weighted = (spread(cols_of(at), 3) * x).astype(BF16)
            state = mm(bt_ref[:, at], weighted)
            st_ref[block, :, here] = state
            if block == 0:
                carry = state
            else:
                carry = chan_ref[block : block + 1, far] * (kept * carry) + state
        carry_block(carry_ref, far, carry, chan_ref[6:7, far])
        carry_block(turned_ref, turned, carry, chan_ref[6:7, far])
        for index, (held, out) in enumerate(moves):
            pltpu.make_async_copy(held.at[..., here], out.at[..., far], sems.at[index]).start()

    def turn(i, none):
        for k in range(2):
            tile(2 * i + k, lambda at, k=k: colp_ref[i + first_piece * tiles // 2, at, 8 * k : 8 * k + 8])
        return none

    lax.fori_loop(0, pieces * tiles // 2, turn, 0)
    for index, (held, out) in enumerate(moves):
        pltpu.make_async_copy(held, out.at[..., own], sems.at[index]).wait()


def unpack_carry(ref):
    state = ref.shape[0] - HALO
    fades = ref[state:].astype(F32)
    return ref[0:state].astype(F32), fades[0:1] + fades[1:2]


def join_kernel(forward, s_ref, own_ref, got_ref, out_ref):
    mine, my_fade = unpack_carry(own_ref)
    his, his_fade = unpack_carry(got_ref)
    later = (jnp.bitwise_and(s_ref[0], 1) == 1) == forward
    state = mine.shape[0]
    total = jnp.where(later, my_fade * his + mine, his_fade * mine + his)
    fade = my_fade * his_fade
    high = fade.astype(BF16).astype(F32)
    row = lax.broadcasted_iota(jnp.int32, (HALO, total.shape[1]), 0)
    out_ref[0:state] = total.astype(BF16)
    out_ref[state:] = jnp.where(row == 0, high, jnp.where(row == 1, fade - high, 0.0)).astype(BF16)


def arrive_kernel(forward, s_ref, near_ref, far_ref, out_ref):
    near, near_fade = unpack_carry(near_ref)
    wide = near.shape[1] // 2
    later = (jnp.bitwise_and(s_ref[0], 1) == 1) == forward
    far_later = (jnp.bitwise_and(s_ref[0], 2) == 2) == forward
    near = jnp.where(later, near, 0.0)
    fade = jnp.where(far_later, jnp.where(later, near_fade, 1.0), 0.0)
    for half in range(2):
        here, there = slice(half * wide, (half + 1) * wide), slice((1 - half) * wide, (2 - half) * wide)
        out_ref[:, here] = near[:, here] + fade[:, here] * far_ref[0 : near.shape[0], there].astype(F32)


def masked_cotangent(s_ref, cot_ref, blocks, block):
    at = slice(block * Q, (block + 1) * Q)
    return cot_ref[at].astype(F32) * valid_of(s_ref, blocks, block)


def masked_kernel(blocks, pieces, s_ref, cot_ref, *refs):
    outs_w = refs[:pieces]
    dny_ref, dbt_ref, db_ref = refs[pieces:]
    for block in range(blocks):
        at = slice(block * Q, (block + 1) * Q)
        masked = masked_cotangent(s_ref, cot_ref, blocks, block)
        db_ref[at] = masked.astype(BF16)
        dbt_ref[:, at] = masked.T.astype(BF16)
    wide = outs_w[0].shape[0]
    for p in range(pieces):
        dny_ref[:, p * wide : (p + 1) * wide] = mm(db_ref[...], outs_w[p][...], 1, 1).astype(BF16)


def intra_kernel(blocks, s_ref, rowp_ref, colp_ref, cb_ref, x_ref, y_ref):
    half = Q // 2
    first = first_lanes()
    tri = lax.broadcasted_iota(jnp.int32, (half, half), 0) >= lax.broadcasted_iota(
        jnp.int32, (half, half), 1
    )

    def work(i, k):
        pair = 2 * i + k
        far = tile_at(pair)
        for block in range(blocks):
            at = pl.ds(block * Q, Q)
            x = x_ref[at, far]
            both = [jnp.where(first, x, 0), jnp.where(first, 0, x)]
            rp = rowp_ref[pair, :, at]
            cp = colp_ref[i, at, 8 * k : 8 * k + 8]
            tops, bots = [], []
            for h in range(2):
                ld, ls = cp[:, h : h + 1], rp[2 + h : 3 + h, :]
                arg = jnp.where(tri, ld[:half] - ls[:, :half], -1e30)
                tops.append((cb_ref[block, 0:half, 0:half] * jnp.exp(arg)).astype(BF16))
                arg = ld[half:] - ls[:, :half]
                bots.append((cb_ref[block, half:, 0:half] * jnp.exp(arg)).astype(BF16))
                arg = jnp.where(tri, ld[half:] - ls[:, half:], -1e30)
                bots.append((cb_ref[block, half:, half:] * jnp.exp(arg)).astype(BF16))
            y_ref[pl.ds(block * Q, half), far] = mm(jnp.concatenate(tops, 1), jnp.concatenate([b[:half] for b in both], 0))
            y_ref[pl.ds(block * Q + half, half), far] = mm(jnp.concatenate(bots, 1), jnp.concatenate(both, 0))

    def two(i, none):
        work(i, 0)
        work(i, 1)
        return none

    lax.fori_loop(0, x_ref.shape[1] // (2 * LANES), two, 0)


def split_store(hi_ref, lo_ref, at, cols, part):
    high = part.astype(BF16)
    hi_ref[at, cols] = high
    lo_ref[at, cols] = (part - high.astype(F32)).astype(BF16)


def head_sums(heads, head_size, hi_ref, lo_ref):
    spots = head_lanes((heads, hi_ref.shape[1]), True, head_size).astype(F32).astype(BF16)
    return mm(spots, hi_ref[...], 1, 1) + mm(spots, lo_ref[...], 1, 1)


def valid_of(s_ref, blocks, block):
    place = s_ref[0] * blocks + block
    last = place == s_ref[1] - 1
    length = jnp.where(place == 0, s_ref[2], jnp.where(last, s_ref[4], s_ref[3]))
    start = jnp.where(place == 0, 0, jnp.where(last, s_ref[1] - 1, 1))
    rows = lax.broadcasted_iota(jnp.int32, (Q, 1), 0) + (place - start) * Q
    return (rows < length).astype(F32)


class Outbound:
    def __init__(self, held, sems, keep, send, tiles):
        self.held, self.sems, self.keep, self.send, self.tiles = held, sems, keep, send, tiles

    def wait(self, slot):
        for k in range(2):
            held = self.held.at[slot, :, k * LANES : (k + 1) * LANES]
            pltpu.make_async_copy(held, self.keep.at[0, :, 0:LANES], self.sems.at[slot, k]).wait()

    def start(self, turn, slot):
        for k in range(2):
            at = 2 * turn + k
            piece, lane = at // self.tiles, at % self.tiles
            held = self.held.at[slot, :, k * LANES : (k + 1) * LANES]
            cols = slice(lane * LANES, (lane + 1) * LANES) if isinstance(lane, int) else tile_at(lane)
            for odd, ref in enumerate((self.keep, self.send)):

                @pl.when(piece % 2 == odd)
                def _(ref=ref, held=held, piece=piece, cols=cols, k=k):
                    pltpu.make_async_copy(held, ref.at[piece // 2, :, cols], self.sems.at[slot, k]).start()


def turns_with_grads(turns, work, grads, out):
    def turn(i, none):
        before = jnp.maximum(i - 1, 0)
        slot = before % 2

        @pl.when(i >= 3)
        def _():
            out.wait(slot)

        grads(before, slot)
        work(i, 0)
        work(i, 1)

        @pl.when(i >= 1)
        def _():
            out.start(before, slot)

        return none

    lax.fori_loop(0, turns, turn, 0)
    last = turns - 1
    if last >= 2:
        out.wait(last % 2)
    grads(last, last % 2)
    out.start(jnp.int32(last), last % 2)
    for slot in range(min(2, turns)):
        out.wait(slot)


def middle_kernel(blocks, tiles, head_size, s_ref, dbt_ref, inc_in, colp_ref, chan_ref, par_ref, c_ref, ct_ref, nt_ref,
                  y_ref, dny_ref, gate_ref, x_ref, st_ref,
                  ny_out, dgate_out, keep_out, send_out, inc_out, di_out, dc_out, rowpart_out, rows_out,
                  dy_ref, carry_ref, turned_ref,
                  ny_ref, dgate_ref, inc_ref, di_ref, dc_ref, rowpart_ref, rows_ref, grad_ref,
                  mix_ref, sq_ref, cr_ref, hi_ref, lo_ref, sems, grad_sems):
    moves = [(ny_ref, ny_out), (dgate_ref, dgate_out), (inc_ref, inc_out), (di_ref, di_out), (dc_ref, dc_out), (rowpart_ref, rowpart_out), (rows_ref, rows_out)]

    def move(index, *where):
        held, out = moves[index]
        pltpu.make_async_copy(held.at[where], out.at[where], sems.at[index]).start()

    depth = dbt_ref.shape[0]
    total = chan_ref.shape[1]
    kept = [keeps_of(s_ref, block, blocks)[1] for block in range(blocks)]
    sq_ref[...] = jnp.zeros_like(sq_ref)
    cr_ref[...] = jnp.zeros_like(cr_ref)

    def forward(i, none):
        for k in range(2):
            far = tile_at(2 * i + k)
            incoming = inc_in[:, far]
            for block in range(blocks):
                at = pl.ds(block * Q, Q)
                incoming = kept[block] * incoming
                inc_low = incoming.astype(BF16)
                inc_ref[block, :, far] = inc_low
                incoming = chan_ref[block : block + 1, far] * incoming + st_ref[block, :, far]
                inter = mm(c_ref[at], inc_low) * spread(colp_ref[i, at, 8 * k : 8 * k + 8], 2)
                mix = y_ref[at, far] + inter + chan_ref[7:8, far] * x_ref[at, far].astype(F32)
                mix_ref[at, far] = mix
                gate = gate_ref[at, far].astype(F32)
                gated = mix * (gate * jax.nn.sigmoid(gate))
                sq_ref[at] += gated * gated
                cr_ref[at] += dny_ref[at, far].astype(F32) * par_ref[5:6, far] * gated
        return none

    lax.fori_loop(0, total // (2 * LANES), forward, 0)
    scale = lax.rsqrt(jnp.sum(sq_ref[...], axis=1, keepdims=True) / total + EPSILON)
    coef = scale * scale * scale * (jnp.sum(cr_ref[...], axis=1, keepdims=True) / total)
    sq_ref[...] = jnp.broadcast_to(scale, sq_ref.shape)
    cr_ref[...] = jnp.broadcast_to(coef, cr_ref.shape)
    rows_ref[...] = jnp.zeros_like(rows_ref)

    def backward(i, k):
        pair = 2 * i + k
        far = tile_at(pair)
        gain = par_ref[5:6, far]
        skip = chan_ref[7:8, far]
        gain_row = jnp.zeros((1, LANES), F32)
        skip_row = jnp.zeros((1, LANES), F32)
        dis = []
        for block in range(blocks):
            at = pl.ds(block * Q, Q)
            gate, mix, x = gate_ref[at, far].astype(F32), mix_ref[at, far], x_ref[at, far].astype(F32)
            sig = jax.nn.sigmoid(gate)
            act = gate * sig
            gated = mix * act
            normed = gated * sq_ref[at]
            dny = dny_ref[at, far].astype(F32)
            ny_ref[at, far] = (normed * gain).astype(BF16)
            gain_row += jnp.sum(dny * normed, axis=0, keepdims=True)
            d_gated = dny * gain * sq_ref[at] - gated * cr_ref[at]
            dgate_ref[at, far] = (d_gated * mix * silu_slope(gate, sig)).astype(BF16)
            dy = d_gated * act
            dy_low = dy.astype(BF16)
            dy_ref[at, far] = dy_low
            skip_row += jnp.sum(dy * x, axis=0, keepdims=True)
            split_store(hi_ref, lo_ref, at, far, dy_low.astype(F32) * (mix - skip * x))
            dye = (dy * spread(colp_ref[i, at, 8 * k : 8 * k + 8], 2)).astype(BF16)
            dc_ref[at] += mm(dye, inc_ref[block, :, far], 1, 1)
            di = mm(ct_ref[:, at], dye).astype(BF16)
            di_ref[block, :, far] = di
            dis.append(di.astype(F32))
        rows_ref[0:1, far] = gain_row
        rows_ref[1:2, far] = skip_row
        back = jnp.zeros_like(dis[0])
        for block in reversed(range(blocks)):
            back = kept[block] * (dis[block] + chan_ref[block : block + 1, far] * back)
        carry_block(carry_ref, far, back, chan_ref[6:7, far])
        turned = tile_at(jnp.bitwise_xor(pair // tiles, 1) * tiles + pair % tiles)
        carry_block(turned_ref, turned, back, chan_ref[6:7, far])
        move(0, slice(None), far)
        move(1, slice(None), far)

    def grads(turn, slot):
        cols = pl.ds(pl.multiple_of(turn * 2 * LANES, 2 * LANES), 2 * LANES)
        grad_ref[slot, 0:depth] = mm(dbt_ref[...], ny_ref[:, cols]).astype(BF16)
        grad_ref[slot, depth:] = mm(nt_ref[...], dgate_ref[:, cols]).astype(BF16)

    dc_ref[...] = jnp.zeros_like(dc_ref)
    turns_with_grads(total // (2 * LANES), backward, grads, Outbound(grad_ref, grad_sems, keep_out, send_out, tiles))
    for index in (2, 3, 4, 6):
        move(index)
    rowpart_ref[...] = head_sums(rowpart_ref.shape[0], head_size, hi_ref, lo_ref)
    move(5)
    for index, (held, out) in enumerate(moves):
        pltpu.make_async_copy(held, out, sems.at[index]).wait()


def back_kernel(blocks, head_size, s_ref, rowp_ref, colp_ref, cbt_ref, b_ref, c_ref, dy_ref, x_ref,
                dx_ref, part_ref, db_ref, dc_ref, acc_ref, hi_ref, lo_ref):
    half = Q // 2
    first = first_lanes()
    tri = lax.broadcasted_iota(jnp.int32, (half, half), 0) <= lax.broadcasted_iota(
        jnp.int32, (half, half), 1
    )
    acc_ref[...] = jnp.zeros_like(acc_ref)

    def two(i, none):
        for block in range(blocks):
            at = pl.ds(block * Q, Q)
            w00 = w01 = w11 = 0.0
            for k in range(2):
                pair = 2 * i + k
                far = tile_at(pair)
                x, dy = x_ref[at, far], dy_ref[at, far]
                dys = [jnp.where(first, dy, 0), jnp.where(first, 0, dy)]
                xs = [jnp.where(first, x, 0), jnp.where(first, 0, x)]
                rp = rowp_ref[pair, :, at]
                cp = colp_ref[i, at, 8 * k : 8 * k + 8]
                tops, bots = [], []
                for h in range(2):
                    ls, ld = cp[:, 2 + h : 3 + h], rp[h : h + 1, :]
                    ds_top = mm(xs[h][:half], dy, 1, 1)
                    ds_bot = mm(xs[h][half:], dy[half:], 1, 1)
                    e00 = jnp.exp(jnp.where(tri, ld[:, :half] - ls[:half], -1e30))
                    e01 = jnp.exp(ld[:, half:] - ls[:half])
                    e11 = jnp.exp(jnp.where(tri, ld[:, half:] - ls[half:], -1e30))
                    tops.append((cbt_ref[block, 0:half, 0:half] * e00).astype(BF16))
                    tops.append((cbt_ref[block, 0:half, half:] * e01).astype(BF16))
                    bots.append((cbt_ref[block, half:, half:] * e11).astype(BF16))
                    w00 += ds_top[:, :half] * e00
                    w01 += ds_top[:, half:] * e01
                    w11 += ds_bot * e11
                dx_top = mm(jnp.concatenate(tops, 1), jnp.concatenate(dys, 0))
                dx_bot = mm(jnp.concatenate(bots, 1), jnp.concatenate([d[half:] for d in dys], 0))
                dx = jnp.concatenate([dx_top, dx_bot], 0)
                dx_ref[at, far] = dx.astype(BF16)
                split_store(hi_ref, lo_ref, at, far, x.astype(F32) * dx)
            acc_ref[block, 0:half, 0:half] += w00
            acc_ref[block, 0:half, half:] += w01
            acc_ref[block, half:, half:] += w11
        return none

    lax.fori_loop(0, x_ref.shape[1] // (2 * LANES), two, 0)
    part_ref[...] = head_sums(part_ref.shape[0], head_size, hi_ref, lo_ref)
    for block in range(blocks):
        at = slice(block * Q, (block + 1) * Q)
        acc = acc_ref[block].astype(BF16)
        db_ref[at] = mm(acc, c_ref[at])
        dc_ref[at] = mm(acc, b_ref[at], 0, 0)


def conv_back(s_ref, blocks, work, taps, values_of, slope_of, store):
    sums = [0.0] * (K + 1)
    for block in range(blocks):
        fresh, _ = keeps_of(s_ref, block, blocks)
        d_pre = slope_of(block)
        work[0, pl.ds(HALO + block * Q, Q)] = d_pre
        sums[K] += jnp.sum(d_pre, axis=0, keepdims=True)
        sums[K - 1] += jnp.sum(d_pre * values_of(HALO + block * Q), axis=0, keepdims=True)
        for distance in range(1, K):
            held = d_pre * row_keep(fresh, distance)
            work[distance, pl.ds(HALO + block * Q, Q)] = held
            sums[K - 1 - distance] += jnp.sum(
                held * values_of(HALO + block * Q - distance), axis=0, keepdims=True
            )
    for begin, count in [(0, HALO)] + [(HALO + b * Q, Q) for b in range(blocks)]:
        out = taps[K - 1 : K] * work[0, pl.ds(begin, count)]
        for distance in range(1, K):
            out = out + taps[K - 1 - distance : K - distance] * work[distance, pl.ds(begin + distance, count)]
        store(begin, count, out.astype(BF16))
    return sums


def tail_kernel(blocks, tiles, head_size, s_ref, back_in, colp_ref, chan_ref, par_ref, b_ref, nt_ref, nx_ref,
                inc_ref, dx_ref, dy_ref, di_ref, x_ref, pre_ref, inner_ref,
                dinner_ref, vgrad_ref, part_ref, lasts_ref, db_ref, keep_out, send_out,
                d_ref, in_ref, hi_ref, lo_ref, grad_ref, grad_sems):
    total = chan_ref.shape[1]
    kept = [keeps_of(s_ref, block, blocks)[1] for block in range(blocks)]
    d_ref[...] = jnp.zeros_like(d_ref)
    vgrad_ref[...] = jnp.zeros_like(vgrad_ref)
    lasts_ref[...] = jnp.zeros_like(lasts_ref)
    db_ref[...] = jnp.zeros_like(db_ref)

    def work(i, k):
        far = tile_at(2 * i + k)
        in_ref[k] = inner_ref[:, far].astype(F32)
        skip = chan_ref[7:8, far]
        back = back_in[:, far]
        lasts, lows = [None] * blocks, [None] * blocks
        for block in reversed(range(blocks)):
            fade = chan_ref[block : block + 1, far]
            lows[block] = back.astype(BF16)
            lasts[block] = fade * jnp.sum(inc_ref[block, :, far].astype(F32) * back, axis=0, keepdims=True)
            back = kept[block] * (di_ref[block, :, far].astype(F32) + fade * back)

        def slope_of(block):
            at = pl.ds(block * Q, Q)
            carry = spread(colp_ref[i, at, 8 * k : 8 * k + 8], 3)
            weighted = carry * x_ref[at, far].astype(F32)
            db_ref[at] += mm(weighted.astype(BF16), lows[block], 1, 1)
            d_weighted = mm(b_ref[at], lows[block])
            moved = weighted * d_weighted
            lasts_ref[block : block + 1, far] = lasts[block] + jnp.sum(moved, axis=0, keepdims=True)
            split_store(hi_ref, lo_ref, at, far, moved)
            d_x = dx_ref[at, far].astype(F32) + carry * d_weighted + skip * dy_ref[at, far].astype(F32)
            pre = pre_ref[at, far].astype(F32)
            return d_x * silu_slope(pre, jax.nn.sigmoid(pre))

        def store(begin, count, value):
            dinner_ref[pl.ds(begin, count), far] = value

        sums = conv_back(
            s_ref, blocks, d_ref.at[k], par_ref[:, far], lambda at: in_ref[k, pl.ds(at, Q)], slope_of, store
        )
        for index in range(K + 1):
            vgrad_ref[index : index + 1, far] = sums[index]

    def grads(turn, slot):
        cols = pl.ds(pl.multiple_of(turn * 2 * LANES, 2 * LANES), 2 * LANES)
        grad = mm(nt_ref[...], dinner_ref[HALO:, cols]) + mm(nx_ref[0:HALO], dinner_ref[0:HALO, cols], 0, 0)
        grad_ref[slot] = grad.astype(BF16)

    turns_with_grads(total // (2 * LANES), work, grads, Outbound(grad_ref, grad_sems, keep_out, send_out, tiles))
    part_ref[...] = head_sums(part_ref.shape[0], head_size, hi_ref, lo_ref)


def state_kernel(blocks, head_size, shares, s_ref, dbx_ref, dbin_ref, dcin_ref, dcx_ref, raw_ref, spre_ref, staps_ref,
                 rowpart_ref, part_a, part_b, step_ref, ratio_ref, sig_ref, hp_ref, rows_ref, lasts_ref, vgrad_ref,
                 nt_ref, nx_ref, dstate_ref, dstep_ref, *refs):
    e_ref, all_ref, step_grad_ref = refs[-3:]
    outs = refs[:-3]
    e_ref[...] = jnp.zeros_like(e_ref)
    d_states = []
    for block in range(blocks):
        at = slice(block * Q, (block + 1) * Q)
        d_states.append(jnp.concatenate([dbin_ref[at] + dbx_ref[at], dcin_ref[at] + dcx_ref[at]], 1))

    def slope_of(block):
        pre = spre_ref[pl.ds(block * Q, Q), :]
        return d_states[block] * silu_slope(pre, jax.nn.sigmoid(pre))

    def store(begin, count, value):
        dstate_ref[pl.ds(begin, count), :] = value

    sgrad = conv_back(s_ref, blocks, e_ref, staps_ref[...], lambda at: raw_ref[pl.ds(at, Q), :], slope_of, store)
    heads = hp_ref.shape[0]
    total = lasts_ref.shape[1]
    depth = hp_ref.shape[1] - LANES
    spots = head_lanes((heads, total), True, head_size).astype(F32)
    lasts = mm(spots, lasts_ref[...], 1, 1, precision=HIGHEST)
    skips = mm(spots, rows_ref[...], 1, 1, precision=HIGHEST)[:, 1:2]
    rate = -jnp.exp(hp_ref[:, depth + 1 : depth + 2])
    lane = lax.broadcasted_iota(jnp.int32, (heads, Q), 1)
    upto = (
        lax.broadcasted_iota(jnp.int32, (Q, Q), 0) >= lax.broadcasted_iota(jnp.int32, (Q, Q), 1)
    ).astype(F32)
    grad_bias = jnp.zeros((heads, 1), F32)
    grad_decay = jnp.zeros((heads, 1), F32)
    for block in range(blocks):
        at = slice(block * Q, (block + 1) * Q)
        cols = part_a[:, at] + part_b[:, at]
        d_log = rowpart_ref[:, at] - cols + jnp.where(lane == Q - 1, lasts[:, block : block + 1], 0.0)
        d_move = mm(d_log, upto, precision=HIGHEST)
        d_raw = cols * ratio_ref[:, at] + rate * d_move * sig_ref[:, at]
        grad_bias += jnp.sum(d_raw, axis=1, keepdims=True)
        grad_decay += rate * jnp.sum(step_ref[:, at] * d_move, axis=1, keepdims=True)
        dstep_ref[:, at] = d_raw.astype(BF16)
    wide_lane = lax.broadcasted_iota(jnp.int32, (heads, LANES), 1)
    per_head = jnp.where(
        wide_lane == 0, grad_bias, jnp.where(wide_lane == 1, grad_decay, jnp.where(wide_lane == 2, skips, 0.0))
    )
    step_grad_ref[...] = mm(dstep_ref[...], nx_ref[HALO:])
    all_ref[...] = jnp.zeros_like(all_ref)
    all_ref[0:depth] = mm(nt_ref[...], dstate_ref[HALO:]) + mm(nx_ref[0:HALO], dstate_ref[0:HALO], 0, 0)
    for index in range(K + 1):
        all_ref[depth + index : depth + index + 1] = sgrad[index]
    if not shares:
        outs[0][...] = all_ref[...]
        outs[1][...] = step_grad_ref[...]
        outs[2][...] = per_head
        return
    ways, share, wide = shares
    quarter = all_ref.shape[0] // ways
    work = outs[-1]
    for p in range(ways):
        span = slice(p * wide, (p + 1) * wide)
        some = slice(p * share, (p + 1) * share)
        work[...] = jnp.zeros_like(work)
        work[0 : K + 1] = vgrad_ref[0 : K + 1, span]
        work[K + 1 : K + 2] = rows_ref[0:1, span]
        for part in range(depth // wide):
            begin = 8 + part * share
            work[begin : begin + share] = step_grad_ref[some, part * wide : (part + 1) * wide]
        work[24 : 24 + share, 0:LANES] = per_head[some]
        owner = jnp.bitwise_xor(s_ref[0], p)
        work[32 : 32 + quarter, 0 : all_ref.shape[1]] = all_ref[pl.ds(pl.multiple_of(owner * quarter, 8), quarter)]
        outs[p % 2][p // 2] = work[...].astype(BF16)


def mixed_kernel(pieces, blocks, s_ref, hid_ref, ny_ref, *refs):
    outs_w, mixed_ref = refs[:pieces], refs[pieces]
    wide = outs_w[0].shape[0]
    for block in range(blocks):
        at = slice(block * Q, (block + 1) * Q)
        branch = mm(ny_ref[at, 0:wide], outs_w[0][...])
        for p in range(1, pieces):
            branch += mm(ny_ref[at, p * wide : (p + 1) * wide], outs_w[p][...])
        mixed_ref[at] = (hid_ref[at].astype(F32) + valid_of(s_ref, blocks, block) * branch).astype(BF16)


def final_kernel(pieces, blocks, mine, s_ref, hid_ref, halo_ref, cot_ref, gain_ref, dgate_ref, dinner_ref,
                 dstate_ref, dstep_ref, hp_ref, sproj_ref, *refs):
    both_in = refs[:pieces]
    grad_out, extra_ref, gain_out, grad_ref, sems, both, dgate_here, dinner_here, in_sems = refs[-9:]
    wide = both.shape[2] // 2
    depth = hid_ref.shape[1]
    own = pl.ds(mine[0] * Q, len(mine) * Q)
    waits = [
        pltpu.make_async_copy(dinner_ref.at[pl.ds(mine[0] * Q, len(mine) * Q + HALO)], dinner_here, in_sems.at[0]),
        pltpu.make_async_copy(dgate_ref.at[own], dgate_here, in_sems.at[1]),
    ]
    for copy in waits:
        copy.start()
    loads = [pltpu.make_async_copy(both_in[p], both.at[p], in_sems.at[2 + p]) for p in range(pieces)]
    for copy in loads:
        copy.start()
    gain = gain_ref[...]
    gain_sum = jnp.zeros((1, depth), F32)

    def finish(values_in, d_normed):
        h = values_in.astype(F32)
        scale = lax.rsqrt(jnp.mean(h * h, axis=1, keepdims=True) + EPSILON)
        weighted = gain * d_normed
        inner = jnp.mean(weighted * h, axis=1, keepdims=True)
        return scale * weighted - h * (scale * scale * scale * inner), jnp.sum(d_normed * h * scale, axis=0, keepdims=True)

    moves = []
    totals = [mm(dstate_ref[0:HALO], sproj_ref[...], 1, 1)]
    for block in mine:
        ext = slice(HALO + block * Q, HALO + (block + 1) * Q)
        part = mm(dstate_ref[ext], sproj_ref[...], 1, 1)
        totals.append(part + mm(dstep_ref[:, block * Q : (block + 1) * Q], hp_ref[:, 0:depth].astype(BF16), 0, 0))
    for copy in waits:
        copy.wait()
    for p in range(pieces):
        loads[p].wait()
        span = slice(p * wide, (p + 1) * wide)
        if mine[0] == 0:
            totals[0] += mm(dinner_here[0:HALO, span], both[p, :, wide:], 1, 1)
        for index in range(len(mine)):
            here = slice(index * Q, (index + 1) * Q)
            ext = slice(HALO + index * Q, HALO + (index + 1) * Q)
            totals[index + 1] += mm(dgate_here[here, span], both[p, :, :wide], 1, 1)
            totals[index + 1] += mm(dinner_here[ext, span], both[p, :, wide:], 1, 1)
    if mine[0] == 0:
        extra_ref[...], part = finish(halo_ref[...], totals[0])
        gain_sum += part
    else:
        extra_ref[...] = jnp.zeros_like(extra_ref)
    for index, block in enumerate(mine):
        at = slice(block * Q, (block + 1) * Q)
        here = slice(index * Q, (index + 1) * Q)
        d_hidden, part = finish(hid_ref[at], totals[index + 1].astype(BF16).astype(F32))
        gain_sum += part
        grad_ref[here] = cot_ref[at].astype(F32) + d_hidden
        moves.append(pltpu.make_async_copy(grad_ref.at[here], grad_out.at[at], sems.at[index]))
        moves[-1].start()
    gain_out[...] = jnp.zeros_like(gain_out)
    side = gain_out.shape[1]
    for index in range(depth // side):
        gain_out[index : index + 1] = gain_sum[:, index * side : (index + 1) * side]
    for copy in moves:
        copy.wait()


def gather_far(value, ahead):
    ways = lax.axis_size("head")
    pieces = {0: value}
    far = {0: after(value, ahead)}
    mask = 2
    while mask < ways:
        for p in list(far):
            far[p | mask] = swap(far[p], "head", mask)
        mask *= 2
    return [value] + [far[p] for p in range(2, ways, 2)]


def near_pair(value, ahead):
    return value, swap(after(value, ahead) if len(ahead) else value, "head", 1)


def swap(value, axis, mask):
    size = lax.axis_size(axis)
    return lax.ppermute(value, axis, [(i, i ^ mask) for i in range(size)])


def pick(value, index):
    return lax.dynamic_index_in_dim(value, index, 0, keepdims=False)


def half_of(value, mask):
    side = jnp.where((lax.axis_index("dp") & mask) != 0, 1, 0)
    parts = value.reshape(2, value.shape[0] // 2, value.shape[1])
    return pick(parts, side).astype(F32), pick(parts, 1 - side).astype(BF16)


def whole_dp(low):
    for bit in range(3, lax.axis_size("dp").bit_length() - 1):
        low = (low.astype(F32) + swap(low, "dp", 1 << bit).astype(F32)).astype(BF16)
    return low


def both_of(low, mask, other):
    upper = (lax.axis_index("dp") & mask) != 0
    return jnp.concatenate([jnp.where(upper, other, low), jnp.where(upper, low, other)], axis=0)


def after(value, *others):
    return lax.optimization_barrier((value, others))[0]


def gather_pieces(value, ahead=()):
    ways = lax.axis_size("head")
    pieces = {0: value, 1: swap(value, "head", 1)}
    far = {0: after(value, ahead) if ahead else value}
    mask = 2
    while mask < ways:
        for p in list(far):
            far[p | mask] = swap(far[p], "head", mask)
        mask *= 2
    for p in far:
        if p:
            pieces[p] = far[p]
            pieces[p | 1] = swap(far[p], "head", 1)
    return [pieces[p] for p in range(ways)]


def reduce_pieces(pieces):
    ways = len(pieces)
    mask = 1
    live = {p: v for p, v in enumerate(pieces)}
    order = [1 << b for b in range(ways.bit_length() - 1)]
    for mask in order:
        got = {p ^ mask: swap(live[p].astype(BF16), "head", mask) for p in live if p & mask}
        live = {p: live[p].astype(F32) + got[p].astype(F32) for p in live if not p & mask}
    return live[0]


def body(hidden, lengths, norm_gain, gate_proj, value_proj, state_proj, step_proj, value_taps, value_bias,
         state_taps, state_bias, step_bias, decay_log, skip_gain, out_gain, out_proj, cotangent):
    rows, depth = hidden.shape
    ways = lax.axis_size("head")
    me = lax.axis_index("head")
    blocks = rows // Q
    wide = gate_proj.shape[1]
    share = step_proj.shape[1]
    total = wide * ways
    heads = share * ways
    head_size = wide // share
    pairs = heads // 2
    side = state_proj.shape[1]
    state = side // 2
    padded = -(-heads // 32) * 32
    plain = wide % LANES == 0
    order = [1 << b for b in range(ways.bit_length() - 1)]
    scalars = jnp.concatenate(
        [jnp.stack([me, blocks * ways]).astype(jnp.int32), lengths[0], jnp.zeros((3,), jnp.int32)]
    )

    top = jnp.concatenate(
        [step_proj.T.astype(F32), step_bias[:, None], decay_log[:, None], skip_gain[:, None], jnp.zeros((share, LANES - 3), F32)],
        axis=1,
    )
    low = jnp.concatenate([value_taps, value_bias[None], out_gain[None]], axis=0)
    pack = jnp.concatenate(
        [
            jnp.pad(top, ((0, 8 - share), (0, 0))),
            jnp.pad(low, ((0, 2), (0, depth + LANES - wide))),
            jnp.pad(hidden[rows - HALO :].astype(F32), ((0, 0), (0, LANES))),
        ],
        axis=0,
    )
    packs = gather_pieces(pack)
    halo = jnp.zeros((HALO, depth), F32)
    for p in range(1, ways):
        halo = jnp.where((me ^ p) == me - 1, packs[p][16:, :depth], halo)
    halo = halo.astype(BF16)
    both = gather_far(jnp.concatenate([gate_proj, value_proj], axis=1), (packs[1],))
    outs = gather_far(out_proj, (packs, both[0]))

    def both_merged(pair):
        if plain:
            return list(pair)
        a, b = pair
        return [jnp.concatenate([a[:, :wide], b[:, :wide], a[:, wide:], b[:, wide:]], axis=1)]

    def outs_merged(pair):
        return list(pair) if plain else [jnp.concatenate(pair, axis=0)]

    pieces = ways if plain else ways // 2
    span = total // pieces
    tiles = span // LANES
    hp = jnp.pad(jnp.concatenate([p[:share] for p in packs], axis=0), ((0, padded - heads), (0, 0)))
    par = jnp.concatenate([p[8:16, :wide] for p in packs], axis=1)
    gain_in = norm_gain[None]
    staps = jnp.pad(jnp.concatenate([state_taps, state_bias[None]], axis=0), ((0, 3), (0, 0)))

    ext = rows + HALO
    (nx, nt, state_raw, state_pre, b_low, c_low, b_t, c_t, cb, cbt) = call(
        functools.partial(pre_kernel, blocks),
        [((ext, depth), BF16), ((depth, rows), BF16), ((ext, side), F32), ((rows, side), F32),
         ((rows, state), BF16), ((rows, state), BF16), ((state, rows), BF16), ((state, rows), BF16),
         ((blocks, Q, Q), F32), ((blocks, Q, Q), F32)],
        [scalars, hidden, halo, gain_in, state_proj, staps],
        cost=2, mib=PRE,
    )
    rowp, colp, step, ratio, sig, chan = call(
        functools.partial(step_kernel, blocks, head_size),
        [((pairs, 8, rows), F32), ((pairs // 2, rows, 16), F32), ((padded, rows), F32), ((padded, rows), F32),
         ((padded, rows), F32), ((8, total), F32)],
        [scalars, nx, hp],
        cost=2,
        mib=PRE,
    )
    vmem = pltpu.VMEM
    hbm = pl.BlockSpec(memory_space=pltpu.HBM)
    front_outs = [((rows, total), BF16), ((ext, total), BF16), ((rows, total), BF16), ((blocks, state, total), F32),
                  ((rows, total), BF16), ((state + HALO, total), BF16), ((state + HALO, total), BF16)]
    fronts, all_both = [], []
    half = pieces // 2
    for begin in (0, half):
        pairs_of = range(begin // 2, begin // 2 + ways // 4) if plain else range(begin, begin + half)
        weights = [w for at in pairs_of for w in both_merged(near_pair(both[at], fronts))]
        all_both += weights
        args = [scalars, nx, par, b_t, colp, chan, *weights]
        aliases = {len(args) + at: at for at in range(len(fronts))}
        fronts = call(
            functools.partial(front_kernel, blocks, begin, half), front_outs, [*args, *fronts], aliases=aliases,
            ins={len(args) + at: hbm for at in range(min(4, len(fronts)))}, out_specs={at: hbm for at in range(4)},
            kinds={at: pltpu.HBM for at in range(4)},
            scratch=[vmem((rows, half * span), BF16), vmem((ext, half * span), BF16), vmem((rows, half * span), BF16),
                     vmem((blocks, state, half * span), F32), vmem((ext, half * span), F32), pltpu.SemaphoreType.DMA((4,))],
            cost=6, mib=FRONT,
        )
    gate, inner, pre, st, x, carry, carry_turned = fronts

    def turned(value, mask):
        parts = [value[..., (p ^ mask) * wide : ((p ^ mask) + 1) * wide] for p in range(ways)]
        return jnp.concatenate(parts, axis=-1)

    def scan(own, own_turned, forward, beside=lambda run: ()):
        def fade_of(value):
            return value[state : state + 1].astype(F32) + value[state + 1 : state + 2].astype(F32)

        if plain and ways == 4:
            near = swap(own_turned, "head", 1)
            (run,) = call(functools.partial(join_kernel, forward), [(own.shape, BF16)], [scalars, own, near], mib=8)
            far = swap(run, "head", 2)
            between = beside(run)
            far = after(far, between[1]) if between else far
            (result,) = call(functools.partial(arrive_kernel, forward), [((state, total), F32)], [scalars, near, far], mib=8)
            return result, between
        before = before_fade = None
        run = own
        for mask in order:
            if mask == 1 and plain:
                got = swap(own_turned, "head", 1)
            else:
                got = turned(swap(run, "head", mask), mask)
            got_fade, run_fade = fade_of(got), fade_of(run)
            got, mine = got[:state].astype(F32), run[:state].astype(F32)
            later = ((me & mask) != 0) if forward else ((me & mask) == 0)
            if before is None:
                before = jnp.where(later, got, 0.0)
                before_fade = jnp.where(later, got_fade, 1.0)
            else:
                before = jnp.where(later, before_fade * got + before, before)
                before_fade = jnp.where(later, before_fade * got_fade, before_fade)
            if mask != order[-1]:
                both_maps = jnp.where(later, run_fade * got + mine, got_fade * mine + got)
                fades = run_fade * got_fade
                high = fades.astype(BF16)
                low_part = (fades - high.astype(F32)).astype(BF16)
                run = jnp.concatenate(
                    [both_maps.astype(BF16), high, low_part, jnp.zeros((HALO - 2, total), BF16)], axis=0
                )
        return before, beside(run)

    def within(run):
        (y_intra,) = call(
            functools.partial(intra_kernel, blocks),
            [((rows, total), F32)],
            [scalars, rowp, colp, cb, after(x, run)],
            cost=5,
            mib=INTRA,
        )
        all_outs = [w for value in outs for w in outs_merged(near_pair(value, run))]
        dny, dbt = call(
            functools.partial(masked_kernel, blocks, pieces),
            [((rows, total), BF16), ((depth, rows), BF16)],
            [scalars, cotangent, *all_outs],
            scratch=[vmem((rows, depth), BF16)],
            cost=3,
            mib=INTRA,
        )
        return y_intra, dny, dbt, all_outs

    inc_in, (y_intra, dny, dbt, all_outs) = scan(carry, carry_turned, True, within)
    wide_bf = vmem((rows, total), BF16)
    held_outs = [((rows, total), BF16), ((rows, total), BF16),
                 ((pieces // 2, 2 * depth, span), BF16), ((pieces // 2, 2 * depth, span), BF16),
                 ((blocks, state, total), BF16), ((blocks, state, total), BF16), ((rows, state), F32),
                 ((padded, rows), F32), ((8, total), F32)]
    (ny, d_gate, a_keep, a_send, inc, d_inc, dc_inter, rowpart, rows_sum, d_y, back_carry, back_turned) = call(
        functools.partial(middle_kernel, blocks, tiles, head_size),
        [*held_outs, ((rows, total), BF16), ((state + HALO, total), BF16), ((state + HALO, total), BF16)],
        [scalars, dbt, inc_in, colp, chan, par, c_low, c_t, nt, y_intra, dny, gate, x, st],
        out_specs={at: hbm for at in range(len(held_outs))}, kinds={at: pltpu.HBM for at in range(len(held_outs))},
        scratch=[*[vmem(*o) for at, o in enumerate(held_outs) if at not in (2, 3)], vmem((2, 2 * depth, 2 * LANES), BF16), vmem((rows, total), F32), vmem((rows, LANES), F32),
                 vmem((rows, LANES), F32), wide_bf, wide_bf, pltpu.SemaphoreType.DMA((len(held_outs) - 2,)),
                 pltpu.SemaphoreType.DMA((2, 2))],
        cost=14, mib=MIDDLE,
    )
    back_runs = []
    back_in, _ = scan(back_carry, back_turned, False, lambda run: back_runs.append(run))

    def over_head(keep, send):
        if not plain:
            parts = [None] * ways
            for m in range(pieces):
                merged = (keep, send)[m % 2][m // 2]
                parts[2 * m], parts[2 * m + 1] = merged[:, :wide], merged[:, wide:]
            return reduce_pieces(parts)
        got = swap(send, "head", 1)
        live = [keep[i].astype(F32) + got[i].astype(F32) for i in range(pieces // 2)]
        return live

    def finish_head(live):
        if not plain:
            return live
        return live[0] + swap(live[1].astype(BF16), "head", 2).astype(F32)

    def halve(value, axis_at=0):
        side = lax.axis_index("dp") & 1
        cut = value.shape[:axis_at] + (2, value.shape[axis_at] // 2) + value.shape[axis_at + 1 :]
        parts = jnp.moveaxis(value.reshape(cut), axis_at, 0)
        got = swap(pick(parts, 1 - side).astype(BF16), "dp", 1)
        return pick(parts, side).astype(F32) + got.astype(F32)

    a_live = over_head(a_keep, after(a_send, *back_runs))
    if plain:
        a_out = finish_head([v[:depth] for v in a_live])
        a_gate = halve(jnp.stack([v[depth:] for v in a_live]), 1)
        gates = (a_out, a_gate)
    else:
        gates = a_live
    dx, part_a, db_in, dc_in = call(
        functools.partial(back_kernel, blocks, head_size),
        [((rows, total), BF16), ((padded, rows), F32), ((rows, state), F32), ((rows, state), F32)],
        [scalars, rowp, colp, cbt, b_low, c_low, d_y, x],
        scratch=[vmem((blocks, Q, Q), F32), wide_bf, wide_bf],
        cost=8,
        mib=BACK,
    )
    (d_inner, vgrad, part_b, lasts, db_x, b_keep, b_send) = call(
        functools.partial(tail_kernel, blocks, tiles, head_size),
        [((ext, total), BF16), ((8, total), F32), ((padded, rows), F32), ((8, total), F32), ((rows, state), F32),
         ((pieces // 2, depth, span), BF16), ((pieces // 2, depth, span), BF16)],
        [scalars, after(back_in, a_live), colp, chan, par, b_low, nt, nx, inc, dx, d_y, d_inc, x, pre, inner],
        out_specs={5: hbm, 6: hbm}, kinds={5: pltpu.HBM, 6: pltpu.HBM},
        scratch=[vmem((2, K, rows + 2 * HALO, LANES), F32), vmem((2, ext, LANES), F32), wide_bf, wide_bf,
                 vmem((2, depth, 2 * LANES), BF16), pltpu.SemaphoreType.DMA((2, 2))],
        cost=10, mib=TAIL,
    )
    small_rows, all_rows = 256, 832
    if plain:
        small_outs = [((pieces // 2, small_rows, span), BF16)] * 2
        shares = (ways, share, wide)
        work = [vmem((small_rows, span), F32)]
    else:
        small_outs = [((all_rows, side), F32), ((padded, depth), F32), ((padded, LANES), F32)]
        shares = None
        work = []
    d_state, d_step, *smalls = call(
        functools.partial(state_kernel, blocks, head_size, shares),
        [((ext, side), BF16), ((padded, rows), BF16)] + small_outs,
        [scalars, after(db_x, gates), db_in, dc_in, dc_inter, state_raw, state_pre, staps, rowpart, part_a, part_b, step, ratio, sig, hp,
         rows_sum, lasts, vgrad, nt, nx],
        scratch=work + [vmem((K, rows + 2 * HALO, side), F32), vmem((all_rows, side), F32), vmem((padded, depth), F32)],
        cost=4, mib=STATE,
    )
    share_rows = all_rows // ways
    if not plain:
        all_grad, step_grad, per_head = smalls
        parts = []
        for p in range(ways):
            cols, some = slice(p * wide, (p + 1) * wide), slice(p * share, (p + 1) * share)
            flat = step_grad[some].reshape(share, depth // wide, wide).swapaxes(0, 1).reshape(-1, wide)
            own = lax.dynamic_slice_in_dim(all_grad, (me ^ p) * share_rows, share_rows, 0).reshape(-1)
            count = -(-own.shape[0] // wide)
            own = jnp.pad(own, (0, count * wide - own.shape[0])).reshape(count, wide)
            part = jnp.concatenate(
                [vgrad[0:5, cols], rows_sum[0:1, cols], jnp.zeros((2, wide), F32), flat, jnp.zeros((16 - flat.shape[0], wide), F32),
                 jnp.pad(per_head[some], ((0, 8 - share), (0, wide - LANES))), own], axis=0)
            parts.append(jnp.pad(part, ((0, small_rows - part.shape[0]), (0, 0))))
        c_live = reduce_pieces(parts)
    else:
        c_live = over_head(smalls[0], smalls[1])
    b_live = over_head(b_keep, after(b_send, gates))
    if plain:
        a_part = jnp.concatenate([halve(a_out), finish_head([a_gate[0], a_gate[1]])], axis=0)
    else:
        a_part = halve(a_live)
    a_keep_z, a_send_z = half_of(a_part, 2)
    if plain:
        b_whole = [jnp.concatenate([b, c], axis=0) for b, c in zip(b_live, c_live)]
        cut = b_whole[0].shape[0] // 2
        side_x = lax.axis_index("dp") & 1
        low, high = [v[:cut] for v in b_whole], jnp.stack([v[cut:] for v in b_whole])
        high = jnp.moveaxis(high.reshape(2, 2, cut // 2, wide), 1, 0)
        b_sends = low[1].astype(BF16), pick(high, 1 - side_x).astype(BF16)
    else:
        b_sends = ()
    a_got_z = swap(after(a_send_z, b_sends), "dp", 2)
    if plain:
        b_got = swap(b_sends[0], "head", 2), swap(b_sends[1], "dp", 1)
    mine = list(range(blocks))
    args = [scalars, hidden, halo, cotangent, gain_in, after(d_gate, b_sends, a_send_z), d_inner, d_state, d_step, hp, state_proj,
            *all_both]
    results = call(
        functools.partial(final_kernel, pieces, blocks, mine),
        [((rows, depth), F32), ((HALO, depth), F32), ((8, span), F32)],
        args,
        ins={at: hbm for at in (5, 6, *range(len(args) - pieces, len(args)))},
        out_specs={0: hbm},
        kinds={0: pltpu.HBM},
        scratch=[vmem((rows, depth), F32), pltpu.SemaphoreType.DMA((blocks,)), vmem((pieces, depth, 2 * span), BF16),
                 vmem((rows, total), BF16), vmem((ext, total), BF16), pltpu.SemaphoreType.DMA((2 + pieces,))],
        cost=9,
        mib=FINAL,
    )
    grad_hidden, extra, gain_part = results
    extra = lax.ppermute(extra, "head", [(i + 1, i) for i in range(ways - 1)])
    grad_hidden = grad_hidden.at[rows - HALO :].add(extra)
    if plain:
        one = low[0] + after(b_got[0], results).astype(F32)
        two = pick(high, side_x) + after(b_got[1], results).astype(F32)
        one_keep, one_send = half_of(one, 1)
        b_sends = one_send, two[1].astype(BF16)
        b_part = [one_keep + swap(one_send, "dp", 1).astype(F32), two[0] + swap(b_sends[1], "head", 2).astype(F32)]
        b_part = jnp.concatenate(b_part, axis=0)
    else:
        b_part = halve(jnp.concatenate([b_live, c_live], axis=0))
    gain_rows = gain_part[: depth // span].reshape(depth // wide, wide)
    b_part = jnp.concatenate([b_part, gain_rows, jnp.zeros((32 - gain_rows.shape[0], wide), F32)], axis=0)
    a_low = (a_keep_z + after(a_got_z, results).astype(F32)).astype(BF16)
    a_got_y = swap(a_low, "dp", 4)
    a_low = whole_dp((a_low.astype(F32) + after(a_got_y, b_sends).astype(F32)).astype(BF16))
    b_keep_z, b_send_z = half_of(b_part, 2)
    b_got_z = swap(after(b_send_z, a_low), "dp", 2)
    a_got_z = swap(a_low, "dp", 2)
    (mixed,) = call(
        functools.partial(mixed_kernel, pieces, blocks),
        [((rows, depth), BF16)],
        [scalars, hidden, after(ny, a_low, b_send_z), *all_outs],
        pin=jax.ShapeDtypeStruct,
        cost=4,
        mib=FINAL,
    )
    b_low = (b_keep_z + after(b_got_z, a_low, mixed).astype(F32)).astype(BF16)
    b_got_y = swap(b_low, "dp", 4)
    a_all = both_of(a_low, 2, a_got_z)
    a_other = swap(a_all, "dp", 1)
    b_low = whole_dp((b_low.astype(F32) + after(b_got_y, a_all).astype(F32)).astype(BF16))
    b_all = both_of(b_low, 2, swap(b_low, "dp", 2))

    def unhalve(value, cuts, other=None):
        upper = (lax.axis_index("dp") & 1) != 0
        other = swap(value, "dp", 1) if other is None else other
        rows_out, begin = [], 0
        for count in cuts:
            mine, his = value[begin : begin + count], other[begin : begin + count]
            rows_out.append(jnp.concatenate([jnp.where(upper, his, mine), jnp.where(upper, mine, his)], axis=0))
            begin += count
        return rows_out

    b_all = after(b_all, a_other)
    a_cuts = [depth // 2, depth // 2] if plain else [depth]
    a_out, a_gate = unhalve(a_all, a_cuts, a_other) if plain else jnp.split(unhalve(a_all, a_cuts, a_other)[0], 2)
    grad_out = a_out.T.astype(F32)
    grad_gate = a_gate.astype(F32)
    cut = b_all.shape[0] - 32 - 256
    *b_rows, gain_all = unhalve(b_all[cut:], [256, 32])
    if plain:
        begin = depth + 32 - 2 * cut
        own_rows = b_rows[-1][begin : begin + share_rows, :side]
        b_rows = unhalve(b_all[:cut], [cut], after(swap(b_all[:cut], "dp", 1), own_rows)) + b_rows
    else:
        b_rows = unhalve(b_all[:cut], [cut]) + b_rows
    if not plain:
        *b_rows, gain_all = unhalve(b_all, [cut + 256, 32])
    b_all = jnp.concatenate(b_rows, axis=0)
    gain_all = (gain_all[:32].astype(F32) + gain_all[32:].astype(F32))[: depth // wide].reshape(1, depth)
    gain_all = jnp.pad(gain_all.reshape(-1, side), ((0, 16 - depth // side), (0, 0)))
    grad_value = b_all[:depth].astype(F32)
    small = b_all[depth:].astype(F32)
    grad_step = jnp.concatenate([small[8 + j * share : 8 + (j + 1) * share].T for j in range(depth // wide)], axis=0)
    if plain:
        own = own_rows
    else:
        own = b_all[depth + 32 : depth + 240].reshape(-1)[: share_rows * side].reshape(share_rows, side)
    smaller = (grad_value, grad_step, small[0:4], small[4], small[5], *[small[24 : 24 + share, at] for at in range(3)])
    stacked, members = own, [0]
    for mask in reversed(order):
        members += [p | mask for p in members]
        gain_low = gain_all.astype(BF16)
        sent = jnp.concatenate([stacked, gain_low], axis=0)
        got = swap(after(sent, smaller if mask == 1 else (grad_out, grad_gate, grad_hidden)), "head", mask)
        stacked = jnp.concatenate([stacked, got[: stacked.shape[0]]], axis=0)
        gain_all = gain_low.astype(F32) + got[-16:].astype(F32)
    stacked = stacked.reshape(ways, share_rows, side)
    stacked = jnp.stack([stacked[members.index(p)] for p in range(ways)])
    full = jnp.concatenate([pick(stacked, me ^ q) for q in range(ways)], axis=0).astype(F32)
    return (
        mixed,
        grad_hidden,
        gain_all[: depth // side].reshape(-1),
        grad_gate,
        smaller[0],
        full[:depth],
        smaller[1],
        smaller[2],
        smaller[3],
        full[depth : depth + 4],
        full[depth + 4],
        smaller[5],
        smaller[6],
        smaller[7],
        smaller[4],
        grad_out,
    )


def solution(mesh):
    rows = P(("dp", "head"), None)
    in_specs = (
        rows, P("dp", None), P(), P(None, "head"), P(None, "head"), P(), P(None, "head"), P(None, "head"),
        P("head"), P(), P(), P("head"), P("head"), P("head"), P("head"), P("head", None), rows,
    )
    out_specs = (
        rows, rows, P(), P(None, "head"), P(None, "head"), P(), P(None, "head"), P(None, "head"),
        P("head"), P(), P(), P("head"), P("head"), P("head"), P("head"), P("head", None),
    )
    return jax.shard_map(body, mesh=mesh, in_specs=in_specs, out_specs=out_specs, check_vma=False)
```

```python
import functools

import jax
import jax.numpy as jnp
from jax import lax
from jax.experimental import pallas as pl
from jax.experimental.pallas import tpu as pltpu
from jax.sharding import PartitionSpec as P

K = 4
Q = 256
HALO = 16
LANES = 128
EPSILON = 1e-05
F32 = jnp.float32
BF16 = jnp.bfloat16
HIGHEST = lax.Precision.HIGHEST


def mm(left, right, lc=1, rc=0, precision=None):
    return lax.dot_general(
        left,
        right,
        (((lc,), (rc,)), ((), ())),
        preferred_element_type=F32,
        precision=precision,
    )


MIB = 1024 * 1024
PRE, FRONT, INTRA, MIDDLE, BACK, TAIL, STATE, FINAL = 12, 14, 12, 18, 56, 14, 12, 56


def whole(shape):
    return pl.BlockSpec(shape, lambda *_: (0,) * len(shape))


def call(kernel, outs, args, scratch=(), grid=(), ins=None, out_specs=None, aliases=None, mib=48, cost=0, pin=pltpu.VMEM, kinds=None):
    ins, out_specs, kinds = ins or {}, out_specs or {}, kinds or {}
    specs = [pl.BlockSpec(memory_space=pltpu.SMEM)]
    for at, value in enumerate(args[1:], 1):
        specs.append(ins[at] if at in ins else whole(value.shape))
    outs_specs = [out_specs[at] if at in out_specs else whole(o[0]) for at, o in enumerate(outs)]
    return pl.pallas_call(
        kernel,
        grid=grid,
        out_shape=[kinds[at](s, d) if at in kinds else pin(s, d) for at, (s, d) in enumerate(outs)],
        in_specs=specs,
        out_specs=outs_specs,
        scratch_shapes=list(scratch),
        input_output_aliases=aliases or {},
        compiler_params=pltpu.CompilerParams(vmem_limit_bytes=mib * MIB),
        cost_estimate=pl.CostEstimate(flops=int(cost * 4e8), bytes_accessed=int(cost * 3e5), transcendentals=0),
    )(*args)


def keeps_of(s_ref, block, blocks):
    place = s_ref[0] * blocks + block
    fresh = (place == 0) | (place == 1) | (place == s_ref[1] - 1)
    return fresh, jnp.where(fresh, 0.0, 1.0).astype(F32)


def row_keep(fresh, distance):
    rows = lax.broadcasted_iota(jnp.int32, (Q, 1), 0)
    return (rows >= jnp.where(fresh, distance, 0)).astype(F32)


def conv_block(ref, base, cols, taps, fresh):
    total = taps[K : K + 1] + taps[K - 1 : K] * ref[pl.ds(base, Q), cols]
    for distance in range(1, K):
        earlier = ref[pl.ds(base - distance, Q), cols]
        total = total + taps[K - 1 - distance : K - distance] * (earlier * row_keep(fresh, distance))
    return total


def silu_slope(values, sig):
    return sig * (1.0 + values * (1.0 - sig))


def first_lanes():
    return lax.broadcasted_iota(jnp.int32, (1, LANES), 1) < LANES // 2


def spread(cols, quantity):
    return jnp.where(
        first_lanes(), cols[:, 2 * quantity : 2 * quantity + 1], cols[:, 2 * quantity + 1 : 2 * quantity + 2]
    )


def head_lanes(rows, heads_first, head_size):
    lane = lax.broadcasted_iota(jnp.int32, rows, 1 if heads_first else 0)
    head = lax.broadcasted_iota(jnp.int32, rows, 0 if heads_first else 1)
    return (lane >= head * head_size) & (lane < (head + 1) * head_size)


def pre_kernel(blocks, s_ref, hid_ref, halo_ref, gain_ref, proj_ref, taps_ref,
               nx_ref, nt_ref, raw_ref, pre_ref, b_ref, c_ref, bt_ref, ct_ref, cb_ref, cbt_ref):
    gain = gain_ref[...]
    rows = blocks * Q

    def norm(v):
        v = v.astype(F32)
        return v * lax.rsqrt(jnp.mean(v * v, axis=1, keepdims=True) + EPSILON) * gain

    halo = norm(halo_ref[...])
    own = norm(hid_ref[...])
    nx_ref[0:HALO] = halo.astype(BF16)
    nx_ref[HALO:] = own.astype(BF16)
    nt_ref[:, 0:rows] = own.T.astype(BF16)
    raw_ref[...] = mm(nx_ref[...], proj_ref[...])
    taps = taps_ref[...]
    state = b_ref.shape[1]
    for block in range(blocks):
        fresh, _ = keeps_of(s_ref, block, blocks)
        pre = conv_block(raw_ref, HALO + block * Q, slice(None), taps, fresh)
        at = pl.ds(block * Q, Q)
        pre_ref[at] = pre
        conv = pre * jax.nn.sigmoid(pre)
        b_mat = conv[:, :state]
        c_mat = conv[:, state:]
        b_low = b_mat.astype(BF16)
        c_low = c_mat.astype(BF16)
        b_ref[at] = b_low
        c_ref[at] = c_low
        bt_ref[:, at] = b_mat.T.astype(BF16)
        ct_ref[:, at] = c_mat.T.astype(BF16)
        cb_ref[block] = mm(c_low, b_low, 1, 1)
        cbt_ref[block] = mm(b_low, c_low, 1, 1)


def step_kernel(blocks, head_size, s_ref, nx_ref, hp_ref, rowp_ref, colp_ref, step_ref, ratio_ref, sig_ref, chan_ref):
    depth = nx_ref.shape[1]
    hp = hp_ref[...]
    u = mm(hp[:, :depth].astype(BF16), nx_ref[HALO:], 1, 1) + hp[:, depth : depth + 1]
    step = jnp.maximum(u, 0.0) + jnp.log1p(jnp.exp(-jnp.abs(u)))
    sig = jax.nn.sigmoid(u)
    step_ref[...] = step
    sig_ref[...] = sig
    ratio_ref[...] = jnp.where(step > 1e-30, sig / jnp.maximum(step, 1e-30), 1.0)
    rate = -jnp.exp(hp[:, depth + 1 : depth + 2])
    move = step * rate
    upto = (
        lax.broadcasted_iota(jnp.int32, (Q, Q), 0) <= lax.broadcasted_iota(jnp.int32, (Q, Q), 1)
    ).astype(F32)
    heads = hp.shape[0]
    lane = lax.broadcasted_iota(jnp.int32, (heads, LANES), 1)
    last_cols = jnp.zeros((heads, LANES), F32)
    lstep = jnp.log(step)
    product = jnp.ones((heads, 1), F32)
    pairs = rowp_ref.shape[0]
    for block in range(blocks):
        at = slice(block * Q, (block + 1) * Q)
        logd = mm(move[:, at], upto, precision=HIGHEST)
        less = logd - lstep[:, at]
        last = logd[:, Q - 1 : Q]
        grown = jnp.exp(logd)
        carry = jnp.exp(last - less)
        final = jnp.exp(last)
        _, kept = keeps_of(s_ref, block, blocks)
        product = product * final * kept
        last_cols = jnp.where(lane == block, final, last_cols)
        for pair in range(pairs):
            for index, values in enumerate((logd, less, grown, carry)):
                rowp_ref[pair, 2 * index : 2 * index + 2, at] = values[2 * pair : 2 * pair + 2]
    last_cols = jnp.where(lane == 6, product, last_cols)
    last_cols = jnp.where(lane == 7, hp[:, depth + 2 : depth + 3], last_cols)
    spots = head_lanes((heads, chan_ref.shape[1]), True, head_size).astype(F32)
    chan_ref[...] = mm(last_cols.T[0:8], spots, precision=HIGHEST)
    for pair in range(0, pairs, 2):
        colp_ref[pair // 2] = jnp.concatenate([rowp_ref[pair], rowp_ref[pair + 1]], 0).T


def carry_block(ref, cols, carry, fades):
    state = carry.shape[0]
    ref[0:state, cols] = carry.astype(BF16)
    high = fades.astype(BF16).astype(F32)
    row = lax.broadcasted_iota(jnp.int32, (HALO, LANES), 0)
    ref[state:, cols] = jnp.where(row == 0, high, jnp.where(row == 1, fades - high, 0.0)).astype(BF16)


def tile_at(index):
    return pl.ds(pl.multiple_of(index * LANES, LANES), LANES)


def front_kernel(blocks, first_piece, pieces, s_ref, nx_ref, par_ref, bt_ref, colp_ref, chan_ref, *refs):
    weights = refs[:pieces]
    (gate_out, inner_out, pre_out, s_out, x_ref, carry_ref, turned_ref,
     gate_ref, inner_ref, pre_ref, st_ref, work, sems) = refs[-13:]
    done = refs[pieces:-13]
    wide = weights[0].shape[1] // 2
    for old, new in zip(done[4:], (x_ref, carry_ref, turned_ref)):
        new[:, 0 : first_piece * wide] = old[:, 0 : first_piece * wide]
    own = slice(first_piece * wide, (first_piece + pieces) * wide)
    moves = [(gate_ref, gate_out), (inner_ref, inner_out), (pre_ref, pre_out), (st_ref, s_out)]
    for p in range(pieces):
        here = slice(p * wide, (p + 1) * wide)
        work[:, here] = mm(nx_ref[...], weights[p][:, wide:])
        gate_ref[:, here] = mm(nx_ref[HALO:], weights[p][:, :wide]).astype(BF16)
    tiles = wide // LANES

    def tile(i, cols_of):
        here = tile_at(i)
        pair = i + first_piece * tiles
        far = tile_at(pair)
        turned = tile_at(jnp.bitwise_xor(pair // tiles, 1) * tiles + pair % tiles)
        taps = par_ref[:, far]
        inner_ref[:, here] = work[:, here].astype(BF16)
        for block in range(blocks):
            at = pl.ds(block * Q, Q)
            fresh, kept = keeps_of(s_ref, block, blocks)
            pre = conv_block(work, HALO + block * Q, here, taps, fresh)
            pre_ref[at, here] = pre.astype(BF16)
            x = pre * jax.nn.sigmoid(pre)
            x_ref[at, far] = x.astype(BF16)
            weighted = (spread(cols_of(at), 3) * x).astype(BF16)
            state = mm(bt_ref[:, at], weighted)
            st_ref[block, :, here] = state
            if block == 0:
                carry = state
            else:
                carry = chan_ref[block : block + 1, far] * (kept * carry) + state
        carry_block(carry_ref, far, carry, chan_ref[6:7, far])
        carry_block(turned_ref, turned, carry, chan_ref[6:7, far])
        for index, (held, out) in enumerate(moves):
            pltpu.make_async_copy(held.at[..., here], out.at[..., far], sems.at[index]).start()

    def turn(i, none):
        for k in range(2):
            tile(2 * i + k, lambda at, k=k: colp_ref[i + first_piece * tiles // 2, at, 8 * k : 8 * k + 8])
        return none

    lax.fori_loop(0, pieces * tiles // 2, turn, 0)
    for index, (held, out) in enumerate(moves):
        pltpu.make_async_copy(held, out.at[..., own], sems.at[index]).wait()


def unpack_carry(ref):
    state = ref.shape[0] - HALO
    fades = ref[state:].astype(F32)
    return ref[0:state].astype(F32), fades[0:1] + fades[1:2]


def join_kernel(forward, s_ref, own_ref, got_ref, out_ref):
    mine, my_fade = unpack_carry(own_ref)
    his, his_fade = unpack_carry(got_ref)
    later = (jnp.bitwise_and(s_ref[0], 1) == 1) == forward
    state = mine.shape[0]
    total = jnp.where(later, my_fade * his + mine, his_fade * mine + his)
    fade = my_fade * his_fade
    high = fade.astype(BF16).astype(F32)
    row = lax.broadcasted_iota(jnp.int32, (HALO, total.shape[1]), 0)
    out_ref[0:state] = total.astype(BF16)
    out_ref[state:] = jnp.where(row == 0, high, jnp.where(row == 1, fade - high, 0.0)).astype(BF16)


def arrive_kernel(forward, s_ref, near_ref, far_ref, out_ref):
    near, near_fade = unpack_carry(near_ref)
    wide = near.shape[1] // 2
    later = (jnp.bitwise_and(s_ref[0], 1) == 1) == forward
    far_later = (jnp.bitwise_and(s_ref[0], 2) == 2) == forward
    near = jnp.where(later, near, 0.0)
    fade = jnp.where(far_later, jnp.where(later, near_fade, 1.0), 0.0)
    for half in range(2):
        here, there = slice(half * wide, (half + 1) * wide), slice((1 - half) * wide, (2 - half) * wide)
        out_ref[:, here] = near[:, here] + fade[:, here] * far_ref[0 : near.shape[0], there].astype(F32)


def masked_cotangent(s_ref, cot_ref, blocks, block):
    at = slice(block * Q, (block + 1) * Q)
    return cot_ref[at].astype(F32) * valid_of(s_ref, blocks, block)


def masked_kernel(blocks, pieces, s_ref, cot_ref, *refs):
    outs_w = refs[:pieces]
    dny_ref, dbt_ref, db_ref = refs[pieces:]
    for block in range(blocks):
        at = slice(block * Q, (block + 1) * Q)
        masked = masked_cotangent(s_ref, cot_ref, blocks, block)
        db_ref[at] = masked.astype(BF16)
        dbt_ref[:, at] = masked.T.astype(BF16)
    wide = outs_w[0].shape[0]
    for p in range(pieces):
        dny_ref[:, p * wide : (p + 1) * wide] = mm(db_ref[...], outs_w[p][...], 1, 1).astype(BF16)


def intra_kernel(blocks, s_ref, rowp_ref, colp_ref, cb_ref, x_ref, y_ref):
    half = Q // 2
    first = first_lanes()
    tri = lax.broadcasted_iota(jnp.int32, (half, half), 0) >= lax.broadcasted_iota(
        jnp.int32, (half, half), 1
    )

    def work(i, k):
        pair = 2 * i + k
        far = tile_at(pair)
        for block in range(blocks):
            at = pl.ds(block * Q, Q)
            x = x_ref[at, far]
            both = [jnp.where(first, x, 0), jnp.where(first, 0, x)]
            rp = rowp_ref[pair, :, at]
            cp = colp_ref[i, at, 8 * k : 8 * k + 8]
            tops, bots = [], []
            for h in range(2):
                ld, ls = cp[:, h : h + 1], rp[2 + h : 3 + h, :]
                arg = jnp.where(tri, ld[:half] - ls[:, :half], -1e30)
                tops.append((cb_ref[block, 0:half, 0:half] * jnp.exp(arg)).astype(BF16))
                arg = ld[half:] - ls[:, :half]
                bots.append((cb_ref[block, half:, 0:half] * jnp.exp(arg)).astype(BF16))
                arg = jnp.where(tri, ld[half:] - ls[:, half:], -1e30)
                bots.append((cb_ref[block, half:, half:] * jnp.exp(arg)).astype(BF16))
            y_ref[pl.ds(block * Q, half), far] = mm(jnp.concatenate(tops, 1), jnp.concatenate([b[:half] for b in both], 0))
            y_ref[pl.ds(block * Q + half, half), far] = mm(jnp.concatenate(bots, 1), jnp.concatenate(both, 0))

    def two(i, none):
        work(i, 0)
        work(i, 1)
        return none

    lax.fori_loop(0, x_ref.shape[1] // (2 * LANES), two, 0)


def split_store(hi_ref, lo_ref, at, cols, part):
    high = part.astype(BF16)
    hi_ref[at, cols] = high
    lo_ref[at, cols] = (part - high.astype(F32)).astype(BF16)


def head_sums(heads, head_size, hi_ref, lo_ref):
    spots = head_lanes((heads, hi_ref.shape[1]), True, head_size).astype(F32).astype(BF16)
    return mm(spots, hi_ref[...], 1, 1) + mm(spots, lo_ref[...], 1, 1)


def valid_of(s_ref, blocks, block):
    place = s_ref[0] * blocks + block
    last = place == s_ref[1] - 1
    length = jnp.where(place == 0, s_ref[2], jnp.where(last, s_ref[4], s_ref[3]))
    start = jnp.where(place == 0, 0, jnp.where(last, s_ref[1] - 1, 1))
    rows = lax.broadcasted_iota(jnp.int32, (Q, 1), 0) + (place - start) * Q
    return (rows < length).astype(F32)


class Outbound:
    def __init__(self, held, sems, keep, send, tiles):
        self.held, self.sems, self.keep, self.send, self.tiles = held, sems, keep, send, tiles

    def wait(self, slot):
        for k in range(2):
            held = self.held.at[slot, :, k * LANES : (k + 1) * LANES]
            pltpu.make_async_copy(held, self.keep.at[0, :, 0:LANES], self.sems.at[slot, k]).wait()

    def start(self, turn, slot):
        for k in range(2):
            at = 2 * turn + k
            piece, lane = at // self.tiles, at % self.tiles
            held = self.held.at[slot, :, k * LANES : (k + 1) * LANES]
            cols = slice(lane * LANES, (lane + 1) * LANES) if isinstance(lane, int) else tile_at(lane)
            for odd, ref in enumerate((self.keep, self.send)):

                @pl.when(piece % 2 == odd)
                def _(ref=ref, held=held, piece=piece, cols=cols, k=k):
                    pltpu.make_async_copy(held, ref.at[piece // 2, :, cols], self.sems.at[slot, k]).start()


def turns_with_grads(turns, work, grads, out):
    def turn(i, none):
        before = jnp.maximum(i - 1, 0)
        slot = before % 2

        @pl.when(i >= 3)
        def _():
            out.wait(slot)

        grads(before, slot)
        work(i, 0)
        work(i, 1)

        @pl.when(i >= 1)
        def _():
            out.start(before, slot)

        return none

    lax.fori_loop(0, turns, turn, 0)
    last = turns - 1
    if last >= 2:
        out.wait(last % 2)
    grads(last, last % 2)
    out.start(jnp.int32(last), last % 2)
    for slot in range(min(2, turns)):
        out.wait(slot)


def middle_kernel(blocks, tiles, head_size, s_ref, dbt_ref, inc_in, colp_ref, chan_ref, par_ref, c_ref, ct_ref, nt_ref,
                  y_ref, dny_ref, gate_ref, x_ref, st_ref,
                  ny_out, dgate_out, keep_out, send_out, inc_out, di_out, dc_out, rowpart_out, rows_out,
                  dy_ref, carry_ref, turned_ref,
                  ny_ref, dgate_ref, inc_ref, di_ref, dc_ref, rowpart_ref, rows_ref, grad_ref,
                  mix_ref, sq_ref, cr_ref, hi_ref, lo_ref, sems, grad_sems):
    moves = [(ny_ref, ny_out), (dgate_ref, dgate_out), (inc_ref, inc_out), (di_ref, di_out), (dc_ref, dc_out), (rowpart_ref, rowpart_out), (rows_ref, rows_out)]

    def move(index, *where):
        held, out = moves[index]
        pltpu.make_async_copy(held.at[where], out.at[where], sems.at[index]).start()

    depth = dbt_ref.shape[0]
    total = chan_ref.shape[1]
    kept = [keeps_of(s_ref, block, blocks)[1] for block in range(blocks)]
    sq_ref[...] = jnp.zeros_like(sq_ref)
    cr_ref[...] = jnp.zeros_like(cr_ref)

    def forward(i, none):
        for k in range(2):
            far = tile_at(2 * i + k)
            incoming = inc_in[:, far]
            for block in range(blocks):
                at = pl.ds(block * Q, Q)
                incoming = kept[block] * incoming
                inc_low = incoming.astype(BF16)
                inc_ref[block, :, far] = inc_low
                incoming = chan_ref[block : block + 1, far] * incoming + st_ref[block, :, far]
                inter = mm(c_ref[at], inc_low) * spread(colp_ref[i, at, 8 * k : 8 * k + 8], 2)
                mix = y_ref[at, far] + inter + chan_ref[7:8, far] * x_ref[at, far].astype(F32)
                mix_ref[at, far] = mix
                gate = gate_ref[at, far].astype(F32)
                gated = mix * (gate * jax.nn.sigmoid(gate))
                sq_ref[at] += gated * gated
                cr_ref[at] += dny_ref[at, far].astype(F32) * par_ref[5:6, far] * gated
        return none

    lax.fori_loop(0, total // (2 * LANES), forward, 0)
    scale = lax.rsqrt(jnp.sum(sq_ref[...], axis=1, keepdims=True) / total + EPSILON)
    coef = scale * scale * scale * (jnp.sum(cr_ref[...], axis=1, keepdims=True) / total)
    sq_ref[...] = jnp.broadcast_to(scale, sq_ref.shape)
    cr_ref[...] = jnp.broadcast_to(coef, cr_ref.shape)
    rows_ref[...] = jnp.zeros_like(rows_ref)

    def backward(i, k):
        pair = 2 * i + k
        far = tile_at(pair)
        gain = par_ref[5:6, far]
        skip = chan_ref[7:8, far]
        gain_row = jnp.zeros((1, LANES), F32)
        skip_row = jnp.zeros((1, LANES), F32)
        dis = []
        for block in range(blocks):
            at = pl.ds(block * Q, Q)
            gate, mix, x = gate_ref[at, far].astype(F32), mix_ref[at, far], x_ref[at, far].astype(F32)
            sig = jax.nn.sigmoid(gate)
            act = gate * sig
            gated = mix * act
            normed = gated * sq_ref[at]
            dny = dny_ref[at, far].astype(F32)
            ny_ref[at, far] = (normed * gain).astype(BF16)
            gain_row += jnp.sum(dny * normed, axis=0, keepdims=True)
            d_gated = dny * gain * sq_ref[at] - gated * cr_ref[at]
            dgate_ref[at, far] = (d_gated * mix * silu_slope(gate, sig)).astype(BF16)
            dy = d_gated * act
            dy_low = dy.astype(BF16)
            dy_ref[at, far] = dy_low
            skip_row += jnp.sum(dy * x, axis=0, keepdims=True)
            split_store(hi_ref, lo_ref, at, far, dy_low.astype(F32) * (mix - skip * x))
            dye = (dy * spread(colp_ref[i, at, 8 * k : 8 * k + 8], 2)).astype(BF16)
            dc_ref[at] += mm(dye, inc_ref[block, :, far], 1, 1)
            di = mm(ct_ref[:, at], dye).astype(BF16)
            di_ref[block, :, far] = di
            dis.append(di.astype(F32))
        rows_ref[0:1, far] = gain_row
        rows_ref[1:2, far] = skip_row
        back = jnp.zeros_like(dis[0])
        for block in reversed(range(blocks)):
            back = kept[block] * (dis[block] + chan_ref[block : block + 1, far] * back)
        carry_block(carry_ref, far, back, chan_ref[6:7, far])
        turned = tile_at(jnp.bitwise_xor(pair // tiles, 1) * tiles + pair % tiles)
        carry_block(turned_ref, turned, back, chan_ref[6:7, far])
        move(0, slice(None), far)
        move(1, slice(None), far)

    def grads(turn, slot):
        cols = pl.ds(pl.multiple_of(turn * 2 * LANES, 2 * LANES), 2 * LANES)
        grad_ref[slot, 0:depth] = mm(dbt_ref[...], ny_ref[:, cols]).astype(BF16)
        grad_ref[slot, depth:] = mm(nt_ref[...], dgate_ref[:, cols]).astype(BF16)

    dc_ref[...] = jnp.zeros_like(dc_ref)
    turns_with_grads(total // (2 * LANES), backward, grads, Outbound(grad_ref, grad_sems, keep_out, send_out, tiles))
    for index in (2, 3, 4, 6):
        move(index)
    rowpart_ref[...] = head_sums(rowpart_ref.shape[0], head_size, hi_ref, lo_ref)
    move(5)
    for index, (held, out) in enumerate(moves):
        pltpu.make_async_copy(held, out, sems.at[index]).wait()


def back_kernel(blocks, head_size, s_ref, rowp_ref, colp_ref, cbt_ref, b_ref, c_ref, dy_ref, x_ref,
                dx_ref, part_ref, db_ref, dc_ref, acc_ref, hi_ref, lo_ref):
    half = Q // 2
    first = first_lanes()
    tri = lax.broadcasted_iota(jnp.int32, (half, half), 0) <= lax.broadcasted_iota(
        jnp.int32, (half, half), 1
    )
    acc_ref[...] = jnp.zeros_like(acc_ref)

    def two(i, none):
        for block in range(blocks):
            at = pl.ds(block * Q, Q)
            w00 = w01 = w11 = 0.0
            for k in range(2):
                pair = 2 * i + k
                far = tile_at(pair)
                x, dy = x_ref[at, far], dy_ref[at, far]
                dys = [jnp.where(first, dy, 0), jnp.where(first, 0, dy)]
                xs = [jnp.where(first, x, 0), jnp.where(first, 0, x)]
                rp = rowp_ref[pair, :, at]
                cp = colp_ref[i, at, 8 * k : 8 * k + 8]
                tops, bots = [], []
                for h in range(2):
                    ls, ld = cp[:, 2 + h : 3 + h], rp[h : h + 1, :]
                    ds_top = mm(xs[h][:half], dy, 1, 1)
                    ds_bot = mm(xs[h][half:], dy[half:], 1, 1)
                    e00 = jnp.exp(jnp.where(tri, ld[:, :half] - ls[:half], -1e30))
                    e01 = jnp.exp(ld[:, half:] - ls[:half])
                    e11 = jnp.exp(jnp.where(tri, ld[:, half:] - ls[half:], -1e30))
                    tops.append((cbt_ref[block, 0:half, 0:half] * e00).astype(BF16))
                    tops.append((cbt_ref[block, 0:half, half:] * e01).astype(BF16))
                    bots.append((cbt_ref[block, half:, half:] * e11).astype(BF16))
                    w00 += ds_top[:, :half] * e00
                    w01 += ds_top[:, half:] * e01
                    w11 += ds_bot * e11
                dx_top = mm(jnp.concatenate(tops, 1), jnp.concatenate(dys, 0))
                dx_bot = mm(jnp.concatenate(bots, 1), jnp.concatenate([d[half:] for d in dys], 0))
                dx = jnp.concatenate([dx_top, dx_bot], 0)
                dx_ref[at, far] = dx.astype(BF16)
                split_store(hi_ref, lo_ref, at, far, x.astype(F32) * dx)
            acc_ref[block, 0:half, 0:half] += w00
            acc_ref[block, 0:half, half:] += w01
            acc_ref[block, half:, half:] += w11
        return none

    lax.fori_loop(0, x_ref.shape[1] // (2 * LANES), two, 0)
    part_ref[...] = head_sums(part_ref.shape[0], head_size, hi_ref, lo_ref)
    for block in range(blocks):
        at = slice(block * Q, (block + 1) * Q)
        acc = acc_ref[block].astype(BF16)
        db_ref[at] = mm(acc, c_ref[at])
        dc_ref[at] = mm(acc, b_ref[at], 0, 0)


def conv_back(s_ref, blocks, work, taps, values_of, slope_of, store):
    sums = [0.0] * (K + 1)
    for block in range(blocks):
        fresh, _ = keeps_of(s_ref, block, blocks)
        d_pre = slope_of(block)
        work[0, pl.ds(HALO + block * Q, Q)] = d_pre
        sums[K] += jnp.sum(d_pre, axis=0, keepdims=True)
        sums[K - 1] += jnp.sum(d_pre * values_of(HALO + block * Q), axis=0, keepdims=True)
        for distance in range(1, K):
            held = d_pre * row_keep(fresh, distance)
            work[distance, pl.ds(HALO + block * Q, Q)] = held
            sums[K - 1 - distance] += jnp.sum(
                held * values_of(HALO + block * Q - distance), axis=0, keepdims=True
            )
    for begin, count in [(0, HALO)] + [(HALO + b * Q, Q) for b in range(blocks)]:
        out = taps[K - 1 : K] * work[0, pl.ds(begin, count)]
        for distance in range(1, K):
            out = out + taps[K - 1 - distance : K - distance] * work[distance, pl.ds(begin + distance, count)]
        store(begin, count, out.astype(BF16))
    return sums


def tail_kernel(blocks, tiles, head_size, s_ref, back_in, colp_ref, chan_ref, par_ref, b_ref, nt_ref, nx_ref,
                inc_ref, dx_ref, dy_ref, di_ref, x_ref, pre_ref, inner_ref,
                dinner_ref, vgrad_ref, part_ref, lasts_ref, db_ref, keep_out, send_out,
                d_ref, in_ref, hi_ref, lo_ref, grad_ref, grad_sems):
    total = chan_ref.shape[1]
    kept = [keeps_of(s_ref, block, blocks)[1] for block in range(blocks)]
    d_ref[...] = jnp.zeros_like(d_ref)
    vgrad_ref[...] = jnp.zeros_like(vgrad_ref)
    lasts_ref[...] = jnp.zeros_like(lasts_ref)
    db_ref[...] = jnp.zeros_like(db_ref)

    def work(i, k):
        far = tile_at(2 * i + k)
        in_ref[k] = inner_ref[:, far].astype(F32)
        skip = chan_ref[7:8, far]
        back = back_in[:, far]
        lasts, lows = [None] * blocks, [None] * blocks
        for block in reversed(range(blocks)):
            fade = chan_ref[block : block + 1, far]
            lows[block] = back.astype(BF16)
            lasts[block] = fade * jnp.sum(inc_ref[block, :, far].astype(F32) * back, axis=0, keepdims=True)
            back = kept[block] * (di_ref[block, :, far].astype(F32) + fade * back)

        def slope_of(block):
            at = pl.ds(block * Q, Q)
            carry = spread(colp_ref[i, at, 8 * k : 8 * k + 8], 3)
            weighted = carry * x_ref[at, far].astype(F32)
            db_ref[at] += mm(weighted.astype(BF16), lows[block], 1, 1)
            d_weighted = mm(b_ref[at], lows[block])
            moved = weighted * d_weighted
            lasts_ref[block : block + 1, far] = lasts[block] + jnp.sum(moved, axis=0, keepdims=True)
            split_store(hi_ref, lo_ref, at, far, moved)
            d_x = dx_ref[at, far].astype(F32) + carry * d_weighted + skip * dy_ref[at, far].astype(F32)
            pre = pre_ref[at, far].astype(F32)
            return d_x * silu_slope(pre, jax.nn.sigmoid(pre))

        def store(begin, count, value):
            dinner_ref[pl.ds(begin, count), far] = value

        sums = conv_back(
            s_ref, blocks, d_ref.at[k], par_ref[:, far], lambda at: in_ref[k, pl.ds(at, Q)], slope_of, store
        )
        for index in range(K + 1):
            vgrad_ref[index : index + 1, far] = sums[index]

    def grads(turn, slot):
        cols = pl.ds(pl.multiple_of(turn * 2 * LANES, 2 * LANES), 2 * LANES)
        grad = mm(nt_ref[...], dinner_ref[HALO:, cols]) + mm(nx_ref[0:HALO], dinner_ref[0:HALO, cols], 0, 0)
        grad_ref[slot] = grad.astype(BF16)

    turns_with_grads(total // (2 * LANES), work, grads, Outbound(grad_ref, grad_sems, keep_out, send_out, tiles))
    part_ref[...] = head_sums(part_ref.shape[0], head_size, hi_ref, lo_ref)


def state_kernel(blocks, head_size, shares, s_ref, dbx_ref, dbin_ref, dcin_ref, dcx_ref, raw_ref, spre_ref, staps_ref,
                 rowpart_ref, part_a, part_b, step_ref, ratio_ref, sig_ref, hp_ref, rows_ref, lasts_ref, vgrad_ref,
                 nt_ref, nx_ref, dstate_ref, dstep_ref, *refs):
    e_ref, all_ref, step_grad_ref = refs[-3:]
    outs = refs[:-3]
    e_ref[...] = jnp.zeros_like(e_ref)
    d_states = []
    for block in range(blocks):
        at = slice(block * Q, (block + 1) * Q)
        d_states.append(jnp.concatenate([dbin_ref[at] + dbx_ref[at], dcin_ref[at] + dcx_ref[at]], 1))

    def slope_of(block):
        pre = spre_ref[pl.ds(block * Q, Q), :]
        return d_states[block] * silu_slope(pre, jax.nn.sigmoid(pre))

    def store(begin, count, value):
        dstate_ref[pl.ds(begin, count), :] = value

    sgrad = conv_back(s_ref, blocks, e_ref, staps_ref[...], lambda at: raw_ref[pl.ds(at, Q), :], slope_of, store)
    heads = hp_ref.shape[0]
    total = lasts_ref.shape[1]
    depth = hp_ref.shape[1] - LANES
    spots = head_lanes((heads, total), True, head_size).astype(F32)
    lasts = mm(spots, lasts_ref[...], 1, 1, precision=HIGHEST)
    skips = mm(spots, rows_ref[...], 1, 1, precision=HIGHEST)[:, 1:2]
    rate = -jnp.exp(hp_ref[:, depth + 1 : depth + 2])
    lane = lax.broadcasted_iota(jnp.int32, (heads, Q), 1)
    upto = (
        lax.broadcasted_iota(jnp.int32, (Q, Q), 0) >= lax.broadcasted_iota(jnp.int32, (Q, Q), 1)
    ).astype(F32)
    grad_bias = jnp.zeros((heads, 1), F32)
    grad_decay = jnp.zeros((heads, 1), F32)
    for block in range(blocks):
        at = slice(block * Q, (block + 1) * Q)
        cols = part_a[:, at] + part_b[:, at]
        d_log = rowpart_ref[:, at] - cols + jnp.where(lane == Q - 1, lasts[:, block : block + 1], 0.0)
        d_move = mm(d_log, upto, precision=HIGHEST)
        d_raw = cols * ratio_ref[:, at] + rate * d_move * sig_ref[:, at]
        grad_bias += jnp.sum(d_raw, axis=1, keepdims=True)
        grad_decay += rate * jnp.sum(step_ref[:, at] * d_move, axis=1, keepdims=True)
        dstep_ref[:, at] = d_raw.astype(BF16)
    wide_lane = lax.broadcasted_iota(jnp.int32, (heads, LANES), 1)
    per_head = jnp.where(
        wide_lane == 0, grad_bias, jnp.where(wide_lane == 1, grad_decay, jnp.where(wide_lane == 2, skips, 0.0))
    )
    step_grad_ref[...] = mm(dstep_ref[...], nx_ref[HALO:])
    all_ref[...] = jnp.zeros_like(all_ref)
    all_ref[0:depth] = mm(nt_ref[...], dstate_ref[HALO:]) + mm(nx_ref[0:HALO], dstate_ref[0:HALO], 0, 0)
    for index in range(K + 1):
        all_ref[depth + index : depth + index + 1] = sgrad[index]
    if not shares:
        outs[0][...] = all_ref[...]
        outs[1][...] = step_grad_ref[...]
        outs[2][...] = per_head
        return
    ways, share, wide = shares
    quarter = all_ref.shape[0] // ways
    work = outs[-1]
    for p in range(ways):
        span = slice(p * wide, (p + 1) * wide)
        some = slice(p * share, (p + 1) * share)
        work[...] = jnp.zeros_like(work)
        work[0 : K + 1] = vgrad_ref[0 : K + 1, span]
        work[K + 1 : K + 2] = rows_ref[0:1, span]
        for part in range(depth // wide):
            begin = 8 + part * share
            work[begin : begin + share] = step_grad_ref[some, part * wide : (part + 1) * wide]
        work[24 : 24 + share, 0:LANES] = per_head[some]
        owner = jnp.bitwise_xor(s_ref[0], p)
        work[32 : 32 + quarter, 0 : all_ref.shape[1]] = all_ref[pl.ds(pl.multiple_of(owner * quarter, 8), quarter)]
        outs[p % 2][p // 2] = work[...].astype(BF16)


def mixed_kernel(pieces, blocks, s_ref, hid_ref, ny_ref, *refs):
    outs_w, mixed_ref = refs[:pieces], refs[pieces]
    wide = outs_w[0].shape[0]
    for block in range(blocks):
        at = slice(block * Q, (block + 1) * Q)
        branch = mm(ny_ref[at, 0:wide], outs_w[0][...])
        for p in range(1, pieces):
            branch += mm(ny_ref[at, p * wide : (p + 1) * wide], outs_w[p][...])
        mixed_ref[at] = (hid_ref[at].astype(F32) + valid_of(s_ref, blocks, block) * branch).astype(BF16)


def final_kernel(pieces, blocks, mine, s_ref, hid_ref, halo_ref, cot_ref, gain_ref, dgate_ref, dinner_ref,
                 dstate_ref, dstep_ref, hp_ref, sproj_ref, *refs):
    both_in = refs[:pieces]
    grad_out, extra_ref, gain_out, grad_ref, sems, both, dgate_here, dinner_here, in_sems = refs[-9:]
    wide = both.shape[2] // 2
    depth = hid_ref.shape[1]
    own = pl.ds(mine[0] * Q, len(mine) * Q)
    waits = [
        pltpu.make_async_copy(dinner_ref.at[pl.ds(mine[0] * Q, len(mine) * Q + HALO)], dinner_here, in_sems.at[0]),
        pltpu.make_async_copy(dgate_ref.at[own], dgate_here, in_sems.at[1]),
    ]
    for copy in waits:
        copy.start()
    loads = [pltpu.make_async_copy(both_in[p], both.at[p], in_sems.at[2 + p]) for p in range(pieces)]
    for copy in loads:
        copy.start()
    gain = gain_ref[...]
    gain_sum = jnp.zeros((1, depth), F32)

    def finish(values_in, d_normed):
        h = values_in.astype(F32)
        scale = lax.rsqrt(jnp.mean(h * h, axis=1, keepdims=True) + EPSILON)
        weighted = gain * d_normed
        inner = jnp.mean(weighted * h, axis=1, keepdims=True)
        return scale * weighted - h * (scale * scale * scale * inner), jnp.sum(d_normed * h * scale, axis=0, keepdims=True)

    moves = []
    totals = [mm(dstate_ref[0:HALO], sproj_ref[...], 1, 1)]
    for block in mine:
        ext = slice(HALO + block * Q, HALO + (block + 1) * Q)
        part = mm(dstate_ref[ext], sproj_ref[...], 1, 1)
        totals.append(part + mm(dstep_ref[:, block * Q : (block + 1) * Q], hp_ref[:, 0:depth].astype(BF16), 0, 0))
    for copy in waits:
        copy.wait()
    for p in range(pieces):
        loads[p].wait()
        span = slice(p * wide, (p + 1) * wide)
        if mine[0] == 0:
            totals[0] += mm(dinner_here[0:HALO, span], both[p, :, wide:], 1, 1)
        for index in range(len(mine)):
            here = slice(index * Q, (index + 1) * Q)
            ext = slice(HALO + index * Q, HALO + (index + 1) * Q)
            totals[index + 1] += mm(dgate_here[here, span], both[p, :, :wide], 1, 1)
            totals[index + 1] += mm(dinner_here[ext, span], both[p, :, wide:], 1, 1)
    if mine[0] == 0:
        extra_ref[...], part = finish(halo_ref[...], totals[0])
        gain_sum += part
    else:
        extra_ref[...] = jnp.zeros_like(extra_ref)
    for index, block in enumerate(mine):
        at = slice(block * Q, (block + 1) * Q)
        here = slice(index * Q, (index + 1) * Q)
        d_hidden, part = finish(hid_ref[at], totals[index + 1].astype(BF16).astype(F32))
        gain_sum += part
        grad_ref[here] = cot_ref[at].astype(F32) + d_hidden
        moves.append(pltpu.make_async_copy(grad_ref.at[here], grad_out.at[at], sems.at[index]))
        moves[-1].start()
    gain_out[...] = jnp.zeros_like(gain_out)
    side = gain_out.shape[1]
    for index in range(depth // side):
        gain_out[index : index + 1] = gain_sum[:, index * side : (index + 1) * side]
    for copy in moves:
        copy.wait()


def gather_far(value, ahead):
    ways = lax.axis_size("head")
    pieces = {0: value}
    far = {0: after(value, ahead)}
    mask = 2
    while mask < ways:
        for p in list(far):
            far[p | mask] = swap(far[p], "head", mask)
        mask *= 2
    return [value] + [far[p] for p in range(2, ways, 2)]


def near_pair(value, ahead):
    return value, swap(after(value, ahead) if len(ahead) else value, "head", 1)


def swap(value, axis, mask):
    size = lax.axis_size(axis)
    return lax.ppermute(value, axis, [(i, i ^ mask) for i in range(size)])


def pick(value, index):
    return lax.dynamic_index_in_dim(value, index, 0, keepdims=False)


def half_of(value, mask):
    side = jnp.where((lax.axis_index("dp") & mask) != 0, 1, 0)
    parts = value.reshape(2, value.shape[0] // 2, value.shape[1])
    return pick(parts, side).astype(F32), pick(parts, 1 - side).astype(BF16)


def whole_dp(low):
    for bit in range(3, lax.axis_size("dp").bit_length() - 1):
        low = (low.astype(F32) + swap(low, "dp", 1 << bit).astype(F32)).astype(BF16)
    return low


def both_of(low, mask, other):
    upper = (lax.axis_index("dp") & mask) != 0
    return jnp.concatenate([jnp.where(upper, other, low), jnp.where(upper, low, other)], axis=0)


def after(value, *others):
    return lax.optimization_barrier((value, others))[0]


def gather_pieces(value, ahead=()):
    ways = lax.axis_size("head")
    pieces = {0: value, 1: swap(value, "head", 1)}
    far = {0: after(value, ahead) if ahead else value}
    mask = 2
    while mask < ways:
        for p in list(far):
            far[p | mask] = swap(far[p], "head", mask)
        mask *= 2
    for p in far:
        if p:
            pieces[p] = far[p]
            pieces[p | 1] = swap(far[p], "head", 1)
    return [pieces[p] for p in range(ways)]


def reduce_pieces(pieces):
    ways = len(pieces)
    mask = 1
    live = {p: v for p, v in enumerate(pieces)}
    order = [1 << b for b in range(ways.bit_length() - 1)]
    for mask in order:
        got = {p ^ mask: swap(live[p].astype(BF16), "head", mask) for p in live if p & mask}
        live = {p: live[p].astype(F32) + got[p].astype(F32) for p in live if not p & mask}
    return live[0]


def body(hidden, lengths, norm_gain, gate_proj, value_proj, state_proj, step_proj, value_taps, value_bias,
         state_taps, state_bias, step_bias, decay_log, skip_gain, out_gain, out_proj, cotangent):
    rows, depth = hidden.shape
    ways = lax.axis_size("head")
    me = lax.axis_index("head")
    blocks = rows // Q
    wide = gate_proj.shape[1]
    share = step_proj.shape[1]
    total = wide * ways
    heads = share * ways
    head_size = wide // share
    pairs = heads // 2
    side = state_proj.shape[1]
    state = side // 2
    padded = -(-heads // 32) * 32
    plain = wide % LANES == 0
    order = [1 << b for b in range(ways.bit_length() - 1)]
    scalars = jnp.concatenate(
        [jnp.stack([me, blocks * ways]).astype(jnp.int32), lengths[0], jnp.zeros((3,), jnp.int32)]
    )

    top = jnp.concatenate(
        [step_proj.T.astype(F32), step_bias[:, None], decay_log[:, None], skip_gain[:, None], jnp.zeros((share, LANES - 3), F32)],
        axis=1,
    )
    low = jnp.concatenate([value_taps, value_bias[None], out_gain[None]], axis=0)
    pack = jnp.concatenate(
        [
            jnp.pad(top, ((0, 8 - share), (0, 0))),
            jnp.pad(low, ((0, 2), (0, depth + LANES - wide))),
            jnp.pad(hidden[rows - HALO :].astype(F32), ((0, 0), (0, LANES))),
        ],
        axis=0,
    )
    packs = gather_pieces(pack)
    halo = jnp.zeros((HALO, depth), F32)
    for p in range(1, ways):
        halo = jnp.where((me ^ p) == me - 1, packs[p][16:, :depth], halo)
    halo = halo.astype(BF16)
    both = gather_far(jnp.concatenate([gate_proj, value_proj], axis=1), (packs[1],))
    outs = gather_far(out_proj, (packs, both[0]))

    def both_merged(pair):
        if plain:
            return list(pair)
        a, b = pair
        return [jnp.concatenate([a[:, :wide], b[:, :wide], a[:, wide:], b[:, wide:]], axis=1)]

    def outs_merged(pair):
        return list(pair) if plain else [jnp.concatenate(pair, axis=0)]

    pieces = ways if plain else ways // 2
    span = total // pieces
    tiles = span // LANES
    hp = jnp.pad(jnp.concatenate([p[:share] for p in packs], axis=0), ((0, padded - heads), (0, 0)))
    par = jnp.concatenate([p[8:16, :wide] for p in packs], axis=1)
    gain_in = norm_gain[None]
    staps = jnp.pad(jnp.concatenate([state_taps, state_bias[None]], axis=0), ((0, 3), (0, 0)))

    ext = rows + HALO
    (nx, nt, state_raw, state_pre, b_low, c_low, b_t, c_t, cb, cbt) = call(
        functools.partial(pre_kernel, blocks),
        [((ext, depth), BF16), ((depth, rows), BF16), ((ext, side), F32), ((rows, side), F32),
         ((rows, state), BF16), ((rows, state), BF16), ((state, rows), BF16), ((state, rows), BF16),
         ((blocks, Q, Q), F32), ((blocks, Q, Q), F32)],
        [scalars, hidden, halo, gain_in, state_proj, staps],
        cost=2, mib=PRE,
    )
    rowp, colp, step, ratio, sig, chan = call(
        functools.partial(step_kernel, blocks, head_size),
        [((pairs, 8, rows), F32), ((pairs // 2, rows, 16), F32), ((padded, rows), F32), ((padded, rows), F32),
         ((padded, rows), F32), ((8, total), F32)],
        [scalars, nx, hp],
        cost=2,
        mib=PRE,
    )
    vmem = pltpu.VMEM
    hbm = pl.BlockSpec(memory_space=pltpu.HBM)
    front_outs = [((rows, total), BF16), ((ext, total), BF16), ((rows, total), BF16), ((blocks, state, total), F32),
                  ((rows, total), BF16), ((state + HALO, total), BF16), ((state + HALO, total), BF16)]
    fronts, all_both = [], []
    half = pieces // 2
    for begin in (0, half):
        pairs_of = range(begin // 2, begin // 2 + ways // 4) if plain else range(begin, begin + half)
        weights = [w for at in pairs_of for w in both_merged(near_pair(both[at], fronts))]
        all_both += weights
        args = [scalars, nx, par, b_t, colp, chan, *weights]
        aliases = {len(args) + at: at for at in range(len(fronts))}
        fronts = call(
            functools.partial(front_kernel, blocks, begin, half), front_outs, [*args, *fronts], aliases=aliases,
            ins={len(args) + at: hbm for at in range(min(4, len(fronts)))}, out_specs={at: hbm for at in range(4)},
            kinds={at: pltpu.HBM for at in range(4)},
            scratch=[vmem((rows, half * span), BF16), vmem((ext, half * span), BF16), vmem((rows, half * span), BF16),
                     vmem((blocks, state, half * span), F32), vmem((ext, half * span), F32), pltpu.SemaphoreType.DMA((4,))],
            cost=6, mib=FRONT,
        )
    gate, inner, pre, st, x, carry, carry_turned = fronts

    def turned(value, mask):
        parts = [value[..., (p ^ mask) * wide : ((p ^ mask) + 1) * wide] for p in range(ways)]
        return jnp.concatenate(parts, axis=-1)

    def scan(own, own_turned, forward, beside=lambda run: ()):
        def fade_of(value):
            return value[state : state + 1].astype(F32) + value[state + 1 : state + 2].astype(F32)

        if plain and ways == 4:
            near = swap(own_turned, "head", 1)
            (run,) = call(functools.partial(join_kernel, forward), [(own.shape, BF16)], [scalars, own, near], mib=8)
            far = swap(run, "head", 2)
            between = beside(run if forward else near)
            far = after(far, between[1]) if between else far
            (result,) = call(functools.partial(arrive_kernel, forward), [((state, total), F32)], [scalars, near, far], mib=8)
            return result, between
        before = before_fade = None
        run = own
        for mask in order:
            if mask == 1 and plain:
                got = swap(own_turned, "head", 1)
            else:
                got = turned(swap(run, "head", mask), mask)
            got_fade, run_fade = fade_of(got), fade_of(run)
            got, mine = got[:state].astype(F32), run[:state].astype(F32)
            later = ((me & mask) != 0) if forward else ((me & mask) == 0)
            if before is None:
                before = jnp.where(later, got, 0.0)
                before_fade = jnp.where(later, got_fade, 1.0)
            else:
                before = jnp.where(later, before_fade * got + before, before)
                before_fade = jnp.where(later, before_fade * got_fade, before_fade)
            if mask != order[-1]:
                both_maps = jnp.where(later, run_fade * got + mine, got_fade * mine + got)
                fades = run_fade * got_fade
                high = fades.astype(BF16)
                low_part = (fades - high.astype(F32)).astype(BF16)
                run = jnp.concatenate(
                    [both_maps.astype(BF16), high, low_part, jnp.zeros((HALO - 2, total), BF16)], axis=0
                )
        return before, beside(run)

    def within(run):
        (y_intra,) = call(
            functools.partial(intra_kernel, blocks),
            [((rows, total), F32)],
            [scalars, rowp, colp, cb, after(x, run)],
            cost=5,
            mib=INTRA,
        )
        all_outs = [w for value in outs for w in outs_merged(near_pair(value, run))]
        dny, dbt = call(
            functools.partial(masked_kernel, blocks, pieces),
            [((rows, total), BF16), ((depth, rows), BF16)],
            [scalars, cotangent, *all_outs],
            scratch=[vmem((rows, depth), BF16)],
            cost=3,
            mib=INTRA,
        )
        return y_intra, dny, dbt, all_outs

    inc_in, (y_intra, dny, dbt, all_outs) = scan(carry, carry_turned, True, within)
    wide_bf = vmem((rows, total), BF16)
    held_outs = [((rows, total), BF16), ((rows, total), BF16),
                 ((pieces // 2, 2 * depth, span), BF16), ((pieces // 2, 2 * depth, span), BF16),
                 ((blocks, state, total), BF16), ((blocks, state, total), BF16), ((rows, state), F32),
                 ((padded, rows), F32), ((8, total), F32)]
    (ny, d_gate, a_keep, a_send, inc, d_inc, dc_inter, rowpart, rows_sum, d_y, back_carry, back_turned) = call(
        functools.partial(middle_kernel, blocks, tiles, head_size),
        [*held_outs, ((rows, total), BF16), ((state + HALO, total), BF16), ((state + HALO, total), BF16)],
        [scalars, dbt, inc_in, colp, chan, par, c_low, c_t, nt, y_intra, dny, gate, x, st],
        out_specs={at: hbm for at in range(len(held_outs))}, kinds={at: pltpu.HBM for at in range(len(held_outs))},
        scratch=[*[vmem(*o) for at, o in enumerate(held_outs) if at not in (2, 3)], vmem((2, 2 * depth, 2 * LANES), BF16), vmem((rows, total), F32), vmem((rows, LANES), F32),
                 vmem((rows, LANES), F32), wide_bf, wide_bf, pltpu.SemaphoreType.DMA((len(held_outs) - 2,)),
                 pltpu.SemaphoreType.DMA((2, 2))],
        cost=14, mib=MIDDLE,
    )
    back_runs = []
    back_in, _ = scan(back_carry, back_turned, False, lambda run: back_runs.append(run))

    def over_head(keep, send):
        if not plain:
            parts = [None] * ways
            for m in range(pieces):
                merged = (keep, send)[m % 2][m // 2]
                parts[2 * m], parts[2 * m + 1] = merged[:, :wide], merged[:, wide:]
            return reduce_pieces(parts)
        got = swap(send, "head", 1)
        live = [keep[i].astype(F32) + got[i].astype(F32) for i in range(pieces // 2)]
        return live

    def finish_head(live):
        if not plain:
            return live
        return live[0] + swap(live[1].astype(BF16), "head", 2).astype(F32)

    def halve(value, axis_at=0):
        side = lax.axis_index("dp") & 1
        cut = value.shape[:axis_at] + (2, value.shape[axis_at] // 2) + value.shape[axis_at + 1 :]
        parts = jnp.moveaxis(value.reshape(cut), axis_at, 0)
        got = swap(pick(parts, 1 - side).astype(BF16), "dp", 1)
        return pick(parts, side).astype(F32) + got.astype(F32)

    a_live = over_head(a_keep, after(a_send, *back_runs))
    if plain:
        a_out = finish_head([v[:depth] for v in a_live])
        a_gate = halve(jnp.stack([v[depth:] for v in a_live]), 1)
        gates = (a_out, a_gate)
    else:
        gates = a_live
    dx, part_a, db_in, dc_in = call(
        functools.partial(back_kernel, blocks, head_size),
        [((rows, total), BF16), ((padded, rows), F32), ((rows, state), F32), ((rows, state), F32)],
        [scalars, rowp, colp, cbt, b_low, c_low, d_y, x],
        scratch=[vmem((blocks, Q, Q), F32), wide_bf, wide_bf],
        cost=8,
        mib=BACK,
    )
    (d_inner, vgrad, part_b, lasts, db_x, b_keep, b_send) = call(
        functools.partial(tail_kernel, blocks, tiles, head_size),
        [((ext, total), BF16), ((8, total), F32), ((padded, rows), F32), ((8, total), F32), ((rows, state), F32),
         ((pieces // 2, depth, span), BF16), ((pieces // 2, depth, span), BF16)],
        [scalars, after(back_in, a_live), colp, chan, par, b_low, nt, nx, inc, dx, d_y, d_inc, x, pre, inner],
        out_specs={5: hbm, 6: hbm}, kinds={5: pltpu.HBM, 6: pltpu.HBM},
        scratch=[vmem((2, K, rows + 2 * HALO, LANES), F32), vmem((2, ext, LANES), F32), wide_bf, wide_bf,
                 vmem((2, depth, 2 * LANES), BF16), pltpu.SemaphoreType.DMA((2, 2))],
        cost=10, mib=TAIL,
    )
    small_rows, all_rows = 256, 832
    if plain:
        small_outs = [((pieces // 2, small_rows, span), BF16)] * 2
        shares = (ways, share, wide)
        work = [vmem((small_rows, span), F32)]
    else:
        small_outs = [((all_rows, side), F32), ((padded, depth), F32), ((padded, LANES), F32)]
        shares = None
        work = []
    d_state, d_step, *smalls = call(
        functools.partial(state_kernel, blocks, head_size, shares),
        [((ext, side), BF16), ((padded, rows), BF16)] + small_outs,
        [scalars, after(db_x, gates), db_in, dc_in, dc_inter, state_raw, state_pre, staps, rowpart, part_a, part_b, step, ratio, sig, hp,
         rows_sum, lasts, vgrad, nt, nx],
        scratch=work + [vmem((K, rows + 2 * HALO, side), F32), vmem((all_rows, side), F32), vmem((padded, depth), F32)],
        cost=4, mib=STATE,
    )
    share_rows = all_rows // ways
    if not plain:
        all_grad, step_grad, per_head = smalls
        parts = []
        for p in range(ways):
            cols, some = slice(p * wide, (p + 1) * wide), slice(p * share, (p + 1) * share)
            flat = step_grad[some].reshape(share, depth // wide, wide).swapaxes(0, 1).reshape(-1, wide)
            own = lax.dynamic_slice_in_dim(all_grad, (me ^ p) * share_rows, share_rows, 0).reshape(-1)
            count = -(-own.shape[0] // wide)
            own = jnp.pad(own, (0, count * wide - own.shape[0])).reshape(count, wide)
            part = jnp.concatenate(
                [vgrad[0:5, cols], rows_sum[0:1, cols], jnp.zeros((2, wide), F32), flat, jnp.zeros((16 - flat.shape[0], wide), F32),
                 jnp.pad(per_head[some], ((0, 8 - share), (0, wide - LANES))), own], axis=0)
            parts.append(jnp.pad(part, ((0, small_rows - part.shape[0]), (0, 0))))
        c_live = reduce_pieces(parts)
    else:
        c_live = over_head(smalls[0], smalls[1])
    b_live = over_head(b_keep, after(b_send, gates))
    if plain:
        a_part = jnp.concatenate([halve(a_out), finish_head([a_gate[0], a_gate[1]])], axis=0)
    else:
        a_part = halve(a_live)
    a_keep_z, a_send_z = half_of(a_part, 2)
    if plain:
        b_whole = [jnp.concatenate([b, c], axis=0) for b, c in zip(b_live, c_live)]
        cut = b_whole[0].shape[0] // 2
        side_x = lax.axis_index("dp") & 1
        low, high = [v[:cut] for v in b_whole], jnp.stack([v[cut:] for v in b_whole])
        high = jnp.moveaxis(high.reshape(2, 2, cut // 2, wide), 1, 0)
        b_sends = low[1].astype(BF16), pick(high, 1 - side_x).astype(BF16)
    else:
        b_sends = ()
    a_got_z = swap(after(a_send_z, b_sends), "dp", 2)
    if plain:
        b_got = swap(b_sends[0], "head", 2), swap(b_sends[1], "dp", 1)
    mine = list(range(blocks))
    args = [scalars, hidden, halo, cotangent, gain_in, after(d_gate, b_sends, a_send_z), d_inner, d_state, d_step, hp, state_proj,
            *all_both]
    results = call(
        functools.partial(final_kernel, pieces, blocks, mine),
        [((rows, depth), F32), ((HALO, depth), F32), ((8, span), F32)],
        args,
        ins={at: hbm for at in (5, 6, *range(len(args) - pieces, len(args)))},
        out_specs={0: hbm},
        kinds={0: pltpu.HBM},
        scratch=[vmem((rows, depth), F32), pltpu.SemaphoreType.DMA((blocks,)), vmem((pieces, depth, 2 * span), BF16),
                 vmem((rows, total), BF16), vmem((ext, total), BF16), pltpu.SemaphoreType.DMA((2 + pieces,))],
        cost=9,
        mib=FINAL,
    )
    grad_hidden, extra, gain_part = results
    extra = lax.ppermute(extra, "head", [(i + 1, i) for i in range(ways - 1)])
    grad_hidden = grad_hidden.at[rows - HALO :].add(extra)
    if plain:
        one = low[0] + after(b_got[0], results).astype(F32)
        two = pick(high, side_x) + after(b_got[1], results).astype(F32)
        one_keep, one_send = half_of(one, 1)
        b_sends = one_send, two[1].astype(BF16)
        b_part = [one_keep + swap(one_send, "dp", 1).astype(F32), two[0] + swap(b_sends[1], "head", 2).astype(F32)]
        b_part = jnp.concatenate(b_part, axis=0)
    else:
        b_part = halve(jnp.concatenate([b_live, c_live], axis=0))
    gain_rows = gain_part[: depth // span].reshape(depth // wide, wide)
    b_part = jnp.concatenate([b_part, gain_rows, jnp.zeros((32 - gain_rows.shape[0], wide), F32)], axis=0)
    a_low = (a_keep_z + after(a_got_z, results).astype(F32)).astype(BF16)
    a_got_y = swap(a_low, "dp", 4)
    a_low = whole_dp((a_low.astype(F32) + after(a_got_y, b_sends).astype(F32)).astype(BF16))
    b_keep_z, b_send_z = half_of(b_part, 2)
    b_got_z = swap(after(b_send_z, a_low), "dp", 2)
    a_got_z = swap(a_low, "dp", 2)
    (mixed,) = call(
        functools.partial(mixed_kernel, pieces, blocks),
        [((rows, depth), BF16)],
        [scalars, hidden, after(ny, a_low, b_send_z), *all_outs],
        pin=jax.ShapeDtypeStruct,
        cost=4,
        mib=FINAL,
    )
    b_low = (b_keep_z + after(b_got_z, a_low, mixed).astype(F32)).astype(BF16)
    b_got_y = swap(b_low, "dp", 4)
    a_all = both_of(a_low, 2, a_got_z)
    a_other = swap(a_all, "dp", 1)
    b_low = whole_dp((b_low.astype(F32) + after(b_got_y, a_all).astype(F32)).astype(BF16))
    b_all = both_of(b_low, 2, swap(b_low, "dp", 2))

    def unhalve(value, cuts, other=None):
        upper = (lax.axis_index("dp") & 1) != 0
        other = swap(value, "dp", 1) if other is None else other
        rows_out, begin = [], 0
        for count in cuts:
            mine, his = value[begin : begin + count], other[begin : begin + count]
            rows_out.append(jnp.concatenate([jnp.where(upper, his, mine), jnp.where(upper, mine, his)], axis=0))
            begin += count
        return rows_out

    b_all = after(b_all, a_other)
    a_cuts = [depth // 2, depth // 2] if plain else [depth]
    a_out, a_gate = unhalve(a_all, a_cuts, a_other) if plain else jnp.split(unhalve(a_all, a_cuts, a_other)[0], 2)
    grad_out = a_out.T.astype(F32)
    grad_gate = a_gate.astype(F32)
    cut = b_all.shape[0] - 32 - 256
    *b_rows, gain_all = unhalve(b_all[cut:], [256, 32])
    if plain:
        begin = depth + 32 - 2 * cut
        own_rows = b_rows[-1][begin : begin + share_rows, :side]
        b_rows = unhalve(b_all[:cut], [cut], after(swap(b_all[:cut], "dp", 1), own_rows)) + b_rows
    else:
        b_rows = unhalve(b_all[:cut], [cut]) + b_rows
    if not plain:
        *b_rows, gain_all = unhalve(b_all, [cut + 256, 32])
    b_all = jnp.concatenate(b_rows, axis=0)
    gain_all = (gain_all[:32].astype(F32) + gain_all[32:].astype(F32))[: depth // wide].reshape(1, depth)
    gain_all = jnp.pad(gain_all.reshape(-1, side), ((0, 16 - depth // side), (0, 0)))
    grad_value = b_all[:depth].astype(F32)
    small = b_all[depth:].astype(F32)
    grad_step = jnp.concatenate([small[8 + j * share : 8 + (j + 1) * share].T for j in range(depth // wide)], axis=0)
    if plain:
        own = own_rows
    else:
        own = b_all[depth + 32 : depth + 240].reshape(-1)[: share_rows * side].reshape(share_rows, side)
    smaller = (grad_value, grad_step, small[0:4], small[4], small[5], *[small[24 : 24 + share, at] for at in range(3)])
    stacked, members = own, [0]
    for mask in reversed(order):
        members += [p | mask for p in members]
        gain_low = gain_all.astype(BF16)
        sent = jnp.concatenate([stacked, gain_low], axis=0)
        got = swap(after(sent, smaller if mask == 1 else (grad_out, grad_gate, grad_hidden)), "head", mask)
        stacked = jnp.concatenate([stacked, got[: stacked.shape[0]]], axis=0)
        gain_all = gain_low.astype(F32) + got[-16:].astype(F32)
    stacked = stacked.reshape(ways, share_rows, side)
    stacked = jnp.stack([stacked[members.index(p)] for p in range(ways)])
    full = jnp.concatenate([pick(stacked, me ^ q) for q in range(ways)], axis=0).astype(F32)
    return (
        mixed,
        grad_hidden,
        gain_all[: depth // side].reshape(-1),
        grad_gate,
        smaller[0],
        full[:depth],
        smaller[1],
        smaller[2],
        smaller[3],
        full[depth : depth + 4],
        full[depth + 4],
        smaller[5],
        smaller[6],
        smaller[7],
        smaller[4],
        grad_out,
    )


def solution(mesh):
    rows = P(("dp", "head"), None)
    in_specs = (
        rows, P("dp", None), P(), P(None, "head"), P(None, "head"), P(), P(None, "head"), P(None, "head"),
        P("head"), P(), P(), P("head"), P("head"), P("head"), P("head"), P("head", None), rows,
    )
    out_specs = (
        rows, rows, P(), P(None, "head"), P(None, "head"), P(), P(None, "head"), P(None, "head"),
        P("head"), P(), P(), P("head"), P("head"), P("head"), P("head"), P("head", None),
    )
    return jax.shard_map(body, mesh=mesh, in_specs=in_specs, out_specs=out_specs, check_vma=False)
```
